32 devices in a mesh: ctx: 4 (over z), fsdp: 8 (over y, x, core).
Axes of the slice: x: 2, y: 2, z: 4, core: 2. Of those that a mesh axis runs over, the one named last changes fastest.
Arguments:
- tokens: bfloat16 [8, 1024, 2048], P('fsdp', 'ctx'), may hold values from -6 to 6
- routes: int32 [8, 1024, 6], P('fsdp', 'ctx'), may hold values from 0 to 15, all different within a row; in each aligned block of 256 rows (0 to 255, 256 to 511, ..., all dimensions but the last counted through in order) at most 128 rows name the same one
- gate_values: float32 [8, 1024, 6], P('fsdp', 'ctx'), may hold values from 1 to 2
- cotangent: bfloat16 [8, 1024, 2048], P('fsdp', 'ctx'), may hold values from -6 to 6
- attention_gain: bfloat16 [2048], P(('ctx', 'fsdp')), may hold values from 0.5 to 1.5
- query_weight: bfloat16 [2048, 3072], P(('ctx', 'fsdp')), may hold values from -0.125 to 0.125
- latent_weight: bfloat16 [2048, 576], P(('ctx', 'fsdp')), may hold values from -0.125 to 0.125
- latent_gain: bfloat16 [512], P(('ctx', 'fsdp')), may hold values from 0.5 to 1.5
- expand_weight: bfloat16 [512, 4096], P(('ctx', 'fsdp')), may hold values from -0.25 to 0.25
- output_weight: bfloat16 [2048, 2048], P(('ctx', 'fsdp')), may hold values from -2 to 2
- feedforward_gain: bfloat16 [2048], P(('ctx', 'fsdp')), may hold values from 0.5 to 1.5
- shared_gate: bfloat16 [2048, 2816], P(('ctx', 'fsdp')), may hold values from -0.125 to 0.125
- shared_up: bfloat16 [2048, 2816], P(('ctx', 'fsdp')), may hold values from -0.125 to 0.125
- shared_down: bfloat16 [2816, 2048], P(('ctx', 'fsdp')), may hold values from -0.109375 to 0.109375
- expert_gate: bfloat16 [16, 2048, 1408], P('fsdp', 'ctx'), may hold values from -0.125 to 0.125
- expert_up: bfloat16 [16, 2048, 1408], P('fsdp', 'ctx'), may hold values from -0.125 to 0.125
- expert_down: bfloat16 [16, 1408, 2048], P('fsdp', None, 'ctx'), may hold values from -0.3125 to 0.3125
Outputs:
- layer_out: bfloat16 [8, 1024, 2048], P('fsdp', 'ctx')
- tokens_grad: float32 [8, 1024, 2048], P('fsdp', 'ctx')
- attention_gain_grad: float32 [2048], P(('ctx', 'fsdp'))
- query_weight_grad: float32 [2048, 3072], P(('ctx', 'fsdp'))
- latent_weight_grad: float32 [2048, 576], P(('ctx', 'fsdp'))
- latent_gain_grad: float32 [512], P(('ctx', 'fsdp'))
- expand_weight_grad: float32 [512, 4096], P(('ctx', 'fsdp'))
- output_weight_grad: float32 [2048, 2048], P(('ctx', 'fsdp'))
- feedforward_gain_grad: float32 [2048], P(('ctx', 'fsdp'))
- shared_gate_grad: float32 [2048, 2816], P(('ctx', 'fsdp'))
- shared_up_grad: float32 [2048, 2816], P(('ctx', 'fsdp'))
- shared_down_grad: float32 [2816, 2048], P(('ctx', 'fsdp'))
- expert_gate_grad: float32 [16, 2048, 1408], P('fsdp', 'ctx')
- expert_up_grad: float32 [16, 2048, 1408], P('fsdp', 'ctx')
- expert_down_grad: float32 [16, 1408, 2048], P('fsdp', None, 'ctx')
The draws below stay inside these ranges and needn't reach their ends.
Inputs may be any that keep to these rules, and one draw needn't show every extreme that they name: `routes`: each row names 6 different experts. Among the 256 rows of one device no expert is named by more than 128 rows, and in some device some expert is named by exactly 128.
All inputs are finite; a program needn't handle non-finite values.
Results may differ from the reference program's by a relative error of at most 0.025.
Values may be sent and summed in bfloat16 or wider, within the bound.
A program may use at most 448 MiB of HBM per device.

```python
import math
import jax
import jax.numpy as jnp
import numpy as np
from jax import lax

D = 2048
HEADS = 16
NOPE = 128
ROPE = 64
LATENT = 512
VDIM = 128
FF = 1408
SFF = 2816
TOP = 6
LEN = 1024
BATCH = 8
TOK_DEV = 256
EXPERTS = 16
CAP = 128
N_CTX = 4


def level_of(key, extent, cuts, low, top_value):
    level = 1.0
    for dim, blocks in cuts:
        heights = jax.random.uniform(jax.random.fold_in(jax.random.fold_in(key, 6), dim), (blocks,), jnp.float32, low / len(cuts), top_value / len(cuts))
        level = level * jnp.repeat(jnp.exp(heights), extent[dim] // blocks).reshape((-1,) + (1,) * (len(extent) - 1 - dim))
    return level


def deal_out(key, own, number, rows, number_of, top, limit, slope):
    sequence = jax.random.permutation(key, number_of)
    packed, common = load_shares(number_of, rows * top, limit, slope, True), load_shares(number_of, rows * top, limit, slope, False)
    places = jnp.arange(number_of)

    def named(sizes, turn):
        used = int((sizes > 0).sum())
        fixed = max(1, used // 4)
        moved = fixed + (places - fixed + turn * (used - fixed)) % max(1, number_of - fixed)
        return jnp.zeros((number_of,), jnp.int32).at[sequence[jnp.where(places < fixed, places, moved)]].set(jnp.asarray(sizes, jnp.int32))

    sizes = jnp.where(number % 4 == 0, named(packed, number // 4), named(common, number - number // 4 - 1))
    mixed = jax.random.permutation(jax.random.fold_in(own, 3), number_of)
    giver, receiver = mixed[0:number_of // 2 * 2:2], mixed[1:number_of // 2 * 2:2]
    margin = jnp.minimum(sizes[giver] - 1, limit - sizes[receiver]) // 2
    margin = jnp.where((giver == sequence[0]) | (receiver == sequence[0]) | (sizes[receiver] == 0), 0, jnp.maximum(margin, 0))
    moved = jax.random.randint(jax.random.fold_in(own, 4), (number_of // 2,), 0, 1 << 20) % (margin + 1)
    sizes = sizes.at[giver].add(-moved).at[receiver].add(moved)
    labels = jnp.searchsorted(jnp.cumsum(sizes), jnp.arange(rows * top), side="right").astype(jnp.int32)
    grid = labels.reshape(top, rows).T
    grid = grid[jax.random.permutation(jax.random.fold_in(own, 1), rows)]
    turn = jax.random.randint(jax.random.fold_in(own, 2), (rows, 1), 0, top)
    return jnp.take_along_axis(grid, (jnp.arange(top)[None, :] + turn) % top, axis=1)


def load_shares(number_of, total, bound, slope, full):
    loads = [(1 << 20) // math.isqrt(standing ** slope) + 1 for standing in range(1, number_of + 1)]
    largest = bound if full else min(bound, max(-(-total // number_of), total * loads[0] // sum(loads)))
    least = 1 if total - largest >= number_of - 1 else 0
    holding, spare = [largest] + [least] * (number_of - 1), total - largest - least * (number_of - 1)
    while spare > 0:
        free = [i for i in range(1, number_of) if holding[i] < largest] or [i for i in range(1, number_of) if holding[i] < bound]
        pool, left = sum([loads[i] for i in free]), spare
        for i in free:
            more = min(bound - holding[i], max(1, left * loads[i] // pool), spare)
            holding[i] = holding[i] + more
            spare = spare - more
    return np.array(holding)


def noise(stream_key, extent, scale, reach, cuts=(), held_as=jnp.bfloat16):
    entries = jax.random.normal(stream_key, extent, jnp.float32) * scale
    if len(cuts) > 0:
        entries = level_of(stream_key, extent, cuts, -0.22, 0.18) * entries
    return jnp.clip(entries, min=-reach, max=reach).astype(held_as)


def setup_inputs(seed: int = 0) -> dict:
    seeds = jax.random.split(jax.random.key(seed), 18)
    tokens = noise(seeds[0], (BATCH, LEN, D), 1.0, 6.0, ((0, 8), (1, 4)))
    routes_keys = jax.random.split(jax.random.fold_in(seeds[1], 1), BATCH * LEN // TOK_DEV)
    routes_turns = jax.random.permutation(jax.random.fold_in(seeds[1], 3), BATCH * LEN // TOK_DEV)
    routes = jax.vmap(lambda own, number: deal_out(jax.random.fold_in(seeds[1], 2), own, number, TOK_DEV, EXPERTS, TOP, CAP, 1))(routes_keys, routes_turns).reshape((BATCH, LEN, TOP))
    gate_values = jnp.clip(1.0 + 1.0 * jax.random.uniform(seeds[2], (BATCH, LEN, TOP), jnp.float32) ** level_of(seeds[2], (BATCH, LEN, TOP), ((0, 8), (1, 4)), -0.2, 0.2), 1.0, 2.0)
    cotangent = noise(seeds[3], (BATCH, LEN, D), 1.0, 6.0, ((0, 8), (1, 4)))
    attention_gain = jnp.clip(1.0 + 0.1 * jax.random.normal(seeds[4], (D,), jnp.float32), 0.5, 1.5).astype(jnp.bfloat16)
    query_weight = noise(seeds[5], (D, HEADS * (NOPE + ROPE)), D ** -0.5, 0.125, ((0, 32),))
    latent_weight = noise(seeds[6], (D, LATENT + ROPE), D ** -0.5, 0.125, ((0, 32),))
    latent_gain = jnp.clip(1.0 + 0.1 * jax.random.normal(seeds[7], (LATENT,), jnp.float32), 0.5, 1.5).astype(jnp.bfloat16)
    expand_weight = noise(seeds[8], (LATENT, HEADS * (NOPE + VDIM)), LATENT ** -0.5, 0.25, ((0, 32),))
    output_weight = noise(seeds[9], (HEADS * VDIM, D), (max(HEADS * VDIM // 256, 1)) ** -0.5, 2.0, ((0, 32),))
    feedforward_gain = jnp.clip(1.0 + 0.1 * jax.random.normal(seeds[10], (D,), jnp.float32), 0.5, 1.5).astype(jnp.bfloat16)
    shared_gate = noise(seeds[11], (D, SFF), D ** -0.5, 0.125, ((0, 32),))
    shared_up = noise(seeds[12], (D, SFF), D ** -0.5, 0.125, ((0, 32),))
    shared_down = noise(seeds[13], (SFF, D), SFF ** -0.5, 0.109375, ((0, 32),))
    expert_gate = noise(seeds[14], (EXPERTS, D, FF), D ** -0.5, 0.125, ((0, 8), (1, 4)))
    expert_up = noise(seeds[15], (EXPERTS, D, FF), D ** -0.5, 0.125, ((0, 8), (1, 4)))
    expert_down = noise(seeds[16], (EXPERTS, FF, D), (max(FF // 4, 1)) ** -0.5, 0.3125, ((0, 8), (2, 4)))
    return {"tokens": tokens, "routes": routes, "gate_values": gate_values, "cotangent": cotangent, "attention_gain": attention_gain, "query_weight": query_weight, "latent_weight": latent_weight, "latent_gain": latent_gain, "expand_weight": expand_weight, "output_weight": output_weight, "feedforward_gain": feedforward_gain, "shared_gate": shared_gate, "shared_up": shared_up, "shared_down": shared_down, "expert_gate": expert_gate, "expert_up": expert_up, "expert_down": expert_down}


@jax.custom_vjp
def low(v):
    return lax.optimization_barrier(v.astype(jnp.bfloat16)).astype(jnp.float32)

@jax.custom_vjp
def low_back(v):
    return v

def low_keep(v):
    return (low(v), None)

def low_pass(kept, grad):
    return (grad,)

def back_keep(v):
    return (v, None)

def back_low(kept, grad):
    return (low(grad),)
low.defvjp(low_keep, low_pass)
low_back.defvjp(back_keep, back_low)
highest = lax.Precision.HIGHEST
epsilon = 1e-06
rope_base = 10000.0
masked_score = -1e+30

def stored_positions(row_index, per_device, block_count):
    device = row_index // per_device
    within = row_index % per_device
    half_block = per_device // 2
    return jnp.where(within >= half_block, (block_count - 1 - device) * half_block + within - half_block, device * half_block + within)

def rotary(values, positions, direction):
    half_rope = values.shape[-1] // 2
    frequency = rope_base ** (-jnp.arange(half_rope, dtype=jnp.float32) / half_rope)
    angles = positions.astype(jnp.float32)[:, None] * frequency[None, :]
    cosine_table = jnp.cos(angles)
    sine_table = direction * jnp.sin(angles)
    if values.ndim == 3:
        cosine_table = cosine_table[:, None, :]
        sine_table = sine_table[:, None, :]
    front_half = values[..., :half_rope]
    back_half = values[..., half_rope:]
    return jnp.concatenate([front_half * cosine_table - back_half * sine_table, back_half * cosine_table + front_half * sine_table], axis=-1)

def root_norm(values, gain):
    return values * lax.rsqrt(lax.optimization_barrier(jnp.mean(values * values, axis=-1, keepdims=True)) + epsilon) * gain

def attend_sequence(normed_seq, query_weight, latent_weight, latent_gain, expand_weight, output_weight):
    positions = stored_positions(jnp.arange(LEN, dtype=jnp.int32), TOK_DEV, 2 * N_CTX)
    query_raw = low_back(jnp.dot(normed_seq, query_weight, precision=highest)).reshape(LEN, HEADS, NOPE + ROPE)
    query_nope = low(query_raw[:, :, :NOPE])
    query_rope = low(rotary(query_raw[:, :, NOPE:], positions, 1.0))
    latent_raw = low_back(jnp.dot(normed_seq, latent_weight, precision=highest))
    latent_norm = low(root_norm(latent_raw[:, :LATENT], latent_gain))
    key_rope = low(rotary(latent_raw[:, LATENT:], positions, 1.0))
    expand = expand_weight.reshape(LATENT, HEADS, NOPE + VDIM)
    query_latent = low(low_back(jnp.einsum('thd,chd->thc', query_nope, expand[:, :, :NOPE], precision=highest)))
    raw_scores = jnp.einsum('thc,kc->htk', query_latent, latent_norm, precision=highest) + jnp.einsum('thd,kd->htk', query_rope, key_rope, precision=highest)
    scores = low_back(raw_scores) * (NOPE + ROPE) ** (-0.5)
    allowed = positions[None, :, None] >= positions[None, None, :]
    scores = jnp.where(allowed, scores, masked_score)
    soft_weights = low(jax.nn.softmax(scores, axis=-1))
    latent_out = low(low_back(jnp.einsum('htk,kc->thc', soft_weights, latent_norm, precision=highest)))
    values_out = low(low_back(jnp.einsum('thc,chv->thv', latent_out, expand[:, :, NOPE:], precision=highest))).reshape(LEN, HEADS * VDIM)
    return low_back(jnp.dot(values_out, output_weight, precision=highest))

def expert_branch(flat_second, member_weight, gate_matrix, up_matrix, down_matrix):
    arrived = low_back(flat_second)
    gate_pre = low_back(jnp.dot(arrived, gate_matrix, precision=highest))
    up_pre = low_back(jnp.dot(arrived, up_matrix, precision=highest))
    hidden_act = low(jax.nn.silu(gate_pre) * up_pre)
    result = low(low_back(jnp.dot(hidden_act, down_matrix, precision=highest)))
    return member_weight[:, None] * result

def layer_forward(tokens, routes, gate_values, attention_gain, query_weight, latent_weight, latent_gain, expand_weight, output_weight, feedforward_gain, shared_gate, shared_up, shared_down, expert_gate, expert_up, expert_down):
    normed = low(root_norm(tokens, attention_gain))

    def one_sequence(normed_seq):
        return attend_sequence(normed_seq, query_weight, latent_weight, latent_gain, expand_weight, output_weight)
    attended = lax.map(jax.checkpoint(one_sequence), normed)
    middle = tokens + attended
    second = low(root_norm(middle, feedforward_gain))
    flat_second = second.reshape(BATCH * LEN, D)
    shared_g = low_back(jnp.dot(flat_second, shared_gate, precision=highest))
    shared_u = low_back(jnp.dot(flat_second, shared_up, precision=highest))
    shared_hidden = low(jax.nn.silu(shared_g) * shared_u)
    shared_out = jnp.dot(shared_hidden, shared_down, precision=highest)
    flat_routes = routes.reshape(BATCH * LEN, TOP)
    flat_gates = gate_values.reshape(BATCH * LEN, TOP)

    def branch_of(expert_index, gate_matrix, up_matrix, down_matrix):
        member_weight = lax.optimization_barrier(jnp.sum(jnp.where(flat_routes == expert_index, flat_gates, 0.0), axis=-1))
        return expert_branch(flat_second, member_weight, gate_matrix, up_matrix, down_matrix)
    saved_branch = jax.checkpoint(branch_of)

    def expert_step(running, pieces):
        return (running + saved_branch(pieces[0], pieces[1], pieces[2], pieces[3]), None)
    routed, unused = lax.scan(expert_step, jnp.zeros_like(flat_second), (jnp.arange(EXPERTS, dtype=jnp.int32), expert_gate, expert_up, expert_down))
    return middle + (shared_out + routed).reshape(BATCH, LEN, D)

def reference(tokens, routes, gate_values, cotangent, attention_gain, query_weight, latent_weight, latent_gain, expand_weight, output_weight, feedforward_gain, shared_gate, shared_up, shared_down, expert_gate, expert_up, expert_down):

    def forward_of(tokens_f, attention_gain_f, query_weight_f, latent_weight_f, latent_gain_f, expand_weight_f, output_weight_f, feedforward_gain_f, shared_gate_f, shared_up_f, shared_down_f, expert_gate_f, expert_up_f, expert_down_f):
        return layer_forward(tokens_f, routes, gate_values, attention_gain_f, query_weight_f, latent_weight_f, latent_gain_f, expand_weight_f, output_weight_f, feedforward_gain_f, shared_gate_f, shared_up_f, shared_down_f, expert_gate_f, expert_up_f, expert_down_f)
    inputs = (tokens, attention_gain, query_weight, latent_weight, latent_gain, expand_weight, output_weight, feedforward_gain, shared_gate, shared_up, shared_down, expert_gate, expert_up, expert_down)
    inputs = tuple((item.astype(jnp.float32) for item in inputs))
    layer_value, pullback = jax.vjp(forward_of, *inputs)
    grads = pullback(cotangent.astype(jnp.float32))
    return (layer_value.astype(jnp.bfloat16), grads[0], grads[1], grads[2], grads[3], grads[4], grads[5], grads[6], grads[7], grads[8], grads[9], grads[10], grads[11], grads[12], grads[13])
```

```python
import functools

import jax
import jax.numpy as jnp
from jax import lax
from jax.experimental import pallas as pl
from jax.experimental.pallas import tpu as pltpu
from jax.sharding import PartitionSpec as P

HEADS = 16
NOPE = 128
ROPE = 64
LATENT = 512
VDIM = 128
TOP = 6
EXP_DEV = 2


epsilon = 1e-06
rope_base = 10000.0
masked_score = -1e30


def stored_positions(row_index, per_device, block_count):
    device = row_index // per_device
    within = row_index % per_device
    half_block = per_device // 2
    return jnp.where(
        within >= half_block,
        (block_count - 1 - device) * half_block + within - half_block,
        device * half_block + within,
    )


def rotary(values, positions, direction):
    half_rope = values.shape[-1] // 2
    frequency = rope_base ** (-jnp.arange(half_rope, dtype=jnp.float32) / half_rope)
    angles = positions.astype(jnp.float32)[:, None] * frequency[None, :]
    cosine_table = jnp.cos(angles)
    sine_table = direction * jnp.sin(angles)
    if values.ndim == 3:
        cosine_table = cosine_table[:, None, :]
        sine_table = sine_table[:, None, :]
    front_half = values[..., :half_rope]
    back_half = values[..., half_rope:]
    return jnp.concatenate(
        [
            front_half * cosine_table - back_half * sine_table,
            back_half * cosine_table + front_half * sine_table,
        ],
        axis=-1,
    )


def norm_forward(values):
    inverse = lax.rsqrt(jnp.mean(values * values, axis=-1, keepdims=True) + epsilon)
    return (values * inverse, inverse)


def norm_backward(normed_grad, plain, inverse, gain):
    gain_grad = jnp.sum(normed_grad * plain, axis=0)
    scaled = normed_grad * gain
    return (
        inverse * (scaled - plain * jnp.mean(scaled * plain, axis=-1, keepdims=True)),
        gain_grad,
    )


def silu_slope(values):
    sigma = jax.nn.sigmoid(values)
    return (values * sigma, sigma * (1.0 + values * (1.0 - sigma)))


def score_block(query_latent, query_rope, all_latent, all_keys, allowed, score_scale):
    raw_scores = jnp.einsum(
        "thc,kc->htk", query_latent, all_latent, preferred_element_type=jnp.float32
    ) + jnp.einsum("thd,kd->htk", query_rope, all_keys, preferred_element_type=jnp.float32)
    return jnp.where(allowed[None], raw_scores * score_scale, masked_score)


LOW = jnp.bfloat16
FULL = jnp.float32


MESH_ID = pl.DeviceIdType.MESH
BIG_VMEM = 60 * 1024 * 1024


def flip(index, bit):
    return index + bit - 2 * bit * lax.rem(lax.div(index, bit), 2)


def toggled(index, mask):
    for bit in (1, 2, 4):
        if mask & bit:
            index = flip(index, bit)
    return index


def nearest(z, step):
    upper = lax.div(z, 2)
    if step == 0:
        return z
    if step == 1:
        return z + 1 - 2 * upper
    if step == 2:
        return 2 - 2 * lax.rem(z, 2) + upper
    return 3 - 3 * upper


def remote(source, target, send, receive, z, f):
    return pltpu.make_async_remote_copy(
        src_ref=source,
        dst_ref=target,
        send_sem=send,
        recv_sem=receive,
        device_id={"ctx": z, "fsdp": f},
        device_id_type=MESH_ID,
    )


def greet(z, f, masks, ctx_count):
    barrier = pltpu.get_barrier_semaphore()
    for mask in masks:
        pl.semaphore_signal(
            barrier,
            inc=1,
            device_id={"ctx": z, "fsdp": toggled(f, mask)},
            device_id_type=MESH_ID,
        )

    @pl.when(z > 0)
    def _():
        pl.semaphore_signal(
            barrier, inc=1, device_id={"ctx": z - 1, "fsdp": f}, device_id_type=MESH_ID
        )

    @pl.when(z < ctx_count - 1)
    def _():
        pl.semaphore_signal(
            barrier, inc=1, device_id={"ctx": z + 1, "fsdp": f}, device_id_type=MESH_ID
        )

    along = lax.div(z + ctx_count - 1, ctx_count) + lax.div(2 * ctx_count - 2 - z, ctx_count)
    pl.semaphore_wait(barrier, len(masks) + along)


def both_ways(z, block, ctx_count, act):
    @pl.when((block <= z) & (z < ctx_count - 1))
    def _():
        act(0, z + 1)

    @pl.when((block >= z) & (z > 0))
    def _():
        act(1, z - 1)


def gather_kernel(
    ctx_count, shard_ref, out_ref, own_sem, z_send, z_recv, p_send, p_recv, c_send, c_recv
):
    z, f = lax.axis_index("ctx"), lax.axis_index("fsdp")
    core, x_near, y_near = flip(f, 1), flip(f, 2), flip(f, 4)
    far = flip(x_near, 4)
    half = shard_ref.shape[0] // 2
    upper, lower = pl.ds(0, half), pl.ds(half, half)
    greet(z, f, (1, 2, 4), ctx_count)
    own = pltpu.make_async_copy(shard_ref, out_ref.at[z, f], own_sem)
    own.start()
    own.wait()

    def z_copy(block, way, target):
        at = out_ref.at[block, f]
        return remote(at, at, z_send.at[block, way], z_recv.at[block], target, f)

    def p_copy(block, which):
        at = (
            out_ref.at[block, f],
            out_ref.at[block, f],
            out_ref.at[block, x_near, upper],
            out_ref.at[block, y_near, lower],
        )[which]
        to = (x_near, y_near, y_near, x_near)[which]
        return remote(at, at, p_send.at[block, which], p_recv.at[block, which], z, to)

    def p_arrived(block, which):
        at = (
            out_ref.at[block, x_near],
            out_ref.at[block, y_near],
            out_ref.at[block, far, upper],
            out_ref.at[block, far, lower],
        )[which]
        remote(at, at, p_send.at[block, which], p_recv.at[block, which], z, x_near).wait_recv()

    def c_copy(block, which):
        at = out_ref.at[block, (f, x_near, y_near, far)[which]]
        return remote(at, at, c_send.at[block, which], c_recv.at[block, which], z, core)

    def c_arrived(block, which):
        at = out_ref.at[block, flip((f, x_near, y_near, far)[which], 1)]
        remote(at, at, c_send.at[block, which], c_recv.at[block, which], z, core).wait_recv()

    def first(step):
        block = nearest(z, step)
        if step > 0:
            at = out_ref.at[block, f]
            remote(at, at, z_send.at[block, 0], z_recv.at[block], z, core).wait_recv()
        both_ways(z, block, ctx_count, lambda way, to: z_copy(block, way, to).start())
        p_copy(block, 0).start()
        p_copy(block, 1).start()
        c_copy(block, 0).start()

    def second(step):
        block = nearest(z, step)
        for which in (0, 1):
            p_arrived(block, which)
            p_copy(block, which + 2).start()
            c_copy(block, which + 1).start()

    def third(step):
        block = nearest(z, step)
        p_arrived(block, 2)
        p_arrived(block, 3)
        c_copy(block, 3).start()

    for step in range(ctx_count + 2):
        if step < ctx_count:
            first(step)
        if 0 <= step - 1 < ctx_count:
            second(step - 1)
        if 0 <= step - 2 < ctx_count:
            third(step - 2)
    for step in range(ctx_count):
        block = nearest(z, step)
        for which in range(4):
            c_arrived(block, which)
    for step in range(ctx_count):
        block = nearest(z, step)
        both_ways(z, block, ctx_count, lambda way, to: z_copy(block, way, to).wait_send())
        for which in range(4):
            p_copy(block, which).wait_send()
            c_copy(block, which).wait_send()


def gather_dense(shard, ctx_count, fsdp_count):
    rows, width = shard.shape
    dma = pltpu.SemaphoreType.DMA
    out = pl.pallas_call(
        functools.partial(gather_kernel, ctx_count),
        out_shape=jax.ShapeDtypeStruct((ctx_count, fsdp_count, rows, width), shard.dtype),
        in_specs=[pl.BlockSpec(memory_space=pl.ANY)],
        out_specs=pl.BlockSpec(memory_space=pl.ANY),
        scratch_shapes=[
            dma,
            dma((ctx_count, 2)),
            dma((ctx_count,)),
            dma((ctx_count, 4)),
            dma((ctx_count, 4)),
            dma((ctx_count, 4)),
            dma((ctx_count, 4)),
        ],
        compiler_params=pltpu.CompilerParams(collective_id=0, has_side_effects=True),
        cost_estimate=pl.CostEstimate(flops=0, bytes_accessed=400_000_000, transcendentals=0),
    )(shard)
    return out.reshape(ctx_count * fsdp_count * rows, width)


def add_rows(target, rows, *terms):
    @pl.loop(0, rows, step=16)
    def _(start):
        part = pl.ds(pl.multiple_of(start, 16), 16)
        total = terms[0][part, :].astype(FULL)
        for term in terms[1:]:
            total = total + term[part, :].astype(FULL)
        target[part, :] = total.astype(target.dtype)


def scatter_kernel(
    ctx_count,
    grad_ref,
    out_ref,
    mine,
    from_core,
    from_x,
    from_y,
    half_x,
    half_y,
    from_z,
    load_sem,
    c_send,
    c_recv,
    p_send,
    p_recv,
    z_send,
    z_recv,
):
    z, f = lax.axis_index("ctx"), lax.axis_index("fsdp")
    side = lax.rem(f, 2)
    chip = lax.div(f, 2)
    core, x_near, y_near = flip(f, 1), flip(f, 2), flip(f, 4)
    x_chip, y_chip = flip(chip, 1), flip(chip, 2)
    far_chip = flip(x_chip, 2)
    rows = out_ref.shape[0]
    half = rows // 2
    upper, lower = pl.ds(0, half), pl.ds(half, half)
    greet(z, f, (1, 2, 4), ctx_count)

    def load(block):
        return pltpu.make_async_copy(
            grad_ref.at[block, :, side], mine.at[block], load_sem.at[block]
        )

    def c_copy(block):
        return remote(
            grad_ref.at[block, :, 1 - side],
            from_core.at[block],
            c_send.at[block],
            c_recv.at[block],
            z,
            core,
        )

    def p_copy(block, which):
        source, target, to = (
            (mine.at[block, far_chip, upper], half_y.at[block], y_near),
            (mine.at[block, far_chip, lower], half_x.at[block], x_near),
            (mine.at[block, x_chip], from_x.at[block], x_near),
            (mine.at[block, y_chip], from_y.at[block], y_near),
        )[which]
        return remote(source, target, p_send.at[block, which], p_recv.at[block, which], z, to)

    def z_copy(block, way, target):
        return remote(
            mine.at[block, chip],
            from_z.at[way, block],
            z_send.at[block],
            z_recv.at[way, block],
            target,
            f,
        )

    def z_arrived(block, way):
        at = from_z.at[way, block]
        remote(at, at, z_send.at[block], z_recv.at[way, block], z, core).wait_recv()

    order = [nearest(z, ctx_count - 1 - step) for step in range(ctx_count)]

    def first(step):
        block = order[step]
        load(block).wait()
        c_copy(block).wait_recv()
        add_rows(
            mine.at[block, far_chip], rows, mine.at[block, far_chip], from_core.at[block, far_chip]
        )
        p_copy(block, 0).start()
        p_copy(block, 1).start()

    def second(step):
        block = order[step]
        add_rows(
            mine.at[block, x_chip], rows, mine.at[block, x_chip], from_core.at[block, x_chip]
        )
        add_rows(
            mine.at[block, y_chip], rows, mine.at[block, y_chip], from_core.at[block, y_chip]
        )
        p_copy(block, 0).wait_recv()
        x_upper = mine.at[block, x_chip, upper]
        add_rows(x_upper, half, x_upper, half_y.at[block])
        p_copy(block, 2).start()
        p_copy(block, 1).wait_recv()
        y_lower = mine.at[block, y_chip, lower]
        add_rows(y_lower, half, y_lower, half_x.at[block])
        p_copy(block, 3).start()

    def third(step):
        block = order[step]
        p_copy(block, 2).wait_recv()
        p_copy(block, 3).wait_recv()
        own = mine.at[block, chip]
        terms = (own, from_core.at[block, chip], from_x.at[block], from_y.at[block])
        if step == ctx_count - 1:

            @pl.when(z > 0)
            def _():
                z_arrived(block, 0)

            @pl.when(z < ctx_count - 1)
            def _():
                z_arrived(block, 1)

            @pl.when(z == 0)
            def _():
                add_rows(out_ref, rows, *terms, from_z.at[1, block])

            @pl.when(z == ctx_count - 1)
            def _():
                add_rows(out_ref, rows, *terms, from_z.at[0, block])

            @pl.when((z > 0) & (z < ctx_count - 1))
            def _():
                add_rows(out_ref, rows, *terms, from_z.at[0, block], from_z.at[1, block])

            return

        for way, above in ((1, True), (0, False)):
            heading = (block < z) if above else (block > z)
            has_more = (z < ctx_count - 1) if above else (z > 0)

            @pl.when(heading & has_more)
            def _():
                z_arrived(block, way)
                add_rows(own, rows, *terms, from_z.at[way, block])

            @pl.when(heading & jnp.logical_not(has_more))
            def _():
                add_rows(own, rows, *terms)

            @pl.when(heading)
            def _():
                z_copy(block, way, z - 1 if above else z + 1).start()

    for step in range(ctx_count):
        c_copy(order[step]).start()
        load(order[step]).start()
    for step in range(ctx_count + 2):
        if step < ctx_count:
            first(step)
        if 0 <= step - 1 < ctx_count:
            second(step - 1)
        if 0 <= step - 2 < ctx_count:
            third(step - 2)
    for step in range(ctx_count):
        block = order[step]
        c_copy(block).wait_send()
        for which in range(4):
            p_copy(block, which).wait_send()
        if step < ctx_count - 1:
            z_copy(block, 0, z).wait_send()


def scatter_dense(grad, ctx_count, fsdp_count):
    width = grad.shape[1]
    rows = grad.shape[0] // (ctx_count * fsdp_count)
    dma = pltpu.SemaphoreType.DMA
    chips = fsdp_count // 2
    vmem = lambda *shape: pltpu.VMEM(shape + (width,), LOW)
    return pl.pallas_call(
        functools.partial(scatter_kernel, ctx_count),
        out_shape=jax.ShapeDtypeStruct((rows, width), FULL),
        in_specs=[pl.BlockSpec(memory_space=pl.ANY)],
        out_specs=pl.BlockSpec(memory_space=pltpu.VMEM),
        scratch_shapes=[
            vmem(ctx_count, chips, rows),
            vmem(ctx_count, chips, rows),
            vmem(ctx_count, rows),
            vmem(ctx_count, rows),
            vmem(ctx_count, rows // 2),
            vmem(ctx_count, rows // 2),
            vmem(2, ctx_count, rows),
            dma((ctx_count,)),
            dma((ctx_count,)),
            dma((ctx_count,)),
            dma((ctx_count, 4)),
            dma((ctx_count, 4)),
            dma((ctx_count,)),
            dma((2, ctx_count)),
        ],
        compiler_params=pltpu.CompilerParams(
            collective_id=1, has_side_effects=True, vmem_limit_bytes=BIG_VMEM
        ),
        cost_estimate=pl.CostEstimate(flops=0, bytes_accessed=500_000_000, transcendentals=0),
    )(grad.reshape(ctx_count, chips, 2, rows, width))


PEERS = (6, 7, 2, 4, 3, 5, 1)


def dispatch_kernel(
    ctx_count,
    rows_ref,
    choose_ref,
    all_ref,
    out_ref,
    blocks,
    chosen,
    own_sem,
    all_sem,
    keep_sem,
    z_send,
    z_recv,
    p_send,
    p_recv,
):
    z, f = lax.axis_index("ctx"), lax.axis_index("fsdp")
    width = rows_ref.shape[1]
    groups, share = chosen.shape[1], chosen.shape[2]
    greet(z, f, PEERS, ctx_count)
    own = pltpu.make_async_copy(rows_ref, blocks.at[z], own_sem)
    own.start()
    own.wait()

    def z_copy(block, way, target):
        at = blocks.at[block]
        return remote(at, at, z_send.at[block, way], z_recv.at[block], target, f)

    def p_copy(block, place):
        to = toggled(f, PEERS[place])
        return remote(
            chosen.at[block, to],
            out_ref.at[block, f],
            p_send.at[block, place],
            p_recv.at[block, place],
            z,
            to,
        )

    def p_arrived(block, place):
        at = out_ref.at[block, toggled(f, PEERS[place])]
        remote(at, at, p_send.at[block, place], p_recv.at[block, place], z, flip(f, 1)).wait_recv()

    def keep(block):
        return pltpu.make_async_copy(
            chosen.at[block, f], out_ref.at[block, f], keep_sem.at[block]
        )

    def store(block):
        return pltpu.make_async_copy(blocks.at[block], all_ref.at[block], all_sem.at[block])

    for step in range(ctx_count):
        block = nearest(z, step)
        if step > 0:
            at = blocks.at[block]
            remote(at, at, z_send.at[block, 0], z_recv.at[block], z, flip(f, 1)).wait_recv()
        both_ways(z, block, ctx_count, lambda way, to: z_copy(block, way, to).start())
        store(block).start()

        @pl.loop(0, width, step=256)
        def _(start):
            part = pl.ds(pl.multiple_of(start, 256), 256)
            tile = jnp.dot(
                choose_ref[block], blocks[block, :, part], preferred_element_type=FULL
            ).astype(LOW)
            chosen[block, :, :, part] = tile.reshape(groups, share, 256)

        for place in range(len(PEERS)):
            p_copy(block, place).start()
        keep(block).start()
    for step in range(ctx_count):
        block = nearest(z, step)
        store(block).wait()
        keep(block).wait()
        for place in range(len(PEERS)):
            p_arrived(block, place)
    for step in range(ctx_count):
        block = nearest(z, step)
        both_ways(z, block, ctx_count, lambda way, to: z_copy(block, way, to).wait_send())
        for place in range(len(PEERS)):
            p_copy(block, place).wait_send()


def dispatch_rows(rows, chooser, ctx_count, fsdp_count):
    count, width = rows.shape
    share = chooser.shape[1] // fsdp_count
    dma = pltpu.SemaphoreType.DMA
    return pl.pallas_call(
        functools.partial(dispatch_kernel, ctx_count),
        out_shape=(
            jax.ShapeDtypeStruct((ctx_count, count, width), LOW),
            jax.ShapeDtypeStruct((ctx_count, fsdp_count, share, width), LOW),
        ),
        in_specs=[pl.BlockSpec(memory_space=pl.ANY), pl.BlockSpec(memory_space=pltpu.VMEM)],
        out_specs=(pl.BlockSpec(memory_space=pl.ANY), pl.BlockSpec(memory_space=pl.ANY)),
        scratch_shapes=[
            pltpu.VMEM((ctx_count, count, width), LOW),
            pltpu.VMEM((ctx_count, fsdp_count, share, width), LOW),
            dma,
            dma((ctx_count,)),
            dma((ctx_count,)),
            dma((ctx_count, 2)),
            dma((ctx_count,)),
            dma((ctx_count, len(PEERS))),
            dma((ctx_count, len(PEERS))),
        ],
        compiler_params=pltpu.CompilerParams(
            collective_id=2, has_side_effects=True, vmem_limit_bytes=BIG_VMEM
        ),
        cost_estimate=pl.CostEstimate(
            flops=2_000_000_000, bytes_accessed=300_000_000, transcendentals=0
        ),
    )(rows, chooser)


def combine_kernel(
    ctx_count,
    slots_ref,
    mix_ref,
    extra_ref,
    out_ref,
    arrived,
    extra,
    parts,
    from_z,
    keep_sem,
    extra_sem,
    p_send,
    p_recv,
    z_send,
    z_recv,
):
    z, f = lax.axis_index("ctx"), lax.axis_index("fsdp")
    count, width = out_ref.shape
    slots = mix_ref.shape[2]
    greet(z, f, PEERS, ctx_count)

    def p_copy(block, place):
        to = toggled(f, PEERS[place])
        return remote(
            slots_ref.at[block, to],
            arrived.at[block, f],
            p_send.at[block, place],
            p_recv.at[block, place],
            z,
            to,
        )

    def p_arrived(block, place):
        at = arrived.at[block, toggled(f, PEERS[place])]
        remote(at, at, p_send.at[block, place], p_recv.at[block, place], z, flip(f, 1)).wait_recv()

    def keep(block):
        return pltpu.make_async_copy(
            slots_ref.at[block, f], arrived.at[block, f], keep_sem.at[block]
        )

    def load(block):
        return pltpu.make_async_copy(extra_ref.at[block], extra.at[block], extra_sem.at[block])

    def z_copy(block, way, target):
        return remote(
            parts.at[block],
            from_z.at[way, block],
            z_send.at[block],
            z_recv.at[way, block],
            target,
            f,
        )

    def z_arrived(block, way):
        at = from_z.at[way, block]
        remote(at, at, z_send.at[block], z_recv.at[way, block], z, flip(f, 1)).wait_recv()

    def mix(block, target, *ways):
        @pl.loop(0, width, step=256)
        def _(start):
            part = pl.ds(pl.multiple_of(start, 256), 256)
            total = jnp.dot(
                mix_ref[block],
                arrived[block, :, :, part].reshape(slots, 256),
                preferred_element_type=FULL,
            ) + extra[block, :, part].astype(FULL)
            for way in ways:
                total = total + from_z[way, block, :, part].astype(FULL)
            target[:, part] = total.astype(target.dtype)

    order = [nearest(z, ctx_count - 1 - step) for step in range(ctx_count)]
    for block in order:
        for place in range(len(PEERS)):
            p_copy(block, place).start()
        keep(block).start()
        load(block).start()
    for step in range(ctx_count):
        block = order[step]
        keep(block).wait()
        load(block).wait()
        for place in range(len(PEERS)):
            p_arrived(block, place)
        if step < ctx_count - 1:
            for way, above in ((1, True), (0, False)):
                heading = (block < z) if above else (block > z)
                has_more = (z < ctx_count - 1) if above else (z > 0)

                @pl.when(heading & has_more)
                def _():
                    z_arrived(block, way)
                    mix(block, parts.at[block], way)

                @pl.when(heading & jnp.logical_not(has_more))
                def _():
                    mix(block, parts.at[block])

                @pl.when(heading)
                def _():
                    z_copy(block, way, z - 1 if above else z + 1).start()

        else:

            @pl.when(z > 0)
            def _():
                z_arrived(block, 0)

            @pl.when(z < ctx_count - 1)
            def _():
                z_arrived(block, 1)

            @pl.when(z == 0)
            def _():
                mix(block, out_ref, 1)

            @pl.when(z == ctx_count - 1)
            def _():
                mix(block, out_ref, 0)

            @pl.when((z > 0) & (z < ctx_count - 1))
            def _():
                mix(block, out_ref, 0, 1)

    for step in range(ctx_count):
        block = order[step]
        for place in range(len(PEERS)):
            p_copy(block, place).wait_send()
        if step < ctx_count - 1:
            z_copy(block, 0, z).wait_send()


def combine_rows(slots, mixer, extra, ctx_count, fsdp_count):
    share, width = slots.shape[2:]
    count = mixer.shape[1]
    dma = pltpu.SemaphoreType.DMA
    return pl.pallas_call(
        functools.partial(combine_kernel, ctx_count),
        out_shape=jax.ShapeDtypeStruct((count, width), FULL),
        in_specs=[
            pl.BlockSpec(memory_space=pl.ANY),
            pl.BlockSpec(memory_space=pltpu.VMEM),
            pl.BlockSpec(memory_space=pl.ANY),
        ],
        out_specs=pl.BlockSpec(memory_space=pltpu.VMEM),
        scratch_shapes=[
            pltpu.VMEM((ctx_count, fsdp_count, share, width), LOW),
            pltpu.VMEM((ctx_count, count, width), LOW),
            pltpu.VMEM((ctx_count, count, width), LOW),
            pltpu.VMEM((2, ctx_count, count, width), LOW),
            dma((ctx_count,)),
            dma((ctx_count,)),
            dma((ctx_count, len(PEERS))),
            dma((ctx_count, len(PEERS))),
            dma((ctx_count,)),
            dma((2, ctx_count)),
        ],
        compiler_params=pltpu.CompilerParams(
            collective_id=3, has_side_effects=True, vmem_limit_bytes=BIG_VMEM
        ),
        cost_estimate=pl.CostEstimate(
            flops=2_000_000_000, bytes_accessed=300_000_000, transcendentals=0
        ),
    )(slots, mixer, extra)


def mm(subscripts, left, right):
    return jnp.einsum(subscripts, left, right, preferred_element_type=FULL)


def member_pairs(fsdp_count, members, step):
    return [
        (f, f // members * members + (f % members + step) % members) for f in range(fsdp_count)
    ]


def by_member(own, others, member, members):
    if members == 2:
        first = member == 0
        return jnp.stack([jnp.where(first, own, others[0]), jnp.where(first, others[0], own)])
    stack = jnp.stack([own] + others)
    return jnp.take(stack, (member - jnp.arange(members)) % members, axis=0)


def part_of(array, member, step, members):
    return lax.dynamic_index_in_dim(array, (member + step) % members, 0, keepdims=False)


def swap_parts(array, members, fsdp_count):
    member = lax.axis_index("fsdp") % members
    others = [
        lax.ppermute(
            part_of(array, member, step, members), "fsdp", member_pairs(fsdp_count, members, step)
        )
        for step in range(1, members)
    ]
    return by_member(part_of(array, member, 0, members), others, member, members)


def share_parts(array, members, fsdp_count):
    member = lax.axis_index("fsdp") % members
    others = [
        lax.ppermute(array, "fsdp", member_pairs(fsdp_count, members, step))
        for step in range(1, members)
    ]
    return by_member(array, others, member, members)


def sum_parts(array, members, fsdp_count):
    member = lax.axis_index("fsdp") % members
    total = part_of(array, member, 0, members).astype(FULL)
    for step in range(1, members):
        total = total + lax.ppermute(
            part_of(array, member, step, members), "fsdp", member_pairs(fsdp_count, members, step)
        ).astype(FULL)
    return total.astype(LOW)


def along_line(array):
    return lax.all_to_all(array, "ctx", split_axis=0, concat_axis=0, tiled=True)


def bring_expert(pieces, members, fsdp_count):
    swapped = swap_parts(pieces, members, fsdp_count)
    moved = along_line(swapped.reshape((-1,) + swapped.shape[2:]))
    return share_parts(moved, members, fsdp_count).swapaxes(0, 1)


def return_expert(grad, members, fsdp_count):
    moved = along_line(sum_parts(grad, members, fsdp_count))
    moved = moved.reshape((members, EXP_DEV) + moved.shape[1:])
    return swap_parts(moved, members, fsdp_count).swapaxes(0, 1)


def gather_rows(rows, chooser, ctx_count, fsdp_count):
    if (ctx_count, fsdp_count) == (4, 8):
        return dispatch_rows(rows, chooser, ctx_count, fsdp_count)
    every = lax.all_gather(rows, "ctx", axis=0)
    chosen = mm("bst,btd->bsd", chooser, every).astype(LOW)
    chosen = chosen.reshape(ctx_count, fsdp_count, -1, rows.shape[1])
    return every, lax.all_to_all(chosen, "fsdp", split_axis=1, concat_axis=1, tiled=True)


def return_rows(slots, mixer, extra, ctx_count, fsdp_count, urgent):
    if urgent and (ctx_count, fsdp_count) == (4, 8):
        return combine_rows(slots, mixer, extra.astype(LOW), ctx_count, fsdp_count)
    back = lax.all_to_all(slots, "fsdp", split_axis=1, concat_axis=1, tiled=True)
    back = back.reshape(ctx_count, mixer.shape[2], -1)
    total = (mm("bts,bsd->btd", mixer, back) + extra).astype(LOW)
    return lax.psum_scatter(total, "ctx", scatter_dimension=0, tiled=False).astype(FULL)


def gather_shards(shard, ctx_count, fsdp_count):
    if (ctx_count, fsdp_count) == (4, 8):
        return gather_dense(shard, ctx_count, fsdp_count)
    return lax.all_gather(shard, ("ctx", "fsdp"), axis=0, tiled=True)


def scatter_shards(grad, ctx_count, fsdp_count):
    if (ctx_count, fsdp_count) == (4, 8):
        return scatter_dense(grad, ctx_count, fsdp_count)
    return lax.psum_scatter(grad, ("ctx", "fsdp"), scatter_dimension=0, tiled=True).astype(FULL)


def local(
    tokens,
    routes,
    gate_values,
    cotangent,
    attention_gain,
    query_weight,
    latent_weight,
    latent_gain,
    expand_weight,
    output_weight,
    feedforward_gain,
    shared_gate,
    shared_up,
    shared_down,
    expert_gate,
    expert_up,
    expert_down,
):
    row_count = tokens.shape[1]
    model_width = tokens.shape[2]
    ctx_count = lax.axis_size("ctx")
    fsdp_count = lax.axis_size("fsdp")
    device_count = ctx_count * fsdp_count
    experts_total = EXP_DEV * fsdp_count
    capacity = row_count * TOP * 4 // (3 * experts_total)
    members = ctx_count // EXP_DEV
    plane_experts = experts_total // ctx_count
    plane_slots = plane_experts * capacity
    share = capacity // members
    sequence = ctx_count * row_count
    z = lax.axis_index("ctx")
    score_scale = (NOPE + ROPE) ** (-0.5)
    source = tokens[0].astype(FULL)
    cot_low = cotangent[0]
    cot_full = cot_low.astype(FULL)
    positions = stored_positions(
        z * row_count + jnp.arange(row_count, dtype=jnp.int32), row_count, 2 * ctx_count
    )
    key_positions = stored_positions(
        jnp.arange(sequence, dtype=jnp.int32), row_count, 2 * ctx_count
    )
    allowed = positions[:, None] >= key_positions[None, :]

    dense_rows = latent_weight.shape[0]
    gain_rows = latent_gain.shape[0]
    rotary_end = LATENT + ROPE
    query_end = query_weight.shape[1]
    packed = jnp.concatenate(
        [
            query_weight,
            output_weight,
            expand_weight.reshape(dense_rows, -1),
            latent_weight,
            attention_gain[:, None],
            feedforward_gain[:, None],
            jnp.pad(latent_gain, (0, dense_rows - gain_rows))[:, None],
            jnp.zeros((dense_rows, 61), LOW),
        ],
        axis=1,
    )
    packed = gather_shards(packed, ctx_count, fsdp_count)
    full_query = packed[:, :query_end]
    output_end = query_end + output_weight.shape[1]
    full_output = packed[:, query_end:output_end]
    expand_end = output_end + expand_weight.shape[1] * gain_rows // dense_rows
    full_expand = packed[:, output_end:expand_end].reshape(LATENT, -1)
    tail = packed[:, expand_end:]
    full_latent = tail[:, :rotary_end]
    gain_one = tail[:, rotary_end].astype(FULL)
    gain_two = tail[:, rotary_end + 1].astype(FULL)
    gain_latent = (
        tail[:, rotary_end + 2].reshape(device_count, dense_rows)[:, :gain_rows].reshape(LATENT)
    ).astype(FULL)

    all_routes = lax.all_gather(routes[0], "ctx", axis=0)
    all_gates = lax.all_gather(gate_values[0], "ctx", axis=0)
    expert_index = jnp.arange(experts_total, dtype=jnp.int32)
    member_of = (all_routes[..., None] == expert_index).astype(FULL)
    counts = jnp.sum(member_of, axis=2)
    before = jnp.cumsum(counts, axis=1) - counts
    within = jnp.sum(member_of * before[:, :, None, :], axis=-1).astype(jnp.int32)
    slot = jnp.where(
        all_routes % ctx_count == z, all_routes // ctx_count * capacity + within, -1
    )
    hits = slot[..., None] == jnp.arange(plane_slots, dtype=jnp.int32)
    chooser = jnp.sum(hits.astype(FULL), axis=2).astype(LOW)
    mixer = jnp.sum(jnp.where(hits, all_gates[..., None], 0.0), axis=2)
    mixer = mixer.astype(LOW)

    all_cot, arrived_grad = gather_rows(
        cot_low, mixer.swapaxes(1, 2), ctx_count, fsdp_count
    )
    all_cot = all_cot.reshape(sequence, model_width)
    arrived_grad = arrived_grad.reshape(-1, model_width)

    hidden_units = expert_gate.shape[2]

    def parts(weight):
        return weight.reshape(
            (EXP_DEV, members, weight.shape[1] // members) + weight.shape[2:]
        ).swapaxes(0, 1)

    gate_all = bring_expert(parts(expert_gate), members, fsdp_count).reshape(
        model_width, hidden_units
    )
    up_all = bring_expert(parts(expert_up), members, fsdp_count).reshape(model_width, hidden_units)
    down_all = (
        bring_expert(parts(expert_down), members, fsdp_count)
        .transpose(1, 2, 0, 3)
        .reshape(hidden_units, model_width)
    )

    pair = jnp.stack([shared_gate, shared_up])
    pair = lax.all_to_all(pair, "ctx", split_axis=2, concat_axis=1, tiled=True)
    shared_units = pair.shape[2]
    pair = lax.all_gather(pair, "fsdp", axis=0)
    pair = (
        pair.reshape(fsdp_count, 2, ctx_count, dense_rows, shared_units)
        .transpose(1, 2, 0, 3, 4)
        .reshape(2, model_width, shared_units)
    )
    full_sgate, full_sup = (pair[0], pair[1])
    full_sdown = lax.all_gather(shared_down, "fsdp", axis=0, tiled=True)

    plain_one, inverse_one = norm_forward(source)
    normed = (plain_one * gain_one).astype(LOW)
    query_raw = jnp.dot(normed, full_query, preferred_element_type=FULL).reshape(
        row_count, HEADS, NOPE + ROPE
    )
    query_nope = query_raw[:, :, :NOPE].astype(LOW)
    query_rope = rotary(query_raw[:, :, NOPE:], positions, 1.0).astype(LOW)
    latent_raw = jnp.dot(normed, full_latent, preferred_element_type=FULL)
    plain_latent, inverse_latent = norm_forward(latent_raw[:, :LATENT])
    latent_norm = (plain_latent * gain_latent).astype(LOW)
    key_rope = rotary(latent_raw[:, LATENT:], positions, 1.0).astype(LOW)
    keys = lax.all_gather(
        jnp.concatenate([latent_norm, key_rope], axis=1), "ctx", axis=0, tiled=True
    )
    all_latent, all_keys = (keys[:, :LATENT], keys[:, LATENT:])
    expand = full_expand.reshape(LATENT, HEADS, NOPE + VDIM)
    expand_key = expand[:, :, :NOPE]
    expand_value = expand[:, :, NOPE:]
    query_latent = mm("thd,chd->thc", query_nope, expand_key).astype(LOW)
    scores = score_block(query_latent, query_rope, all_latent, all_keys, allowed, score_scale)
    row_max = jnp.max(scores, axis=-1, keepdims=True)
    row_sum = jnp.sum(jnp.exp(scores - row_max), axis=-1, keepdims=True)
    log_total = row_max + jnp.log(row_sum)
    soft_weights = jnp.exp(scores - log_total)
    latent_out = mm("htk,kc->thc", soft_weights.astype(LOW), all_latent).astype(LOW)
    values_out = (
        mm("thc,chv->thv", latent_out, expand_value).astype(LOW).reshape(row_count, HEADS * VDIM)
    )
    middle = source + jnp.dot(values_out, full_output, preferred_element_type=FULL)
    plain_two, inverse_two = norm_forward(middle)
    second = (plain_two * gain_two).astype(LOW)

    all_second, arrived_rows = gather_rows(
        second, chooser.swapaxes(1, 2), ctx_count, fsdp_count
    )
    all_second = all_second.reshape(sequence, model_width)
    arrived_rows = arrived_rows.reshape(-1, model_width)
    gate_pre = jnp.dot(arrived_rows, gate_all, preferred_element_type=FULL)
    up_pre = jnp.dot(arrived_rows, up_all, preferred_element_type=FULL)
    gate_silu, gate_slope = silu_slope(gate_pre)
    hidden_act = (gate_silu * up_pre).astype(LOW)
    hidden_grad = mm("sd,fd->sf", arrived_grad, down_all)
    up_back = (hidden_grad * gate_silu).astype(LOW)
    gate_back = (hidden_grad * up_pre * gate_slope).astype(LOW)
    arrived_back = (mm("sf,df->sd", gate_back, gate_all) + mm("sf,df->sd", up_back, up_all)).astype(
        LOW
    )
    result = jnp.dot(hidden_act, down_all, preferred_element_type=FULL).astype(LOW)

    shared_g = jnp.dot(all_second, full_sgate, preferred_element_type=FULL)
    shared_u = jnp.dot(all_second, full_sup, preferred_element_type=FULL)
    shared_silu, shared_slope = silu_slope(shared_g)
    shared_hidden = (shared_silu * shared_u).astype(LOW)
    shared_hidden_grad = mm("td,fd->tf", all_cot, full_sdown)
    sup_back = (shared_hidden_grad * shared_silu).astype(LOW)
    sgate_back = (shared_hidden_grad * shared_u * shared_slope).astype(LOW)
    shared_second_grad = mm("tf,df->td", sgate_back, full_sgate) + mm(
        "tf,df->td", sup_back, full_sup
    )
    slots_shape = (ctx_count, fsdp_count, share, model_width)
    rows_shape = (ctx_count, row_count, model_width)
    second_grad = return_rows(
        arrived_back.reshape(slots_shape),
        chooser,
        shared_second_grad.reshape(rows_shape),
        ctx_count,
        fsdp_count,
        True,
    )
    shared_out = jnp.dot(shared_hidden, full_sdown, preferred_element_type=FULL)
    out_sum = return_rows(
        result.reshape(slots_shape),
        mixer,
        shared_out.reshape(rows_shape),
        ctx_count,
        fsdp_count,
        False,
    )
    layer_out = (middle + out_sum).astype(LOW)[None]

    gate_grad = mm("sd,sf->df", arrived_rows, gate_back).astype(LOW)
    up_grad = mm("sd,sf->df", arrived_rows, up_back).astype(LOW)
    down_grad = mm("sf,sd->fd", hidden_act, arrived_grad).astype(LOW)

    def give_back(grad, like):
        return return_expert(grad, members, fsdp_count).reshape(like.shape).astype(FULL)

    part_rows = model_width // ctx_count // members
    line_shape = (ctx_count, members, part_rows, hidden_units)
    expert_grads = (
        give_back(gate_grad.reshape(line_shape).swapaxes(0, 1), expert_gate),
        give_back(up_grad.reshape(line_shape).swapaxes(0, 1), expert_up),
        give_back(
            down_grad.reshape(members, hidden_units // members, ctx_count, -1).swapaxes(1, 2),
            expert_down,
        ),
    )
    pair_grad = jnp.stack(
        [mm("td,tf->df", all_second, sgate_back), mm("td,tf->df", all_second, sup_back)]
    ).astype(LOW)
    pair_grad = (
        pair_grad.reshape(2, ctx_count, fsdp_count, dense_rows, shared_units)
        .transpose(2, 0, 1, 3, 4)
        .reshape(fsdp_count, 2, ctx_count * dense_rows, shared_units)
    )
    pair_grad = lax.psum_scatter(pair_grad, "fsdp", scatter_dimension=0, tiled=False)
    pair_grad = lax.all_to_all(
        pair_grad, "ctx", split_axis=1, concat_axis=2, tiled=True
    ).astype(FULL)
    sdown_grad = mm("tf,td->fd", shared_hidden, all_cot).astype(LOW)
    sdown_grad = lax.psum_scatter(sdown_grad, "fsdp", scatter_dimension=0, tiled=True).astype(FULL)

    middle_part, gain_two_grad = norm_backward(second_grad, plain_two, inverse_two, gain_two)
    middle_grad = cot_full + middle_part
    attended_grad = middle_grad.astype(LOW)
    output_weight_grad = mm("tv,td->vd", values_out, attended_grad)
    values_grad = (
        mm("td,vd->tv", attended_grad, full_output).astype(LOW).reshape(row_count, HEADS, VDIM)
    )
    latent_out_grad = mm("thv,chv->thc", values_grad, expand_value).astype(LOW)
    expand_value_grad = mm("thc,thv->chv", latent_out, values_grad)
    scores = score_block(query_latent, query_rope, all_latent, all_keys, allowed, score_scale)
    soft_weights = jnp.exp(scores - log_total)
    soft_grad = mm("thc,kc->htk", latent_out_grad, all_latent)
    all_latent_grad = mm("htk,thc->kc", soft_weights.astype(LOW), latent_out_grad)
    row_inner = jnp.sum(soft_weights * soft_grad, axis=-1, keepdims=True)
    score_grad = (soft_weights * (soft_grad - row_inner) * score_scale).astype(LOW)
    query_latent_grad = mm("htk,kc->thc", score_grad, all_latent).astype(LOW)
    all_latent_grad = all_latent_grad + mm("htk,thc->kc", score_grad, query_latent)
    query_rope_grad = mm("htk,kd->thd", score_grad, all_keys)
    all_keys_grad = mm("htk,thd->kd", score_grad, query_rope)
    keys_part = lax.psum_scatter(
        jnp.concatenate([all_latent_grad, all_keys_grad], axis=1),
        "ctx",
        scatter_dimension=0,
        tiled=True,
    )
    latent_grad, keys_grad = (keys_part[:, :LATENT], keys_part[:, LATENT:])
    query_nope_grad = mm("thc,chd->thd", query_latent_grad, expand_key)
    expand_key_grad = mm("thd,thc->chd", query_nope, query_latent_grad)
    expand_grad = jnp.concatenate([expand_key_grad, expand_value_grad], axis=-1).reshape(
        LATENT, HEADS * (NOPE + VDIM)
    )
    query_grad = (
        jnp.concatenate([query_nope_grad, rotary(query_rope_grad, positions, -1.0)], axis=-1)
        .astype(LOW)
        .reshape(row_count, HEADS * (NOPE + ROPE))
    )
    latent_part_grad, gain_latent_grad = norm_backward(
        latent_grad, plain_latent, inverse_latent, gain_latent
    )
    latent_raw_grad = jnp.concatenate(
        [latent_part_grad, rotary(keys_grad, positions, -1.0)], axis=-1
    ).astype(LOW)
    query_weight_grad = mm("td,tq->dq", normed, query_grad)
    latent_weight_grad = mm("td,tq->dq", normed, latent_raw_grad)
    normed_grad = mm("tq,dq->td", query_grad, full_query) + mm(
        "tq,dq->td", latent_raw_grad, full_latent
    )
    source_part, gain_one_grad = norm_backward(normed_grad, plain_one, inverse_one, gain_one)
    tokens_grad = (middle_grad + source_part)[None]

    gain_latent_column = jnp.pad(
        gain_latent_grad.reshape(device_count, gain_rows), ((0, 0), (0, dense_rows - gain_rows))
    ).reshape(model_width)
    packed_grad = scatter_shards(
        jnp.concatenate(
            [
                query_weight_grad.astype(LOW),
                output_weight_grad.astype(LOW),
                expand_grad.astype(LOW).reshape(model_width, -1),
                latent_weight_grad.astype(LOW),
                gain_one_grad[:, None].astype(LOW),
                gain_two_grad[:, None].astype(LOW),
                gain_latent_column[:, None].astype(LOW),
                jnp.zeros((model_width, 61), LOW),
            ],
            axis=1,
        ),
        ctx_count,
        fsdp_count,
    )
    tail_grad = packed_grad[:, expand_end:]
    return (
        layer_out,
        tokens_grad,
        tail_grad[:, rotary_end],
        packed_grad[:, :query_end],
        tail_grad[:, :rotary_end],
        tail_grad[:gain_rows, rotary_end + 2],
        packed_grad[:, output_end:expand_end].reshape(expand_weight.shape),
        packed_grad[:, query_end:output_end],
        tail_grad[:, rotary_end + 1],
        pair_grad[0],
        pair_grad[1],
        sdown_grad,
        expert_grads[0],
        expert_grads[1],
        expert_grads[2],
    )


def solution(mesh):
    in_specs = (
        P("fsdp", "ctx", None),
        P("fsdp", "ctx", None),
        P("fsdp", "ctx", None),
        P("fsdp", "ctx", None),
        P(("ctx", "fsdp")),
        P(("ctx", "fsdp"), None),
        P(("ctx", "fsdp"), None),
        P(("ctx", "fsdp")),
        P(("ctx", "fsdp"), None),
        P(("ctx", "fsdp"), None),
        P(("ctx", "fsdp")),
        P(("ctx", "fsdp"), None),
        P(("ctx", "fsdp"), None),
        P(("ctx", "fsdp"), None),
        P("fsdp", "ctx", None),
        P("fsdp", "ctx", None),
        P("fsdp", None, "ctx"),
    )
    out_specs = (
        P("fsdp", "ctx", None),
        P("fsdp", "ctx", None),
        P(("ctx", "fsdp")),
        P(("ctx", "fsdp"), None),
        P(("ctx", "fsdp"), None),
        P(("ctx", "fsdp")),
        P(("ctx", "fsdp"), None),
        P(("ctx", "fsdp"), None),
        P(("ctx", "fsdp")),
        P(("ctx", "fsdp"), None),
        P(("ctx", "fsdp"), None),
        P(("ctx", "fsdp"), None),
        P("fsdp", "ctx", None),
        P("fsdp", "ctx", None),
        P("fsdp", None, "ctx"),
    )
    return jax.shard_map(local, mesh=mesh, in_specs=in_specs, out_specs=out_specs, check_vma=False)
```

```python
import functools

import jax
import jax.numpy as jnp
from jax import lax
from jax.experimental import pallas as pl
from jax.experimental.pallas import tpu as pltpu
from jax.sharding import PartitionSpec as P

HEADS = 16
NOPE = 128
ROPE = 64
LATENT = 512
VDIM = 128
TOP = 6
EXP_DEV = 2


epsilon = 1e-06
rope_base = 10000.0
masked_score = -1e30


def stored_positions(row_index, per_device, block_count):
    device = row_index // per_device
    within = row_index % per_device
    half_block = per_device // 2
    return jnp.where(
        within >= half_block,
        (block_count - 1 - device) * half_block + within - half_block,
        device * half_block + within,
    )


def rotary(values, positions, direction):
    half_rope = values.shape[-1] // 2
    frequency = rope_base ** (-jnp.arange(half_rope, dtype=jnp.float32) / half_rope)
    angles = positions.astype(jnp.float32)[:, None] * frequency[None, :]
    cosine_table = jnp.cos(angles)
    sine_table = direction * jnp.sin(angles)
    if values.ndim == 3:
        cosine_table = cosine_table[:, None, :]
        sine_table = sine_table[:, None, :]
    front_half = values[..., :half_rope]
    back_half = values[..., half_rope:]
    return jnp.concatenate(
        [
            front_half * cosine_table - back_half * sine_table,
            back_half * cosine_table + front_half * sine_table,
        ],
        axis=-1,
    )


def norm_forward(values):
    inverse = lax.rsqrt(jnp.mean(values * values, axis=-1, keepdims=True) + epsilon)
    return (values * inverse, inverse)


def norm_backward(normed_grad, plain, inverse, gain):
    gain_grad = jnp.sum(normed_grad * plain, axis=0)
    scaled = normed_grad * gain
    return (
        inverse * (scaled - plain * jnp.mean(scaled * plain, axis=-1, keepdims=True)),
        gain_grad,
    )


def silu_slope(values):
    sigma = jax.nn.sigmoid(values)
    return (values * sigma, sigma * (1.0 + values * (1.0 - sigma)))


def score_block(query_latent, query_rope, all_latent, all_keys, allowed, score_scale):
    raw_scores = jnp.einsum(
        "thc,kc->htk", query_latent, all_latent, preferred_element_type=jnp.float32
    ) + jnp.einsum("thd,kd->htk", query_rope, all_keys, preferred_element_type=jnp.float32)
    return jnp.where(allowed[None], raw_scores * score_scale, masked_score)


LOW = jnp.bfloat16
FULL = jnp.float32


MESH_ID = pl.DeviceIdType.MESH
BIG_VMEM = 60 * 1024 * 1024


def flip(index, bit):
    return index + bit - 2 * bit * lax.rem(lax.div(index, bit), 2)


def toggled(index, mask):
    for bit in (1, 2, 4):
        if mask & bit:
            index = flip(index, bit)
    return index


def nearest(z, step):
    upper = lax.div(z, 2)
    if step == 0:
        return z
    if step == 1:
        return z + 1 - 2 * upper
    if step == 2:
        return 2 - 2 * lax.rem(z, 2) + upper
    return 3 - 3 * upper


def remote(source, target, send, receive, z, f):
    return pltpu.make_async_remote_copy(
        src_ref=source,
        dst_ref=target,
        send_sem=send,
        recv_sem=receive,
        device_id={"ctx": z, "fsdp": f},
        device_id_type=MESH_ID,
    )


def greet(z, f, masks, ctx_count, whole_line=False):
    barrier = pltpu.get_barrier_semaphore()

    def hello(to_z, to_f):
        pl.semaphore_signal(
            barrier, inc=1, device_id={"ctx": to_z, "fsdp": to_f}, device_id_type=MESH_ID
        )

    for mask in masks:
        hello(z, toggled(f, mask))
    if whole_line:
        for step in range(1, ctx_count):
            hello(lax.rem(z + step, ctx_count), f)
        pl.semaphore_wait(barrier, len(masks) + ctx_count - 1)
        return

    @pl.when(z > 0)
    def _():
        hello(z - 1, f)

    @pl.when(z < ctx_count - 1)
    def _():
        hello(z + 1, f)

    along = lax.div(z + ctx_count - 1, ctx_count) + lax.div(2 * ctx_count - 2 - z, ctx_count)
    pl.semaphore_wait(barrier, len(masks) + along)


def both_ways(z, block, ctx_count, act):
    @pl.when((block <= z) & (z < ctx_count - 1))
    def _():
        act(0, z + 1)

    @pl.when((block >= z) & (z > 0))
    def _():
        act(1, z - 1)


def halves(rows, width):
    if rows % 32 == 0:
        return tuple((pl.ds(start, rows // 2), slice(None)) for start in (0, rows // 2))
    return tuple((slice(None), pl.ds(start, width // 2)) for start in (0, width // 2))


def gather_kernel(ctx_count, kinds, *refs):
    count = len(kinds)
    shards, outs = refs[:count], refs[count : 2 * count]
    own_sem, z_send, z_recv, p_send, p_recv, c_send, c_recv = refs[2 * count :]
    z, f = lax.axis_index("ctx"), lax.axis_index("fsdp")
    core, x_near, y_near = flip(f, 1), flip(f, 2), flip(f, 4)
    far = flip(x_near, 4)
    greet(z, f, (1, 2, 4), ctx_count, True)

    def slot(item, step):
        return 0 if kinds[item] == "plane" else nearest(z, step)

    def steps(item, step):
        return step == 0 if kinds[item] == "plane" else 0 <= step < ctx_count

    def z_view(item, block):
        return outs[item].at[block] if kinds[item] == "column" else outs[item].at[block, f]

    def own(item):
        source = shards[item].at[z] if kinds[item] == "line" else shards[item]
        return pltpu.make_async_copy(source, z_view(item, slot(item, 0)), own_sem.at[item])

    def z_copy(item, block, way, target):
        at = z_view(item, block)
        return remote(at, at, z_send.at[item, block, way], z_recv.at[item, block], target, f)

    def piece(item, step):
        target = lax.rem(z + step, ctx_count)
        return remote(
            shards[item].at[target],
            outs[item].at[z, f],
            z_send.at[item, target, 0],
            z_recv.at[item, z],
            target,
            f,
        )

    def part(item, block, at, which):
        rows, columns = halves(*outs[item].shape[2:])[which]
        return outs[item].at[block, at, rows, columns]

    def p_copy(item, block, which):
        at = (
            lambda: outs[item].at[block, f],
            lambda: outs[item].at[block, f],
            lambda: part(item, block, x_near, 0),
            lambda: part(item, block, y_near, 1),
        )[which]()
        to = (x_near, y_near, y_near, x_near)[which]
        sems = (p_send.at[item, block, which], p_recv.at[item, block, which])
        return remote(at, at, *sems, z, to)

    def p_arrived(item, block, which):
        at = (
            lambda: outs[item].at[block, x_near],
            lambda: outs[item].at[block, y_near],
            lambda: part(item, block, far, 0),
            lambda: part(item, block, far, 1),
        )[which]()
        sems = (p_send.at[item, block, which], p_recv.at[item, block, which])
        remote(at, at, *sems, z, x_near).wait_recv()

    def c_copy(item, block, which):
        at = outs[item].at[block, (f, x_near, y_near, far)[which]]
        sems = (c_send.at[item, block, which], c_recv.at[item, block, which])
        return remote(at, at, *sems, z, core)

    def c_arrived(item, block, which):
        at = outs[item].at[block, flip((f, x_near, y_near, far)[which], 1)]
        sems = (c_send.at[item, block, which], c_recv.at[item, block, which])
        remote(at, at, *sems, z, core).wait_recv()

    def first(item, step):
        block = slot(item, step)
        if step == 0:
            own(item).wait()
        else:
            at = z_view(item, block)
            sems = (z_send.at[item, block, 0], z_recv.at[item, block])
            remote(at, at, *sems, z, core).wait_recv()
        if kinds[item] in ("all", "column"):
            both_ways(z, block, ctx_count, lambda way, to: z_copy(item, block, way, to).start())
        if kinds[item] != "column":
            p_copy(item, block, 0).start()
            p_copy(item, block, 1).start()
            c_copy(item, block, 0).start()

    def second(item, step):
        block = slot(item, step)
        for which in (0, 1):
            p_arrived(item, block, which)
            p_copy(item, block, which + 2).start()
            c_copy(item, block, which + 1).start()

    def third(item, step):
        block = slot(item, step)
        p_arrived(item, block, 2)
        p_arrived(item, block, 3)
        c_copy(item, block, 3).start()

    for item in range(count):
        own(item).start()
        if kinds[item] == "line":
            for step in range(1, ctx_count):
                piece(item, step).start()
    for step in range(ctx_count + 2):
        for lag, stage in ((0, first), (1, second), (2, third)):
            for item in range(count):
                if steps(item, step - lag) and (lag == 0 or kinds[item] != "column"):
                    stage(item, step - lag)
    for item in range(count):
        for step in range(ctx_count):
            if not steps(item, step):
                continue
            block = slot(item, step)
            if kinds[item] != "column":
                for which in range(4):
                    c_arrived(item, block, which)
                    p_copy(item, block, which).wait_send()
                    c_copy(item, block, which).wait_send()
            if kinds[item] == "line" and step > 0:
                piece(item, step).wait_send()
            if kinds[item] in ("all", "column"):
                both_ways(
                    z, block, ctx_count, lambda way, to: z_copy(item, block, way, to).wait_send()
                )


def gather_arrays(items, ctx_count, fsdp_count):
    kinds = tuple(kind for kind, shard in items)
    shards = [shard for kind, shard in items]
    lead = {
        "all": (ctx_count, fsdp_count),
        "line": (ctx_count, fsdp_count),
        "plane": (1, fsdp_count),
        "column": (ctx_count,),
    }
    shapes = [
        lead[kind] + (shard.shape[1:] if kind == "line" else shard.shape) for kind, shard in items
    ]
    count = len(items)
    dma = pltpu.SemaphoreType.DMA
    four = dma((count, ctx_count, 4))
    return pl.pallas_call(
        functools.partial(gather_kernel, ctx_count, kinds),
        out_shape=[
            jax.ShapeDtypeStruct(shape, shard.dtype) for shape, shard in zip(shapes, shards)
        ],
        in_specs=[pl.BlockSpec(memory_space=pl.ANY)] * count,
        out_specs=[pl.BlockSpec(memory_space=pl.ANY)] * count,
        scratch_shapes=[
            dma((count,)),
            dma((count, ctx_count, 2)),
            dma((count, ctx_count)),
            four,
            four,
            four,
            four,
        ],
        compiler_params=pltpu.CompilerParams(collective_id=0, has_side_effects=True),
        cost_estimate=pl.CostEstimate(flops=0, bytes_accessed=500_000_000, transcendentals=0),
    )(*shards)


def add_rows(target, rows, *terms):
    @pl.loop(0, rows, step=16)
    def _(start):
        part = pl.ds(pl.multiple_of(start, 16), 16)
        total = terms[0][part, :].astype(FULL)
        for term in terms[1:]:
            total = total + term[part, :].astype(FULL)
        target[part, :] = total.astype(target.dtype)


def scatter_kernel(ctx_count, count, *refs):
    grads, outs = refs[:count], refs[count : 2 * count]
    banks = [refs[(2 + kind) * count : (3 + kind) * count] for kind in range(7)]
    load_sem, c_send, c_recv, p_send, p_recv, z_send, z_recv = refs[9 * count :]
    z, f = lax.axis_index("ctx"), lax.axis_index("fsdp")
    side = lax.rem(f, 2)
    chip = lax.div(f, 2)
    core, x_near, y_near = flip(f, 1), flip(f, 2), flip(f, 4)
    x_chip, y_chip = flip(chip, 1), flip(chip, 2)
    far_chip = flip(x_chip, 2)
    greet(z, f, (1, 2, 4), ctx_count)
    order = [nearest(z, ctx_count - 1 - step) for step in range(ctx_count)]

    def work(item):
        grad_ref, out_ref = grads[item], outs[item]
        mine, from_core, from_x, from_y, half_x, half_y, from_z = [bank[item] for bank in banks]
        rows, width = out_ref.shape
        left, right = pl.ds(0, width // 2), pl.ds(width // 2, width // 2)

        def load(block):
            return pltpu.make_async_copy(
                grad_ref.at[block, :, side], mine.at[block], load_sem.at[item, block]
            )

        def c_copy(block):
            return remote(
                grad_ref.at[block, :, 1 - side],
                from_core.at[block],
                c_send.at[item, block],
                c_recv.at[item, block],
                z,
                core,
            )

        def p_copy(block, which):
            source, target, to = (
                (mine.at[block, far_chip, :, left], half_y.at[block], y_near),
                (mine.at[block, far_chip, :, right], half_x.at[block], x_near),
                (mine.at[block, x_chip], from_x.at[block], x_near),
                (mine.at[block, y_chip], from_y.at[block], y_near),
            )[which]
            sems = (p_send.at[item, block, which], p_recv.at[item, block, which])
            return remote(source, target, *sems, z, to)

        def z_copy(block, way, target):
            return remote(
                mine.at[block, chip],
                from_z.at[way, block],
                z_send.at[item, block],
                z_recv.at[item, way, block],
                target,
                f,
            )

        def z_arrived(block, way):
            at = from_z.at[way, block]
            sems = (z_send.at[item, block], z_recv.at[item, way, block])
            remote(at, at, *sems, z, core).wait_recv()

        def start(step):
            c_copy(order[step]).start()
            load(order[step]).start()

        def first(step):
            block = order[step]
            load(block).wait()
            c_copy(block).wait_recv()
            far_part = mine.at[block, far_chip]
            add_rows(far_part, rows, far_part, from_core.at[block, far_chip])
            p_copy(block, 0).start()
            p_copy(block, 1).start()

        def second(step):
            block = order[step]
            x_part, y_part = mine.at[block, x_chip], mine.at[block, y_chip]
            add_rows(x_part, rows, x_part, from_core.at[block, x_chip])
            add_rows(y_part, rows, y_part, from_core.at[block, y_chip])
            p_copy(block, 0).wait_recv()
            x_left = mine.at[block, x_chip, :, left]
            add_rows(x_left, rows, x_left, half_y.at[block])
            p_copy(block, 2).start()
            p_copy(block, 1).wait_recv()
            y_right = mine.at[block, y_chip, :, right]
            add_rows(y_right, rows, y_right, half_x.at[block])
            p_copy(block, 3).start()

        def third(step):
            block = order[step]
            p_copy(block, 2).wait_recv()
            p_copy(block, 3).wait_recv()
            own = mine.at[block, chip]
            terms = (own, from_core.at[block, chip], from_x.at[block], from_y.at[block])
            if step == ctx_count - 1:

                @pl.when(z > 0)
                def _():
                    z_arrived(block, 0)

                @pl.when(z < ctx_count - 1)
                def _():
                    z_arrived(block, 1)

                @pl.when(z == 0)
                def _():
                    add_rows(out_ref, rows, *terms, from_z.at[1, block])

                @pl.when(z == ctx_count - 1)
                def _():
                    add_rows(out_ref, rows, *terms, from_z.at[0, block])

                @pl.when((z > 0) & (z < ctx_count - 1))
                def _():
                    add_rows(out_ref, rows, *terms, from_z.at[0, block], from_z.at[1, block])

                return

            for way, above in ((1, True), (0, False)):
                heading = (block < z) if above else (block > z)
                has_more = (z < ctx_count - 1) if above else (z > 0)

                @pl.when(heading & has_more)
                def _():
                    z_arrived(block, way)
                    add_rows(own, rows, *terms, from_z.at[way, block])

                @pl.when(heading & jnp.logical_not(has_more))
                def _():
                    add_rows(own, rows, *terms)

                @pl.when(heading)
                def _():
                    z_copy(block, way, z - 1 if above else z + 1).start()

        def finish(step):
            block = order[step]
            c_copy(block).wait_send()
            for which in range(4):
                p_copy(block, which).wait_send()
            if step < ctx_count - 1:
                z_copy(block, 0, z).wait_send()

        return start, first, second, third, finish

    stages = list(zip(*[work(item) for item in range(count)]))
    for step in range(ctx_count):
        for act in stages[0]:
            act(step)
    for step in range(ctx_count + 2):
        for lag in (0, 1, 2):
            if 0 <= step - lag < ctx_count:
                for act in stages[1 + lag]:
                    act(step - lag)
    for step in range(ctx_count):
        for act in stages[4]:
            act(step)


def scatter_arrays(grads, ctx_count, fsdp_count):
    count = len(grads)
    chips = fsdp_count // 2
    shapes = [
        (grad.shape[0] // (ctx_count * fsdp_count), grad.shape[1]) for grad in grads
    ]
    dma = pltpu.SemaphoreType.DMA
    leads = [(ctx_count, chips), (ctx_count, chips), (ctx_count,), (ctx_count,)]
    banks = [pltpu.VMEM(lead + shape, LOW) for lead in leads for shape in shapes]
    banks += [
        pltpu.VMEM((ctx_count, shape[0], shape[1] // 2), LOW) for _ in range(2) for shape in shapes
    ]
    banks += [pltpu.VMEM((2, ctx_count) + shape, LOW) for shape in shapes]
    return pl.pallas_call(
        functools.partial(scatter_kernel, ctx_count, count),
        out_shape=[jax.ShapeDtypeStruct(shape, FULL) for shape in shapes],
        in_specs=[pl.BlockSpec(memory_space=pl.ANY)] * count,
        out_specs=[pl.BlockSpec(memory_space=pltpu.VMEM)] * count,
        scratch_shapes=banks
        + [
            dma((count, ctx_count)),
            dma((count, ctx_count)),
            dma((count, ctx_count)),
            dma((count, ctx_count, 4)),
            dma((count, ctx_count, 4)),
            dma((count, ctx_count)),
            dma((count, 2, ctx_count)),
        ],
        compiler_params=pltpu.CompilerParams(
            collective_id=1, has_side_effects=True, vmem_limit_bytes=BIG_VMEM
        ),
        cost_estimate=pl.CostEstimate(flops=0, bytes_accessed=500_000_000, transcendentals=0),
    )(
        *[
            grad.reshape((ctx_count, chips, 2) + shape)
            for grad, shape in zip(grads, shapes)
        ]
    )


PEERS = (6, 7, 2, 4, 3, 5, 1)


def dispatch_kernel(
    ctx_count,
    rows_ref,
    choose_ref,
    all_ref,
    out_ref,
    blocks,
    chosen,
    own_sem,
    all_sem,
    keep_sem,
    z_send,
    z_recv,
    p_send,
    p_recv,
):
    z, f = lax.axis_index("ctx"), lax.axis_index("fsdp")
    width = rows_ref.shape[1]
    groups, share = chosen.shape[1], chosen.shape[2]
    greet(z, f, PEERS, ctx_count)
    own = pltpu.make_async_copy(rows_ref, blocks.at[z], own_sem)
    own.start()
    own.wait()

    def z_copy(block, way, target):
        at = blocks.at[block]
        return remote(at, at, z_send.at[block, way], z_recv.at[block], target, f)

    def p_copy(block, place):
        to = toggled(f, PEERS[place])
        return remote(
            chosen.at[block, to],
            out_ref.at[block, f],
            p_send.at[block, place],
            p_recv.at[block, place],
            z,
            to,
        )

    def p_arrived(block, place):
        at = out_ref.at[block, toggled(f, PEERS[place])]
        remote(at, at, p_send.at[block, place], p_recv.at[block, place], z, flip(f, 1)).wait_recv()

    def keep(block):
        return pltpu.make_async_copy(
            chosen.at[block, f], out_ref.at[block, f], keep_sem.at[block]
        )

    def store(block):
        return pltpu.make_async_copy(blocks.at[block], all_ref.at[block], all_sem.at[block])

    for step in range(ctx_count):
        block = nearest(z, step)
        if step > 0:
            at = blocks.at[block]
            remote(at, at, z_send.at[block, 0], z_recv.at[block], z, flip(f, 1)).wait_recv()
        both_ways(z, block, ctx_count, lambda way, to: z_copy(block, way, to).start())
        store(block).start()

        @pl.loop(0, width, step=256)
        def _(start):
            part = pl.ds(pl.multiple_of(start, 256), 256)
            tile = jnp.dot(
                choose_ref[block], blocks[block, :, part], preferred_element_type=FULL
            ).astype(LOW)
            chosen[block, :, :, part] = tile.reshape(groups, share, 256)

        for place in range(len(PEERS)):
            p_copy(block, place).start()
        keep(block).start()
    for step in range(ctx_count):
        block = nearest(z, step)
        store(block).wait()
        keep(block).wait()
        for place in range(len(PEERS)):
            p_arrived(block, place)
    for step in range(ctx_count):
        block = nearest(z, step)
        both_ways(z, block, ctx_count, lambda way, to: z_copy(block, way, to).wait_send())
        for place in range(len(PEERS)):
            p_copy(block, place).wait_send()


def dispatch_rows(rows, chooser, ctx_count, fsdp_count):
    count, width = rows.shape
    share = chooser.shape[1] // fsdp_count
    dma = pltpu.SemaphoreType.DMA
    return pl.pallas_call(
        functools.partial(dispatch_kernel, ctx_count),
        out_shape=(
            jax.ShapeDtypeStruct((ctx_count, count, width), LOW),
            jax.ShapeDtypeStruct((ctx_count, fsdp_count, share, width), LOW),
        ),
        in_specs=[pl.BlockSpec(memory_space=pl.ANY), pl.BlockSpec(memory_space=pltpu.VMEM)],
        out_specs=(pl.BlockSpec(memory_space=pl.ANY), pl.BlockSpec(memory_space=pl.ANY)),
        scratch_shapes=[
            pltpu.VMEM((ctx_count, count, width), LOW),
            pltpu.VMEM((ctx_count, fsdp_count, share, width), LOW),
            dma,
            dma((ctx_count,)),
            dma((ctx_count,)),
            dma((ctx_count, 2)),
            dma((ctx_count,)),
            dma((ctx_count, len(PEERS))),
            dma((ctx_count, len(PEERS))),
        ],
        compiler_params=pltpu.CompilerParams(
            collective_id=2, has_side_effects=True, vmem_limit_bytes=BIG_VMEM
        ),
        cost_estimate=pl.CostEstimate(
            flops=2_000_000_000, bytes_accessed=300_000_000, transcendentals=0
        ),
    )(rows, chooser)


def combine_kernel(
    ctx_count,
    slots_ref,
    mix_ref,
    extra_ref,
    out_ref,
    arrived,
    extra,
    parts,
    from_z,
    keep_sem,
    extra_sem,
    p_send,
    p_recv,
    z_send,
    z_recv,
):
    z, f = lax.axis_index("ctx"), lax.axis_index("fsdp")
    count, width = out_ref.shape
    slots = mix_ref.shape[2]
    greet(z, f, PEERS, ctx_count)

    def p_copy(block, place):
        to = toggled(f, PEERS[place])
        return remote(
            slots_ref.at[block, to],
            arrived.at[block, f],
            p_send.at[block, place],
            p_recv.at[block, place],
            z,
            to,
        )

    def p_arrived(block, place):
        at = arrived.at[block, toggled(f, PEERS[place])]
        remote(at, at, p_send.at[block, place], p_recv.at[block, place], z, flip(f, 1)).wait_recv()

    def keep(block):
        return pltpu.make_async_copy(
            slots_ref.at[block, f], arrived.at[block, f], keep_sem.at[block]
        )

    def load(block):
        return pltpu.make_async_copy(extra_ref.at[block], extra.at[block], extra_sem.at[block])

    def z_copy(block, way, target):
        return remote(
            parts.at[block],
            from_z.at[way, block],
            z_send.at[block],
            z_recv.at[way, block],
            target,
            f,
        )

    def z_arrived(block, way):
        at = from_z.at[way, block]
        remote(at, at, z_send.at[block], z_recv.at[way, block], z, flip(f, 1)).wait_recv()

    def mix(block, target, *ways):
        @pl.loop(0, width, step=256)
        def _(start):
            part = pl.ds(pl.multiple_of(start, 256), 256)
            total = jnp.dot(
                mix_ref[block],
                arrived[block, :, :, part].reshape(slots, 256),
                preferred_element_type=FULL,
            ) + extra[block, :, part].astype(FULL)
            for way in ways:
                total = total + from_z[way, block, :, part].astype(FULL)
            target[:, part] = total.astype(target.dtype)

    order = [nearest(z, ctx_count - 1 - step) for step in range(ctx_count)]
    for block in order:
        for place in range(len(PEERS)):
            p_copy(block, place).start()
        keep(block).start()
        load(block).start()
    for step in range(ctx_count):
        block = order[step]
        keep(block).wait()
        load(block).wait()
        for place in range(len(PEERS)):
            p_arrived(block, place)
        if step < ctx_count - 1:
            for way, above in ((1, True), (0, False)):
                heading = (block < z) if above else (block > z)
                has_more = (z < ctx_count - 1) if above else (z > 0)

                @pl.when(heading & has_more)
                def _():
                    z_arrived(block, way)
                    mix(block, parts.at[block], way)

                @pl.when(heading & jnp.logical_not(has_more))
                def _():
                    mix(block, parts.at[block])

                @pl.when(heading)
                def _():
                    z_copy(block, way, z - 1 if above else z + 1).start()

        else:

            @pl.when(z > 0)
            def _():
                z_arrived(block, 0)

            @pl.when(z < ctx_count - 1)
            def _():
                z_arrived(block, 1)

            @pl.when(z == 0)
            def _():
                mix(block, out_ref, 1)

            @pl.when(z == ctx_count - 1)
            def _():
                mix(block, out_ref, 0)

            @pl.when((z > 0) & (z < ctx_count - 1))
            def _():
                mix(block, out_ref, 0, 1)

    for step in range(ctx_count):
        block = order[step]
        for place in range(len(PEERS)):
            p_copy(block, place).wait_send()
        if step < ctx_count - 1:
            z_copy(block, 0, z).wait_send()


def combine_rows(slots, mixer, extra, ctx_count, fsdp_count):
    share, width = slots.shape[2:]
    count = mixer.shape[1]
    dma = pltpu.SemaphoreType.DMA
    return pl.pallas_call(
        functools.partial(combine_kernel, ctx_count),
        out_shape=jax.ShapeDtypeStruct((count, width), FULL),
        in_specs=[
            pl.BlockSpec(memory_space=pl.ANY),
            pl.BlockSpec(memory_space=pltpu.VMEM),
            pl.BlockSpec(memory_space=pl.ANY),
        ],
        out_specs=pl.BlockSpec(memory_space=pltpu.VMEM),
        scratch_shapes=[
            pltpu.VMEM((ctx_count, fsdp_count, share, width), LOW),
            pltpu.VMEM((ctx_count, count, width), LOW),
            pltpu.VMEM((ctx_count, count, width), LOW),
            pltpu.VMEM((2, ctx_count, count, width), LOW),
            dma((ctx_count,)),
            dma((ctx_count,)),
            dma((ctx_count, len(PEERS))),
            dma((ctx_count, len(PEERS))),
            dma((ctx_count,)),
            dma((2, ctx_count)),
        ],
        compiler_params=pltpu.CompilerParams(
            collective_id=3, has_side_effects=True, vmem_limit_bytes=BIG_VMEM
        ),
        cost_estimate=pl.CostEstimate(
            flops=2_000_000_000, bytes_accessed=300_000_000, transcendentals=0
        ),
    )(slots, mixer, extra)


def mm(subscripts, left, right):
    return jnp.einsum(subscripts, left, right, preferred_element_type=FULL)


def member_pairs(fsdp_count, members, step):
    return [
        (f, f // members * members + (f % members + step) % members) for f in range(fsdp_count)
    ]


def by_member(own, others, member, members):
    if members == 2:
        first = member == 0
        return jnp.stack([jnp.where(first, own, others[0]), jnp.where(first, others[0], own)])
    stack = jnp.stack([own] + others)
    return jnp.take(stack, (member - jnp.arange(members)) % members, axis=0)


def part_of(array, member, step, members):
    return lax.dynamic_index_in_dim(array, (member + step) % members, 0, keepdims=False)


def swap_parts(array, members, fsdp_count):
    member = lax.axis_index("fsdp") % members
    others = [
        lax.ppermute(
            part_of(array, member, step, members), "fsdp", member_pairs(fsdp_count, members, step)
        )
        for step in range(1, members)
    ]
    return by_member(part_of(array, member, 0, members), others, member, members)


def share_parts(array, members, fsdp_count):
    member = lax.axis_index("fsdp") % members
    others = [
        lax.ppermute(array, "fsdp", member_pairs(fsdp_count, members, step))
        for step in range(1, members)
    ]
    return by_member(array, others, member, members)


def sum_parts(array, members, fsdp_count):
    member = lax.axis_index("fsdp") % members
    total = part_of(array, member, 0, members).astype(FULL)
    for step in range(1, members):
        total = total + lax.ppermute(
            part_of(array, member, step, members), "fsdp", member_pairs(fsdp_count, members, step)
        ).astype(FULL)
    return total.astype(LOW)


def return_expert(grad, members, fsdp_count):
    moved = along_line(sum_parts(grad, members, fsdp_count))
    moved = moved.reshape((members, EXP_DEV) + moved.shape[1:])
    return swap_parts(moved, members, fsdp_count).swapaxes(0, 1)


def gather_rows(rows, chooser, ctx_count, fsdp_count):
    if (ctx_count, fsdp_count) == (4, 8):
        return dispatch_rows(rows, chooser, ctx_count, fsdp_count)
    every = lax.all_gather(rows, "ctx", axis=0)
    chosen = mm("bst,btd->bsd", chooser, every).astype(LOW)
    chosen = chosen.reshape(ctx_count, fsdp_count, -1, rows.shape[1])
    return every, lax.all_to_all(chosen, "fsdp", split_axis=1, concat_axis=1, tiled=True)


def return_rows(slots, mixer, extra, ctx_count, fsdp_count, urgent):
    if urgent and (ctx_count, fsdp_count) == (4, 8):
        return combine_rows(slots, mixer, extra.astype(LOW), ctx_count, fsdp_count)
    back = lax.all_to_all(slots, "fsdp", split_axis=1, concat_axis=1, tiled=True)
    back = back.reshape(ctx_count, mixer.shape[2], -1)
    total = (mm("bts,bsd->btd", mixer, back) + extra).astype(LOW)
    return lax.psum_scatter(total, "ctx", scatter_dimension=0, tiled=False).astype(FULL)


def gather_all(items, ctx_count, fsdp_count):
    if (ctx_count, fsdp_count) == (4, 8):
        return gather_arrays(items, ctx_count, fsdp_count)
    results = []
    for kind, shard in items:
        if kind == "line":
            shard = lax.all_to_all(shard, "ctx", split_axis=0, concat_axis=0, tiled=True)
            result = lax.all_gather(shard, "fsdp", axis=1)
        elif kind == "plane":
            result = lax.all_gather(shard, "fsdp", axis=0)[None]
        elif kind == "column":
            result = lax.all_gather(shard, "ctx", axis=0)
        else:
            result = lax.all_gather(shard, ("ctx", "fsdp"), axis=0)
            result = result.reshape((ctx_count, fsdp_count) + shard.shape)
        results.append(result)
    return results


def scatter_all(grads, ctx_count, fsdp_count):
    grads = [grad.astype(LOW) for grad in grads]
    if (ctx_count, fsdp_count) == (4, 8):
        return scatter_arrays(grads, ctx_count, fsdp_count)
    return [
        lax.psum_scatter(grad, ("ctx", "fsdp"), scatter_dimension=0, tiled=True).astype(FULL)
        for grad in grads
    ]


def along_line(array):
    return lax.all_to_all(array, "ctx", split_axis=0, concat_axis=0, tiled=True)


def after(values, *others):
    tied = lax.optimization_barrier((tuple(values), others))
    return tied[0]


def local(
    tokens,
    routes,
    gate_values,
    cotangent,
    attention_gain,
    query_weight,
    latent_weight,
    latent_gain,
    expand_weight,
    output_weight,
    feedforward_gain,
    shared_gate,
    shared_up,
    shared_down,
    expert_gate,
    expert_up,
    expert_down,
):
    row_count = tokens.shape[1]
    model_width = tokens.shape[2]
    ctx_count = lax.axis_size("ctx")
    fsdp_count = lax.axis_size("fsdp")
    device_count = ctx_count * fsdp_count
    experts_total = EXP_DEV * fsdp_count
    capacity = row_count * TOP * 4 // (3 * experts_total)
    members = ctx_count // EXP_DEV
    plane_experts = experts_total // ctx_count
    plane_slots = plane_experts * capacity
    share = capacity // members
    sequence = ctx_count * row_count
    z = lax.axis_index("ctx")
    score_scale = (NOPE + ROPE) ** (-0.5)
    source = tokens[0].astype(FULL)
    cot_low = cotangent[0]
    cot_full = cot_low.astype(FULL)
    positions = stored_positions(
        z * row_count + jnp.arange(row_count, dtype=jnp.int32), row_count, 2 * ctx_count
    )
    key_positions = stored_positions(
        jnp.arange(sequence, dtype=jnp.int32), row_count, 2 * ctx_count
    )
    allowed = positions[:, None] >= key_positions[None, :]

    dense_rows = latent_weight.shape[0]
    gain_rows = latent_gain.shape[0]
    rotary_end = LATENT + ROPE
    hidden_units = expert_gate.shape[2]
    shared_units = shared_gate.shape[1] // ctx_count

    def swapped(weight):
        weight = weight.reshape((EXP_DEV, members, weight.shape[1] // members) + weight.shape[2:])
        weight = swap_parts(weight.swapaxes(0, 1), members, fsdp_count)
        return weight.reshape((ctx_count,) + weight.shape[2:])

    gate_swapped, up_swapped, down_swapped = (
        swapped(expert_gate),
        swapped(expert_up),
        swapped(expert_down),
    )
    gate_moved, up_moved, down_moved = (
        along_line(gate_swapped),
        along_line(up_swapped),
        along_line(down_swapped),
    )

    local_routes = routes[0]
    expert_index = jnp.arange(experts_total, dtype=jnp.int32)
    member_of = (local_routes[..., None] == expert_index).astype(FULL)
    counts = jnp.sum(member_of, axis=1)
    before = jnp.cumsum(counts, axis=0) - counts
    within = jnp.sum(member_of * before[:, None, :], axis=-1).astype(jnp.int32)
    info = jnp.concatenate(
        [
            (local_routes * capacity + within).astype(FULL).T,
            gate_values[0].T,
            jnp.zeros((16 - 2 * TOP, row_count), FULL),
        ]
    )

    tail = jnp.concatenate(
        [
            latent_weight,
            attention_gain[:, None],
            feedforward_gain[:, None],
            jnp.pad(latent_gain, (0, dense_rows - gain_rows))[:, None],
            jnp.zeros((dense_rows, 256 - ROPE - 3), LOW),
        ],
        axis=1,
    )

    def by_line(weight):
        return weight.reshape(dense_rows, ctx_count, shared_units).swapaxes(0, 1)

    dense = (
        info,
        query_weight,
        tail,
        expand_weight,
        output_weight,
        by_line(shared_gate),
        by_line(shared_up),
        shared_down,
    )
    dense = after(dense, gate_swapped, up_swapped, down_swapped)
    kinds = ("column", "all", "all", "all", "all", "line", "line", "plane")
    gathered = gather_all(list(zip(kinds, dense)), ctx_count, fsdp_count)
    all_info = gathered[0]
    full_query, full_tail, full_expand, full_output, full_sgate, full_sup, full_sdown = [
        item.reshape(-1, item.shape[-1]) for item in gathered[1:]
    ]
    full_latent = full_tail[:, :rotary_end]
    gain_one = full_tail[:, rotary_end].astype(FULL)
    gain_two = full_tail[:, rotary_end + 1].astype(FULL)
    gain_latent = (
        full_tail[:, rotary_end + 2].reshape(device_count, dense_rows)[:, :gain_rows]
    ).reshape(LATENT).astype(FULL)

    flat = all_info[:, :TOP].astype(jnp.int32)
    all_gates = all_info[:, TOP : 2 * TOP]
    owner = flat // capacity
    slot = jnp.where(
        owner % ctx_count == z, owner // ctx_count * capacity + flat % capacity, -1
    )
    slot_index = jnp.arange(plane_slots, dtype=jnp.int32)
    hits = slot[:, :, :, None] == slot_index
    chooser = jnp.sum(hits.astype(FULL), axis=1).astype(LOW)
    mixer = jnp.sum(jnp.where(hits, all_gates[:, :, :, None], 0.0), axis=1).astype(LOW)
    hits = slot[:, :, None, :] == slot_index[:, None]
    chooser_turned = jnp.sum(hits.astype(FULL), axis=1).astype(LOW)
    mixer_turned = jnp.sum(jnp.where(hits, all_gates[:, :, None, :], 0.0), axis=1).astype(LOW)

    (cot_sent,) = after((cot_low,), gate_moved)
    all_cot, arrived_grad = gather_rows(cot_sent, mixer_turned, ctx_count, fsdp_count)
    all_cot = all_cot.reshape(sequence, model_width)
    arrived_grad = arrived_grad.reshape(-1, model_width)

    def whole(moved):
        return share_parts(moved, members, fsdp_count).swapaxes(0, 1)

    gate_all = whole(gate_moved).reshape(model_width, hidden_units)
    up_all = whole(up_moved).reshape(model_width, hidden_units)
    down_all = whole(down_moved).transpose(1, 2, 0, 3).reshape(hidden_units, model_width)

    plain_one, inverse_one = norm_forward(source)
    normed = (plain_one * gain_one).astype(LOW)
    (normed,) = after((normed,), arrived_grad, up_moved)
    query_raw = jnp.dot(normed, full_query, preferred_element_type=FULL).reshape(
        row_count, HEADS, NOPE + ROPE
    )
    query_nope = query_raw[:, :, :NOPE].astype(LOW)
    query_rope = rotary(query_raw[:, :, NOPE:], positions, 1.0).astype(LOW)
    latent_raw = jnp.dot(normed, full_latent, preferred_element_type=FULL)
    plain_latent, inverse_latent = norm_forward(latent_raw[:, :LATENT])
    latent_norm = (plain_latent * gain_latent).astype(LOW)
    key_rope = rotary(latent_raw[:, LATENT:], positions, 1.0).astype(LOW)
    keys = lax.all_gather(
        jnp.concatenate([latent_norm, key_rope], axis=1), "ctx", axis=0, tiled=True
    )
    all_latent, all_keys = (keys[:, :LATENT], keys[:, LATENT:])
    expand = full_expand.reshape(LATENT, HEADS, NOPE + VDIM)
    expand_key = expand[:, :, :NOPE]
    expand_value = expand[:, :, NOPE:]
    query_latent = mm("thd,chd->thc", query_nope, expand_key).astype(LOW)
    scores = score_block(query_latent, query_rope, all_latent, all_keys, allowed, score_scale)
    row_max = jnp.max(scores, axis=-1, keepdims=True)
    row_sum = jnp.sum(jnp.exp(scores - row_max), axis=-1, keepdims=True)
    log_total = row_max + jnp.log(row_sum)
    soft_weights = jnp.exp(scores - log_total)
    latent_out = mm("htk,kc->thc", soft_weights.astype(LOW), all_latent).astype(LOW)
    values_out = (
        mm("thc,chv->thv", latent_out, expand_value).astype(LOW).reshape(row_count, HEADS * VDIM)
    )
    middle = source + jnp.dot(values_out, full_output, preferred_element_type=FULL)
    plain_two, inverse_two = norm_forward(middle)
    second = (plain_two * gain_two).astype(LOW)

    (second_sent,) = after((second,), down_moved)
    all_second, arrived_rows = gather_rows(second_sent, chooser_turned, ctx_count, fsdp_count)
    all_second = all_second.reshape(sequence, model_width)
    arrived_rows = arrived_rows.reshape(-1, model_width)
    gate_pre = jnp.dot(arrived_rows, gate_all, preferred_element_type=FULL)
    up_pre = jnp.dot(arrived_rows, up_all, preferred_element_type=FULL)
    gate_silu, gate_slope = silu_slope(gate_pre)
    hidden_act = (gate_silu * up_pre).astype(LOW)
    hidden_grad = mm("sd,fd->sf", arrived_grad, down_all)
    up_back = (hidden_grad * gate_silu).astype(LOW)
    gate_back = (hidden_grad * up_pre * gate_slope).astype(LOW)
    arrived_back = (mm("sf,df->sd", gate_back, gate_all) + mm("sf,df->sd", up_back, up_all)).astype(
        LOW
    )

    shared_g = jnp.dot(all_second, full_sgate, preferred_element_type=FULL)
    shared_u = jnp.dot(all_second, full_sup, preferred_element_type=FULL)
    shared_silu, shared_slope = silu_slope(shared_g)
    shared_hidden = (shared_silu * shared_u).astype(LOW)
    shared_hidden_grad = mm("td,fd->tf", all_cot, full_sdown)
    sup_back = (shared_hidden_grad * shared_silu).astype(LOW)
    sgate_back = (shared_hidden_grad * shared_u * shared_slope).astype(LOW)
    shared_second_grad = mm("tf,df->td", sgate_back, full_sgate) + mm(
        "tf,df->td", sup_back, full_sup
    )
    slots_shape = (ctx_count, fsdp_count, share, model_width)
    rows_shape = (ctx_count, row_count, model_width)
    second_grad = return_rows(
        arrived_back.reshape(slots_shape),
        chooser,
        shared_second_grad.reshape(rows_shape),
        ctx_count,
        fsdp_count,
        True,
    )
    hidden_act, gate_back, up_back, shared_hidden, sgate_back, sup_back = after(
        (hidden_act, gate_back, up_back, shared_hidden, sgate_back, sup_back), second_grad
    )
    result = jnp.dot(hidden_act, down_all, preferred_element_type=FULL).astype(LOW)
    shared_out = jnp.dot(shared_hidden, full_sdown, preferred_element_type=FULL)
    out_sum = return_rows(
        result.reshape(slots_shape),
        mixer,
        shared_out.reshape(rows_shape),
        ctx_count,
        fsdp_count,
        False,
    )
    layer_out = (middle + out_sum).astype(LOW)[None]

    gate_grad = mm("sd,sf->df", arrived_rows, gate_back).astype(LOW)
    up_grad = mm("sd,sf->df", arrived_rows, up_back).astype(LOW)
    down_grad = mm("sf,sd->fd", hidden_act, arrived_grad).astype(LOW)

    def give_back(grad, like):
        return return_expert(grad, members, fsdp_count).reshape(like.shape).astype(FULL)

    part_rows = model_width // ctx_count // members
    line_shape = (ctx_count, members, part_rows, hidden_units)
    expert_grads = (
        give_back(gate_grad.reshape(line_shape).swapaxes(0, 1), expert_gate),
        give_back(up_grad.reshape(line_shape).swapaxes(0, 1), expert_up),
        give_back(
            down_grad.reshape(members, hidden_units // members, ctx_count, -1).swapaxes(1, 2),
            expert_down,
        ),
    )
    pair_grad = jnp.stack(
        [mm("td,tf->df", all_second, sgate_back), mm("td,tf->df", all_second, sup_back)]
    ).astype(LOW)
    pair_grad = (
        pair_grad.reshape(2, ctx_count, fsdp_count, dense_rows, shared_units)
        .transpose(2, 0, 1, 3, 4)
        .reshape(fsdp_count, 2, ctx_count * dense_rows, shared_units)
    )
    pair_grad = lax.psum_scatter(pair_grad, "fsdp", scatter_dimension=0, tiled=False)
    pair_grad = lax.all_to_all(
        pair_grad, "ctx", split_axis=1, concat_axis=2, tiled=True
    ).astype(FULL)
    sdown_grad = mm("tf,td->fd", shared_hidden, all_cot).astype(LOW)
    sdown_grad = lax.psum_scatter(sdown_grad, "fsdp", scatter_dimension=0, tiled=True).astype(FULL)

    middle_part, gain_two_grad = norm_backward(second_grad, plain_two, inverse_two, gain_two)
    middle_grad = cot_full + middle_part
    attended_grad = middle_grad.astype(LOW)
    output_weight_grad = mm("tv,td->vd", values_out, attended_grad)
    values_grad = (
        mm("td,vd->tv", attended_grad, full_output).astype(LOW).reshape(row_count, HEADS, VDIM)
    )
    latent_out_grad = mm("thv,chv->thc", values_grad, expand_value).astype(LOW)
    expand_value_grad = mm("thc,thv->chv", latent_out, values_grad)
    scores = score_block(query_latent, query_rope, all_latent, all_keys, allowed, score_scale)
    soft_weights = jnp.exp(scores - log_total)
    soft_grad = mm("thc,kc->htk", latent_out_grad, all_latent)
    all_latent_grad = mm("htk,thc->kc", soft_weights.astype(LOW), latent_out_grad)
    row_inner = jnp.sum(soft_weights * soft_grad, axis=-1, keepdims=True)
    score_grad = (soft_weights * (soft_grad - row_inner) * score_scale).astype(LOW)
    query_latent_grad = mm("htk,kc->thc", score_grad, all_latent).astype(LOW)
    all_latent_grad = all_latent_grad + mm("htk,thc->kc", score_grad, query_latent)
    query_rope_grad = mm("htk,kd->thd", score_grad, all_keys)
    all_keys_grad = mm("htk,thd->kd", score_grad, query_rope)
    keys_part = lax.psum_scatter(
        jnp.concatenate([all_latent_grad, all_keys_grad], axis=1),
        "ctx",
        scatter_dimension=0,
        tiled=True,
    )
    latent_grad, keys_grad = (keys_part[:, :LATENT], keys_part[:, LATENT:])
    query_nope_grad = mm("thc,chd->thd", query_latent_grad, expand_key)
    expand_key_grad = mm("thd,thc->chd", query_nope, query_latent_grad)
    expand_grad = jnp.concatenate([expand_key_grad, expand_value_grad], axis=-1).reshape(
        LATENT, HEADS * (NOPE + VDIM)
    )
    query_grad = (
        jnp.concatenate([query_nope_grad, rotary(query_rope_grad, positions, -1.0)], axis=-1)
        .astype(LOW)
        .reshape(row_count, HEADS * (NOPE + ROPE))
    )
    latent_part_grad, gain_latent_grad = norm_backward(
        latent_grad, plain_latent, inverse_latent, gain_latent
    )
    latent_raw_grad = jnp.concatenate(
        [latent_part_grad, rotary(keys_grad, positions, -1.0)], axis=-1
    ).astype(LOW)
    query_weight_grad = mm("td,tq->dq", normed, query_grad)
    latent_weight_grad = mm("td,tq->dq", normed, latent_raw_grad)
    normed_grad = mm("tq,dq->td", query_grad, full_query) + mm(
        "tq,dq->td", latent_raw_grad, full_latent
    )
    source_part, gain_one_grad = norm_backward(normed_grad, plain_one, inverse_one, gain_one)
    tokens_grad = (middle_grad + source_part)[None]

    gain_latent_column = jnp.pad(
        gain_latent_grad.reshape(device_count, gain_rows), ((0, 0), (0, dense_rows - gain_rows))
    ).reshape(model_width)
    tail_grad = jnp.concatenate(
        [
            latent_weight_grad,
            gain_one_grad[:, None],
            gain_two_grad[:, None],
            gain_latent_column[:, None],
            jnp.zeros((model_width, 256 - ROPE - 3), FULL),
        ],
        axis=1,
    )
    query_sum, tail_sum, expand_sum, output_sum = scatter_all(
        (query_weight_grad, tail_grad, expand_grad, output_weight_grad), ctx_count, fsdp_count
    )
    return (
        layer_out,
        tokens_grad,
        tail_sum[:, rotary_end],
        query_sum,
        tail_sum[:, :rotary_end],
        tail_sum[:gain_rows, rotary_end + 2],
        expand_sum,
        output_sum,
        tail_sum[:, rotary_end + 1],
        pair_grad[0],
        pair_grad[1],
        sdown_grad,
        expert_grads[0],
        expert_grads[1],
        expert_grads[2],
    )


def solution(mesh):
    in_specs = (
        P("fsdp", "ctx", None),
        P("fsdp", "ctx", None),
        P("fsdp", "ctx", None),
        P("fsdp", "ctx", None),
        P(("ctx", "fsdp")),
        P(("ctx", "fsdp"), None),
        P(("ctx", "fsdp"), None),
        P(("ctx", "fsdp")),
        P(("ctx", "fsdp"), None),
        P(("ctx", "fsdp"), None),
        P(("ctx", "fsdp")),
        P(("ctx", "fsdp"), None),
        P(("ctx", "fsdp"), None),
        P(("ctx", "fsdp"), None),
        P("fsdp", "ctx", None),
        P("fsdp", "ctx", None),
        P("fsdp", None, "ctx"),
    )
    out_specs = (
        P("fsdp", "ctx", None),
        P("fsdp", "ctx", None),
        P(("ctx", "fsdp")),
        P(("ctx", "fsdp"), None),
        P(("ctx", "fsdp"), None),
        P(("ctx", "fsdp")),
        P(("ctx", "fsdp"), None),
        P(("ctx", "fsdp"), None),
        P(("ctx", "fsdp")),
        P(("ctx", "fsdp"), None),
        P(("ctx", "fsdp"), None),
        P(("ctx", "fsdp"), None),
        P("fsdp", "ctx", None),
        P("fsdp", "ctx", None),
        P("fsdp", None, "ctx"),
    )
    return jax.shard_map(local, mesh=mesh, in_specs=in_specs, out_specs=out_specs, check_vma=False)
```

```python
import functools

import jax
import jax.numpy as jnp
from jax import lax
from jax.experimental import pallas as pl
from jax.experimental.pallas import tpu as pltpu
from jax.sharding import PartitionSpec as P

HEADS = 16
NOPE = 128
ROPE = 64
LATENT = 512
VDIM = 128
TOP = 6
EXP_DEV = 2


epsilon = 1e-06
rope_base = 10000.0
masked_score = -1e30


def stored_positions(row_index, per_device, block_count):
    device = row_index // per_device
    within = row_index % per_device
    half_block = per_device // 2
    return jnp.where(
        within >= half_block,
        (block_count - 1 - device) * half_block + within - half_block,
        device * half_block + within,
    )


def rotary(values, positions, direction):
    half_rope = values.shape[-1] // 2
    frequency = rope_base ** (-jnp.arange(half_rope, dtype=jnp.float32) / half_rope)
    angles = positions.astype(jnp.float32)[:, None] * frequency[None, :]
    cosine_table = jnp.cos(angles)
    sine_table = direction * jnp.sin(angles)
    if values.ndim == 3:
        cosine_table = cosine_table[:, None, :]
        sine_table = sine_table[:, None, :]
    front_half = values[..., :half_rope]
    back_half = values[..., half_rope:]
    return jnp.concatenate(
        [
            front_half * cosine_table - back_half * sine_table,
            back_half * cosine_table + front_half * sine_table,
        ],
        axis=-1,
    )


def norm_forward(values):
    inverse = lax.rsqrt(jnp.mean(values * values, axis=-1, keepdims=True) + epsilon)
    return (values * inverse, inverse)


def norm_backward(normed_grad, plain, inverse, gain):
    gain_grad = jnp.sum(normed_grad * plain, axis=0)
    scaled = normed_grad * gain
    return (
        inverse * (scaled - plain * jnp.mean(scaled * plain, axis=-1, keepdims=True)),
        gain_grad,
    )


def silu_slope(values):
    sigma = jax.nn.sigmoid(values)
    return (values * sigma, sigma * (1.0 + values * (1.0 - sigma)))


LOW = jnp.bfloat16
FULL = jnp.float32


MESH_ID = pl.DeviceIdType.MESH
BIG_VMEM = 60 * 1024 * 1024


def flip(index, bit):
    return index + bit - 2 * bit * lax.rem(lax.div(index, bit), 2)


def toggled(index, mask):
    for bit in (1, 2, 4):
        if mask & bit:
            index = flip(index, bit)
    return index


def nearest(z, step):
    upper = lax.div(z, 2)
    if step == 0:
        return z
    if step == 1:
        return z + 1 - 2 * upper
    if step == 2:
        return 2 - 2 * lax.rem(z, 2) + upper
    return 3 - 3 * upper


def remote(source, target, send, receive, z, f):
    return pltpu.make_async_remote_copy(
        src_ref=source,
        dst_ref=target,
        send_sem=send,
        recv_sem=receive,
        device_id={"ctx": z, "fsdp": f},
        device_id_type=MESH_ID,
    )


def greet(z, f, masks, ctx_count, whole_line=False):
    barrier = pltpu.get_barrier_semaphore()

    def hello(to_z, to_f):
        pl.semaphore_signal(
            barrier, inc=1, device_id={"ctx": to_z, "fsdp": to_f}, device_id_type=MESH_ID
        )

    for mask in masks:
        hello(z, toggled(f, mask))
    if whole_line:
        for step in range(1, ctx_count):
            hello(lax.rem(z + step, ctx_count), f)
        pl.semaphore_wait(barrier, len(masks) + ctx_count - 1)
        return

    @pl.when(z > 0)
    def _():
        hello(z - 1, f)

    @pl.when(z < ctx_count - 1)
    def _():
        hello(z + 1, f)

    along = lax.div(z + ctx_count - 1, ctx_count) + lax.div(2 * ctx_count - 2 - z, ctx_count)
    pl.semaphore_wait(barrier, len(masks) + along)


def both_ways(z, block, ctx_count, act):
    @pl.when((block <= z) & (z < ctx_count - 1))
    def _():
        act(0, z + 1)

    @pl.when((block >= z) & (z > 0))
    def _():
        act(1, z - 1)


def halves(rows, width):
    if rows % 32 == 0:
        return tuple((pl.ds(start, rows // 2), slice(None)) for start in (0, rows // 2))
    return tuple((slice(None), pl.ds(start, width // 2)) for start in (0, width // 2))


def gather_kernel(ctx_count, kinds, *refs):
    count = len(kinds)
    shards, outs = refs[:count], refs[count : 2 * count]
    own_sem, z_send, z_recv, p_send, p_recv, c_send, c_recv = refs[2 * count :]
    z, f = lax.axis_index("ctx"), lax.axis_index("fsdp")
    core, x_near, y_near = flip(f, 1), flip(f, 2), flip(f, 4)
    far = flip(x_near, 4)
    greet(z, f, (1, 2, 4), ctx_count, True)

    def slot(item, step):
        return 0 if kinds[item] == "plane" else nearest(z, step)

    def steps(item, step):
        return step == 0 if kinds[item] == "plane" else 0 <= step < ctx_count

    def z_view(item, block):
        return outs[item].at[block] if kinds[item] == "column" else outs[item].at[block, f]

    def own(item):
        source = shards[item].at[z] if kinds[item] == "line" else shards[item]
        return pltpu.make_async_copy(source, z_view(item, slot(item, 0)), own_sem.at[item])

    def z_copy(item, block, way, target):
        at = z_view(item, block)
        return remote(at, at, z_send.at[item, block, way], z_recv.at[item, block], target, f)

    def piece(item, step):
        target = lax.rem(z + step, ctx_count)
        return remote(
            shards[item].at[target],
            outs[item].at[z, f],
            z_send.at[item, target, 0],
            z_recv.at[item, z],
            target,
            f,
        )

    def part(item, block, at, which):
        rows, columns = halves(*outs[item].shape[2:])[which]
        return outs[item].at[block, at, rows, columns]

    def p_copy(item, block, which):
        at = (
            lambda: outs[item].at[block, f],
            lambda: outs[item].at[block, f],
            lambda: part(item, block, x_near, 0),
            lambda: part(item, block, y_near, 1),
        )[which]()
        to = (x_near, y_near, y_near, x_near)[which]
        sems = (p_send.at[item, block, which], p_recv.at[item, block, which])
        return remote(at, at, *sems, z, to)

    def p_arrived(item, block, which):
        at = (
            lambda: outs[item].at[block, x_near],
            lambda: outs[item].at[block, y_near],
            lambda: part(item, block, far, 0),
            lambda: part(item, block, far, 1),
        )[which]()
        sems = (p_send.at[item, block, which], p_recv.at[item, block, which])
        remote(at, at, *sems, z, x_near).wait_recv()

    def c_copy(item, block, which):
        at = outs[item].at[block, (f, x_near, y_near, far)[which]]
        sems = (c_send.at[item, block, which], c_recv.at[item, block, which])
        return remote(at, at, *sems, z, core)

    def c_arrived(item, block, which):
        at = outs[item].at[block, flip((f, x_near, y_near, far)[which], 1)]
        sems = (c_send.at[item, block, which], c_recv.at[item, block, which])
        remote(at, at, *sems, z, core).wait_recv()

    def first(item, step):
        block = slot(item, step)
        if step == 0:
            own(item).wait()
        else:
            at = z_view(item, block)
            sems = (z_send.at[item, block, 0], z_recv.at[item, block])
            remote(at, at, *sems, z, core).wait_recv()
        if kinds[item] in ("all", "column"):
            both_ways(z, block, ctx_count, lambda way, to: z_copy(item, block, way, to).start())
        if kinds[item] != "column":
            p_copy(item, block, 0).start()
            p_copy(item, block, 1).start()
            c_copy(item, block, 0).start()

    def second(item, step):
        block = slot(item, step)
        for which in (0, 1):
            p_arrived(item, block, which)
            p_copy(item, block, which + 2).start()
            c_copy(item, block, which + 1).start()

    def third(item, step):
        block = slot(item, step)
        p_arrived(item, block, 2)
        p_arrived(item, block, 3)
        c_copy(item, block, 3).start()

    for item in range(count):
        own(item).start()
        if kinds[item] == "line":
            for step in range(1, ctx_count):
                piece(item, step).start()
    for step in range(ctx_count + 2):
        for lag, stage in ((0, first), (1, second), (2, third)):
            for item in range(count):
                if steps(item, step - lag) and (lag == 0 or kinds[item] != "column"):
                    stage(item, step - lag)
    for item in range(count):
        for step in range(ctx_count):
            if not steps(item, step):
                continue
            block = slot(item, step)
            if kinds[item] != "column":
                for which in range(4):
                    c_arrived(item, block, which)
                    p_copy(item, block, which).wait_send()
                    c_copy(item, block, which).wait_send()
            if kinds[item] == "line" and step > 0:
                piece(item, step).wait_send()
            if kinds[item] in ("all", "column"):
                both_ways(
                    z, block, ctx_count, lambda way, to: z_copy(item, block, way, to).wait_send()
                )


def gather_arrays(items, ctx_count, fsdp_count):
    kinds = tuple(kind for kind, shard in items)
    shards = [shard for kind, shard in items]
    lead = {
        "all": (ctx_count, fsdp_count),
        "line": (ctx_count, fsdp_count),
        "plane": (1, fsdp_count),
        "column": (ctx_count,),
    }
    shapes = [
        lead[kind] + (shard.shape[1:] if kind == "line" else shard.shape) for kind, shard in items
    ]
    count = len(items)
    dma = pltpu.SemaphoreType.DMA
    four = dma((count, ctx_count, 4))
    return pl.pallas_call(
        functools.partial(gather_kernel, ctx_count, kinds),
        out_shape=[
            jax.ShapeDtypeStruct(shape, shard.dtype) for shape, shard in zip(shapes, shards)
        ],
        in_specs=[pl.BlockSpec(memory_space=pl.ANY)] * count,
        out_specs=[pl.BlockSpec(memory_space=pl.ANY)] * count,
        scratch_shapes=[
            dma((count,)),
            dma((count, ctx_count, 2)),
            dma((count, ctx_count)),
            four,
            four,
            four,
            four,
        ],
        compiler_params=pltpu.CompilerParams(collective_id=0, has_side_effects=True),
        cost_estimate=pl.CostEstimate(flops=0, bytes_accessed=500_000_000, transcendentals=0),
    )(*shards)


def add_rows(target, rows, *terms):
    @pl.loop(0, rows, step=16)
    def _(start):
        part = pl.ds(pl.multiple_of(start, 16), 16)
        total = terms[0][part, :].astype(FULL)
        for term in terms[1:]:
            total = total + term[part, :].astype(FULL)
        target[part, :] = total.astype(target.dtype)


def scatter_kernel(ctx_count, count, *refs):
    grads, outs = refs[:count], refs[count : 2 * count]
    banks = [refs[(2 + kind) * count : (3 + kind) * count] for kind in range(7)]
    load_sem, c_send, c_recv, p_send, p_recv, z_send, z_recv = refs[9 * count :]
    z, f = lax.axis_index("ctx"), lax.axis_index("fsdp")
    side = lax.rem(f, 2)
    chip = lax.div(f, 2)
    core, x_near, y_near = flip(f, 1), flip(f, 2), flip(f, 4)
    x_chip, y_chip = flip(chip, 1), flip(chip, 2)
    far_chip = flip(x_chip, 2)
    greet(z, f, (1, 2, 4), ctx_count)
    order = [nearest(z, ctx_count - 1 - step) for step in range(ctx_count)]

    def work(item):
        grad_ref, out_ref = grads[item], outs[item]
        mine, from_core, from_x, from_y, half_x, half_y, from_z = [bank[item] for bank in banks]
        rows, width = out_ref.shape
        left, right = pl.ds(0, width // 2), pl.ds(width // 2, width // 2)

        def load(block):
            return pltpu.make_async_copy(
                grad_ref.at[block, :, side], mine.at[block], load_sem.at[item, block]
            )

        def c_copy(block):
            return remote(
                grad_ref.at[block, :, 1 - side],
                from_core.at[block],
                c_send.at[item, block],
                c_recv.at[item, block],
                z,
                core,
            )

        def p_copy(block, which):
            source, target, to = (
                (mine.at[block, far_chip, :, left], half_y.at[block], y_near),
                (mine.at[block, far_chip, :, right], half_x.at[block], x_near),
                (mine.at[block, x_chip], from_x.at[block], x_near),
                (mine.at[block, y_chip], from_y.at[block], y_near),
            )[which]
            sems = (p_send.at[item, block, which], p_recv.at[item, block, which])
            return remote(source, target, *sems, z, to)

        def z_copy(block, way, target):
            return remote(
                mine.at[block, chip],
                from_z.at[way, block],
                z_send.at[item, block],
                z_recv.at[item, way, block],
                target,
                f,
            )

        def z_arrived(block, way):
            at = from_z.at[way, block]
            sems = (z_send.at[item, block], z_recv.at[item, way, block])
            remote(at, at, *sems, z, core).wait_recv()

        def start(step):
            c_copy(order[step]).start()
            load(order[step]).start()

        def first(step):
            block = order[step]
            load(block).wait()
            c_copy(block).wait_recv()
            far_part = mine.at[block, far_chip]
            add_rows(far_part, rows, far_part, from_core.at[block, far_chip])
            p_copy(block, 0).start()
            p_copy(block, 1).start()

        def second(step):
            block = order[step]
            x_part, y_part = mine.at[block, x_chip], mine.at[block, y_chip]
            add_rows(x_part, rows, x_part, from_core.at[block, x_chip])
            add_rows(y_part, rows, y_part, from_core.at[block, y_chip])
            p_copy(block, 0).wait_recv()
            x_left = mine.at[block, x_chip, :, left]
            add_rows(x_left, rows, x_left, half_y.at[block])
            p_copy(block, 2).start()
            p_copy(block, 1).wait_recv()
            y_right = mine.at[block, y_chip, :, right]
            add_rows(y_right, rows, y_right, half_x.at[block])
            p_copy(block, 3).start()

        def third(step):
            block = order[step]
            p_copy(block, 2).wait_recv()
            p_copy(block, 3).wait_recv()
            own = mine.at[block, chip]
            terms = (own, from_core.at[block, chip], from_x.at[block], from_y.at[block])
            if step == ctx_count - 1:

                @pl.when(z > 0)
                def _():
                    z_arrived(block, 0)

                @pl.when(z < ctx_count - 1)
                def _():
                    z_arrived(block, 1)

                @pl.when(z == 0)
                def _():
                    add_rows(out_ref, rows, *terms, from_z.at[1, block])

                @pl.when(z == ctx_count - 1)
                def _():
                    add_rows(out_ref, rows, *terms, from_z.at[0, block])

                @pl.when((z > 0) & (z < ctx_count - 1))
                def _():
                    add_rows(out_ref, rows, *terms, from_z.at[0, block], from_z.at[1, block])

                return

            for way, above in ((1, True), (0, False)):
                heading = (block < z) if above else (block > z)
                has_more = (z < ctx_count - 1) if above else (z > 0)

                @pl.when(heading & has_more)
                def _():
                    z_arrived(block, way)
                    add_rows(own, rows, *terms, from_z.at[way, block])

                @pl.when(heading & jnp.logical_not(has_more))
                def _():
                    add_rows(own, rows, *terms)

                @pl.when(heading)
                def _():
                    z_copy(block, way, z - 1 if above else z + 1).start()

        def finish(step):
            block = order[step]
            c_copy(block).wait_send()
            for which in range(4):
                p_copy(block, which).wait_send()
            if step < ctx_count - 1:
                z_copy(block, 0, z).wait_send()

        return start, first, second, third, finish

    stages = list(zip(*[work(item) for item in range(count)]))
    for step in range(ctx_count):
        for act in stages[0]:
            act(step)
    for step in range(ctx_count + 2):
        for lag in (0, 1, 2):
            if 0 <= step - lag < ctx_count:
                for act in stages[1 + lag]:
                    act(step - lag)
    for step in range(ctx_count):
        for act in stages[4]:
            act(step)


def scatter_arrays(grads, ctx_count, fsdp_count):
    count = len(grads)
    chips = fsdp_count // 2
    shapes = [
        (grad.shape[0] // (ctx_count * fsdp_count), grad.shape[1]) for grad in grads
    ]
    dma = pltpu.SemaphoreType.DMA
    leads = [(ctx_count, chips), (ctx_count, chips), (ctx_count,), (ctx_count,)]
    banks = [pltpu.VMEM(lead + shape, LOW) for lead in leads for shape in shapes]
    banks += [
        pltpu.VMEM((ctx_count, shape[0], shape[1] // 2), LOW) for _ in range(2) for shape in shapes
    ]
    banks += [pltpu.VMEM((2, ctx_count) + shape, LOW) for shape in shapes]
    return pl.pallas_call(
        functools.partial(scatter_kernel, ctx_count, count),
        out_shape=[jax.ShapeDtypeStruct(shape, FULL) for shape in shapes],
        in_specs=[pl.BlockSpec(memory_space=pl.ANY)] * count,
        out_specs=[pl.BlockSpec(memory_space=pltpu.VMEM)] * count,
        scratch_shapes=banks
        + [
            dma((count, ctx_count)),
            dma((count, ctx_count)),
            dma((count, ctx_count)),
            dma((count, ctx_count, 4)),
            dma((count, ctx_count, 4)),
            dma((count, ctx_count)),
            dma((count, 2, ctx_count)),
        ],
        compiler_params=pltpu.CompilerParams(
            collective_id=1, has_side_effects=True, vmem_limit_bytes=BIG_VMEM
        ),
        cost_estimate=pl.CostEstimate(flops=0, bytes_accessed=500_000_000, transcendentals=0),
    )(
        *[
            grad.reshape((ctx_count, chips, 2) + shape)
            for grad, shape in zip(grads, shapes)
        ]
    )


PEERS = (6, 7, 2, 4, 3, 5, 1)


def dispatch_kernel(
    ctx_count,
    rows_ref,
    choose_ref,
    all_ref,
    out_ref,
    blocks,
    chosen,
    own_sem,
    all_sem,
    keep_sem,
    z_send,
    z_recv,
    p_send,
    p_recv,
):
    z, f = lax.axis_index("ctx"), lax.axis_index("fsdp")
    width = rows_ref.shape[1]
    groups, share = chosen.shape[1], chosen.shape[2]
    greet(z, f, PEERS, ctx_count)
    own = pltpu.make_async_copy(rows_ref, blocks.at[z], own_sem)
    own.start()
    own.wait()

    def z_copy(block, way, target):
        at = blocks.at[block]
        return remote(at, at, z_send.at[block, way], z_recv.at[block], target, f)

    def p_copy(block, place):
        to = toggled(f, PEERS[place])
        return remote(
            chosen.at[block, to],
            out_ref.at[block, f],
            p_send.at[block, place],
            p_recv.at[block, place],
            z,
            to,
        )

    def p_arrived(block, place):
        at = out_ref.at[block, toggled(f, PEERS[place])]
        remote(at, at, p_send.at[block, place], p_recv.at[block, place], z, flip(f, 1)).wait_recv()

    def keep(block):
        return pltpu.make_async_copy(
            chosen.at[block, f], out_ref.at[block, f], keep_sem.at[block]
        )

    def store(block):
        return pltpu.make_async_copy(blocks.at[block], all_ref.at[block], all_sem.at[block])

    for step in range(ctx_count):
        block = nearest(z, step)
        if step > 0:
            at = blocks.at[block]
            remote(at, at, z_send.at[block, 0], z_recv.at[block], z, flip(f, 1)).wait_recv()
        both_ways(z, block, ctx_count, lambda way, to: z_copy(block, way, to).start())
        store(block).start()

        @pl.loop(0, width, step=256)
        def _(start):
            part = pl.ds(pl.multiple_of(start, 256), 256)
            tile = jnp.dot(
                choose_ref[block], blocks[block, :, part], preferred_element_type=FULL
            ).astype(LOW)
            chosen[block, :, :, part] = tile.reshape(groups, share, 256)

        for place in range(len(PEERS)):
            p_copy(block, place).start()
        keep(block).start()
    for step in range(ctx_count):
        block = nearest(z, step)
        store(block).wait()
        keep(block).wait()
        for place in range(len(PEERS)):
            p_arrived(block, place)
    for step in range(ctx_count):
        block = nearest(z, step)
        both_ways(z, block, ctx_count, lambda way, to: z_copy(block, way, to).wait_send())
        for place in range(len(PEERS)):
            p_copy(block, place).wait_send()


def dispatch_rows(rows, chooser, ctx_count, fsdp_count):
    count, width = rows.shape
    share = chooser.shape[1] // fsdp_count
    dma = pltpu.SemaphoreType.DMA
    return pl.pallas_call(
        functools.partial(dispatch_kernel, ctx_count),
        out_shape=(
            jax.ShapeDtypeStruct((ctx_count, count, width), LOW),
            jax.ShapeDtypeStruct((ctx_count, fsdp_count, share, width), LOW),
        ),
        in_specs=[pl.BlockSpec(memory_space=pl.ANY), pl.BlockSpec(memory_space=pltpu.VMEM)],
        out_specs=(pl.BlockSpec(memory_space=pl.ANY), pl.BlockSpec(memory_space=pl.ANY)),
        scratch_shapes=[
            pltpu.VMEM((ctx_count, count, width), LOW),
            pltpu.VMEM((ctx_count, fsdp_count, share, width), LOW),
            dma,
            dma((ctx_count,)),
            dma((ctx_count,)),
            dma((ctx_count, 2)),
            dma((ctx_count,)),
            dma((ctx_count, len(PEERS))),
            dma((ctx_count, len(PEERS))),
        ],
        compiler_params=pltpu.CompilerParams(
            collective_id=2, has_side_effects=True, vmem_limit_bytes=BIG_VMEM
        ),
        cost_estimate=pl.CostEstimate(
            flops=2_000_000_000, bytes_accessed=300_000_000, transcendentals=0
        ),
    )(rows, chooser)


def combine_kernel(
    ctx_count,
    slots_ref,
    mix_ref,
    extra_ref,
    out_ref,
    arrived,
    extra,
    parts,
    from_z,
    keep_sem,
    extra_sem,
    p_send,
    p_recv,
    z_send,
    z_recv,
):
    z, f = lax.axis_index("ctx"), lax.axis_index("fsdp")
    count, width = out_ref.shape
    slots = mix_ref.shape[2]
    greet(z, f, PEERS, ctx_count)

    def p_copy(block, place):
        to = toggled(f, PEERS[place])
        return remote(
            slots_ref.at[block, to],
            arrived.at[block, f],
            p_send.at[block, place],
            p_recv.at[block, place],
            z,
            to,
        )

    def p_arrived(block, place):
        at = arrived.at[block, toggled(f, PEERS[place])]
        remote(at, at, p_send.at[block, place], p_recv.at[block, place], z, flip(f, 1)).wait_recv()

    def keep(block):
        return pltpu.make_async_copy(
            slots_ref.at[block, f], arrived.at[block, f], keep_sem.at[block]
        )

    def load(block):
        return pltpu.make_async_copy(extra_ref.at[block], extra.at[block], extra_sem.at[block])

    def z_copy(block, way, target):
        return remote(
            parts.at[block],
            from_z.at[way, block],
            z_send.at[block],
            z_recv.at[way, block],
            target,
            f,
        )

    def z_arrived(block, way):
        at = from_z.at[way, block]
        remote(at, at, z_send.at[block], z_recv.at[way, block], z, flip(f, 1)).wait_recv()

    def mix(block, target, *ways):
        @pl.loop(0, width, step=256)
        def _(start):
            part = pl.ds(pl.multiple_of(start, 256), 256)
            total = jnp.dot(
                mix_ref[block],
                arrived[block, :, :, part].reshape(slots, 256),
                preferred_element_type=FULL,
            ) + extra[block, :, part].astype(FULL)
            for way in ways:
                total = total + from_z[way, block, :, part].astype(FULL)
            target[:, part] = total.astype(target.dtype)

    order = [nearest(z, ctx_count - 1 - step) for step in range(ctx_count)]
    for block in order:
        for place in range(len(PEERS)):
            p_copy(block, place).start()
        keep(block).start()
        load(block).start()
    for step in range(ctx_count):
        block = order[step]
        keep(block).wait()
        load(block).wait()
        for place in range(len(PEERS)):
            p_arrived(block, place)
        if step < ctx_count - 1:
            for way, above in ((1, True), (0, False)):
                heading = (block < z) if above else (block > z)
                has_more = (z < ctx_count - 1) if above else (z > 0)

                @pl.when(heading & has_more)
                def _():
                    z_arrived(block, way)
                    mix(block, parts.at[block], way)

                @pl.when(heading & jnp.logical_not(has_more))
                def _():
                    mix(block, parts.at[block])

                @pl.when(heading)
                def _():
                    z_copy(block, way, z - 1 if above else z + 1).start()

        else:

            @pl.when(z > 0)
            def _():
                z_arrived(block, 0)

            @pl.when(z < ctx_count - 1)
            def _():
                z_arrived(block, 1)

            @pl.when(z == 0)
            def _():
                mix(block, out_ref, 1)

            @pl.when(z == ctx_count - 1)
            def _():
                mix(block, out_ref, 0)

            @pl.when((z > 0) & (z < ctx_count - 1))
            def _():
                mix(block, out_ref, 0, 1)

    for step in range(ctx_count):
        block = order[step]
        for place in range(len(PEERS)):
            p_copy(block, place).wait_send()
        if step < ctx_count - 1:
            z_copy(block, 0, z).wait_send()


def combine_rows(slots, mixer, extra, ctx_count, fsdp_count):
    share, width = slots.shape[2:]
    count = mixer.shape[1]
    dma = pltpu.SemaphoreType.DMA
    return pl.pallas_call(
        functools.partial(combine_kernel, ctx_count),
        out_shape=jax.ShapeDtypeStruct((count, width), FULL),
        in_specs=[
            pl.BlockSpec(memory_space=pl.ANY),
            pl.BlockSpec(memory_space=pltpu.VMEM),
            pl.BlockSpec(memory_space=pl.ANY),
        ],
        out_specs=pl.BlockSpec(memory_space=pltpu.VMEM),
        scratch_shapes=[
            pltpu.VMEM((ctx_count, fsdp_count, share, width), LOW),
            pltpu.VMEM((ctx_count, count, width), LOW),
            pltpu.VMEM((ctx_count, count, width), LOW),
            pltpu.VMEM((2, ctx_count, count, width), LOW),
            dma((ctx_count,)),
            dma((ctx_count,)),
            dma((ctx_count, len(PEERS))),
            dma((ctx_count, len(PEERS))),
            dma((ctx_count,)),
            dma((2, ctx_count)),
        ],
        compiler_params=pltpu.CompilerParams(
            collective_id=3, has_side_effects=True, vmem_limit_bytes=BIG_VMEM
        ),
        cost_estimate=pl.CostEstimate(
            flops=2_000_000_000, bytes_accessed=300_000_000, transcendentals=0
        ),
    )(slots, mixer, extra)


HEAD_GROUP = 4
KEYS = 256


def dot_last(left, right):
    return lax.dot_general(left, right, (((1,), (1,)), ((), ())), preferred_element_type=FULL)


def dot_first(left, right):
    return lax.dot_general(left, right, (((0,), (0,)), ((), ())), preferred_element_type=FULL)


def reach(half, rows, ctx_count):
    ctx = lax.axis_index("ctx")
    first = jnp.where(half == 0, ctx, 2 * ctx_count - 1 - ctx) * rows
    return first, lax.div(first + rows + KEYS - 1, KEYS)


def block_scores(query, turned, keys_ref, rope_ref, index, first, rows, scale):
    part = pl.ds(pl.multiple_of(index * KEYS, KEYS), KEYS)
    keys, rope = keys_ref[part, :], rope_ref[part, :]
    scores = (dot_last(query, keys) + dot_last(turned, rope)) * scale
    shape = scores.shape
    at = first + lax.rem(lax.broadcasted_iota(jnp.int32, shape, 0), rows)
    key_at = index * KEYS + lax.broadcasted_iota(jnp.int32, shape, 1)
    return part, keys, rope, scores, at >= key_at


def attend_kernel(
    ctx_count, scale, query_ref, turned_ref, keys_ref, rope_ref, out_ref, log_ref, total, top, norm
):
    heads, rows, width = query_ref.shape
    first, blocks = reach(pl.program_id(0), rows, ctx_count)
    query = query_ref[...].reshape(heads * rows, width)
    turned = turned_ref[...].reshape(heads * rows, -1)
    total[...] = jnp.zeros_like(total)
    norm[...] = jnp.zeros_like(norm)
    top[...] = jnp.full_like(top, masked_score)

    @pl.loop(0, blocks)
    def _(index):
        part, keys, rope, scores, seen = block_scores(
            query, turned, keys_ref, rope_ref, index, first, rows, scale
        )
        scores = jnp.where(seen, scores, masked_score)
        old = top[...]
        new = jnp.maximum(old, jnp.max(scores, axis=1, keepdims=True))
        weights = jnp.exp(scores - new)
        shrink = jnp.exp(old - new)
        top[...] = new
        norm[...] = norm[...] * shrink + jnp.sum(weights, axis=1, keepdims=True)
        total[...] = total[...] * shrink + jnp.dot(
            weights.astype(LOW), keys, preferred_element_type=FULL
        )

    out_ref[...] = (total[...] / norm[...]).astype(LOW).reshape(out_ref.shape)
    log_ref[...] = (top[...] + jnp.log(norm[...])).reshape(log_ref.shape)


def attend_back_kernel(
    ctx_count,
    scale,
    query_ref,
    turned_ref,
    keys_ref,
    rope_ref,
    out_ref,
    log_ref,
    grad_ref,
    query_grad_ref,
    turned_grad_ref,
    keys_grad_ref,
    rope_grad_ref,
    query_total,
    turned_total,
):
    heads, rows, width = query_ref.shape
    first, blocks = reach(pl.program_id(0), rows, ctx_count)
    query = query_ref[...].reshape(heads * rows, width)
    turned = turned_ref[...].reshape(heads * rows, -1)
    grad = grad_ref[...].reshape(heads * rows, width)
    out = out_ref[...].reshape(heads * rows, width)
    logs = log_ref[...].reshape(heads * rows, 1)
    inner = jnp.sum(grad.astype(FULL) * out.astype(FULL), axis=1, keepdims=True)
    query_total[...] = jnp.zeros_like(query_total)
    turned_total[...] = jnp.zeros_like(turned_total)

    @pl.when((pl.program_id(0) == 0) & (pl.program_id(1) == 0))
    def _():
        keys_grad_ref[...] = jnp.zeros_like(keys_grad_ref)
        rope_grad_ref[...] = jnp.zeros_like(rope_grad_ref)

    @pl.loop(0, blocks)
    def _(index):
        part, keys, rope, scores, seen = block_scores(
            query, turned, keys_ref, rope_ref, index, first, rows, scale
        )
        weights = jnp.where(seen, jnp.exp(scores - logs), 0.0)
        change = (weights * (dot_last(grad, keys) - inner) * scale).astype(LOW)
        query_total[...] += jnp.dot(change, keys, preferred_element_type=FULL)
        turned_total[...] += jnp.dot(change, rope, preferred_element_type=FULL)
        keys_grad_ref[part, :] += dot_first(change, query) + dot_first(weights.astype(LOW), grad)
        rope_grad_ref[part, :] += dot_first(change, turned)

    query_grad_ref[...] = query_total[...].astype(LOW).reshape(query_grad_ref.shape)
    turned_grad_ref[...] = turned_total[...].reshape(turned_grad_ref.shape)


def attend_specs(heads, group, rows, widths):
    return [pl.BlockSpec((group, rows, width), lambda half, g: (g, half, 0)) for width in widths]


def whole_spec(array):
    return pl.BlockSpec(array.shape, lambda half, g: (0, 0))


def attend(query, turned, keys, rope, ctx_count, scale):
    heads, count, width = query.shape
    group, rows = HEAD_GROUP, count // 2
    lanes = turned.shape[2]
    return pl.pallas_call(
        functools.partial(attend_kernel, ctx_count, scale),
        grid=(2, heads // group),
        out_shape=(
            jax.ShapeDtypeStruct((heads, count, width), LOW),
            jax.ShapeDtypeStruct((heads, count, 1), FULL),
        ),
        in_specs=attend_specs(heads, group, rows, (width, lanes))
        + [whole_spec(keys), whole_spec(rope)],
        out_specs=tuple(attend_specs(heads, group, rows, (width, 1))),
        scratch_shapes=[
            pltpu.VMEM((group * rows, width), FULL),
            pltpu.VMEM((group * rows, 1), FULL),
            pltpu.VMEM((group * rows, 1), FULL),
        ],
        compiler_params=pltpu.CompilerParams(vmem_limit_bytes=BIG_VMEM),
        cost_estimate=pl.CostEstimate(
            flops=12_000_000_000, bytes_accessed=12_000_000, transcendentals=3_000_000
        ),
    )(query, turned, keys, rope)


def attend_back(query, turned, keys, rope, out, logs, grad, ctx_count, scale):
    heads, count, width = query.shape
    group, rows = HEAD_GROUP, count // 2
    lanes = turned.shape[2]
    return pl.pallas_call(
        functools.partial(attend_back_kernel, ctx_count, scale),
        grid=(2, heads // group),
        out_shape=(
            jax.ShapeDtypeStruct((heads, count, width), LOW),
            jax.ShapeDtypeStruct((heads, count, lanes), FULL),
            jax.ShapeDtypeStruct(keys.shape, FULL),
            jax.ShapeDtypeStruct(rope.shape, FULL),
        ),
        in_specs=attend_specs(heads, group, rows, (width, lanes))
        + [whole_spec(keys), whole_spec(rope)]
        + attend_specs(heads, group, rows, (width, 1, width)),
        out_specs=tuple(
            attend_specs(heads, group, rows, (width, lanes)) + [whole_spec(keys), whole_spec(rope)]
        ),
        scratch_shapes=[
            pltpu.VMEM((group * rows, width), FULL),
            pltpu.VMEM((group * rows, lanes), FULL),
        ],
        compiler_params=pltpu.CompilerParams(vmem_limit_bytes=BIG_VMEM),
        cost_estimate=pl.CostEstimate(
            flops=30_000_000_000, bytes_accessed=30_000_000, transcendentals=3_000_000
        ),
    )(query, turned, keys, rope, out, logs, grad)


def mm(subscripts, left, right):
    return jnp.einsum(subscripts, left, right, preferred_element_type=FULL)


def member_pairs(fsdp_count, members, step):
    return [
        (f, f // members * members + (f % members + step) % members) for f in range(fsdp_count)
    ]


def by_member(own, others, member, members):
    if members == 2:
        first = member == 0
        return jnp.stack([jnp.where(first, own, others[0]), jnp.where(first, others[0], own)])
    stack = jnp.stack([own] + others)
    return jnp.take(stack, (member - jnp.arange(members)) % members, axis=0)


def part_of(array, member, step, members):
    return lax.dynamic_index_in_dim(array, (member + step) % members, 0, keepdims=False)


def swap_parts(array, members, fsdp_count):
    member = lax.axis_index("fsdp") % members
    others = [
        lax.ppermute(
            part_of(array, member, step, members), "fsdp", member_pairs(fsdp_count, members, step)
        )
        for step in range(1, members)
    ]
    return by_member(part_of(array, member, 0, members), others, member, members)


def share_parts(array, members, fsdp_count):
    member = lax.axis_index("fsdp") % members
    others = [
        lax.ppermute(array, "fsdp", member_pairs(fsdp_count, members, step))
        for step in range(1, members)
    ]
    return by_member(array, others, member, members)


def sum_parts(array, members, fsdp_count):
    member = lax.axis_index("fsdp") % members
    total = part_of(array, member, 0, members).astype(FULL)
    for step in range(1, members):
        total = total + lax.ppermute(
            part_of(array, member, step, members), "fsdp", member_pairs(fsdp_count, members, step)
        ).astype(FULL)
    return total.astype(LOW)


def gather_rows(rows, chooser, ctx_count, fsdp_count):
    if (ctx_count, fsdp_count) == (4, 8):
        return dispatch_rows(rows, chooser, ctx_count, fsdp_count)
    every = lax.all_gather(rows, "ctx", axis=0)
    chosen = mm("bst,btd->bsd", chooser, every).astype(LOW)
    chosen = chosen.reshape(ctx_count, fsdp_count, -1, rows.shape[1])
    return every, lax.all_to_all(chosen, "fsdp", split_axis=1, concat_axis=1, tiled=True)


def return_rows(slots, mixer, extra, ctx_count, fsdp_count):
    if (ctx_count, fsdp_count) == (4, 8):
        return combine_rows(slots, mixer, extra.astype(LOW), ctx_count, fsdp_count)
    back = lax.all_to_all(slots, "fsdp", split_axis=1, concat_axis=1, tiled=True)
    back = back.reshape(ctx_count, mixer.shape[2], -1)
    total = (mm("bts,bsd->btd", mixer, back) + extra).astype(LOW)
    return lax.psum_scatter(total, "ctx", scatter_dimension=0, tiled=False).astype(FULL)


def gather_all(items, ctx_count, fsdp_count):
    if (ctx_count, fsdp_count) == (4, 8):
        return gather_arrays(items, ctx_count, fsdp_count)
    results = []
    for kind, shard in items:
        if kind == "line":
            shard = lax.all_to_all(shard, "ctx", split_axis=0, concat_axis=0, tiled=True)
            result = lax.all_gather(shard, "fsdp", axis=1)
        elif kind == "plane":
            result = lax.all_gather(shard, "fsdp", axis=0)[None]
        elif kind == "column":
            result = lax.all_gather(shard, "ctx", axis=0)
        else:
            result = lax.all_gather(shard, ("ctx", "fsdp"), axis=0)
            result = result.reshape((ctx_count, fsdp_count) + shard.shape)
        results.append(result)
    return results


def scatter_all(grads, ctx_count, fsdp_count):
    grads = [grad.astype(LOW) for grad in grads]
    if (ctx_count, fsdp_count) == (4, 8):
        return scatter_arrays(grads, ctx_count, fsdp_count)
    return [
        lax.psum_scatter(grad, ("ctx", "fsdp"), scatter_dimension=0, tiled=True).astype(FULL)
        for grad in grads
    ]


def along_line(array):
    return lax.all_to_all(array, "ctx", split_axis=0, concat_axis=0, tiled=True)


def after(values, *others):
    tied = lax.optimization_barrier((tuple(values), others))
    return tied[0]


def local(
    tokens,
    routes,
    gate_values,
    cotangent,
    attention_gain,
    query_weight,
    latent_weight,
    latent_gain,
    expand_weight,
    output_weight,
    feedforward_gain,
    shared_gate,
    shared_up,
    shared_down,
    expert_gate,
    expert_up,
    expert_down,
):
    row_count = tokens.shape[1]
    model_width = tokens.shape[2]
    ctx_count = lax.axis_size("ctx")
    fsdp_count = lax.axis_size("fsdp")
    device_count = ctx_count * fsdp_count
    experts_total = EXP_DEV * fsdp_count
    capacity = row_count * TOP * 4 // (3 * experts_total)
    members = ctx_count // EXP_DEV
    plane_experts = experts_total // ctx_count
    plane_slots = plane_experts * capacity
    share = capacity // members
    sequence = ctx_count * row_count
    z = lax.axis_index("ctx")
    score_scale = (NOPE + ROPE) ** (-0.5)
    source = tokens[0].astype(FULL)
    cot_low = cotangent[0]
    cot_full = cot_low.astype(FULL)
    positions = stored_positions(
        z * row_count + jnp.arange(row_count, dtype=jnp.int32), row_count, 2 * ctx_count
    )
    dense_rows = latent_weight.shape[0]
    gain_rows = latent_gain.shape[0]
    rotary_end = LATENT + ROPE
    hidden_units = expert_gate.shape[2]
    shared_units = shared_gate.shape[1] // ctx_count

    def swapped(weight):
        weight = weight.reshape((EXP_DEV, members, weight.shape[1] // members) + weight.shape[2:])
        weight = swap_parts(weight.swapaxes(0, 1), members, fsdp_count)
        return weight.reshape((ctx_count,) + weight.shape[2:])

    gate_swapped, up_swapped, down_swapped = (
        swapped(expert_gate),
        swapped(expert_up),
        swapped(expert_down),
    )
    gate_moved = along_line(gate_swapped)

    local_routes = routes[0]
    expert_index = jnp.arange(experts_total, dtype=jnp.int32)
    member_of = (local_routes[..., None] == expert_index).astype(FULL)
    counts = jnp.sum(member_of, axis=1)
    before = jnp.cumsum(counts, axis=0) - counts
    within = jnp.sum(member_of * before[:, None, :], axis=-1).astype(jnp.int32)
    info = jnp.concatenate(
        [
            (local_routes * capacity + within).astype(FULL).T,
            gate_values[0].T,
            jnp.zeros((16 - 2 * TOP, row_count), FULL),
        ]
    )

    tail = jnp.concatenate(
        [
            latent_weight,
            attention_gain[:, None],
            feedforward_gain[:, None],
            jnp.pad(latent_gain, (0, dense_rows - gain_rows))[:, None],
            jnp.zeros((dense_rows, 256 - ROPE - 3), LOW),
        ],
        axis=1,
    )

    def by_line(weight):
        return weight.reshape(dense_rows, ctx_count, shared_units).swapaxes(0, 1)

    dense = (
        info,
        query_weight,
        tail,
        expand_weight,
        output_weight,
        by_line(shared_gate),
        by_line(shared_up),
        shared_down,
    )
    dense = after(dense, gate_swapped, up_swapped, down_swapped)
    kinds = ("column", "all", "all", "all", "all", "line", "line", "plane")
    gathered = gather_all(list(zip(kinds, dense)), ctx_count, fsdp_count)
    all_info = gathered[0]
    full_query, full_tail, full_expand, full_output, full_sgate, full_sup, full_sdown = [
        item.reshape(-1, item.shape[-1]) for item in gathered[1:]
    ]
    full_latent = full_tail[:, :rotary_end]
    gain_one = full_tail[:, rotary_end].astype(FULL)
    gain_two = full_tail[:, rotary_end + 1].astype(FULL)
    gain_latent = (
        full_tail[:, rotary_end + 2].reshape(device_count, dense_rows)[:, :gain_rows]
    ).reshape(LATENT).astype(FULL)

    flat = all_info[:, :TOP].astype(jnp.int32)
    all_gates = all_info[:, TOP : 2 * TOP]
    owner = flat // capacity
    slot = jnp.where(
        owner % ctx_count == z, owner // ctx_count * capacity + flat % capacity, -1
    )
    slot_index = jnp.arange(plane_slots, dtype=jnp.int32)
    hits = slot[:, :, :, None] == slot_index
    chooser = jnp.sum(hits.astype(FULL), axis=1).astype(LOW)
    mixer = jnp.sum(jnp.where(hits, all_gates[:, :, :, None], 0.0), axis=1).astype(LOW)
    hits = slot[:, :, None, :] == slot_index[:, None]
    chooser_turned = jnp.sum(hits.astype(FULL), axis=1).astype(LOW)
    mixer_turned = jnp.sum(jnp.where(hits, all_gates[:, :, None, :], 0.0), axis=1).astype(LOW)

    (up_swapped,) = after((up_swapped,), all_info)
    up_moved = along_line(up_swapped)
    (cot_sent,) = after((cot_low,), gate_moved)
    all_cot, arrived_grad = gather_rows(cot_sent, mixer_turned, ctx_count, fsdp_count)
    (down_swapped,) = after((down_swapped,), arrived_grad)
    down_moved = along_line(down_swapped)
    all_cot = all_cot.reshape(sequence, model_width)
    arrived_grad = arrived_grad.reshape(-1, model_width)

    def whole(moved):
        return share_parts(moved, members, fsdp_count).swapaxes(0, 1)

    gate_all = whole(gate_moved).reshape(model_width, hidden_units)
    up_all = whole(up_moved).reshape(model_width, hidden_units)
    down_all = whole(down_moved).transpose(1, 2, 0, 3).reshape(hidden_units, model_width)

    plain_one, inverse_one = norm_forward(source)
    normed = (plain_one * gain_one).astype(LOW)
    (normed,) = after((normed,), arrived_grad, up_moved)
    (query_raw,) = after((jnp.dot(normed, full_query, preferred_element_type=FULL),))
    query_raw = query_raw.reshape(row_count, HEADS, NOPE + ROPE)
    query_nope = query_raw[:, :, :NOPE].astype(LOW)
    query_rope = rotary(query_raw[:, :, NOPE:], positions, 1.0).astype(LOW)
    latent_raw = jnp.dot(normed, full_latent, preferred_element_type=FULL)
    plain_latent, inverse_latent = norm_forward(latent_raw[:, :LATENT])
    latent_norm = (plain_latent * gain_latent).astype(LOW)
    key_rope = rotary(latent_raw[:, LATENT:], positions, 1.0).astype(LOW)
    half_rows = row_count // 2
    pad_rope = ((0, 0), (0, 128 - ROPE))
    keys = lax.all_gather(
        jnp.concatenate([latent_norm, jnp.pad(key_rope, pad_rope)], axis=1), "ctx", axis=0
    )
    keys = keys.reshape(ctx_count, 2, half_rows, LATENT + 128)
    keys = jnp.concatenate([keys[:, 0], keys[::-1, 1]]).reshape(sequence, LATENT + 128)
    all_latent, all_keys = (keys[:, :LATENT], keys[:, LATENT:])
    expand = full_expand.reshape(LATENT, HEADS, NOPE + VDIM)
    expand_key = expand[:, :, :NOPE]
    expand_value = expand[:, :, NOPE:]
    query_latent = mm("thd,chd->htc", query_nope, expand_key).astype(LOW)
    query_turned = jnp.pad(query_rope.swapaxes(0, 1), ((0, 0),) + pad_rope)
    latent_out, log_total = attend(
        query_latent, query_turned, all_latent, all_keys, ctx_count, score_scale
    )
    values_out = (
        mm("htc,chv->thv", latent_out, expand_value).astype(LOW).reshape(row_count, HEADS * VDIM)
    )
    middle = source + jnp.dot(values_out, full_output, preferred_element_type=FULL)
    plain_two, inverse_two = norm_forward(middle)
    second = (plain_two * gain_two).astype(LOW)

    (second_sent,) = after((second,), down_moved)
    all_second, arrived_rows = gather_rows(second_sent, chooser_turned, ctx_count, fsdp_count)
    all_second = all_second.reshape(sequence, model_width)
    arrived_rows = arrived_rows.reshape(-1, model_width)
    gate_pre = jnp.dot(arrived_rows, gate_all, preferred_element_type=FULL)
    up_pre = jnp.dot(arrived_rows, up_all, preferred_element_type=FULL)
    gate_silu, gate_slope = silu_slope(gate_pre)
    hidden_act = (gate_silu * up_pre).astype(LOW)
    hidden_grad = mm("sd,fd->sf", arrived_grad, down_all)
    up_back = (hidden_grad * gate_silu).astype(LOW)
    gate_back = (hidden_grad * up_pre * gate_slope).astype(LOW)
    arrived_back = (mm("sf,df->sd", gate_back, gate_all) + mm("sf,df->sd", up_back, up_all)).astype(
        LOW
    )

    shared_g = jnp.dot(all_second, full_sgate, preferred_element_type=FULL)
    shared_u = jnp.dot(all_second, full_sup, preferred_element_type=FULL)
    shared_silu, shared_slope = silu_slope(shared_g)
    shared_hidden = (shared_silu * shared_u).astype(LOW)
    shared_hidden_grad = mm("td,fd->tf", all_cot, full_sdown)
    sup_back = (shared_hidden_grad * shared_silu).astype(LOW)
    sgate_back = (shared_hidden_grad * shared_u * shared_slope).astype(LOW)
    shared_second_grad = mm("tf,df->td", sgate_back, full_sgate) + mm(
        "tf,df->td", sup_back, full_sup
    )
    slots_shape = (ctx_count, fsdp_count, share, model_width)
    rows_shape = (ctx_count, row_count, model_width)
    second_grad = return_rows(
        arrived_back.reshape(slots_shape),
        chooser,
        shared_second_grad.reshape(rows_shape),
        ctx_count,
        fsdp_count,
    )
    shared_hidden, sgate_back, sup_back = after(
        (shared_hidden, sgate_back, sup_back), second_grad
    )
    pair_grad = jnp.stack(
        [mm("td,tf->df", all_second, sgate_back), mm("td,tf->df", all_second, sup_back)]
    ).astype(LOW)
    pair_grad = (
        pair_grad.reshape(2, ctx_count, fsdp_count, dense_rows, shared_units)
        .transpose(2, 0, 1, 3, 4)
        .reshape(fsdp_count, 2, ctx_count * dense_rows, shared_units)
    )
    sdown_grad = mm("tf,td->fd", shared_hidden, all_cot).astype(LOW)
    (hidden_act,) = after((hidden_act,), pair_grad, sdown_grad)
    pair_grad = lax.psum_scatter(pair_grad, "fsdp", scatter_dimension=0, tiled=False)
    sdown_grad = lax.psum_scatter(sdown_grad, "fsdp", scatter_dimension=0, tiled=True)
    result = jnp.dot(hidden_act, down_all, preferred_element_type=FULL).astype(LOW)
    came_back = lax.all_to_all(
        result.reshape(slots_shape), "fsdp", split_axis=1, concat_axis=1, tiled=True
    ).reshape(ctx_count, plane_slots, model_width)
    hidden_act, gate_back, up_back, shared_hidden = after(
        (hidden_act, gate_back, up_back, shared_hidden), result
    )
    gate_grad = mm("sd,sf->df", arrived_rows, gate_back).astype(LOW)
    up_grad = mm("sd,sf->df", arrived_rows, up_back).astype(LOW)
    down_grad = mm("sf,sd->fd", hidden_act, arrived_grad).astype(LOW)
    line_shape = (ctx_count, members, model_width // ctx_count // members, hidden_units)
    gate_sum = sum_parts(gate_grad.reshape(line_shape).swapaxes(0, 1), members, fsdp_count)
    up_sum = sum_parts(up_grad.reshape(line_shape).swapaxes(0, 1), members, fsdp_count)
    down_sum = sum_parts(
        down_grad.reshape(members, hidden_units // members, ctx_count, -1).swapaxes(1, 2),
        members,
        fsdp_count,
    )
    shared_out = jnp.dot(shared_hidden, full_sdown, preferred_element_type=FULL)
    (second_grad,) = after((second_grad,), gate_sum, up_sum, down_sum, came_back, shared_out)
    (gate_sum,) = after((gate_sum,), came_back)
    gate_returned = along_line(gate_sum)

    middle_part, gain_two_grad = norm_backward(second_grad, plain_two, inverse_two, gain_two)
    middle_grad = cot_full + middle_part
    attended_grad = middle_grad.astype(LOW)
    output_weight_grad = mm("tv,td->vd", values_out, attended_grad)
    values_grad = (
        mm("td,vd->tv", attended_grad, full_output).astype(LOW).reshape(row_count, HEADS, VDIM)
    )
    latent_out_grad = mm("thv,chv->htc", values_grad, expand_value).astype(LOW)
    query_latent_grad, turned_grad, all_latent_grad, all_keys_grad = attend_back(
        query_latent,
        query_turned,
        all_latent,
        all_keys,
        latent_out,
        log_total,
        latent_out_grad,
        ctx_count,
        score_scale,
    )
    query_rope_grad = turned_grad[:, :, :ROPE].swapaxes(0, 1)
    keys_part = jnp.concatenate([all_latent_grad, all_keys_grad[:, :ROPE]], axis=1)
    keys_part = keys_part.reshape(2, ctx_count, half_rows, LATENT + ROPE)
    keys_part = jnp.stack([keys_part[0], keys_part[1, ::-1]], axis=1)
    (keys_part,) = after((keys_part,), pair_grad, sdown_grad)
    keys_part = lax.psum_scatter(
        keys_part.reshape(sequence, LATENT + ROPE), "ctx", scatter_dimension=0, tiled=True
    )
    latent_grad, keys_grad = (keys_part[:, :LATENT], keys_part[:, LATENT:])
    expand_value_grad = mm("htc,thv->chv", latent_out, values_grad)

    (up_sum,) = after((up_sum,), gate_returned, all_latent_grad)
    up_returned = along_line(up_sum)
    (out_part,) = after(
        (
            (
                mm("bts,bsd->btd", mixer, came_back)
                + shared_out.reshape(ctx_count, row_count, model_width)
            ).astype(LOW),
        ),
        keys_part,
    )
    out_sum = lax.psum_scatter(out_part, "ctx", scatter_dimension=0, tiled=False).astype(FULL)
    layer_out = (middle + out_sum).astype(LOW)[None]
    (pair_grad,) = after((pair_grad,), up_returned)
    pair_grad = lax.all_to_all(
        pair_grad, "ctx", split_axis=1, concat_axis=2, tiled=True
    ).astype(FULL)
    sdown_grad = sdown_grad.astype(FULL)

    query_nope_grad = mm("htc,chd->thd", query_latent_grad, expand_key)
    expand_key_grad = mm("thd,htc->chd", query_nope, query_latent_grad)
    expand_grad = jnp.concatenate([expand_key_grad, expand_value_grad], axis=-1).reshape(
        LATENT, HEADS * (NOPE + VDIM)
    )
    query_grad = (
        jnp.concatenate([query_nope_grad, rotary(query_rope_grad, positions, -1.0)], axis=-1)
        .astype(LOW)
        .reshape(row_count, HEADS * (NOPE + ROPE))
    )
    latent_part_grad, gain_latent_grad = norm_backward(
        latent_grad, plain_latent, inverse_latent, gain_latent
    )
    latent_raw_grad = jnp.concatenate(
        [latent_part_grad, rotary(keys_grad, positions, -1.0)], axis=-1
    ).astype(LOW)
    query_weight_grad = mm("td,tq->dq", normed, query_grad)
    latent_weight_grad = mm("td,tq->dq", normed, latent_raw_grad)
    normed_grad = mm("tq,dq->td", query_grad, full_query) + mm(
        "tq,dq->td", latent_raw_grad, full_latent
    )
    source_part, gain_one_grad = norm_backward(normed_grad, plain_one, inverse_one, gain_one)
    tokens_grad = (middle_grad + source_part)[None]

    gain_latent_column = jnp.pad(
        gain_latent_grad.reshape(device_count, gain_rows), ((0, 0), (0, dense_rows - gain_rows))
    ).reshape(model_width)
    tail_grad = jnp.concatenate(
        [
            latent_weight_grad,
            gain_one_grad[:, None],
            gain_two_grad[:, None],
            gain_latent_column[:, None],
            jnp.zeros((model_width, 256 - ROPE - 3), FULL),
        ],
        axis=1,
    )
    (down_sum,) = after((down_sum,), up_returned, normed_grad, pair_grad)
    down_returned = along_line(down_sum)
    dense_grads = after(
        (query_weight_grad, tail_grad, expand_grad, output_weight_grad), up_returned
    )
    query_sum, tail_sum, expand_sum, output_sum = scatter_all(
        dense_grads, ctx_count, fsdp_count
    )

    def owned(moved, like):
        moved = moved.reshape((members, EXP_DEV) + moved.shape[1:])
        moved = swap_parts(moved, members, fsdp_count).swapaxes(0, 1)
        return moved.reshape(like.shape).astype(FULL)

    expert_grads = (
        owned(gate_returned, expert_gate),
        owned(up_returned, expert_up),
        owned(down_returned, expert_down),
    )
    return (
        layer_out,
        tokens_grad,
        tail_sum[:, rotary_end],
        query_sum,
        tail_sum[:, :rotary_end],
        tail_sum[:gain_rows, rotary_end + 2],
        expand_sum,
        output_sum,
        tail_sum[:, rotary_end + 1],
        pair_grad[0],
        pair_grad[1],
        sdown_grad,
        expert_grads[0],
        expert_grads[1],
        expert_grads[2],
    )


def solution(mesh):
    in_specs = (
        P("fsdp", "ctx", None),
        P("fsdp", "ctx", None),
        P("fsdp", "ctx", None),
        P("fsdp", "ctx", None),
        P(("ctx", "fsdp")),
        P(("ctx", "fsdp"), None),
        P(("ctx", "fsdp"), None),
        P(("ctx", "fsdp")),
        P(("ctx", "fsdp"), None),
        P(("ctx", "fsdp"), None),
        P(("ctx", "fsdp")),
        P(("ctx", "fsdp"), None),
        P(("ctx", "fsdp"), None),
        P(("ctx", "fsdp"), None),
        P("fsdp", "ctx", None),
        P("fsdp", "ctx", None),
        P("fsdp", None, "ctx"),
    )
    out_specs = (
        P("fsdp", "ctx", None),
        P("fsdp", "ctx", None),
        P(("ctx", "fsdp")),
        P(("ctx", "fsdp"), None),
        P(("ctx", "fsdp"), None),
        P(("ctx", "fsdp")),
        P(("ctx", "fsdp"), None),
        P(("ctx", "fsdp"), None),
        P(("ctx", "fsdp")),
        P(("ctx", "fsdp"), None),
        P(("ctx", "fsdp"), None),
        P(("ctx", "fsdp"), None),
        P("fsdp", "ctx", None),
        P("fsdp", "ctx", None),
        P("fsdp", None, "ctx"),
    )
    return jax.shard_map(local, mesh=mesh, in_specs=in_specs, out_specs=out_specs, check_vma=False)
```

```python
import functools

import jax
import jax.numpy as jnp
from jax import lax
from jax.experimental import pallas as pl
from jax.experimental.pallas import tpu as pltpu
from jax.sharding import PartitionSpec as P

HEADS = 16
NOPE = 128
ROPE = 64
LATENT = 512
VDIM = 128
TOP = 6
EXP_DEV = 2


epsilon = 1e-06
rope_base = 10000.0
masked_score = -1e30


def stored_positions(row_index, per_device, block_count):
    device = row_index // per_device
    within = row_index % per_device
    half_block = per_device // 2
    return jnp.where(
        within >= half_block,
        (block_count - 1 - device) * half_block + within - half_block,
        device * half_block + within,
    )


def rotary(values, positions, direction):
    half_rope = values.shape[-1] // 2
    frequency = rope_base ** (-jnp.arange(half_rope, dtype=jnp.float32) / half_rope)
    angles = positions.astype(jnp.float32)[:, None] * frequency[None, :]
    cosine_table = jnp.cos(angles)
    sine_table = direction * jnp.sin(angles)
    if values.ndim == 3:
        cosine_table = cosine_table[:, None, :]
        sine_table = sine_table[:, None, :]
    front_half = values[..., :half_rope]
    back_half = values[..., half_rope:]
    return jnp.concatenate(
        [
            front_half * cosine_table - back_half * sine_table,
            back_half * cosine_table + front_half * sine_table,
        ],
        axis=-1,
    )


def norm_forward(values):
    inverse = lax.rsqrt(jnp.mean(values * values, axis=-1, keepdims=True) + epsilon)
    return (values * inverse, inverse)


def norm_backward(normed_grad, plain, inverse, gain):
    gain_grad = jnp.sum(normed_grad * plain, axis=0)
    scaled = normed_grad * gain
    return (
        inverse * (scaled - plain * jnp.mean(scaled * plain, axis=-1, keepdims=True)),
        gain_grad,
    )


def silu_slope(values):
    sigma = jax.nn.sigmoid(values)
    return (values * sigma, sigma * (1.0 + values * (1.0 - sigma)))


LOW = jnp.bfloat16
FULL = jnp.float32


MESH_ID = pl.DeviceIdType.MESH
BIG_VMEM = 60 * 1024 * 1024


def flip(index, bit):
    return index + bit - 2 * bit * lax.rem(lax.div(index, bit), 2)


def toggled(index, mask):
    for bit in (1, 2, 4):
        if mask & bit:
            index = flip(index, bit)
    return index


def nearest(z, step):
    upper = lax.div(z, 2)
    if step == 0:
        return z
    if step == 1:
        return z + 1 - 2 * upper
    if step == 2:
        return 2 - 2 * lax.rem(z, 2) + upper
    return 3 - 3 * upper


def remote(source, target, send, receive, z, f):
    return pltpu.make_async_remote_copy(
        src_ref=source,
        dst_ref=target,
        send_sem=send,
        recv_sem=receive,
        device_id={"ctx": z, "fsdp": f},
        device_id_type=MESH_ID,
    )


def greet(z, f, masks, ctx_count, whole_line=False):
    barrier = pltpu.get_barrier_semaphore()

    def hello(to_z, to_f):
        pl.semaphore_signal(
            barrier, inc=1, device_id={"ctx": to_z, "fsdp": to_f}, device_id_type=MESH_ID
        )

    for mask in masks:
        hello(z, toggled(f, mask))
    if whole_line:
        for step in range(1, ctx_count):
            hello(lax.rem(z + step, ctx_count), f)
        pl.semaphore_wait(barrier, len(masks) + ctx_count - 1)
        return

    @pl.when(z > 0)
    def _():
        hello(z - 1, f)

    @pl.when(z < ctx_count - 1)
    def _():
        hello(z + 1, f)

    along = lax.div(z + ctx_count - 1, ctx_count) + lax.div(2 * ctx_count - 2 - z, ctx_count)
    pl.semaphore_wait(barrier, len(masks) + along)


def both_ways(z, block, ctx_count, act):
    @pl.when((block <= z) & (z < ctx_count - 1))
    def _():
        act(0, z + 1)

    @pl.when((block >= z) & (z > 0))
    def _():
        act(1, z - 1)


def halves(rows, width):
    if rows % 32 == 0:
        return tuple((pl.ds(start, rows // 2), slice(None)) for start in (0, rows // 2))
    return tuple((slice(None), pl.ds(start, width // 2)) for start in (0, width // 2))


def gather_kernel(ctx_count, kinds, *refs):
    count = len(kinds)
    shards, outs = refs[:count], refs[count : 2 * count]
    own_sem, z_send, z_recv, p_send, p_recv, c_send, c_recv = refs[2 * count :]
    z, f = lax.axis_index("ctx"), lax.axis_index("fsdp")
    core, x_near, y_near = flip(f, 1), flip(f, 2), flip(f, 4)
    far = flip(x_near, 4)
    greet(z, f, (1, 2, 4), ctx_count, True)

    def slot(item, step):
        return 0 if kinds[item] == "plane" else nearest(z, step)

    def steps(item, step):
        return step == 0 if kinds[item] == "plane" else 0 <= step < ctx_count

    def z_view(item, block):
        return outs[item].at[block] if kinds[item] == "column" else outs[item].at[block, f]

    def own(item):
        source = shards[item].at[z] if kinds[item] == "line" else shards[item]
        return pltpu.make_async_copy(source, z_view(item, slot(item, 0)), own_sem.at[item])

    def z_copy(item, block, way, target):
        at = z_view(item, block)
        return remote(at, at, z_send.at[item, block, way], z_recv.at[item, block], target, f)

    def piece(item, step):
        target = lax.rem(z + step, ctx_count)
        return remote(
            shards[item].at[target],
            outs[item].at[z, f],
            z_send.at[item, target, 0],
            z_recv.at[item, z],
            target,
            f,
        )

    def part(item, block, at, which):
        rows, columns = halves(*outs[item].shape[2:])[which]
        return outs[item].at[block, at, rows, columns]

    def p_copy(item, block, which):
        at = (
            lambda: outs[item].at[block, f],
            lambda: outs[item].at[block, f],
            lambda: part(item, block, x_near, 0),
            lambda: part(item, block, y_near, 1),
        )[which]()
        to = (x_near, y_near, y_near, x_near)[which]
        sems = (p_send.at[item, block, which], p_recv.at[item, block, which])
        return remote(at, at, *sems, z, to)

    def p_arrived(item, block, which):
        at = (
            lambda: outs[item].at[block, x_near],
            lambda: outs[item].at[block, y_near],
            lambda: part(item, block, far, 0),
            lambda: part(item, block, far, 1),
        )[which]()
        sems = (p_send.at[item, block, which], p_recv.at[item, block, which])
        remote(at, at, *sems, z, x_near).wait_recv()

    def c_copy(item, block, which):
        at = outs[item].at[block, (f, x_near, y_near, far)[which]]
        sems = (c_send.at[item, block, which], c_recv.at[item, block, which])
        return remote(at, at, *sems, z, core)

    def c_arrived(item, block, which):
        at = outs[item].at[block, flip((f, x_near, y_near, far)[which], 1)]
        sems = (c_send.at[item, block, which], c_recv.at[item, block, which])
        remote(at, at, *sems, z, core).wait_recv()

    def first(item, step):
        block = slot(item, step)
        if step == 0:
            own(item).wait()
        else:
            at = z_view(item, block)
            sems = (z_send.at[item, block, 0], z_recv.at[item, block])
            remote(at, at, *sems, z, core).wait_recv()
        if kinds[item] in ("all", "column"):
            both_ways(z, block, ctx_count, lambda way, to: z_copy(item, block, way, to).start())
        if kinds[item] != "column":
            p_copy(item, block, 0).start()
            p_copy(item, block, 1).start()
            c_copy(item, block, 0).start()

    def second(item, step):
        block = slot(item, step)
        for which in (0, 1):
            p_arrived(item, block, which)
            p_copy(item, block, which + 2).start()
            c_copy(item, block, which + 1).start()

    def third(item, step):
        block = slot(item, step)
        p_arrived(item, block, 2)
        p_arrived(item, block, 3)
        c_copy(item, block, 3).start()

    for item in range(count):
        own(item).start()
        if kinds[item] == "line":
            for step in range(1, ctx_count):
                piece(item, step).start()
    for step in range(ctx_count + 2):
        for lag, stage in ((0, first), (1, second), (2, third)):
            for item in range(count):
                if steps(item, step - lag) and (lag == 0 or kinds[item] != "column"):
                    stage(item, step - lag)
    for item in range(count):
        for step in range(ctx_count):
            if not steps(item, step):
                continue
            block = slot(item, step)
            if kinds[item] != "column":
                for which in range(4):
                    c_arrived(item, block, which)
                    p_copy(item, block, which).wait_send()
                    c_copy(item, block, which).wait_send()
            if kinds[item] == "line" and step > 0:
                piece(item, step).wait_send()
            if kinds[item] in ("all", "column"):
                both_ways(
                    z, block, ctx_count, lambda way, to: z_copy(item, block, way, to).wait_send()
                )


def gather_arrays(items, ctx_count, fsdp_count):
    kinds = tuple(kind for kind, shard in items)
    shards = [shard for kind, shard in items]
    lead = {
        "all": (ctx_count, fsdp_count),
        "line": (ctx_count, fsdp_count),
        "plane": (1, fsdp_count),
        "column": (ctx_count,),
    }
    shapes = [
        lead[kind] + (shard.shape[1:] if kind == "line" else shard.shape) for kind, shard in items
    ]
    count = len(items)
    dma = pltpu.SemaphoreType.DMA
    four = dma((count, ctx_count, 4))
    return pl.pallas_call(
        functools.partial(gather_kernel, ctx_count, kinds),
        out_shape=[
            jax.ShapeDtypeStruct(shape, shard.dtype) for shape, shard in zip(shapes, shards)
        ],
        in_specs=[pl.BlockSpec(memory_space=pl.ANY)] * count,
        out_specs=[pl.BlockSpec(memory_space=pl.ANY)] * count,
        scratch_shapes=[
            dma((count,)),
            dma((count, ctx_count, 2)),
            dma((count, ctx_count)),
            four,
            four,
            four,
            four,
        ],
        compiler_params=pltpu.CompilerParams(collective_id=0, has_side_effects=True),
        cost_estimate=pl.CostEstimate(flops=0, bytes_accessed=500_000_000, transcendentals=0),
    )(*shards)


def add_rows(target, rows, *terms):
    @pl.loop(0, rows, step=16)
    def _(start):
        part = pl.ds(pl.multiple_of(start, 16), 16)
        total = terms[0][part, :].astype(FULL)
        for term in terms[1:]:
            total = total + term[part, :].astype(FULL)
        target[part, :] = total.astype(target.dtype)


def scatter_kernel(ctx_count, count, *refs):
    grads, outs = refs[:count], refs[count : 2 * count]
    banks = [refs[(2 + kind) * count : (3 + kind) * count] for kind in range(7)]
    load_sem, c_send, c_recv, p_send, p_recv, z_send, z_recv = refs[9 * count :]
    z, f = lax.axis_index("ctx"), lax.axis_index("fsdp")
    side = lax.rem(f, 2)
    chip = lax.div(f, 2)
    core, x_near, y_near = flip(f, 1), flip(f, 2), flip(f, 4)
    x_chip, y_chip = flip(chip, 1), flip(chip, 2)
    far_chip = flip(x_chip, 2)
    greet(z, f, (1, 2, 4), ctx_count)
    order = [nearest(z, ctx_count - 1 - step) for step in range(ctx_count)]

    def work(item):
        grad_ref, out_ref = grads[item], outs[item]
        mine, from_core, from_x, from_y, half_x, half_y, from_z = [bank[item] for bank in banks]
        rows, width = out_ref.shape
        left, right = pl.ds(0, width // 2), pl.ds(width // 2, width // 2)

        def load(block):
            return pltpu.make_async_copy(
                grad_ref.at[block, :, side], mine.at[block], load_sem.at[item, block]
            )

        def c_copy(block):
            return remote(
                grad_ref.at[block, :, 1 - side],
                from_core.at[block],
                c_send.at[item, block],
                c_recv.at[item, block],
                z,
                core,
            )

        def p_copy(block, which):
            source, target, to = (
                (mine.at[block, far_chip, :, left], half_y.at[block], y_near),
                (mine.at[block, far_chip, :, right], half_x.at[block], x_near),
                (mine.at[block, x_chip], from_x.at[block], x_near),
                (mine.at[block, y_chip], from_y.at[block], y_near),
            )[which]
            sems = (p_send.at[item, block, which], p_recv.at[item, block, which])
            return remote(source, target, *sems, z, to)

        def z_copy(block, way, target):
            return remote(
                mine.at[block, chip],
                from_z.at[way, block],
                z_send.at[item, block],
                z_recv.at[item, way, block],
                target,
                f,
            )

        def z_arrived(block, way):
            at = from_z.at[way, block]
            sems = (z_send.at[item, block], z_recv.at[item, way, block])
            remote(at, at, *sems, z, core).wait_recv()

        def start(step):
            c_copy(order[step]).start()
            load(order[step]).start()

        def first(step):
            block = order[step]
            load(block).wait()
            c_copy(block).wait_recv()
            far_part = mine.at[block, far_chip]
            add_rows(far_part, rows, far_part, from_core.at[block, far_chip])
            p_copy(block, 0).start()
            p_copy(block, 1).start()

        def second(step):
            block = order[step]
            x_part, y_part = mine.at[block, x_chip], mine.at[block, y_chip]
            add_rows(x_part, rows, x_part, from_core.at[block, x_chip])
            add_rows(y_part, rows, y_part, from_core.at[block, y_chip])
            p_copy(block, 0).wait_recv()
            x_left = mine.at[block, x_chip, :, left]
            add_rows(x_left, rows, x_left, half_y.at[block])
            p_copy(block, 2).start()
            p_copy(block, 1).wait_recv()
            y_right = mine.at[block, y_chip, :, right]
            add_rows(y_right, rows, y_right, half_x.at[block])
            p_copy(block, 3).start()

        def third(step):
            block = order[step]
            p_copy(block, 2).wait_recv()
            p_copy(block, 3).wait_recv()
            own = mine.at[block, chip]
            terms = (own, from_core.at[block, chip], from_x.at[block], from_y.at[block])
            if step == ctx_count - 1:

                @pl.when(z > 0)
                def _():
                    z_arrived(block, 0)

                @pl.when(z < ctx_count - 1)
                def _():
                    z_arrived(block, 1)

                @pl.when(z == 0)
                def _():
                    add_rows(out_ref, rows, *terms, from_z.at[1, block])

                @pl.when(z == ctx_count - 1)
                def _():
                    add_rows(out_ref, rows, *terms, from_z.at[0, block])

                @pl.when((z > 0) & (z < ctx_count - 1))
                def _():
                    add_rows(out_ref, rows, *terms, from_z.at[0, block], from_z.at[1, block])

                return

            for way, above in ((1, True), (0, False)):
                heading = (block < z) if above else (block > z)
                has_more = (z < ctx_count - 1) if above else (z > 0)

                @pl.when(heading & has_more)
                def _():
                    z_arrived(block, way)
                    add_rows(own, rows, *terms, from_z.at[way, block])

                @pl.when(heading & jnp.logical_not(has_more))
                def _():
                    add_rows(own, rows, *terms)

                @pl.when(heading)
                def _():
                    z_copy(block, way, z - 1 if above else z + 1).start()

        def finish(step):
            block = order[step]
            c_copy(block).wait_send()
            for which in range(4):
                p_copy(block, which).wait_send()
            if step < ctx_count - 1:
                z_copy(block, 0, z).wait_send()

        return start, first, second, third, finish

    stages = list(zip(*[work(item) for item in range(count)]))
    for step in range(ctx_count):
        for act in stages[0]:
            act(step)
    for step in range(ctx_count + 2):
        for lag in (0, 1, 2):
            if 0 <= step - lag < ctx_count:
                for act in stages[1 + lag]:
                    act(step - lag)
    for step in range(ctx_count):
        for act in stages[4]:
            act(step)


def scatter_arrays(grads, ctx_count, fsdp_count):
    count = len(grads)
    chips = fsdp_count // 2
    shapes = [
        (grad.shape[0] // (ctx_count * fsdp_count), grad.shape[1]) for grad in grads
    ]
    dma = pltpu.SemaphoreType.DMA
    leads = [(ctx_count, chips), (ctx_count, chips), (ctx_count,), (ctx_count,)]
    banks = [pltpu.VMEM(lead + shape, LOW) for lead in leads for shape in shapes]
    banks += [
        pltpu.VMEM((ctx_count, shape[0], shape[1] // 2), LOW) for _ in range(2) for shape in shapes
    ]
    banks += [pltpu.VMEM((2, ctx_count) + shape, LOW) for shape in shapes]
    return pl.pallas_call(
        functools.partial(scatter_kernel, ctx_count, count),
        out_shape=[jax.ShapeDtypeStruct(shape, FULL) for shape in shapes],
        in_specs=[pl.BlockSpec(memory_space=pl.ANY)] * count,
        out_specs=[pl.BlockSpec(memory_space=pltpu.VMEM)] * count,
        scratch_shapes=banks
        + [
            dma((count, ctx_count)),
            dma((count, ctx_count)),
            dma((count, ctx_count)),
            dma((count, ctx_count, 4)),
            dma((count, ctx_count, 4)),
            dma((count, ctx_count)),
            dma((count, 2, ctx_count)),
        ],
        compiler_params=pltpu.CompilerParams(
            collective_id=1, has_side_effects=True, vmem_limit_bytes=BIG_VMEM
        ),
        cost_estimate=pl.CostEstimate(flops=0, bytes_accessed=500_000_000, transcendentals=0),
    )(
        *[
            grad.reshape((ctx_count, chips, 2) + shape)
            for grad, shape in zip(grads, shapes)
        ]
    )


HEAD_GROUP = 4
KEYS = 256


def dot_last(left, right):
    return lax.dot_general(left, right, (((1,), (1,)), ((), ())), preferred_element_type=FULL)


def dot_first(left, right):
    return lax.dot_general(left, right, (((0,), (0,)), ((), ())), preferred_element_type=FULL)


def reach(half, rows, ctx_count):
    ctx = lax.axis_index("ctx")
    first = jnp.where(half == 0, ctx, 2 * ctx_count - 1 - ctx) * rows
    return first, lax.div(first + rows + KEYS - 1, KEYS)


def block_scores(query, turned, keys_ref, rope_ref, index, first, rows, scale):
    part = pl.ds(pl.multiple_of(index * KEYS, KEYS), KEYS)
    keys, rope = keys_ref[part, :], rope_ref[part, :]
    scores = (dot_last(query, keys) + dot_last(turned, rope)) * scale
    shape = scores.shape
    at = first + lax.rem(lax.broadcasted_iota(jnp.int32, shape, 0), rows)
    key_at = index * KEYS + lax.broadcasted_iota(jnp.int32, shape, 1)
    return part, keys, rope, scores, at >= key_at


def attend_kernel(
    ctx_count, scale, query_ref, turned_ref, keys_ref, rope_ref, out_ref, log_ref, total, top, norm
):
    heads, rows, width = query_ref.shape
    first, blocks = reach(pl.program_id(0), rows, ctx_count)
    query = query_ref[...].reshape(heads * rows, width)
    turned = turned_ref[...].reshape(heads * rows, -1)
    total[...] = jnp.zeros_like(total)
    norm[...] = jnp.zeros_like(norm)
    top[...] = jnp.full_like(top, masked_score)

    @pl.loop(0, blocks)
    def _(index):
        part, keys, rope, scores, seen = block_scores(
            query, turned, keys_ref, rope_ref, index, first, rows, scale
        )
        scores = jnp.where(seen, scores, masked_score)
        old = top[...]
        new = jnp.maximum(old, jnp.max(scores, axis=1, keepdims=True))
        weights = jnp.exp(scores - new)
        shrink = jnp.exp(old - new)
        top[...] = new
        norm[...] = norm[...] * shrink + jnp.sum(weights, axis=1, keepdims=True)
        total[...] = total[...] * shrink + jnp.dot(
            weights.astype(LOW), keys, preferred_element_type=FULL
        )

    out_ref[...] = (total[...] / norm[...]).astype(LOW).reshape(out_ref.shape)
    log_ref[...] = (top[...] + jnp.log(norm[...])).reshape(log_ref.shape)


def attend_back_kernel(
    ctx_count,
    scale,
    query_ref,
    turned_ref,
    keys_ref,
    rope_ref,
    out_ref,
    log_ref,
    grad_ref,
    query_grad_ref,
    turned_grad_ref,
    keys_grad_ref,
    rope_grad_ref,
    query_total,
    turned_total,
):
    heads, rows, width = query_ref.shape
    first, blocks = reach(pl.program_id(0), rows, ctx_count)
    query = query_ref[...].reshape(heads * rows, width)
    turned = turned_ref[...].reshape(heads * rows, -1)
    grad = grad_ref[...].reshape(heads * rows, width)
    out = out_ref[...].reshape(heads * rows, width)
    logs = log_ref[...].reshape(heads * rows, 1)
    inner = jnp.sum(grad.astype(FULL) * out.astype(FULL), axis=1, keepdims=True)
    query_total[...] = jnp.zeros_like(query_total)
    turned_total[...] = jnp.zeros_like(turned_total)

    @pl.when((pl.program_id(0) == 0) & (pl.program_id(1) == 0))
    def _():
        keys_grad_ref[...] = jnp.zeros_like(keys_grad_ref)
        rope_grad_ref[...] = jnp.zeros_like(rope_grad_ref)

    @pl.loop(0, blocks)
    def _(index):
        part, keys, rope, scores, seen = block_scores(
            query, turned, keys_ref, rope_ref, index, first, rows, scale
        )
        weights = jnp.where(seen, jnp.exp(scores - logs), 0.0)
        change = (weights * (dot_last(grad, keys) - inner) * scale).astype(LOW)
        query_total[...] += jnp.dot(change, keys, preferred_element_type=FULL)
        turned_total[...] += jnp.dot(change, rope, preferred_element_type=FULL)
        keys_grad_ref[part, :] += dot_first(change, query) + dot_first(weights.astype(LOW), grad)
        rope_grad_ref[part, :] += dot_first(change, turned)

    query_grad_ref[...] = query_total[...].astype(LOW).reshape(query_grad_ref.shape)
    turned_grad_ref[...] = turned_total[...].reshape(turned_grad_ref.shape)


def attend_specs(heads, group, rows, widths):
    return [pl.BlockSpec((group, rows, width), lambda half, g: (g, half, 0)) for width in widths]


def whole_spec(array):
    return pl.BlockSpec(array.shape, lambda half, g: (0, 0))


def attend(query, turned, keys, rope, ctx_count, scale):
    heads, count, width = query.shape
    group, rows = HEAD_GROUP, count // 2
    lanes = turned.shape[2]
    return pl.pallas_call(
        functools.partial(attend_kernel, ctx_count, scale),
        grid=(2, heads // group),
        out_shape=(
            jax.ShapeDtypeStruct((heads, count, width), LOW),
            jax.ShapeDtypeStruct((heads, count, 1), FULL),
        ),
        in_specs=attend_specs(heads, group, rows, (width, lanes))
        + [whole_spec(keys), whole_spec(rope)],
        out_specs=tuple(attend_specs(heads, group, rows, (width, 1))),
        scratch_shapes=[
            pltpu.VMEM((group * rows, width), FULL),
            pltpu.VMEM((group * rows, 1), FULL),
            pltpu.VMEM((group * rows, 1), FULL),
        ],
        compiler_params=pltpu.CompilerParams(vmem_limit_bytes=BIG_VMEM),
        cost_estimate=pl.CostEstimate(
            flops=12_000_000_000, bytes_accessed=12_000_000, transcendentals=3_000_000
        ),
    )(query, turned, keys, rope)


def attend_back(query, turned, keys, rope, out, logs, grad, ctx_count, scale):
    heads, count, width = query.shape
    group, rows = HEAD_GROUP, count // 2
    lanes = turned.shape[2]
    return pl.pallas_call(
        functools.partial(attend_back_kernel, ctx_count, scale),
        grid=(2, heads // group),
        out_shape=(
            jax.ShapeDtypeStruct((heads, count, width), LOW),
            jax.ShapeDtypeStruct((heads, count, lanes), FULL),
            jax.ShapeDtypeStruct(keys.shape, FULL),
            jax.ShapeDtypeStruct(rope.shape, FULL),
        ),
        in_specs=attend_specs(heads, group, rows, (width, lanes))
        + [whole_spec(keys), whole_spec(rope)]
        + attend_specs(heads, group, rows, (width, 1, width)),
        out_specs=tuple(
            attend_specs(heads, group, rows, (width, lanes)) + [whole_spec(keys), whole_spec(rope)]
        ),
        scratch_shapes=[
            pltpu.VMEM((group * rows, width), FULL),
            pltpu.VMEM((group * rows, lanes), FULL),
        ],
        compiler_params=pltpu.CompilerParams(vmem_limit_bytes=BIG_VMEM),
        cost_estimate=pl.CostEstimate(
            flops=30_000_000_000, bytes_accessed=30_000_000, transcendentals=3_000_000
        ),
    )(query, turned, keys, rope, out, logs, grad)


PEERS = (6, 7, 2, 4, 3, 5, 1)
COLUMN_AT, GATE_AT, INFO_ROWS = 8, 16, 24


def one_hot(info, z, slots, gated):
    count = info.shape[1]
    at = lax.broadcasted_iota(jnp.int32, (slots, count), 0).astype(FULL)
    plane = z.astype(FULL)
    total = jnp.zeros((slots, count), FULL)
    for route in range(TOP):
        hit = (info[COLUMN_AT + route][None, :] == at) & (info[route][None, :] == plane)
        value = info[GATE_AT + route][None, :] if gated else 1.0
        total = total + jnp.where(hit, value, 0.0)
    return total.astype(LOW)


class Dispatch:
    def __init__(self, ctx_count, gated, rows_ref, info_ref, all_ref, blocks, chosen, arrived, sems):
        self.own_sem, self.all_sem, self.keep_sem = sems[:3]
        self.z_send, self.z_recv, self.p_send, self.p_recv = sems[3:]
        self.ctx_count, self.gated = ctx_count, gated
        self.rows_ref, self.info_ref, self.all_ref = rows_ref, info_ref, all_ref
        self.blocks, self.chosen, self.arrived = blocks, chosen, arrived
        self.z, self.f = lax.axis_index("ctx"), lax.axis_index("fsdp")
        self.core = flip(self.f, 1)

    def z_copy(self, block, way, target):
        at = self.blocks.at[block]
        sems = (self.z_send.at[block, way], self.z_recv.at[block])
        return remote(at, at, *sems, target, self.f)

    def p_copy(self, block, place):
        to = toggled(self.f, PEERS[place])
        sems = (self.p_send.at[block, place], self.p_recv.at[block, place])
        return remote(
            self.chosen.at[block, to], self.arrived.at[block, self.f], *sems, self.z, to
        )

    def keep(self, block):
        source, target = self.chosen.at[block, self.f], self.arrived.at[block, self.f]
        return pltpu.make_async_copy(source, target, self.keep_sem.at[block])

    def store(self, block):
        source, target = self.blocks.at[block], self.all_ref.at[block]
        return pltpu.make_async_copy(source, target, self.all_sem.at[block])

    def begin(self):
        greet(self.z, self.f, PEERS, self.ctx_count)
        own = pltpu.make_async_copy(self.rows_ref, self.blocks.at[self.z], self.own_sem)
        own.start()
        own.wait()

    def pass_on(self, block, own):
        if not own:
            at = self.blocks.at[block]
            sems = (self.z_send.at[block, 0], self.z_recv.at[block])
            remote(at, at, *sems, self.z, self.core).wait_recv()
        both_ways(
            self.z, block, self.ctx_count, lambda way, to: self.z_copy(block, way, to).start()
        )
        self.store(block).start()
        groups, share, width = self.chosen.shape[1:]
        choose = one_hot(self.info_ref[block], self.z, groups * share, self.gated)

        @pl.loop(0, width, step=256)
        def _(start):
            part = pl.ds(pl.multiple_of(start, 256), 256)
            tile = jnp.dot(choose, self.blocks[block, :, part], preferred_element_type=FULL)
            self.chosen[block, :, :, part] = tile.astype(LOW).reshape(groups, share, 256)

        for place in range(len(PEERS)):
            self.p_copy(block, place).start()
        self.keep(block).start()

    def await_slots(self, block):
        self.keep(block).wait()
        for place in range(len(PEERS)):
            at = self.arrived.at[block, toggled(self.f, PEERS[place])]
            sems = (self.p_send.at[block, place], self.p_recv.at[block, place])
            remote(at, at, *sems, self.z, self.core).wait_recv()

    def finish(self):
        for step in range(self.ctx_count):
            block = nearest(self.z, step)
            self.store(block).wait()
            both_ways(
                self.z,
                block,
                self.ctx_count,
                lambda way, to: self.z_copy(block, way, to).wait_send(),
            )
            for place in range(len(PEERS)):
                self.p_copy(block, place).wait_send()


def dispatch_scratch(ctx_count, fsdp_count, count, share, width):
    dma = pltpu.SemaphoreType.DMA
    return [
        pltpu.VMEM((ctx_count, count, width), LOW),
        pltpu.VMEM((ctx_count, fsdp_count, share, width), LOW),
    ], [
        dma,
        dma((ctx_count,)),
        dma((ctx_count,)),
        dma((ctx_count, 2)),
        dma((ctx_count,)),
        dma((ctx_count, len(PEERS))),
        dma((ctx_count, len(PEERS))),
    ]


def dispatch_kernel(ctx_count, rows_ref, info_ref, all_ref, out_ref, blocks, chosen, *sems):
    move = Dispatch(ctx_count, True, rows_ref, info_ref, all_ref, blocks, chosen, out_ref, sems)
    move.begin()
    for step in range(ctx_count):
        move.pass_on(nearest(move.z, step), step == 0)
    for step in range(ctx_count):
        move.await_slots(nearest(move.z, step))
    move.finish()


def dispatch_rows(rows, info, slots, ctx_count, fsdp_count):
    count, width = rows.shape
    share = slots // fsdp_count
    buffers, sems = dispatch_scratch(ctx_count, fsdp_count, count, share, width)
    return pl.pallas_call(
        functools.partial(dispatch_kernel, ctx_count),
        out_shape=(
            jax.ShapeDtypeStruct((ctx_count, count, width), LOW),
            jax.ShapeDtypeStruct((ctx_count, fsdp_count, share, width), LOW),
        ),
        in_specs=[pl.BlockSpec(memory_space=pl.ANY), pl.BlockSpec(memory_space=pltpu.VMEM)],
        out_specs=(pl.BlockSpec(memory_space=pl.ANY), pl.BlockSpec(memory_space=pl.ANY)),
        scratch_shapes=buffers + sems,
        compiler_params=pltpu.CompilerParams(
            collective_id=2, has_side_effects=True, vmem_limit_bytes=BIG_VMEM
        ),
        cost_estimate=pl.CostEstimate(
            flops=2_000_000_000, bytes_accessed=300_000_000, transcendentals=0
        ),
    )(rows, info)


def tiles(width, size=256):
    return width // size, width % size


def each_tile(width, act, size=256):
    whole, rest = tiles(width, size)

    @pl.loop(0, whole)
    def _(index):
        act(pl.ds(pl.multiple_of(index * size, size), size))

    if rest:
        act(pl.ds(whole * size, rest))


def expert_kernel(ctx_count, rows_ref, info_ref, gate_ref, up_ref, down_ref, grads_ref, *refs):
    all_ref, slots_ref, hidden_ref, gate_back_ref, up_back_ref, back_ref = refs[:6]
    blocks, chosen, arrived, gate, up, down, grads, hidden, gate_back, up_back, back = refs[6:17]
    weight_sem, grad_sem, slot_sem, side_sem, back_sem = refs[17:22]
    move = Dispatch(
        ctx_count, False, rows_ref, info_ref, all_ref, blocks, chosen, arrived, refs[22:]
    )
    slots, width = back.shape
    units = hidden.shape[1]
    order = [nearest(move.z, step) for step in range(ctx_count)]

    def block_at(step):
        block = order[0]
        for place in range(1, ctx_count):
            block = jnp.where(step == place, order[place], block)
        return block

    loads = [
        pltpu.make_async_copy(source, target, weight_sem.at[place])
        for place, (source, target) in enumerate(((gate_ref, gate), (up_ref, up), (down_ref, down)))
    ]

    def load_grads(step):
        slot = lax.rem(step, 2)
        return pltpu.make_async_copy(
            grads_ref.at[block_at(step)], grads.at[slot], grad_sem.at[slot]
        )

    def store_slots(block):
        return pltpu.make_async_copy(arrived.at[block], slots_ref.at[block], slot_sem.at[block])

    def store_sides(block):
        return [
            pltpu.make_async_copy(source, target.at[block], side_sem.at[place])
            for place, (source, target) in enumerate(
                ((hidden, hidden_ref), (gate_back, gate_back_ref), (up_back, up_back_ref))
            )
        ]

    def store_back(block):
        return pltpu.make_async_copy(back, back_ref.at[block], back_sem)

    move.begin()
    for load in loads:
        load.start()
    load_grads(0).start()
    move.pass_on(order[0], True)
    move.pass_on(order[1], False)
    for load in loads:
        load.wait()

    @pl.loop(0, ctx_count)
    def _(step):
        block = block_at(step)
        slot = lax.rem(step, 2)

        @pl.when(step + 1 < ctx_count)
        def _():
            load_grads(step + 1).start()

        load_grads(step).wait()
        move.await_slots(block)
        store_slots(block).start()

        @pl.when(step > 0)
        def _():
            for copy in store_sides(block):
                copy.wait()

        rows = arrived[block].reshape(slots, width)

        def hidden_tile(part):
            pre = jnp.dot(rows, gate[:, part], preferred_element_type=FULL)
            linear = jnp.dot(rows, up[:, part], preferred_element_type=FULL)
            grad = dot_last(grads[slot], down[part, :])
            sigma = jax.nn.sigmoid(pre)
            act = pre * sigma
            hidden[:, part] = (act * linear).astype(LOW)
            up_back[:, part] = (grad * act).astype(LOW)
            gate_back[:, part] = (
                grad * linear * (sigma * (1.0 + pre * (1.0 - sigma)))
            ).astype(LOW)

        each_tile(units, hidden_tile)
        for copy in store_sides(block):
            copy.start()

        @pl.when(step > 0)
        def _():
            store_back(block).wait()

        def back_tile(part):
            total = dot_last(gate_back[...], gate[part, :]) + dot_last(up_back[...], up[part, :])
            back[:, part] = total.astype(LOW)

        each_tile(width, back_tile)
        store_back(block).start()

        @pl.when(step + 2 < ctx_count)
        def _():
            move.pass_on(block_at(step + 2), False)

    for step in range(ctx_count):
        store_slots(order[step]).wait()
    for copy in store_sides(order[-1]):
        copy.wait()
    store_back(order[-1]).wait()
    move.finish()


def expert_rows(rows, info, gate, up, down, grads, ctx_count, fsdp_count):
    count, width = rows.shape
    slots = grads.shape[1]
    share = slots // fsdp_count
    units = gate.shape[1]
    buffers, sems = dispatch_scratch(ctx_count, fsdp_count, count, share, width)
    dma = pltpu.SemaphoreType.DMA
    anywhere = pl.BlockSpec(memory_space=pl.ANY)
    low = lambda *shape: jax.ShapeDtypeStruct((ctx_count,) + shape, LOW)
    vmem = lambda *shape: pltpu.VMEM(shape, LOW)
    return pl.pallas_call(
        functools.partial(expert_kernel, ctx_count),
        out_shape=(
            low(count, width),
            low(fsdp_count, share, width),
            low(slots, units),
            low(slots, units),
            low(slots, units),
            low(slots, width),
        ),
        in_specs=[anywhere, pl.BlockSpec(memory_space=pltpu.VMEM)] + [anywhere] * 4,
        out_specs=(anywhere,) * 6,
        scratch_shapes=buffers
        + [
            vmem(ctx_count, fsdp_count, share, width),
            vmem(width, units),
            vmem(width, units),
            vmem(units, width),
            vmem(2, slots, width),
            vmem(slots, units),
            vmem(slots, units),
            vmem(slots, units),
            vmem(slots, width),
            dma((3,)),
            dma((2,)),
            dma((ctx_count,)),
            dma((3,)),
            dma,
        ]
        + sems,
        compiler_params=pltpu.CompilerParams(
            collective_id=4, has_side_effects=True, vmem_limit_bytes=BIG_VMEM
        ),
        cost_estimate=pl.CostEstimate(
            flops=60_000_000_000, bytes_accessed=400_000_000, transcendentals=3_000_000
        ),
    )(rows, info, gate, up, down, grads)


def combine_kernel(ctx_count, slots_ref, info_ref, extra_ref, *refs):
    rows_ref, grads_ref, hidden_ref, gate_back_ref, up_back_ref = refs[:5]
    out_ref, gate_grad_ref, up_grad_ref, down_grad_ref = refs[5:9]
    arrived, extra, parts, from_z, wide, left, right, gate_tile, up_tile, down_tile = refs[9:19]
    keep_sem, extra_sem, p_send, p_recv, z_send, z_recv, load_sem, store_sem = refs[19:]
    z, f = lax.axis_index("ctx"), lax.axis_index("fsdp")
    core = flip(f, 1)
    width = out_ref.shape[1]
    units = left.shape[1]
    slots = arrived.shape[1] * arrived.shape[2]
    greet(z, f, PEERS, ctx_count)

    def p_copy(block, place):
        to = toggled(f, PEERS[place])
        sems = (p_send.at[block, place], p_recv.at[block, place])
        return remote(slots_ref.at[block, to], arrived.at[block, f], *sems, z, to)

    def p_arrived(block, place):
        at = arrived.at[block, toggled(f, PEERS[place])]
        sems = (p_send.at[block, place], p_recv.at[block, place])
        remote(at, at, *sems, z, core).wait_recv()

    def keep(block):
        return pltpu.make_async_copy(
            slots_ref.at[block, f], arrived.at[block, f], keep_sem.at[block]
        )

    def load(block):
        return pltpu.make_async_copy(extra_ref.at[block], extra.at[block], extra_sem.at[block])

    def z_copy(block, way, target):
        sems = (z_send.at[block], z_recv.at[way, block])
        return remote(parts.at[block], from_z.at[way, block], *sems, target, f)

    def z_arrived(block, way):
        at = from_z.at[way, block]
        remote(at, at, z_send.at[block], z_recv.at[way, block], z, core).wait_recv()

    def mix(block, target, *ways):
        choose = one_hot(info_ref[block], z, slots, False)

        @pl.loop(0, width, step=256)
        def _(start):
            part = pl.ds(pl.multiple_of(start, 256), 256)
            total = dot_first(choose, arrived[block, :, :, part].reshape(slots, 256))
            total = total + extra[block, :, part].astype(FULL)
            for way in ways:
                total = total + from_z[way, block, :, part].astype(FULL)
            target[:, part] = total.astype(target.dtype)

    def inner_step(block):
        for way, above in ((1, True), (0, False)):
            heading = (block < z) if above else (block > z)
            has_more = (z < ctx_count - 1) if above else (z > 0)

            @pl.when(heading & has_more)
            def _():
                z_arrived(block, way)
                mix(block, parts.at[block], way)

            @pl.when(heading & jnp.logical_not(has_more))
            def _():
                mix(block, parts.at[block])

            @pl.when(heading)
            def _():
                z_copy(block, way, z - 1 if above else z + 1).start()

    def last_step(block):
        @pl.when(z > 0)
        def _():
            z_arrived(block, 0)

        @pl.when(z < ctx_count - 1)
        def _():
            z_arrived(block, 1)

        @pl.when(z == 0)
        def _():
            mix(block, out_ref, 1)

        @pl.when(z == ctx_count - 1)
        def _():
            mix(block, out_ref, 0)

        @pl.when((z > 0) & (z < ctx_count - 1))
        def _():
            mix(block, out_ref, 0, 1)

    def fetch(source, target, place):
        return pltpu.make_async_copy(source, target, load_sem.at[place])

    first_loads = [
        fetch(rows_ref, wide, 0),
        fetch(gate_back_ref, left, 1),
        fetch(up_back_ref, right, 2),
    ]
    second_loads = [fetch(grads_ref, wide, 3), fetch(hidden_ref, left, 4)]

    def stores(part):
        return [
            pltpu.make_async_copy(gate_tile, gate_grad_ref.at[part, :], store_sem.at[0]),
            pltpu.make_async_copy(up_tile, up_grad_ref.at[part, :], store_sem.at[1]),
        ]

    def store_down(start, count):
        source, target = down_tile, down_grad_ref.at[pl.ds(start, count), :]
        if count != down_tile.shape[0]:
            source = down_tile.at[pl.ds(0, count), :]
        return pltpu.make_async_copy(source, target, store_sem.at[2])

    def outer_tiles(begin, end):
        @pl.loop(begin, end)
        def _(index):
            part = pl.ds(pl.multiple_of(index * 256, 256), 256)
            turned = wide[:, part]
            gate_part = dot_first(turned, left[...]).astype(LOW)
            up_part = dot_first(turned, right[...]).astype(LOW)

            @pl.when(index > 0)
            def _():
                for copy in stores(part):
                    copy.wait()

            gate_tile[...] = gate_part
            up_tile[...] = up_part
            for copy in stores(part):
                copy.start()

    def down_tiles(begin, end):
        @pl.loop(begin, end)
        def _(index):
            start = pl.multiple_of(index * 256, 256)
            down_part = dot_first(left[:, pl.ds(start, 256)], wide[...]).astype(LOW)

            @pl.when(index > 0)
            def _():
                store_down(start, 256).wait()

            down_tile[...] = down_part
            store_down(start, 256).start()

    order = [nearest(z, ctx_count - 1 - step) for step in range(ctx_count)]
    for copy in first_loads:
        copy.start()
    for block in order:
        for place in range(len(PEERS)):
            p_copy(block, place).start()
        keep(block).start()
        load(block).start()
    for copy in first_loads:
        copy.wait()

    def step_waits(block):
        keep(block).wait()
        load(block).wait()
        for place in range(len(PEERS)):
            p_arrived(block, place)

    outer = width // 256
    whole, rest = tiles(units)
    outer_tiles(0, outer // 2)
    step_waits(order[0])
    inner_step(order[0])
    outer_tiles(outer // 2, outer)
    for copy in second_loads:
        copy.start()
    step_waits(order[1])
    inner_step(order[1])
    for copy in second_loads:
        copy.wait()
    down_tiles(0, whole // 2)
    step_waits(order[2])
    inner_step(order[2])
    down_tiles(whole // 2, whole)
    store_down(0, 256).wait()
    if rest:
        down_tile[pl.ds(0, rest), :] = dot_first(
            left[:, pl.ds(whole * 256, rest)], wide[...]
        ).astype(LOW)
        store_down(whole * 256, rest).start()
    step_waits(order[3])
    last_step(order[3])
    if rest:
        store_down(whole * 256, rest).wait()
    for copy in stores(pl.ds(0, 256)):
        copy.wait()
    for step in range(ctx_count):
        block = order[step]
        for place in range(len(PEERS)):
            p_copy(block, place).wait_send()
        if step < ctx_count - 1:
            z_copy(block, 0, z).wait_send()


def combine_rows(
    slots, info, extra, rows, grads, hidden, gate_back, up_back, ctx_count, fsdp_count
):
    share, width = slots.shape[2:]
    count = extra.shape[1]
    units = hidden.shape[1]
    dma = pltpu.SemaphoreType.DMA
    anywhere = pl.BlockSpec(memory_space=pl.ANY)
    resident = pl.BlockSpec(memory_space=pltpu.VMEM)
    vmem = lambda *shape: pltpu.VMEM(shape, LOW)
    return pl.pallas_call(
        functools.partial(combine_kernel, ctx_count),
        out_shape=(
            jax.ShapeDtypeStruct((count, width), FULL),
            jax.ShapeDtypeStruct((width, units), LOW),
            jax.ShapeDtypeStruct((width, units), LOW),
            jax.ShapeDtypeStruct((units, width), LOW),
        ),
        in_specs=[anywhere, resident] + [anywhere] * 6,
        out_specs=(resident, anywhere, anywhere, anywhere),
        scratch_shapes=[
            vmem(ctx_count, fsdp_count, share, width),
            vmem(ctx_count, count, width),
            vmem(ctx_count, count, width),
            vmem(2, ctx_count, count, width),
            vmem(rows.shape[0], width),
            vmem(rows.shape[0], units),
            vmem(rows.shape[0], units),
            vmem(256, units),
            vmem(256, units),
            vmem(256, width),
            dma((ctx_count,)),
            dma((ctx_count,)),
            dma((ctx_count, len(PEERS))),
            dma((ctx_count, len(PEERS))),
            dma((ctx_count,)),
            dma((2, ctx_count)),
            dma((5,)),
            dma((3,)),
        ],
        compiler_params=pltpu.CompilerParams(
            collective_id=3, has_side_effects=True, vmem_limit_bytes=BIG_VMEM
        ),
        cost_estimate=pl.CostEstimate(
            flops=40_000_000_000, bytes_accessed=300_000_000, transcendentals=0
        ),
    )(slots, info, extra, rows, grads, hidden, gate_back, up_back)


def mm(subscripts, left, right):
    return jnp.einsum(subscripts, left, right, preferred_element_type=FULL)


def member_pairs(fsdp_count, members, step):
    return [
        (f, f // members * members + (f % members + step) % members) for f in range(fsdp_count)
    ]


def by_member(own, others, member, members):
    if members == 2:
        first = member == 0
        return jnp.stack([jnp.where(first, own, others[0]), jnp.where(first, others[0], own)])
    stack = jnp.stack([own] + others)
    return jnp.take(stack, (member - jnp.arange(members)) % members, axis=0)


def part_of(array, member, step, members):
    return lax.dynamic_index_in_dim(array, (member + step) % members, 0, keepdims=False)


def swap_parts(array, members, fsdp_count):
    member = lax.axis_index("fsdp") % members
    others = [
        lax.ppermute(
            part_of(array, member, step, members), "fsdp", member_pairs(fsdp_count, members, step)
        )
        for step in range(1, members)
    ]
    return by_member(part_of(array, member, 0, members), others, member, members)


def share_parts(array, members, fsdp_count):
    member = lax.axis_index("fsdp") % members
    others = [
        lax.ppermute(array, "fsdp", member_pairs(fsdp_count, members, step))
        for step in range(1, members)
    ]
    return by_member(array, others, member, members)


def sum_parts(array, members, fsdp_count):
    member = lax.axis_index("fsdp") % members
    total = part_of(array, member, 0, members).astype(FULL)
    for step in range(1, members):
        total = total + lax.ppermute(
            part_of(array, member, step, members), "fsdp", member_pairs(fsdp_count, members, step)
        ).astype(FULL)
    return total.astype(LOW)


def routing(info, z, slots, gated):
    at = jnp.arange(slots, dtype=jnp.int32).astype(FULL)[:, None, None]
    hit = (info[:, None, COLUMN_AT : COLUMN_AT + TOP].swapaxes(2, 3) == at.reshape(-1, 1, 1)) & (
        info[:, None, :TOP].swapaxes(2, 3) == z.astype(FULL)
    )
    values = info[:, None, GATE_AT : GATE_AT + TOP].swapaxes(2, 3) if gated else 1.0
    return jnp.sum(jnp.where(hit, values, 0.0), axis=3).astype(LOW)


def swap_slots(slots):
    return lax.all_to_all(slots, "fsdp", split_axis=1, concat_axis=1, tiled=True)


def send_rows(rows, info, slots, gated, ctx_count, fsdp_count):
    every = lax.all_gather(rows, "ctx", axis=0)
    choose = routing(info, lax.axis_index("ctx"), slots, gated)
    chosen = mm("bst,btd->bsd", choose, every).astype(LOW)
    return every, swap_slots(chosen.reshape(ctx_count, fsdp_count, -1, rows.shape[1]))


def send_grads(rows, info, slots, ctx_count, fsdp_count):
    if (ctx_count, fsdp_count) == (4, 8):
        return dispatch_rows(rows, info, slots, ctx_count, fsdp_count)
    return send_rows(rows, info, slots, True, ctx_count, fsdp_count)


def run_expert(rows, info, gate, up, down, grads, ctx_count, fsdp_count):
    if (ctx_count, fsdp_count) == (4, 8):
        return expert_rows(rows, info, gate, up, down, grads, ctx_count, fsdp_count)
    every, arrived = send_rows(rows, info, grads.shape[1], False, ctx_count, fsdp_count)
    slots = arrived.reshape(grads.shape)
    pre = mm("bsd,df->bsf", slots, gate)
    linear = mm("bsd,df->bsf", slots, up)
    act, slope = silu_slope(pre)
    grad = mm("bsd,fd->bsf", grads, down)
    hidden = (act * linear).astype(LOW)
    up_back = (grad * act).astype(LOW)
    gate_back = (grad * linear * slope).astype(LOW)
    back = (mm("bsf,df->bsd", gate_back, gate) + mm("bsf,df->bsd", up_back, up)).astype(LOW)
    return every, arrived, hidden, gate_back, up_back, back


def return_grads(
    slots, info, extra, rows, grads, hidden, gate_back, up_back, ctx_count, fsdp_count
):
    extra = extra.astype(LOW)
    if (ctx_count, fsdp_count) == (4, 8):
        return combine_rows(
            slots, info, extra, rows, grads, hidden, gate_back, up_back, ctx_count, fsdp_count
        )
    back = swap_slots(slots).reshape(ctx_count, -1, slots.shape[3])
    choose = routing(info, lax.axis_index("ctx"), back.shape[1], False)
    total = (mm("bst,bsd->btd", choose, back) + extra).astype(LOW)
    return (
        lax.psum_scatter(total, "ctx", scatter_dimension=0, tiled=False).astype(FULL),
        mm("sd,sf->df", rows, gate_back).astype(LOW),
        mm("sd,sf->df", rows, up_back).astype(LOW),
        mm("sf,sd->fd", hidden, grads).astype(LOW),
    )


def gather_all(items, ctx_count, fsdp_count):
    if (ctx_count, fsdp_count) == (4, 8):
        return gather_arrays(items, ctx_count, fsdp_count)
    results = []
    for kind, shard in items:
        if kind == "line":
            shard = lax.all_to_all(shard, "ctx", split_axis=0, concat_axis=0, tiled=True)
            result = lax.all_gather(shard, "fsdp", axis=1)
        elif kind == "plane":
            result = lax.all_gather(shard, "fsdp", axis=0)[None]
        elif kind == "column":
            result = lax.all_gather(shard, "ctx", axis=0)
        else:
            result = lax.all_gather(shard, ("ctx", "fsdp"), axis=0)
            result = result.reshape((ctx_count, fsdp_count) + shard.shape)
        results.append(result)
    return results


def scatter_all(grads, ctx_count, fsdp_count):
    grads = [grad.astype(LOW) for grad in grads]
    if (ctx_count, fsdp_count) == (4, 8):
        return scatter_arrays(grads, ctx_count, fsdp_count)
    return [
        lax.psum_scatter(grad, ("ctx", "fsdp"), scatter_dimension=0, tiled=True).astype(FULL)
        for grad in grads
    ]


def along_line(array):
    return lax.all_to_all(array, "ctx", split_axis=0, concat_axis=0, tiled=True)


def after(values, *others):
    tied = lax.optimization_barrier((tuple(values), others))
    return tied[0]


def local(
    tokens,
    routes,
    gate_values,
    cotangent,
    attention_gain,
    query_weight,
    latent_weight,
    latent_gain,
    expand_weight,
    output_weight,
    feedforward_gain,
    shared_gate,
    shared_up,
    shared_down,
    expert_gate,
    expert_up,
    expert_down,
):
    row_count = tokens.shape[1]
    model_width = tokens.shape[2]
    ctx_count = lax.axis_size("ctx")
    fsdp_count = lax.axis_size("fsdp")
    device_count = ctx_count * fsdp_count
    experts_total = EXP_DEV * fsdp_count
    capacity = row_count * TOP * 4 // (3 * experts_total)
    members = ctx_count // EXP_DEV
    plane_experts = experts_total // ctx_count
    plane_slots = plane_experts * capacity
    share = capacity // members
    sequence = ctx_count * row_count
    z = lax.axis_index("ctx")
    score_scale = (NOPE + ROPE) ** (-0.5)
    source = tokens[0].astype(FULL)
    cot_low = cotangent[0]
    cot_full = cot_low.astype(FULL)
    positions = stored_positions(
        z * row_count + jnp.arange(row_count, dtype=jnp.int32), row_count, 2 * ctx_count
    )
    dense_rows = latent_weight.shape[0]
    gain_rows = latent_gain.shape[0]
    rotary_end = LATENT + ROPE
    hidden_units = expert_gate.shape[2]
    shared_units = shared_gate.shape[1] // ctx_count

    def swapped(weight):
        weight = weight.reshape((EXP_DEV, members, weight.shape[1] // members) + weight.shape[2:])
        weight = swap_parts(weight.swapaxes(0, 1), members, fsdp_count)
        return weight.reshape((ctx_count,) + weight.shape[2:])

    gate_swapped, up_swapped, down_swapped = (
        swapped(expert_gate),
        swapped(expert_up),
        swapped(expert_down),
    )
    gate_moved = along_line(gate_swapped)

    local_routes = routes[0]
    expert_index = jnp.arange(experts_total, dtype=jnp.int32)
    member_of = (local_routes[..., None] == expert_index).astype(FULL)
    counts = jnp.sum(member_of, axis=1)
    before = jnp.cumsum(counts, axis=0) - counts
    within = jnp.sum(member_of * before[:, None, :], axis=-1).astype(jnp.int32)
    info = jnp.zeros((INFO_ROWS, row_count), FULL)
    info = info.at[:TOP].set((local_routes % ctx_count).astype(FULL).T)
    info = info.at[COLUMN_AT : COLUMN_AT + TOP].set(
        (local_routes // ctx_count * capacity + within).astype(FULL).T
    )
    info = info.at[GATE_AT : GATE_AT + TOP].set(gate_values[0].T)

    tail = jnp.concatenate(
        [
            latent_weight,
            attention_gain[:, None],
            feedforward_gain[:, None],
            jnp.pad(latent_gain, (0, dense_rows - gain_rows))[:, None],
            jnp.zeros((dense_rows, 256 - ROPE - 3), LOW),
        ],
        axis=1,
    )

    def by_line(weight):
        return weight.reshape(dense_rows, ctx_count, shared_units).swapaxes(0, 1)

    dense = (
        info,
        query_weight,
        tail,
        expand_weight,
        output_weight,
        by_line(shared_gate),
        by_line(shared_up),
        shared_down,
    )
    dense = after(dense, gate_swapped, up_swapped, down_swapped)
    kinds = ("column", "all", "all", "all", "all", "line", "line", "plane")
    gathered = gather_all(list(zip(kinds, dense)), ctx_count, fsdp_count)
    all_info = gathered[0]
    full_query, full_tail, full_expand, full_output, full_sgate, full_sup, full_sdown = [
        item.reshape(-1, item.shape[-1]) for item in gathered[1:]
    ]
    full_latent = full_tail[:, :rotary_end]
    gain_one = full_tail[:, rotary_end].astype(FULL)
    gain_two = full_tail[:, rotary_end + 1].astype(FULL)
    gain_latent = (
        full_tail[:, rotary_end + 2].reshape(device_count, dense_rows)[:, :gain_rows]
    ).reshape(LATENT).astype(FULL)

    (up_swapped,) = after((up_swapped,), all_info)
    up_moved = along_line(up_swapped)
    (cot_sent,) = after((cot_low,), gate_moved)
    all_cot, arrived_grad = send_grads(cot_sent, all_info, plane_slots, ctx_count, fsdp_count)
    (down_swapped,) = after((down_swapped,), arrived_grad)
    down_moved = along_line(down_swapped)
    all_cot = all_cot.reshape(sequence, model_width)
    arrived_grad = arrived_grad.reshape(ctx_count, plane_slots, model_width)

    def whole(moved):
        return share_parts(moved, members, fsdp_count).swapaxes(0, 1)

    gate_all = whole(gate_moved).reshape(model_width, hidden_units)
    up_all = whole(up_moved).reshape(model_width, hidden_units)
    down_all = whole(down_moved).transpose(1, 2, 0, 3).reshape(hidden_units, model_width)

    plain_one, inverse_one = norm_forward(source)
    normed = (plain_one * gain_one).astype(LOW)
    (normed,) = after((normed,), arrived_grad, up_moved)
    (query_raw,) = after((jnp.dot(normed, full_query, preferred_element_type=FULL),))
    query_raw = query_raw.reshape(row_count, HEADS, NOPE + ROPE)
    query_nope = query_raw[:, :, :NOPE].astype(LOW)
    query_rope = rotary(query_raw[:, :, NOPE:], positions, 1.0).astype(LOW)
    latent_raw = jnp.dot(normed, full_latent, preferred_element_type=FULL)
    plain_latent, inverse_latent = norm_forward(latent_raw[:, :LATENT])
    latent_norm = (plain_latent * gain_latent).astype(LOW)
    key_rope = rotary(latent_raw[:, LATENT:], positions, 1.0).astype(LOW)
    half_rows = row_count // 2
    pad_rope = ((0, 0), (0, 128 - ROPE))
    keys = lax.all_gather(
        jnp.concatenate([latent_norm, jnp.pad(key_rope, pad_rope)], axis=1), "ctx", axis=0
    )
    keys = keys.reshape(ctx_count, 2, half_rows, LATENT + 128)
    keys = jnp.concatenate([keys[:, 0], keys[::-1, 1]]).reshape(sequence, LATENT + 128)
    all_latent, all_keys = (keys[:, :LATENT], keys[:, LATENT:])
    expand = full_expand.reshape(LATENT, HEADS, NOPE + VDIM)
    expand_key = expand[:, :, :NOPE]
    expand_value = expand[:, :, NOPE:]
    query_latent = mm("thd,chd->htc", query_nope, expand_key).astype(LOW)
    query_turned = jnp.pad(query_rope.swapaxes(0, 1), ((0, 0),) + pad_rope)
    latent_out, log_total = attend(
        query_latent, query_turned, all_latent, all_keys, ctx_count, score_scale
    )
    values_out = (
        mm("htc,chv->thv", latent_out, expand_value).astype(LOW).reshape(row_count, HEADS * VDIM)
    )
    middle = source + jnp.dot(values_out, full_output, preferred_element_type=FULL)
    plain_two, inverse_two = norm_forward(middle)
    second = (plain_two * gain_two).astype(LOW)

    (second_sent,) = after((second,), down_moved)
    all_second, arrived_rows, hidden_act, gate_back, up_back, arrived_back = run_expert(
        second_sent, all_info, gate_all, up_all, down_all, arrived_grad, ctx_count, fsdp_count
    )
    all_second = all_second.reshape(sequence, model_width)
    hidden_act, gate_back, up_back = [
        item.reshape(-1, hidden_units) for item in (hidden_act, gate_back, up_back)
    ]
    shared_g = jnp.dot(all_second, full_sgate, preferred_element_type=FULL)
    shared_u = jnp.dot(all_second, full_sup, preferred_element_type=FULL)
    shared_silu, shared_slope = silu_slope(shared_g)
    shared_hidden = (shared_silu * shared_u).astype(LOW)
    shared_hidden_grad = mm("td,fd->tf", all_cot, full_sdown)
    sup_back = (shared_hidden_grad * shared_silu).astype(LOW)
    sgate_back = (shared_hidden_grad * shared_u * shared_slope).astype(LOW)
    shared_second_grad = mm("tf,df->td", sgate_back, full_sgate) + mm(
        "tf,df->td", sup_back, full_sup
    )
    slots_shape = (ctx_count, fsdp_count, share, model_width)
    rows_shape = (ctx_count, row_count, model_width)
    second_grad, gate_grad, up_grad, down_grad = return_grads(
        arrived_back.reshape(slots_shape),
        all_info,
        shared_second_grad.reshape(rows_shape),
        arrived_rows.reshape(-1, model_width),
        arrived_grad.reshape(-1, model_width),
        hidden_act,
        gate_back,
        up_back,
        ctx_count,
        fsdp_count,
    )
    line_shape = (ctx_count, members, model_width // ctx_count // members, hidden_units)
    gate_sum = sum_parts(gate_grad.reshape(line_shape).swapaxes(0, 1), members, fsdp_count)
    gate_returned = along_line(gate_sum)
    up_sum = sum_parts(up_grad.reshape(line_shape).swapaxes(0, 1), members, fsdp_count)
    down_sum = sum_parts(
        down_grad.reshape(members, hidden_units // members, ctx_count, -1).swapaxes(1, 2),
        members,
        fsdp_count,
    )
    shared_hidden, sgate_back, sup_back, hidden_act = after(
        (shared_hidden, sgate_back, sup_back, hidden_act), second_grad
    )
    sgate_back, sup_back, hidden_act = after((sgate_back, sup_back, hidden_act), gate_sum)
    pair_grad = jnp.stack(
        [mm("td,tf->df", all_second, sgate_back), mm("td,tf->df", all_second, sup_back)]
    ).astype(LOW)
    pair_grad = (
        pair_grad.reshape(2, ctx_count, fsdp_count, dense_rows, shared_units)
        .transpose(2, 0, 1, 3, 4)
        .reshape(fsdp_count, 2, ctx_count * dense_rows, shared_units)
    )
    sdown_grad = mm("tf,td->fd", shared_hidden, all_cot).astype(LOW)
    pair_sent, sdown_sent = (pair_grad, sdown_grad)
    pair_grad = lax.psum_scatter(pair_grad, "fsdp", scatter_dimension=0, tiled=False)
    sdown_grad = lax.psum_scatter(sdown_grad, "fsdp", scatter_dimension=0, tiled=True)
    result = jnp.dot(hidden_act, down_all, preferred_element_type=FULL).astype(LOW)
    shared_out = jnp.dot(shared_hidden, full_sdown, preferred_element_type=FULL)
    (second_grad,) = after(
        (second_grad,), gate_sum, up_sum, down_sum, pair_sent, sdown_sent, result, shared_out
    )
    middle_part, gain_two_grad = norm_backward(second_grad, plain_two, inverse_two, gain_two)
    middle_grad = cot_full + middle_part
    attended_grad = middle_grad.astype(LOW)
    output_weight_grad = mm("tv,td->vd", values_out, attended_grad)
    values_grad = (
        mm("td,vd->tv", attended_grad, full_output).astype(LOW).reshape(row_count, HEADS, VDIM)
    )
    latent_out_grad = mm("thv,chv->htc", values_grad, expand_value).astype(LOW)
    (latent_out_grad,) = after((latent_out_grad,), gate_returned)
    (result,) = after((result,), latent_out_grad)
    came_back = swap_slots(result.reshape(slots_shape)).reshape(ctx_count, plane_slots, model_width)
    query_latent_grad, turned_grad, all_latent_grad, all_keys_grad = attend_back(
        query_latent,
        query_turned,
        all_latent,
        all_keys,
        latent_out,
        log_total,
        latent_out_grad,
        ctx_count,
        score_scale,
    )
    query_rope_grad = turned_grad[:, :, :ROPE].swapaxes(0, 1)
    keys_part = jnp.concatenate([all_latent_grad, all_keys_grad[:, :ROPE]], axis=1)
    keys_part = keys_part.reshape(2, ctx_count, half_rows, LATENT + ROPE)
    keys_part = jnp.stack([keys_part[0], keys_part[1, ::-1]], axis=1)
    (keys_part,) = after((keys_part,), pair_grad, sdown_grad)
    keys_part = lax.psum_scatter(
        keys_part.reshape(sequence, LATENT + ROPE).astype(LOW),
        "ctx",
        scatter_dimension=0,
        tiled=True,
    ).astype(FULL)
    latent_grad, keys_grad = (keys_part[:, :LATENT], keys_part[:, LATENT:])
    expand_value_grad = mm("htc,thv->chv", latent_out, values_grad)

    out_part = (
        mm("bst,bsd->btd", routing(all_info, z, plane_slots, True), came_back)
        + shared_out.reshape(ctx_count, row_count, model_width)
    ).astype(LOW)
    (out_part,) = after((out_part,), keys_part)
    out_sum = lax.psum_scatter(out_part, "ctx", scatter_dimension=0, tiled=False).astype(FULL)
    layer_out = (middle + out_sum).astype(LOW)[None]
    sdown_grad = sdown_grad.astype(FULL)

    query_nope_grad = mm("htc,chd->thd", query_latent_grad, expand_key)
    expand_key_grad = mm("thd,htc->chd", query_nope, query_latent_grad)
    expand_grad = jnp.concatenate([expand_key_grad, expand_value_grad], axis=-1).reshape(
        LATENT, HEADS * (NOPE + VDIM)
    )
    query_grad = (
        jnp.concatenate([query_nope_grad, rotary(query_rope_grad, positions, -1.0)], axis=-1)
        .astype(LOW)
        .reshape(row_count, HEADS * (NOPE + ROPE))
    )
    latent_part_grad, gain_latent_grad = norm_backward(
        latent_grad, plain_latent, inverse_latent, gain_latent
    )
    latent_raw_grad = jnp.concatenate(
        [latent_part_grad, rotary(keys_grad, positions, -1.0)], axis=-1
    ).astype(LOW)
    query_weight_grad = mm("td,tq->dq", normed, query_grad)
    latent_weight_grad = mm("td,tq->dq", normed, latent_raw_grad)
    normed_grad = mm("tq,dq->td", query_grad, full_query) + mm(
        "tq,dq->td", latent_raw_grad, full_latent
    )
    source_part, gain_one_grad = norm_backward(normed_grad, plain_one, inverse_one, gain_one)
    tokens_grad = (middle_grad + source_part)[None]

    gain_latent_column = jnp.pad(
        gain_latent_grad.reshape(device_count, gain_rows), ((0, 0), (0, dense_rows - gain_rows))
    ).reshape(model_width)
    tail_grad = jnp.concatenate(
        [
            latent_weight_grad,
            gain_one_grad[:, None],
            gain_two_grad[:, None],
            gain_latent_column[:, None],
            jnp.zeros((model_width, 256 - ROPE - 3), FULL),
        ],
        axis=1,
    )
    (up_sum,) = after((up_sum,), came_back, query_nope_grad)
    up_returned = along_line(up_sum)
    (pair_grad,) = after((pair_grad,), up_returned)
    pair_grad = lax.all_to_all(
        pair_grad, "ctx", split_axis=1, concat_axis=2, tiled=True
    ).astype(FULL)
    (down_sum,) = after((down_sum,), up_returned, normed_grad, pair_grad)
    down_returned = along_line(down_sum)
    dense_grads = after(
        (query_weight_grad, tail_grad, expand_grad, output_weight_grad), up_returned
    )
    query_sum, tail_sum, expand_sum, output_sum = scatter_all(
        dense_grads, ctx_count, fsdp_count
    )

    def owned(moved, like):
        moved = moved.reshape((members, EXP_DEV) + moved.shape[1:])
        moved = swap_parts(moved, members, fsdp_count).swapaxes(0, 1)
        return moved.reshape(like.shape).astype(FULL)

    expert_grads = (
        owned(gate_returned, expert_gate),
        owned(up_returned, expert_up),
        owned(down_returned, expert_down),
    )
    return (
        layer_out,
        tokens_grad,
        tail_sum[:, rotary_end],
        query_sum,
        tail_sum[:, :rotary_end],
        tail_sum[:gain_rows, rotary_end + 2],
        expand_sum,
        output_sum,
        tail_sum[:, rotary_end + 1],
        pair_grad[0],
        pair_grad[1],
        sdown_grad,
        expert_grads[0],
        expert_grads[1],
        expert_grads[2],
    )


def solution(mesh):
    in_specs = (
        P("fsdp", "ctx", None),
        P("fsdp", "ctx", None),
        P("fsdp", "ctx", None),
        P("fsdp", "ctx", None),
        P(("ctx", "fsdp")),
        P(("ctx", "fsdp"), None),
        P(("ctx", "fsdp"), None),
        P(("ctx", "fsdp")),
        P(("ctx", "fsdp"), None),
        P(("ctx", "fsdp"), None),
        P(("ctx", "fsdp")),
        P(("ctx", "fsdp"), None),
        P(("ctx", "fsdp"), None),
        P(("ctx", "fsdp"), None),
        P("fsdp", "ctx", None),
        P("fsdp", "ctx", None),
        P("fsdp", None, "ctx"),
    )
    out_specs = (
        P("fsdp", "ctx", None),
        P("fsdp", "ctx", None),
        P(("ctx", "fsdp")),
        P(("ctx", "fsdp"), None),
        P(("ctx", "fsdp"), None),
        P(("ctx", "fsdp")),
        P(("ctx", "fsdp"), None),
        P(("ctx", "fsdp"), None),
        P(("ctx", "fsdp")),
        P(("ctx", "fsdp"), None),
        P(("ctx", "fsdp"), None),
        P(("ctx", "fsdp"), None),
        P("fsdp", "ctx", None),
        P("fsdp", "ctx", None),
        P("fsdp", None, "ctx"),
    )
    return jax.shard_map(local, mesh=mesh, in_specs=in_specs, out_specs=out_specs, check_vma=False)
```

```python
import functools

import jax
import jax.numpy as jnp
from jax import lax
from jax.experimental import pallas as pl
from jax.experimental.pallas import tpu as pltpu
from jax.sharding import PartitionSpec as P

HEADS = 16
NOPE = 128
ROPE = 64
LATENT = 512
VDIM = 128
TOP = 6
EXP_DEV = 2


epsilon = 1e-06
rope_base = 10000.0
masked_score = -1e30


def stored_positions(row_index, per_device, block_count):
    device = row_index // per_device
    within = row_index % per_device
    half_block = per_device // 2
    return jnp.where(
        within >= half_block,
        (block_count - 1 - device) * half_block + within - half_block,
        device * half_block + within,
    )


def rotary(values, positions, direction):
    half_rope = values.shape[-1] // 2
    frequency = rope_base ** (-jnp.arange(half_rope, dtype=jnp.float32) / half_rope)
    angles = positions.astype(jnp.float32)[:, None] * frequency[None, :]
    cosine_table = jnp.cos(angles)
    sine_table = direction * jnp.sin(angles)
    if values.ndim == 3:
        cosine_table = cosine_table[:, None, :]
        sine_table = sine_table[:, None, :]
    front_half = values[..., :half_rope]
    back_half = values[..., half_rope:]
    return jnp.concatenate(
        [
            front_half * cosine_table - back_half * sine_table,
            back_half * cosine_table + front_half * sine_table,
        ],
        axis=-1,
    )


def norm_forward(values):
    inverse = lax.rsqrt(jnp.mean(values * values, axis=-1, keepdims=True) + epsilon)
    return (values * inverse, inverse)


def norm_backward(normed_grad, plain, inverse, gain):
    gain_grad = jnp.sum(normed_grad * plain, axis=0)
    scaled = normed_grad * gain
    return (
        inverse * (scaled - plain * jnp.mean(scaled * plain, axis=-1, keepdims=True)),
        gain_grad,
    )


def silu_slope(values):
    sigma = jax.nn.sigmoid(values)
    return (values * sigma, sigma * (1.0 + values * (1.0 - sigma)))


LOW = jnp.bfloat16
FULL = jnp.float32


MESH_ID = pl.DeviceIdType.MESH
BIG_VMEM = 60 * 1024 * 1024


def flip(index, bit):
    return index + bit - 2 * bit * lax.rem(lax.div(index, bit), 2)


def toggled(index, mask):
    for bit in (1, 2, 4):
        if mask & bit:
            index = flip(index, bit)
    return index


def nearest(z, step):
    upper = lax.div(z, 2)
    if step == 0:
        return z
    if step == 1:
        return z + 1 - 2 * upper
    if step == 2:
        return 2 - 2 * lax.rem(z, 2) + upper
    return 3 - 3 * upper


def remote(source, target, send, receive, z, f):
    return pltpu.make_async_remote_copy(
        src_ref=source,
        dst_ref=target,
        send_sem=send,
        recv_sem=receive,
        device_id={"ctx": z, "fsdp": f},
        device_id_type=MESH_ID,
    )


def greet(z, f, masks, ctx_count, whole_line=False):
    barrier = pltpu.get_barrier_semaphore()

    def hello(to_z, to_f):
        pl.semaphore_signal(
            barrier, inc=1, device_id={"ctx": to_z, "fsdp": to_f}, device_id_type=MESH_ID
        )

    for mask in masks:
        hello(z, toggled(f, mask))
    if whole_line:
        for step in range(1, ctx_count):
            hello(lax.rem(z + step, ctx_count), f)
        pl.semaphore_wait(barrier, len(masks) + ctx_count - 1)
        return

    @pl.when(z > 0)
    def _():
        hello(z - 1, f)

    @pl.when(z < ctx_count - 1)
    def _():
        hello(z + 1, f)

    along = lax.div(z + ctx_count - 1, ctx_count) + lax.div(2 * ctx_count - 2 - z, ctx_count)
    pl.semaphore_wait(barrier, len(masks) + along)


def both_ways(z, block, ctx_count, act):
    @pl.when((block <= z) & (z < ctx_count - 1))
    def _():
        act(0, z + 1)

    @pl.when((block >= z) & (z > 0))
    def _():
        act(1, z - 1)


def halves(rows, width):
    if rows % 32 == 0:
        return tuple((pl.ds(start, rows // 2), slice(None)) for start in (0, rows // 2))
    return tuple((slice(None), pl.ds(start, width // 2)) for start in (0, width // 2))


def add_rows(target, rows, *terms):
    @pl.loop(0, rows, step=16)
    def _(start):
        part = pl.ds(pl.multiple_of(start, 16), 16)
        total = terms[0][part, :].astype(FULL)
        for term in terms[1:]:
            total = total + term[part, :].astype(FULL)
        target[part, :] = total.astype(target.dtype)


def scatter_kernel(ctx_count, kinds, *refs):
    count = len(kinds)
    grads, outs = refs[:count], refs[count : 2 * count]
    banks = [refs[(2 + kind) * count : (3 + kind) * count] for kind in range(7)]
    load_sem, c_send, c_recv, p_send, p_recv, z_send, z_recv = refs[9 * count :]
    z, f = lax.axis_index("ctx"), lax.axis_index("fsdp")
    side = lax.rem(f, 2)
    chip = lax.div(f, 2)
    core, x_near, y_near = flip(f, 1), flip(f, 2), flip(f, 4)
    x_chip, y_chip = flip(chip, 1), flip(chip, 2)
    far_chip = flip(x_chip, 2)
    greet(z, f, (1, 2, 4), ctx_count, True)
    order = [nearest(z, ctx_count - 1 - step) for step in range(ctx_count)]

    def work(item):
        grad_ref, out_ref = grads[item], outs[item]
        mine, from_core, from_x, from_y, half_x, half_y, from_z = [bank[item] for bank in banks]
        rows, width = out_ref.shape[-2:]
        left, right = halves(rows, width)
        half_rows = half_x.shape[1]

        def load(block):
            return pltpu.make_async_copy(
                grad_ref.at[block, :, side], mine.at[block], load_sem.at[item, block]
            )

        def c_copy(block):
            return remote(
                grad_ref.at[block, :, 1 - side],
                from_core.at[block],
                c_send.at[item, block],
                c_recv.at[item, block],
                z,
                core,
            )

        def p_copy(block, which):
            source, target, to = (
                (mine.at[(block, far_chip) + left], half_y.at[block], y_near),
                (mine.at[(block, far_chip) + right], half_x.at[block], x_near),
                (mine.at[block, x_chip], from_x.at[block], x_near),
                (mine.at[block, y_chip], from_y.at[block], y_near),
            )[which]
            sems = (p_send.at[item, block, which], p_recv.at[item, block, which])
            return remote(source, target, *sems, z, to)

        def z_copy(block, way, target):
            return remote(
                mine.at[block, chip],
                from_z.at[way, block],
                z_send.at[item, block],
                z_recv.at[item, way, block],
                target,
                f,
            )

        def z_arrived(block, way):
            at = from_z.at[way, block]
            sems = (z_send.at[item, block], z_recv.at[item, way, block])
            remote(at, at, *sems, z, core).wait_recv()

        def piece(block):
            sems = (z_send.at[item, block], z_recv.at[item, 0, z])
            return remote(mine.at[block, chip], out_ref.at[z], *sems, block, f)

        def start(step):
            c_copy(order[step]).start()
            load(order[step]).start()

        def first(step):
            block = order[step]
            load(block).wait()
            c_copy(block).wait_recv()
            far_part = mine.at[block, far_chip]
            add_rows(far_part, rows, far_part, from_core.at[block, far_chip])
            p_copy(block, 0).start()
            p_copy(block, 1).start()

        def second(step):
            block = order[step]
            x_part, y_part = mine.at[block, x_chip], mine.at[block, y_chip]
            add_rows(x_part, rows, x_part, from_core.at[block, x_chip])
            add_rows(y_part, rows, y_part, from_core.at[block, y_chip])
            p_copy(block, 0).wait_recv()
            x_left = mine.at[(block, x_chip) + left]
            add_rows(x_left, half_rows, x_left, half_y.at[block])
            p_copy(block, 2).start()
            p_copy(block, 1).wait_recv()
            y_right = mine.at[(block, y_chip) + right]
            add_rows(y_right, half_rows, y_right, half_x.at[block])
            p_copy(block, 3).start()

        def third(step):
            block = order[step]
            p_copy(block, 2).wait_recv()
            p_copy(block, 3).wait_recv()
            own = mine.at[block, chip]
            terms = (own, from_core.at[block, chip], from_x.at[block], from_y.at[block])
            if kinds[item] == "line":
                add_rows(out_ref.at[z] if step == ctx_count - 1 else own, rows, *terms)
                if step < ctx_count - 1:
                    piece(block).start()
                return

            if step == ctx_count - 1:

                @pl.when(z > 0)
                def _():
                    z_arrived(block, 0)

                @pl.when(z < ctx_count - 1)
                def _():
                    z_arrived(block, 1)

                @pl.when(z == 0)
                def _():
                    add_rows(out_ref, rows, *terms, from_z.at[1, block])

                @pl.when(z == ctx_count - 1)
                def _():
                    add_rows(out_ref, rows, *terms, from_z.at[0, block])

                @pl.when((z > 0) & (z < ctx_count - 1))
                def _():
                    add_rows(out_ref, rows, *terms, from_z.at[0, block], from_z.at[1, block])

                return

            for way, above in ((1, True), (0, False)):
                heading = (block < z) if above else (block > z)
                has_more = (z < ctx_count - 1) if above else (z > 0)

                @pl.when(heading & has_more)
                def _():
                    z_arrived(block, way)
                    add_rows(own, rows, *terms, from_z.at[way, block])

                @pl.when(heading & jnp.logical_not(has_more))
                def _():
                    add_rows(own, rows, *terms)

                @pl.when(heading)
                def _():
                    z_copy(block, way, z - 1 if above else z + 1).start()

        def finish(step):
            block = order[step]
            c_copy(block).wait_send()
            for which in range(4):
                p_copy(block, which).wait_send()
            if step == ctx_count - 1:
                return
            if kinds[item] == "line":
                piece(block).wait_send()
                at = out_ref.at[block]
                sems = (z_send.at[item, block], z_recv.at[item, 0, block])
                remote(at, at, *sems, z, core).wait_recv()
            else:
                z_copy(block, 0, z).wait_send()

        return start, first, second, third, finish

    stages = list(zip(*[work(item) for item in range(count)]))
    for step in range(ctx_count):
        for act in stages[0]:
            act(step)
    for step in range(ctx_count + 2):
        for lag in (0, 1, 2):
            if 0 <= step - lag < ctx_count:
                for act in stages[1 + lag]:
                    act(step - lag)
    for step in range(ctx_count):
        for act in stages[4]:
            act(step)


def scatter_arrays(items, ctx_count, fsdp_count):
    kinds = tuple(kind for kind, grad in items)
    grads = [grad for kind, grad in items]
    count = len(grads)
    chips = fsdp_count // 2
    shapes = [
        (grad.shape[0] // (ctx_count * fsdp_count), grad.shape[1]) for grad in grads
    ]
    half_shapes = [
        (rows // 2, width) if rows % 32 == 0 else (rows, width // 2) for rows, width in shapes
    ]
    dma = pltpu.SemaphoreType.DMA
    leads = [(ctx_count, chips), (ctx_count, chips), (ctx_count,), (ctx_count,)]
    banks = [pltpu.VMEM(lead + shape, LOW) for lead in leads for shape in shapes]
    banks += [pltpu.VMEM((ctx_count,) + shape, LOW) for _ in range(2) for shape in half_shapes]
    banks += [
        pltpu.VMEM((2, ctx_count) + shape if kind == "all" else (1, 1, 16, 128), LOW)
        for kind, shape in zip(kinds, shapes)
    ]
    return pl.pallas_call(
        functools.partial(scatter_kernel, ctx_count, kinds),
        out_shape=[
            jax.ShapeDtypeStruct(shape, FULL)
            if kind == "all"
            else jax.ShapeDtypeStruct((ctx_count,) + shape, LOW)
            for kind, shape in zip(kinds, shapes)
        ],
        in_specs=[pl.BlockSpec(memory_space=pl.ANY)] * count,
        out_specs=[pl.BlockSpec(memory_space=pltpu.VMEM)] * count,
        scratch_shapes=banks
        + [
            dma((count, ctx_count)),
            dma((count, ctx_count)),
            dma((count, ctx_count)),
            dma((count, ctx_count, 4)),
            dma((count, ctx_count, 4)),
            dma((count, ctx_count)),
            dma((count, 2, ctx_count)),
        ],
        compiler_params=pltpu.CompilerParams(
            collective_id=1, has_side_effects=True, vmem_limit_bytes=BIG_VMEM
        ),
        cost_estimate=pl.CostEstimate(flops=0, bytes_accessed=500_000_000, transcendentals=0),
    )(
        *[
            grad.reshape((ctx_count, chips, 2) + shape)
            for grad, shape in zip(grads, shapes)
        ]
    )


HEAD_GROUP = 4
KEYS = 256


def dot_last(left, right):
    return lax.dot_general(left, right, (((1,), (1,)), ((), ())), preferred_element_type=FULL)


def dot_first(left, right):
    return lax.dot_general(left, right, (((0,), (0,)), ((), ())), preferred_element_type=FULL)


def reach(half, rows, ctx_count):
    ctx = lax.axis_index("ctx")
    first = jnp.where(half == 0, ctx, 2 * ctx_count - 1 - ctx) * rows
    return first, lax.div(first + rows + KEYS - 1, KEYS)


def block_scores(query, turned, keys_ref, rope_ref, index, first, rows, scale):
    part = pl.ds(pl.multiple_of(index * KEYS, KEYS), KEYS)
    keys, rope = keys_ref[part, :], rope_ref[part, :]
    scores = (dot_last(query, keys) + dot_last(turned, rope)) * scale
    shape = scores.shape
    at = first + lax.rem(lax.broadcasted_iota(jnp.int32, shape, 0), rows)
    key_at = index * KEYS + lax.broadcasted_iota(jnp.int32, shape, 1)
    return part, keys, rope, scores, at >= key_at


def attend_kernel(
    ctx_count, scale, query_ref, turned_ref, keys_ref, rope_ref, out_ref, log_ref, total, top, norm
):
    heads, rows, width = query_ref.shape
    first, blocks = reach(pl.program_id(0), rows, ctx_count)
    query = query_ref[...].reshape(heads * rows, width)
    turned = turned_ref[...].reshape(heads * rows, -1)
    total[...] = jnp.zeros_like(total)
    norm[...] = jnp.zeros_like(norm)
    top[...] = jnp.full_like(top, masked_score)

    @pl.loop(0, blocks)
    def _(index):
        part, keys, rope, scores, seen = block_scores(
            query, turned, keys_ref, rope_ref, index, first, rows, scale
        )
        scores = jnp.where(seen, scores, masked_score)
        old = top[...]
        new = jnp.maximum(old, jnp.max(scores, axis=1, keepdims=True))
        weights = jnp.exp(scores - new)
        shrink = jnp.exp(old - new)
        top[...] = new
        norm[...] = norm[...] * shrink + jnp.sum(weights, axis=1, keepdims=True)
        total[...] = total[...] * shrink + jnp.dot(
            weights.astype(LOW), keys, preferred_element_type=FULL
        )

    out_ref[...] = (total[...] / norm[...]).astype(LOW).reshape(out_ref.shape)
    log_ref[...] = (top[...] + jnp.log(norm[...])).reshape(log_ref.shape)


def attend_back_kernel(
    ctx_count,
    scale,
    query_ref,
    turned_ref,
    keys_ref,
    rope_ref,
    out_ref,
    log_ref,
    grad_ref,
    query_grad_ref,
    turned_grad_ref,
    keys_grad_ref,
    rope_grad_ref,
    query_total,
    turned_total,
):
    heads, rows, width = query_ref.shape
    first, blocks = reach(pl.program_id(0), rows, ctx_count)
    query = query_ref[...].reshape(heads * rows, width)
    turned = turned_ref[...].reshape(heads * rows, -1)
    grad = grad_ref[...].reshape(heads * rows, width)
    out = out_ref[...].reshape(heads * rows, width)
    logs = log_ref[...].reshape(heads * rows, 1)
    inner = jnp.sum(grad.astype(FULL) * out.astype(FULL), axis=1, keepdims=True)
    query_total[...] = jnp.zeros_like(query_total)
    turned_total[...] = jnp.zeros_like(turned_total)

    @pl.when((pl.program_id(0) == 0) & (pl.program_id(1) == 0))
    def _():
        keys_grad_ref[...] = jnp.zeros_like(keys_grad_ref)
        rope_grad_ref[...] = jnp.zeros_like(rope_grad_ref)

    @pl.loop(0, blocks)
    def _(index):
        part, keys, rope, scores, seen = block_scores(
            query, turned, keys_ref, rope_ref, index, first, rows, scale
        )
        weights = jnp.where(seen, jnp.exp(scores - logs), 0.0)
        change = (weights * (dot_last(grad, keys) - inner) * scale).astype(LOW)
        query_total[...] += jnp.dot(change, keys, preferred_element_type=FULL)
        turned_total[...] += jnp.dot(change, rope, preferred_element_type=FULL)
        keys_grad_ref[part, :] += dot_first(change, query) + dot_first(weights.astype(LOW), grad)
        rope_grad_ref[part, :] += dot_first(change, turned)

    query_grad_ref[...] = query_total[...].astype(LOW).reshape(query_grad_ref.shape)
    turned_grad_ref[...] = turned_total[...].reshape(turned_grad_ref.shape)


def attend_specs(heads, group, rows, widths):
    return [pl.BlockSpec((group, rows, width), lambda half, g: (g, half, 0)) for width in widths]


def whole_spec(array):
    return pl.BlockSpec(array.shape, lambda half, g: (0, 0))


def attend(query, turned, keys, rope, ctx_count, scale):
    heads, count, width = query.shape
    group, rows = HEAD_GROUP, count // 2
    lanes = turned.shape[2]
    return pl.pallas_call(
        functools.partial(attend_kernel, ctx_count, scale),
        grid=(2, heads // group),
        out_shape=(
            jax.ShapeDtypeStruct((heads, count, width), LOW),
            jax.ShapeDtypeStruct((heads, count, 1), FULL),
        ),
        in_specs=attend_specs(heads, group, rows, (width, lanes))
        + [whole_spec(keys), whole_spec(rope)],
        out_specs=tuple(attend_specs(heads, group, rows, (width, 1))),
        scratch_shapes=[
            pltpu.VMEM((group * rows, width), FULL),
            pltpu.VMEM((group * rows, 1), FULL),
            pltpu.VMEM((group * rows, 1), FULL),
        ],
        compiler_params=pltpu.CompilerParams(vmem_limit_bytes=BIG_VMEM),
        cost_estimate=pl.CostEstimate(
            flops=12_000_000_000, bytes_accessed=12_000_000, transcendentals=3_000_000
        ),
    )(query, turned, keys, rope)


def attend_back(query, turned, keys, rope, out, logs, grad, ctx_count, scale):
    heads, count, width = query.shape
    group, rows = HEAD_GROUP, count // 2
    lanes = turned.shape[2]
    return pl.pallas_call(
        functools.partial(attend_back_kernel, ctx_count, scale),
        grid=(2, heads // group),
        out_shape=(
            jax.ShapeDtypeStruct((heads, count, width), LOW),
            jax.ShapeDtypeStruct((heads, count, lanes), FULL),
            jax.ShapeDtypeStruct(keys.shape, FULL),
            jax.ShapeDtypeStruct(rope.shape, FULL),
        ),
        in_specs=attend_specs(heads, group, rows, (width, lanes))
        + [whole_spec(keys), whole_spec(rope)]
        + attend_specs(heads, group, rows, (width, 1, width)),
        out_specs=tuple(
            attend_specs(heads, group, rows, (width, lanes)) + [whole_spec(keys), whole_spec(rope)]
        ),
        scratch_shapes=[
            pltpu.VMEM((group * rows, width), FULL),
            pltpu.VMEM((group * rows, lanes), FULL),
        ],
        compiler_params=pltpu.CompilerParams(vmem_limit_bytes=BIG_VMEM),
        cost_estimate=pl.CostEstimate(
            flops=30_000_000_000, bytes_accessed=30_000_000, transcendentals=3_000_000
        ),
    )(query, turned, keys, rope, out, logs, grad)


PEERS = (6, 7, 2, 4, 3, 5, 1)
COLUMN_AT, GATE_AT, INFO_ROWS = 8, 16, 24


def one_hot(info, z, slots, gated):
    count = info.shape[1]
    at = lax.broadcasted_iota(jnp.int32, (slots, count), 0).astype(FULL)
    plane = z.astype(FULL)
    total = jnp.zeros((slots, count), FULL)
    for route in range(TOP):
        hit = (info[COLUMN_AT + route][None, :] == at) & (info[route][None, :] == plane)
        value = info[GATE_AT + route][None, :] if gated else 1.0
        total = total + jnp.where(hit, value, 0.0)
    return total.astype(LOW)


class Dispatch:
    def __init__(self, ctx_count, gated, rows_ref, info_ref, all_ref, blocks, chosen, arrived, sems):
        self.own_sem, self.all_sem, self.keep_sem = sems[:3]
        self.z_send, self.z_recv, self.p_send, self.p_recv = sems[3:]
        self.ctx_count, self.gated = ctx_count, gated
        self.rows_ref, self.info_ref, self.all_ref = rows_ref, info_ref, all_ref
        self.blocks, self.chosen, self.arrived = blocks, chosen, arrived
        self.z, self.f = lax.axis_index("ctx"), lax.axis_index("fsdp")
        self.core = flip(self.f, 1)

    def z_copy(self, block, way, target):
        at = self.blocks.at[block]
        sems = (self.z_send.at[block, way], self.z_recv.at[block])
        return remote(at, at, *sems, target, self.f)

    def p_copy(self, block, place):
        to = toggled(self.f, PEERS[place])
        sems = (self.p_send.at[block, place], self.p_recv.at[block, place])
        return remote(
            self.chosen.at[block, to], self.arrived.at[block, self.f], *sems, self.z, to
        )

    def keep(self, block):
        source, target = self.chosen.at[block, self.f], self.arrived.at[block, self.f]
        return pltpu.make_async_copy(source, target, self.keep_sem.at[block])

    def store(self, block):
        source, target = self.blocks.at[block], self.all_ref.at[block]
        return pltpu.make_async_copy(source, target, self.all_sem.at[block])

    def begin(self):
        own = pltpu.make_async_copy(self.rows_ref, self.blocks.at[self.z], self.own_sem)
        own.start()
        own.wait()

    def pass_on(self, block, own):
        if not own:
            at = self.blocks.at[block]
            sems = (self.z_send.at[block, 0], self.z_recv.at[block])
            remote(at, at, *sems, self.z, self.core).wait_recv()
        both_ways(
            self.z, block, self.ctx_count, lambda way, to: self.z_copy(block, way, to).start()
        )
        self.store(block).start()
        groups, share, width = self.chosen.shape[1:]
        choose = one_hot(self.info_ref[block], self.z, groups * share, self.gated)

        @pl.loop(0, width, step=256)
        def _(start):
            part = pl.ds(pl.multiple_of(start, 256), 256)
            tile = jnp.dot(choose, self.blocks[block, :, part], preferred_element_type=FULL)
            self.chosen[block, :, :, part] = tile.astype(LOW).reshape(groups, share, 256)

        for place in range(len(PEERS)):
            self.p_copy(block, place).start()
        self.keep(block).start()

    def await_slots(self, block):
        self.keep(block).wait()
        for place in range(len(PEERS)):
            at = self.arrived.at[block, toggled(self.f, PEERS[place])]
            sems = (self.p_send.at[block, place], self.p_recv.at[block, place])
            remote(at, at, *sems, self.z, self.core).wait_recv()

    def finish(self):
        for step in range(self.ctx_count):
            block = nearest(self.z, step)
            self.store(block).wait()
            both_ways(
                self.z,
                block,
                self.ctx_count,
                lambda way, to: self.z_copy(block, way, to).wait_send(),
            )
            for place in range(len(PEERS)):
                self.p_copy(block, place).wait_send()


def dispatch_scratch(ctx_count, fsdp_count, count, share, width):
    dma = pltpu.SemaphoreType.DMA
    return [
        pltpu.VMEM((ctx_count, count, width), LOW),
        pltpu.VMEM((ctx_count, fsdp_count, share, width), LOW),
    ], [
        dma,
        dma((ctx_count,)),
        dma((ctx_count,)),
        dma((ctx_count, 2)),
        dma((ctx_count,)),
        dma((ctx_count, len(PEERS))),
        dma((ctx_count, len(PEERS))),
    ]


def gather_kernel(ctx_count, kinds, *refs):
    count = len(kinds)
    shards, rows_ref = refs[:count], refs[count]
    outs, all_ref, slots_ref = refs[count + 1 : 2 * count + 1], refs[2 * count + 1], refs[2 * count + 2]
    blocks, chosen = refs[2 * count + 3 : 2 * count + 5]
    own_sem, z_send, z_recv, p_send, p_recv, c_send, c_recv = refs[2 * count + 5 : 2 * count + 12]
    z, f = lax.axis_index("ctx"), lax.axis_index("fsdp")
    core, x_near, y_near = flip(f, 1), flip(f, 2), flip(f, 4)
    far = flip(x_near, 4)
    move = Dispatch(
        ctx_count, True, rows_ref, outs[0], all_ref, blocks, chosen, slots_ref, refs[2 * count + 12 :]
    )
    greet(z, f, PEERS, ctx_count, True)

    def slot(item, step):
        return 0 if kinds[item] == "plane" else nearest(z, step)

    def steps(item, step):
        return step == 0 if kinds[item] == "plane" else 0 <= step < ctx_count

    def z_view(item, block):
        return outs[item].at[block] if kinds[item] == "column" else outs[item].at[block, f]

    def own(item):
        source = shards[item].at[z] if kinds[item] == "line" else shards[item]
        return pltpu.make_async_copy(source, z_view(item, slot(item, 0)), own_sem.at[item])

    def z_copy(item, block, way, target):
        at = z_view(item, block)
        return remote(at, at, z_send.at[item, block, way], z_recv.at[item, block], target, f)

    def piece(item, step):
        target = lax.rem(z + step, ctx_count)
        return remote(
            shards[item].at[target],
            outs[item].at[z, f],
            z_send.at[item, target, 0],
            z_recv.at[item, z],
            target,
            f,
        )

    def part(item, block, at, which):
        rows, columns = halves(*outs[item].shape[2:])[which]
        return outs[item].at[block, at, rows, columns]

    def p_copy(item, block, which):
        at = (
            lambda: outs[item].at[block, f],
            lambda: outs[item].at[block, f],
            lambda: part(item, block, x_near, 0),
            lambda: part(item, block, y_near, 1),
        )[which]()
        to = (x_near, y_near, y_near, x_near)[which]
        sems = (p_send.at[item, block, which], p_recv.at[item, block, which])
        return remote(at, at, *sems, z, to)

    def p_arrived(item, block, which):
        at = (
            lambda: outs[item].at[block, x_near],
            lambda: outs[item].at[block, y_near],
            lambda: part(item, block, far, 0),
            lambda: part(item, block, far, 1),
        )[which]()
        sems = (p_send.at[item, block, which], p_recv.at[item, block, which])
        remote(at, at, *sems, z, x_near).wait_recv()

    def c_copy(item, block, which):
        at = outs[item].at[block, (f, x_near, y_near, far)[which]]
        sems = (c_send.at[item, block, which], c_recv.at[item, block, which])
        return remote(at, at, *sems, z, core)

    def c_arrived(item, block, which):
        at = outs[item].at[block, flip((f, x_near, y_near, far)[which], 1)]
        sems = (c_send.at[item, block, which], c_recv.at[item, block, which])
        remote(at, at, *sems, z, core).wait_recv()

    def first(item, step):
        block = slot(item, step)
        if step == 0:
            own(item).wait()
        else:
            at = z_view(item, block)
            sems = (z_send.at[item, block, 0], z_recv.at[item, block])
            remote(at, at, *sems, z, core).wait_recv()
        if kinds[item] in ("all", "column"):
            both_ways(z, block, ctx_count, lambda way, to: z_copy(item, block, way, to).start())
        if kinds[item] != "column":
            p_copy(item, block, 0).start()
            p_copy(item, block, 1).start()
            c_copy(item, block, 0).start()

    def second(item, step):
        block = slot(item, step)
        for which in (0, 1):
            p_arrived(item, block, which)
            p_copy(item, block, which + 2).start()
            c_copy(item, block, which + 1).start()

    def third(item, step):
        block = slot(item, step)
        p_arrived(item, block, 2)
        p_arrived(item, block, 3)
        c_copy(item, block, 3).start()

    for item in range(count):
        own(item).start()
        if kinds[item] == "line":
            for step in range(1, ctx_count):
                piece(item, step).start()
    move.begin()
    for step in range(ctx_count + 2):
        for lag, stage in ((0, first), (1, second), (2, third)):
            for item in range(count):
                if steps(item, step - lag) and (lag == 0 or kinds[item] != "column"):
                    stage(item, step - lag)
            if lag == 0 and step < ctx_count:
                move.pass_on(nearest(z, step), step == 0)
    for step in range(ctx_count):
        move.await_slots(nearest(z, step))
    move.finish()
    for item in range(count):
        for step in range(ctx_count):
            if not steps(item, step):
                continue
            block = slot(item, step)
            if kinds[item] != "column":
                for which in range(4):
                    c_arrived(item, block, which)
                    p_copy(item, block, which).wait_send()
                    c_copy(item, block, which).wait_send()
            if kinds[item] == "line" and step > 0:
                piece(item, step).wait_send()
            if kinds[item] in ("all", "column"):
                both_ways(
                    z, block, ctx_count, lambda way, to: z_copy(item, block, way, to).wait_send()
                )


def gather_arrays(items, rows, slots, ctx_count, fsdp_count):
    kinds = tuple(kind for kind, shard in items)
    shards = [shard for kind, shard in items]
    lead = {
        "all": (ctx_count, fsdp_count),
        "line": (ctx_count, fsdp_count),
        "plane": (1, fsdp_count),
        "column": (ctx_count,),
    }
    shapes = [
        lead[kind] + (shard.shape[1:] if kind == "line" else shard.shape) for kind, shard in items
    ]
    row_count, width = rows.shape
    share = slots // fsdp_count
    shapes += [(ctx_count, row_count, width), (ctx_count, fsdp_count, share, width)]
    buffers, sems = dispatch_scratch(ctx_count, fsdp_count, row_count, share, width)
    count = len(items)
    dma = pltpu.SemaphoreType.DMA
    four = dma((count, ctx_count, 4))
    anywhere = pl.BlockSpec(memory_space=pl.ANY)
    results = pl.pallas_call(
        functools.partial(gather_kernel, ctx_count, kinds),
        out_shape=[
            jax.ShapeDtypeStruct(shape, item.dtype)
            for shape, item in zip(shapes, shards + [rows, rows])
        ],
        in_specs=[anywhere] * (count + 1),
        out_specs=[pl.BlockSpec(memory_space=pltpu.VMEM)] + [anywhere] * (count + 1),
        scratch_shapes=buffers
        + [
            dma((count,)),
            dma((count, ctx_count, 2)),
            dma((count, ctx_count)),
            four,
            four,
            four,
            four,
        ]
        + sems,
        compiler_params=pltpu.CompilerParams(
            collective_id=0, has_side_effects=True, vmem_limit_bytes=BIG_VMEM
        ),
        cost_estimate=pl.CostEstimate(
            flops=2_000_000_000, bytes_accessed=800_000_000, transcendentals=0
        ),
    )(*shards, rows)
    return results[:count], results[count], results[count + 1]


def tiles(width, size=256):
    return width // size, width % size


def each_tile(width, act, size=256):
    whole, rest = tiles(width, size)

    @pl.loop(0, whole)
    def _(index):
        act(pl.ds(pl.multiple_of(index * size, size), size))

    if rest:
        act(pl.ds(whole * size, rest))


def expert_kernel(ctx_count, rows_ref, info_ref, gate_ref, up_ref, down_ref, grads_ref, *refs):
    all_ref, slots_ref, hidden_ref, gate_back_ref, up_back_ref, back_ref = refs[:6]
    blocks, chosen, arrived, gate, up, down, grads, hidden, gate_back, up_back, back = refs[6:17]
    weight_sem, grad_sem, slot_sem, side_sem, back_sem = refs[17:22]
    move = Dispatch(
        ctx_count, False, rows_ref, info_ref, all_ref, blocks, chosen, arrived, refs[22:]
    )
    slots, width = back.shape
    units = hidden.shape[1]
    order = [nearest(move.z, step) for step in range(ctx_count)]

    def block_at(step):
        block = order[0]
        for place in range(1, ctx_count):
            block = jnp.where(step == place, order[place], block)
        return block

    loads = [
        pltpu.make_async_copy(source, target, weight_sem.at[place])
        for place, (source, target) in enumerate(((gate_ref, gate), (up_ref, up), (down_ref, down)))
    ]

    def load_grads(step):
        slot = lax.rem(step, 2)
        return pltpu.make_async_copy(
            grads_ref.at[block_at(step)], grads.at[slot], grad_sem.at[slot]
        )

    def store_slots(block):
        return pltpu.make_async_copy(arrived.at[block], slots_ref.at[block], slot_sem.at[block])

    def store_sides(block):
        return [
            pltpu.make_async_copy(source, target.at[block], side_sem.at[place])
            for place, (source, target) in enumerate(
                ((hidden, hidden_ref), (gate_back, gate_back_ref), (up_back, up_back_ref))
            )
        ]

    def store_back(block):
        return pltpu.make_async_copy(back, back_ref.at[block], back_sem)

    greet(move.z, move.f, PEERS, ctx_count)
    move.begin()
    for load in loads:
        load.start()
    load_grads(0).start()
    move.pass_on(order[0], True)
    move.pass_on(order[1], False)
    for load in loads:
        load.wait()

    @pl.loop(0, ctx_count)
    def _(step):
        block = block_at(step)
        slot = lax.rem(step, 2)

        @pl.when(step + 1 < ctx_count)
        def _():
            load_grads(step + 1).start()

        load_grads(step).wait()
        move.await_slots(block)
        store_slots(block).start()

        @pl.when(step > 0)
        def _():
            for copy in store_sides(block):
                copy.wait()

        rows = arrived[block].reshape(slots, width)

        def hidden_tile(part):
            pre = jnp.dot(rows, gate[:, part], preferred_element_type=FULL)
            linear = jnp.dot(rows, up[:, part], preferred_element_type=FULL)
            grad = dot_last(grads[slot], down[part, :])
            sigma = jax.nn.sigmoid(pre)
            act = pre * sigma
            hidden[:, part] = (act * linear).astype(LOW)
            up_back[:, part] = (grad * act).astype(LOW)
            gate_back[:, part] = (
                grad * linear * (sigma * (1.0 + pre * (1.0 - sigma)))
            ).astype(LOW)

        each_tile(units, hidden_tile)
        for copy in store_sides(block):
            copy.start()

        @pl.when(step > 0)
        def _():
            store_back(block).wait()

        def back_tile(part):
            total = dot_last(gate_back[...], gate[part, :]) + dot_last(up_back[...], up[part, :])
            back[:, part] = total.astype(LOW)

        each_tile(width, back_tile)
        store_back(block).start()

        @pl.when(step + 2 < ctx_count)
        def _():
            move.pass_on(block_at(step + 2), False)

    for step in range(ctx_count):
        store_slots(order[step]).wait()
    for copy in store_sides(order[-1]):
        copy.wait()
    store_back(order[-1]).wait()
    move.finish()


def expert_rows(rows, info, gate, up, down, grads, ctx_count, fsdp_count):
    count, width = rows.shape
    slots = grads.shape[1]
    share = slots // fsdp_count
    units = gate.shape[1]
    buffers, sems = dispatch_scratch(ctx_count, fsdp_count, count, share, width)
    dma = pltpu.SemaphoreType.DMA
    anywhere = pl.BlockSpec(memory_space=pl.ANY)
    low = lambda *shape: jax.ShapeDtypeStruct((ctx_count,) + shape, LOW)
    vmem = lambda *shape: pltpu.VMEM(shape, LOW)
    return pl.pallas_call(
        functools.partial(expert_kernel, ctx_count),
        out_shape=(
            low(count, width),
            low(fsdp_count, share, width),
            low(slots, units),
            low(slots, units),
            low(slots, units),
            low(slots, width),
        ),
        in_specs=[anywhere, pl.BlockSpec(memory_space=pltpu.VMEM)] + [anywhere] * 4,
        out_specs=(anywhere,) * 6,
        scratch_shapes=buffers
        + [
            vmem(ctx_count, fsdp_count, share, width),
            vmem(width, units),
            vmem(width, units),
            vmem(units, width),
            vmem(2, slots, width),
            vmem(slots, units),
            vmem(slots, units),
            vmem(slots, units),
            vmem(slots, width),
            dma((3,)),
            dma((2,)),
            dma((ctx_count,)),
            dma((3,)),
            dma,
        ]
        + sems,
        compiler_params=pltpu.CompilerParams(
            collective_id=4, has_side_effects=True, vmem_limit_bytes=BIG_VMEM
        ),
        cost_estimate=pl.CostEstimate(
            flops=60_000_000_000, bytes_accessed=400_000_000, transcendentals=3_000_000
        ),
    )(rows, info, gate, up, down, grads)


class Combine:
    def __init__(
        self, ctx_count, gated, slots_ref, info_ref, extra_ref, out_ref, buffers, sems
    ):
        self.ctx_count, self.gated = ctx_count, gated
        self.slots_ref, self.info_ref = slots_ref, info_ref
        self.extra_ref, self.out_ref = extra_ref, out_ref
        self.arrived, self.extra, self.parts, self.from_z = buffers
        self.keep_sem, self.extra_sem, self.p_send, self.p_recv, self.z_send, self.z_recv = sems
        self.z, self.f = lax.axis_index("ctx"), lax.axis_index("fsdp")
        self.core = flip(self.f, 1)
        self.order = [nearest(self.z, ctx_count - 1 - step) for step in range(ctx_count)]

    def p_copy(self, block, place):
        to = toggled(self.f, PEERS[place])
        sems = (self.p_send.at[block, place], self.p_recv.at[block, place])
        return remote(
            self.slots_ref.at[block, to], self.arrived.at[block, self.f], *sems, self.z, to
        )

    def keep(self, block):
        source, target = self.slots_ref.at[block, self.f], self.arrived.at[block, self.f]
        return pltpu.make_async_copy(source, target, self.keep_sem.at[block])

    def load(self, step):
        return pltpu.make_async_copy(
            self.extra_ref.at[self.order[step]], self.extra, self.extra_sem
        )

    def place(self, way, block, z):
        return jnp.where(block == z, self.ctx_count, block) if way == 0 else block

    def send_along(self, step, way, to):
        block = self.order[step]
        sems = (self.z_send.at[step], self.z_recv.at[way, block])
        target = self.from_z.at[self.place(way, block, to)]
        return remote(self.parts.at[step], target, *sems, to, self.f)

    def z_arrived(self, block, way):
        at = self.from_z.at[self.place(way, block, self.z)]
        sems = (self.z_send.at[0], self.z_recv.at[way, block])
        remote(at, at, *sems, self.z, self.core).wait_recv()

    def start(self):
        for block in self.order:
            for place in range(len(PEERS)):
                self.p_copy(block, place).start()
            self.keep(block).start()
        self.load(0).start()

    def mix(self, block, target, *ways):
        slots = self.arrived.shape[1] * self.arrived.shape[2]
        choose = one_hot(self.info_ref[block], self.z, slots, self.gated)

        @pl.loop(0, target.shape[1], step=256)
        def _(start):
            part = pl.ds(pl.multiple_of(start, 256), 256)
            total = dot_first(choose, self.arrived[block, :, :, part].reshape(slots, 256))
            total = total + self.extra[:, part].astype(FULL)
            for way in ways:
                total = total + self.from_z[self.place(way, block, self.z), :, part].astype(FULL)
            target[:, part] = total.astype(target.dtype)

    def step(self, step):
        block, z, last = self.order[step], self.z, self.ctx_count - 1
        self.keep(block).wait()
        self.load(step).wait()
        for place in range(len(PEERS)):
            at = self.arrived.at[block, toggled(self.f, PEERS[place])]
            sems = (self.p_send.at[block, place], self.p_recv.at[block, place])
            remote(at, at, *sems, z, self.core).wait_recv()
        if step < last:
            target = self.parts.at[step]
            for way, above in ((1, True), (0, False)):
                heading = (block < z) if above else (block > z)
                has_more = (z < last) if above else (z > 0)

                @pl.when(heading & has_more)
                def _():
                    self.z_arrived(block, way)
                    self.mix(block, target, way)

                @pl.when(heading & jnp.logical_not(has_more))
                def _():
                    self.mix(block, target)

                @pl.when(heading)
                def _():
                    self.send_along(step, way, z - 1 if above else z + 1).start()

            self.load(step + 1).start()
            return

        @pl.when(z > 0)
        def _():
            self.z_arrived(block, 0)

        @pl.when(z < last)
        def _():
            self.z_arrived(block, 1)

        @pl.when(z == 0)
        def _():
            self.mix(block, self.out_ref, 1)

        @pl.when(z == last)
        def _():
            self.mix(block, self.out_ref, 0)

        @pl.when((z > 0) & (z < last))
        def _():
            self.mix(block, self.out_ref, 0, 1)

    def finish(self):
        for step in range(self.ctx_count):
            for place in range(len(PEERS)):
                self.p_copy(self.order[step], place).wait_send()
            if step < self.ctx_count - 1:
                self.send_along(step, 0, self.z).wait_send()


def combine_kernel(ctx_count, info_ref, *refs):
    streams = refs[0:4]
    rows_ref, grads_ref, hidden_ref, gate_back_ref, up_back_ref = refs[4:9]
    outs = refs[9:11]
    gate_grad_ref, up_grad_ref, down_grad_ref = refs[11:14]
    narrow, left, right, gate_tile, up_tile = refs[14:19]
    side_sem, tile_sem, store_sem = refs[19:22]
    buffers, sems = refs[22:30], refs[30:42]
    moves = [
        Combine(
            ctx_count,
            place == 1,
            streams[2 * place],
            info_ref,
            streams[2 * place + 1],
            outs[place],
            buffers[4 * place : 4 * place + 4],
            sems[6 * place : 6 * place + 6],
        )
        for place in range(2)
    ]
    greet(moves[0].z, moves[0].f, PEERS, ctx_count)
    tile_count = rows_ref.shape[1] // 256

    def sides(source, target, place):
        return pltpu.make_async_copy(source, target, side_sem.at[place])

    first_sides = [sides(gate_back_ref, left, 0), sides(up_back_ref, right, 1)]
    last_side = sides(hidden_ref, left, 2)

    def fetch(source, index):
        part = pl.ds(pl.multiple_of(index * 256, 256), 256)
        slot = lax.rem(index, 2)
        return pltpu.make_async_copy(source.at[:, part], narrow.at[slot], tile_sem.at[slot])

    def store(tile, target, place, index):
        part = pl.ds(pl.multiple_of(index * 256, 256), 256)
        return pltpu.make_async_copy(tile, target.at[part, :], store_sem.at[place])

    def products(source, begin, end, pairs):
        @pl.loop(begin, end)
        def _(index):
            @pl.when(index + 1 < tile_count)
            def _():
                fetch(source, index + 1).start()

            fetch(source, index).wait()
            turned = narrow[lax.rem(index, 2)]
            for place, (factor, tile, target) in enumerate(pairs):
                part = dot_first(turned, factor[...]).astype(LOW)

                @pl.when(index > 0)
                def _():
                    store(tile, target, place, index).wait()

                tile[...] = part
                store(tile, target, place, index).start()

    both = ((left, gate_tile, gate_grad_ref), (right, up_tile, up_grad_ref))
    alone = ((left, gate_tile, down_grad_ref),)
    half = tile_count // 2
    for copy in first_sides:
        copy.start()
    fetch(rows_ref, 0).start()
    for move in moves:
        move.start()
    for copy in first_sides:
        copy.wait()
    products(rows_ref, 0, half, both)
    moves[0].step(0)
    products(rows_ref, half, tile_count, both)
    for place, (factor, tile, target) in enumerate(both):
        store(tile, target, place, 0).wait()
    last_side.start()
    fetch(grads_ref, 0).start()
    moves[0].step(1)
    last_side.wait()
    products(grads_ref, 0, half, alone)
    moves[0].step(2)
    products(grads_ref, half, tile_count, alone)
    store(gate_tile, down_grad_ref, 0, 0).wait()
    for step in range(3, ctx_count):
        moves[0].step(step)
    for step in range(ctx_count):
        moves[1].step(step)
    for move in moves:
        move.finish()


def combine_rows(
    slots, extra, out_slots, out_extra, info, sides, ctx_count, fsdp_count
):
    share, width = slots.shape[2:]
    count = extra.shape[1]
    total, units = sides[2].shape
    dma = pltpu.SemaphoreType.DMA
    anywhere = pl.BlockSpec(memory_space=pl.ANY)
    resident = pl.BlockSpec(memory_space=pltpu.VMEM)
    vmem = lambda *shape: pltpu.VMEM(shape, LOW)
    buffers = [
        vmem(ctx_count, fsdp_count, share, width),
        vmem(count, width),
        vmem(ctx_count - 1, count, width),
        vmem(ctx_count + 1, count, width),
    ]
    sems = [
        dma((ctx_count,)),
        dma,
        dma((ctx_count, len(PEERS))),
        dma((ctx_count, len(PEERS))),
        dma((ctx_count - 1,)),
        dma((2, ctx_count)),
    ]
    return pl.pallas_call(
        functools.partial(combine_kernel, ctx_count),
        out_shape=(jax.ShapeDtypeStruct((count, width), FULL),) * 2
        + (jax.ShapeDtypeStruct((width, units), LOW),) * 3,
        in_specs=[resident] + [anywhere] * 9,
        out_specs=(resident,) * 2 + (anywhere,) * 3,
        scratch_shapes=[
            vmem(2, total, 256),
            vmem(total, units),
            vmem(total, units),
            vmem(256, units),
            vmem(256, units),
            dma((3,)),
            dma((2,)),
            dma((2,)),
        ]
        + buffers * 2
        + sems * 2,
        compiler_params=pltpu.CompilerParams(
            collective_id=3, has_side_effects=True, vmem_limit_bytes=BIG_VMEM
        ),
        cost_estimate=pl.CostEstimate(
            flops=40_000_000_000, bytes_accessed=600_000_000, transcendentals=0
        ),
    )(info, slots, extra, out_slots, out_extra, *sides)


def mm(subscripts, left, right):
    return jnp.einsum(subscripts, left, right, preferred_element_type=FULL)


def member_pairs(fsdp_count, members, step):
    return [
        (f, f // members * members + (f % members + step) % members) for f in range(fsdp_count)
    ]


def by_member(own, others, member, members):
    if members == 2:
        first = member == 0
        return jnp.stack([jnp.where(first, own, others[0]), jnp.where(first, others[0], own)])
    stack = jnp.stack([own] + others)
    return jnp.take(stack, (member - jnp.arange(members)) % members, axis=0)


def part_of(array, member, step, members):
    return lax.dynamic_index_in_dim(array, (member + step) % members, 0, keepdims=False)


def swap_parts(array, members, fsdp_count):
    member = lax.axis_index("fsdp") % members
    others = [
        lax.ppermute(
            part_of(array, member, step, members), "fsdp", member_pairs(fsdp_count, members, step)
        )
        for step in range(1, members)
    ]
    return by_member(part_of(array, member, 0, members), others, member, members)


def share_parts(array, members, fsdp_count):
    member = lax.axis_index("fsdp") % members
    others = [
        lax.ppermute(array, "fsdp", member_pairs(fsdp_count, members, step))
        for step in range(1, members)
    ]
    return by_member(array, others, member, members)


def sum_parts(array, members, fsdp_count):
    member = lax.axis_index("fsdp") % members
    total = part_of(array, member, 0, members).astype(FULL)
    for step in range(1, members):
        total = total + lax.ppermute(
            part_of(array, member, step, members), "fsdp", member_pairs(fsdp_count, members, step)
        ).astype(FULL)
    return total.astype(LOW)


def routing(info, z, slots, gated):
    at = jnp.arange(slots, dtype=jnp.int32).astype(FULL)[:, None, None]
    hit = (info[:, None, COLUMN_AT : COLUMN_AT + TOP].swapaxes(2, 3) == at.reshape(-1, 1, 1)) & (
        info[:, None, :TOP].swapaxes(2, 3) == z.astype(FULL)
    )
    values = info[:, None, GATE_AT : GATE_AT + TOP].swapaxes(2, 3) if gated else 1.0
    return jnp.sum(jnp.where(hit, values, 0.0), axis=3).astype(LOW)


def swap_slots(slots):
    return lax.all_to_all(slots, "fsdp", split_axis=1, concat_axis=1, tiled=True)


def send_rows(rows, info, slots, gated, ctx_count, fsdp_count):
    every = lax.all_gather(rows, "ctx", axis=0)
    choose = routing(info, lax.axis_index("ctx"), slots, gated)
    chosen = mm("bst,btd->bsd", choose, every).astype(LOW)
    return every, swap_slots(chosen.reshape(ctx_count, fsdp_count, -1, rows.shape[1]))


def run_expert(rows, info, gate, up, down, grads, ctx_count, fsdp_count):
    if (ctx_count, fsdp_count) == (4, 8):
        return expert_rows(rows, info, gate, up, down, grads, ctx_count, fsdp_count)
    every, arrived = send_rows(rows, info, grads.shape[1], False, ctx_count, fsdp_count)
    slots = arrived.reshape(grads.shape)
    pre = mm("bsd,df->bsf", slots, gate)
    linear = mm("bsd,df->bsf", slots, up)
    act, slope = silu_slope(pre)
    grad = mm("bsd,fd->bsf", grads, down)
    hidden = (act * linear).astype(LOW)
    up_back = (grad * act).astype(LOW)
    gate_back = (grad * linear * slope).astype(LOW)
    back = (mm("bsf,df->bsd", gate_back, gate) + mm("bsf,df->bsd", up_back, up)).astype(LOW)
    return every, arrived, hidden, gate_back, up_back, back


def return_slots(slots, info, extra, gated):
    back = swap_slots(slots).reshape(slots.shape[0], -1, slots.shape[3])
    choose = routing(info, lax.axis_index("ctx"), back.shape[1], gated)
    total = (mm("bst,bsd->btd", choose, back) + extra).astype(LOW)
    return lax.psum_scatter(total, "ctx", scatter_dimension=0, tiled=False).astype(FULL)


def return_both(slots, extra, out_slots, out_extra, info, sides, ctx_count, fsdp_count):
    extra, out_extra = extra.astype(LOW), out_extra.astype(LOW)
    if (ctx_count, fsdp_count) == (4, 8):
        return combine_rows(
            slots, extra, out_slots, out_extra, info, sides, ctx_count, fsdp_count
        )
    rows, grads, hidden, gate_back, up_back = sides
    return (
        return_slots(slots, info, extra, False),
        return_slots(out_slots, info, out_extra, True),
        mm("sd,sf->df", rows, gate_back).astype(LOW),
        mm("sd,sf->df", rows, up_back).astype(LOW),
        mm("sd,sf->df", grads, hidden).astype(LOW),
    )


def gather_all(items, rows, slots, ctx_count, fsdp_count):
    if (ctx_count, fsdp_count) == (4, 8):
        return gather_arrays(items, rows, slots, ctx_count, fsdp_count)
    results = []
    for kind, shard in items:
        if kind == "line":
            shard = lax.all_to_all(shard, "ctx", split_axis=0, concat_axis=0, tiled=True)
            result = lax.all_gather(shard, "fsdp", axis=1)
        elif kind == "plane":
            result = lax.all_gather(shard, "fsdp", axis=0)[None]
        elif kind == "column":
            result = lax.all_gather(shard, "ctx", axis=0)
        else:
            result = lax.all_gather(shard, ("ctx", "fsdp"), axis=0)
            result = result.reshape((ctx_count, fsdp_count) + shard.shape)
        results.append(result)
    return (results,) + send_rows(rows, results[0], slots, True, ctx_count, fsdp_count)


def scatter_all(items, ctx_count, fsdp_count):
    items = [(kind, grad.astype(LOW)) for kind, grad in items]
    if (ctx_count, fsdp_count) == (4, 8):
        return scatter_arrays(items, ctx_count, fsdp_count)
    results = []
    for kind, grad in items:
        if kind == "line":
            grad = grad.reshape(ctx_count, fsdp_count, -1, grad.shape[1]).swapaxes(0, 1)
            grad = lax.psum_scatter(grad, "fsdp", scatter_dimension=0, tiled=False)
            results.append(along_line(grad))
        else:
            total = lax.psum_scatter(grad, ("ctx", "fsdp"), scatter_dimension=0, tiled=True)
            results.append(total.astype(FULL))
    return results


def along_line(array):
    return lax.all_to_all(array, "ctx", split_axis=0, concat_axis=0, tiled=True)


def after(values, *others):
    tied = lax.optimization_barrier((tuple(values), others))
    return tied[0]


def local(
    tokens,
    routes,
    gate_values,
    cotangent,
    attention_gain,
    query_weight,
    latent_weight,
    latent_gain,
    expand_weight,
    output_weight,
    feedforward_gain,
    shared_gate,
    shared_up,
    shared_down,
    expert_gate,
    expert_up,
    expert_down,
):
    row_count = tokens.shape[1]
    model_width = tokens.shape[2]
    ctx_count = lax.axis_size("ctx")
    fsdp_count = lax.axis_size("fsdp")
    device_count = ctx_count * fsdp_count
    experts_total = EXP_DEV * fsdp_count
    capacity = row_count * TOP * 4 // (3 * experts_total)
    members = ctx_count // EXP_DEV
    plane_experts = experts_total // ctx_count
    plane_slots = plane_experts * capacity
    share = capacity // members
    sequence = ctx_count * row_count
    z = lax.axis_index("ctx")
    score_scale = (NOPE + ROPE) ** (-0.5)
    source = tokens[0].astype(FULL)
    cot_low = cotangent[0]
    cot_full = cot_low.astype(FULL)
    positions = stored_positions(
        z * row_count + jnp.arange(row_count, dtype=jnp.int32), row_count, 2 * ctx_count
    )
    dense_rows = latent_weight.shape[0]
    gain_rows = latent_gain.shape[0]
    rotary_end = LATENT + ROPE
    hidden_units = expert_gate.shape[2]
    shared_units = shared_gate.shape[1] // ctx_count

    def swapped(weight):
        weight = weight.reshape((EXP_DEV, members, weight.shape[1] // members) + weight.shape[2:])
        weight = swap_parts(weight.swapaxes(0, 1), members, fsdp_count)
        return weight.reshape((ctx_count,) + weight.shape[2:])

    gate_swapped, up_swapped, down_swapped = (
        swapped(expert_gate),
        swapped(expert_up),
        swapped(expert_down),
    )
    gate_moved = along_line(gate_swapped)

    local_routes = routes[0]
    expert_index = jnp.arange(experts_total, dtype=jnp.int32)
    member_of = (local_routes[..., None] == expert_index).astype(FULL)
    counts = jnp.sum(member_of, axis=1)
    before = jnp.cumsum(counts, axis=0) - counts
    within = jnp.sum(member_of * before[:, None, :], axis=-1).astype(jnp.int32)
    info = jnp.zeros((INFO_ROWS, row_count), FULL)
    info = info.at[:TOP].set((local_routes % ctx_count).astype(FULL).T)
    info = info.at[COLUMN_AT : COLUMN_AT + TOP].set(
        (local_routes // ctx_count * capacity + within).astype(FULL).T
    )
    info = info.at[GATE_AT : GATE_AT + TOP].set(gate_values[0].T)

    tail = jnp.concatenate(
        [
            latent_weight,
            attention_gain[:, None],
            feedforward_gain[:, None],
            jnp.pad(latent_gain, (0, dense_rows - gain_rows))[:, None],
            jnp.zeros((dense_rows, 256 - ROPE - 3), LOW),
        ],
        axis=1,
    )

    def by_line(weight):
        return weight.reshape(dense_rows, ctx_count, shared_units).swapaxes(0, 1)

    dense = (
        info,
        query_weight,
        tail,
        expand_weight,
        output_weight,
        by_line(shared_gate),
        by_line(shared_up),
        shared_down,
    )
    dense = after(dense, gate_swapped, up_swapped, down_swapped)
    kinds = ("column", "all", "all", "all", "all", "line", "line", "plane")
    gathered, all_cot, arrived_grad = gather_all(
        list(zip(kinds, dense)), cot_low, plane_slots, ctx_count, fsdp_count
    )
    all_info = gathered[0]
    full_query, full_tail, full_expand, full_output, full_sgate, full_sup, full_sdown = [
        item.reshape(-1, item.shape[-1]) for item in gathered[1:]
    ]
    full_latent = full_tail[:, :rotary_end]
    gain_one = full_tail[:, rotary_end].astype(FULL)
    gain_two = full_tail[:, rotary_end + 1].astype(FULL)
    gain_latent = (
        full_tail[:, rotary_end + 2].reshape(device_count, dense_rows)[:, :gain_rows]
    ).reshape(LATENT).astype(FULL)

    (up_swapped,) = after((up_swapped,), all_info)
    up_moved = along_line(up_swapped)
    all_cot = all_cot.reshape(sequence, model_width)
    arrived_grad = arrived_grad.reshape(ctx_count, plane_slots, model_width)

    plain_one, inverse_one = norm_forward(source)
    normed = (plain_one * gain_one).astype(LOW)
    (normed,) = after((normed,), gate_moved)
    (query_raw,) = after((jnp.dot(normed, full_query, preferred_element_type=FULL),))
    query_raw = query_raw.reshape(row_count, HEADS, NOPE + ROPE)
    query_nope = query_raw[:, :, :NOPE].astype(LOW)
    query_rope = rotary(query_raw[:, :, NOPE:], positions, 1.0).astype(LOW)
    latent_raw = jnp.dot(normed, full_latent, preferred_element_type=FULL)
    plain_latent, inverse_latent = norm_forward(latent_raw[:, :LATENT])
    latent_norm = (plain_latent * gain_latent).astype(LOW)
    key_rope = rotary(latent_raw[:, LATENT:], positions, 1.0).astype(LOW)
    half_rows = row_count // 2
    pad_rope = ((0, 0), (0, 128 - ROPE))
    keys = lax.all_gather(
        jnp.concatenate([latent_norm, jnp.pad(key_rope, pad_rope)], axis=1), "ctx", axis=0
    )
    keys = keys.reshape(ctx_count, 2, half_rows, LATENT + 128)
    keys = jnp.concatenate([keys[:, 0], keys[::-1, 1]]).reshape(sequence, LATENT + 128)
    all_latent, all_keys = (keys[:, :LATENT], keys[:, LATENT:])
    expand = full_expand.reshape(LATENT, HEADS, NOPE + VDIM)
    expand_key = expand[:, :, :NOPE]
    expand_value = expand[:, :, NOPE:]
    query_latent = mm("thd,chd->htc", query_nope, expand_key).astype(LOW)
    (down_swapped,) = after((down_swapped,), up_moved, query_latent)
    down_moved = along_line(down_swapped)
    query_turned = jnp.pad(query_rope.swapaxes(0, 1), ((0, 0),) + pad_rope)
    latent_out, log_total = attend(
        query_latent, query_turned, all_latent, all_keys, ctx_count, score_scale
    )
    values_out = (
        mm("htc,chv->thv", latent_out, expand_value).astype(LOW).reshape(row_count, HEADS * VDIM)
    )
    middle = source + jnp.dot(values_out, full_output, preferred_element_type=FULL)
    plain_two, inverse_two = norm_forward(middle)
    second = (plain_two * gain_two).astype(LOW)

    def whole(moved):
        return share_parts(moved, members, fsdp_count).swapaxes(0, 1)

    gate_all = whole(gate_moved).reshape(model_width, hidden_units)
    up_all = whole(up_moved).reshape(model_width, hidden_units)
    down_all = whole(down_moved).transpose(1, 2, 0, 3).reshape(hidden_units, model_width)
    (second_sent,) = after((second,), down_moved)
    all_second, arrived_rows, hidden_act, gate_back, up_back, arrived_back = run_expert(
        second_sent, all_info, gate_all, up_all, down_all, arrived_grad, ctx_count, fsdp_count
    )
    all_second = all_second.reshape(sequence, model_width)
    hidden_act, gate_back, up_back = [
        item.reshape(-1, hidden_units) for item in (hidden_act, gate_back, up_back)
    ]
    shared_g = jnp.dot(all_second, full_sgate, preferred_element_type=FULL)
    shared_u = jnp.dot(all_second, full_sup, preferred_element_type=FULL)
    shared_silu, shared_slope = silu_slope(shared_g)
    shared_hidden = (shared_silu * shared_u).astype(LOW)
    shared_hidden_grad = mm("td,fd->tf", all_cot, full_sdown)
    sup_back = (shared_hidden_grad * shared_silu).astype(LOW)
    sgate_back = (shared_hidden_grad * shared_u * shared_slope).astype(LOW)
    shared_second_grad = mm("tf,df->td", sgate_back, full_sgate) + mm(
        "tf,df->td", sup_back, full_sup
    )
    slots_shape = (ctx_count, fsdp_count, share, model_width)
    rows_shape = (ctx_count, row_count, model_width)
    shared_out = jnp.dot(shared_hidden, full_sdown, preferred_element_type=FULL)
    result = jnp.dot(hidden_act, down_all, preferred_element_type=FULL).astype(LOW)
    second_grad, out_sum, gate_grad, up_grad, down_grad = return_both(
        arrived_back.reshape(slots_shape),
        shared_second_grad.reshape(rows_shape),
        result.reshape(slots_shape),
        shared_out.reshape(rows_shape),
        all_info,
        (
            arrived_rows.reshape(-1, model_width),
            arrived_grad.reshape(-1, model_width),
            hidden_act,
            gate_back,
            up_back,
        ),
        ctx_count,
        fsdp_count,
    )
    layer_out = (middle + out_sum).astype(LOW)[None]

    def line_sum(grad):
        grad = grad.reshape(ctx_count, members, -1, hidden_units).swapaxes(0, 1)
        return sum_parts(grad, members, fsdp_count)

    gate_sum, up_sum, down_sum = (line_sum(gate_grad), line_sum(up_grad), line_sum(down_grad))
    gate_returned = along_line(gate_sum)
    sgate_back, sup_back = after((sgate_back, sup_back), gate_sum)
    shared_hidden, sgate_back, sup_back = after(
        (shared_hidden, sgate_back, sup_back), second_grad
    )
    sgate_grad = mm("td,tf->df", all_second, sgate_back).astype(LOW)
    sup_grad = mm("td,tf->df", all_second, sup_back).astype(LOW)
    sdown_grad = mm("tf,td->fd", shared_hidden, all_cot).astype(LOW)
    (second_grad,) = after(
        (second_grad,), gate_sum, up_sum, down_sum, sgate_grad, sup_grad, sdown_grad
    )
    sdown_grad = lax.psum_scatter(sdown_grad, "fsdp", scatter_dimension=0, tiled=True)

    middle_part, gain_two_grad = norm_backward(second_grad, plain_two, inverse_two, gain_two)
    middle_grad = cot_full + middle_part
    attended_grad = middle_grad.astype(LOW)
    output_weight_grad = mm("tv,td->vd", values_out, attended_grad)
    values_grad = (
        mm("td,vd->tv", attended_grad, full_output).astype(LOW).reshape(row_count, HEADS, VDIM)
    )
    latent_out_grad = mm("thv,chv->htc", values_grad, expand_value).astype(LOW)
    (latent_out_grad,) = after((latent_out_grad,), gate_returned)
    (up_sum,) = after((up_sum,), gate_returned, latent_out_grad)
    up_returned = along_line(up_sum)
    query_latent_grad, turned_grad, all_latent_grad, all_keys_grad = attend_back(
        query_latent,
        query_turned,
        all_latent,
        all_keys,
        latent_out,
        log_total,
        latent_out_grad,
        ctx_count,
        score_scale,
    )
    query_rope_grad = turned_grad[:, :, :ROPE].swapaxes(0, 1)
    keys_part = jnp.concatenate([all_latent_grad, all_keys_grad[:, :ROPE]], axis=1)
    keys_part = keys_part.reshape(2, ctx_count, half_rows, LATENT + ROPE)
    keys_part = jnp.stack([keys_part[0], keys_part[1, ::-1]], axis=1)
    keys_part = lax.psum_scatter(
        keys_part.reshape(sequence, LATENT + ROPE).astype(LOW),
        "ctx",
        scatter_dimension=0,
        tiled=True,
    ).astype(FULL)
    latent_grad, keys_grad = (keys_part[:, :LATENT], keys_part[:, LATENT:])
    expand_value_grad = mm("htc,thv->chv", latent_out, values_grad)

    sdown_grad = sdown_grad.astype(FULL)

    query_nope_grad = mm("htc,chd->thd", query_latent_grad, expand_key)
    expand_key_grad = mm("thd,htc->chd", query_nope, query_latent_grad)
    expand_grad = jnp.concatenate([expand_key_grad, expand_value_grad], axis=-1).reshape(
        LATENT, HEADS * (NOPE + VDIM)
    )
    query_grad = (
        jnp.concatenate([query_nope_grad, rotary(query_rope_grad, positions, -1.0)], axis=-1)
        .astype(LOW)
        .reshape(row_count, HEADS * (NOPE + ROPE))
    )
    latent_part_grad, gain_latent_grad = norm_backward(
        latent_grad, plain_latent, inverse_latent, gain_latent
    )
    latent_raw_grad = jnp.concatenate(
        [latent_part_grad, rotary(keys_grad, positions, -1.0)], axis=-1
    ).astype(LOW)
    query_weight_grad = mm("td,tq->dq", normed, query_grad)
    latent_weight_grad = mm("td,tq->dq", normed, latent_raw_grad)
    normed_grad = mm("tq,dq->td", query_grad, full_query) + mm(
        "tq,dq->td", latent_raw_grad, full_latent
    )
    source_part, gain_one_grad = norm_backward(normed_grad, plain_one, inverse_one, gain_one)
    tokens_grad = (middle_grad + source_part)[None]

    gain_latent_column = jnp.pad(
        gain_latent_grad.reshape(device_count, gain_rows), ((0, 0), (0, dense_rows - gain_rows))
    ).reshape(model_width)
    tail_grad = jnp.concatenate(
        [
            latent_weight_grad,
            gain_one_grad[:, None],
            gain_two_grad[:, None],
            gain_latent_column[:, None],
            jnp.zeros((model_width, 256 - ROPE - 3), FULL),
        ],
        axis=1,
    )
    (down_sum,) = after((down_sum,), up_returned, query_nope_grad)
    down_returned = along_line(down_sum)
    dense_grads = after(
        (query_weight_grad, tail_grad, expand_grad, output_weight_grad, sgate_grad, sup_grad),
        up_returned,
    )
    kinds = ("all",) * 4 + ("line",) * 2
    query_sum, tail_sum, expand_sum, output_sum, sgate_sum, sup_sum = scatter_all(
        list(zip(kinds, dense_grads)), ctx_count, fsdp_count
    )

    def joined(pieces):
        return pieces.swapaxes(0, 1).reshape(dense_rows, -1).astype(FULL)

    def owned(moved):
        moved = moved.reshape((members, EXP_DEV) + moved.shape[1:])
        moved = swap_parts(moved, members, fsdp_count).swapaxes(0, 1)
        return moved.reshape(EXP_DEV, -1, hidden_units).astype(FULL)

    expert_grads = (
        owned(gate_returned),
        owned(up_returned),
        owned(down_returned).swapaxes(1, 2),
    )
    return (
        layer_out,
        tokens_grad,
        tail_sum[:, rotary_end],
        query_sum,
        tail_sum[:, :rotary_end],
        tail_sum[:gain_rows, rotary_end + 2],
        expand_sum,
        output_sum,
        tail_sum[:, rotary_end + 1],
        joined(sgate_sum),
        joined(sup_sum),
        sdown_grad,
        expert_grads[0],
        expert_grads[1],
        expert_grads[2],
    )


def solution(mesh):
    in_specs = (
        P("fsdp", "ctx", None),
        P("fsdp", "ctx", None),
        P("fsdp", "ctx", None),
        P("fsdp", "ctx", None),
        P(("ctx", "fsdp")),
        P(("ctx", "fsdp"), None),
        P(("ctx", "fsdp"), None),
        P(("ctx", "fsdp")),
        P(("ctx", "fsdp"), None),
        P(("ctx", "fsdp"), None),
        P(("ctx", "fsdp")),
        P(("ctx", "fsdp"), None),
        P(("ctx", "fsdp"), None),
        P(("ctx", "fsdp"), None),
        P("fsdp", "ctx", None),
        P("fsdp", "ctx", None),
        P("fsdp", None, "ctx"),
    )
    out_specs = (
        P("fsdp", "ctx", None),
        P("fsdp", "ctx", None),
        P(("ctx", "fsdp")),
        P(("ctx", "fsdp"), None),
        P(("ctx", "fsdp"), None),
        P(("ctx", "fsdp")),
        P(("ctx", "fsdp"), None),
        P(("ctx", "fsdp"), None),
        P(("ctx", "fsdp")),
        P(("ctx", "fsdp"), None),
        P(("ctx", "fsdp"), None),
        P(("ctx", "fsdp"), None),
        P("fsdp", "ctx", None),
        P("fsdp", "ctx", None),
        P("fsdp", None, "ctx"),
    )
    return jax.shard_map(local, mesh=mesh, in_specs=in_specs, out_specs=out_specs, check_vma=False)
```

```python
import functools

import jax
import jax.numpy as jnp
from jax import lax
from jax.experimental import pallas as pl
from jax.experimental.pallas import tpu as pltpu
from jax.sharding import PartitionSpec as P

HEADS = 16
NOPE = 128
ROPE = 64
LATENT = 512
VDIM = 128
TOP = 6
EXP_DEV = 2


epsilon = 1e-06
rope_base = 10000.0
masked_score = -1e30


def stored_positions(row_index, per_device, block_count):
    device = row_index // per_device
    within = row_index % per_device
    half_block = per_device // 2
    return jnp.where(
        within >= half_block,
        (block_count - 1 - device) * half_block + within - half_block,
        device * half_block + within,
    )


def rotary(values, positions, direction):
    half_rope = values.shape[-1] // 2
    frequency = rope_base ** (-jnp.arange(half_rope, dtype=jnp.float32) / half_rope)
    angles = positions.astype(jnp.float32)[:, None] * frequency[None, :]
    cosine_table = jnp.cos(angles)
    sine_table = direction * jnp.sin(angles)
    if values.ndim == 3:
        cosine_table = cosine_table[:, None, :]
        sine_table = sine_table[:, None, :]
    front_half = values[..., :half_rope]
    back_half = values[..., half_rope:]
    return jnp.concatenate(
        [
            front_half * cosine_table - back_half * sine_table,
            back_half * cosine_table + front_half * sine_table,
        ],
        axis=-1,
    )


def norm_forward(values):
    inverse = lax.rsqrt(jnp.mean(values * values, axis=-1, keepdims=True) + epsilon)
    return (values * inverse, inverse)


def norm_backward(normed_grad, plain, inverse, gain):
    gain_grad = jnp.sum(normed_grad * plain, axis=0)
    scaled = normed_grad * gain
    return (
        inverse * (scaled - plain * jnp.mean(scaled * plain, axis=-1, keepdims=True)),
        gain_grad,
    )


def silu_slope(values):
    sigma = jax.nn.sigmoid(values)
    return (values * sigma, sigma * (1.0 + values * (1.0 - sigma)))


LOW = jnp.bfloat16
FULL = jnp.float32


MESH_ID = pl.DeviceIdType.MESH
BIG_VMEM = 60 * 1024 * 1024


def flip(index, bit):
    return index + bit - 2 * bit * lax.rem(lax.div(index, bit), 2)


def toggled(index, mask):
    for bit in (1, 2, 4):
        if mask & bit:
            index = flip(index, bit)
    return index


def nearest(z, step):
    upper = lax.div(z, 2)
    if step == 0:
        return z
    if step == 1:
        return z + 1 - 2 * upper
    if step == 2:
        return 2 - 2 * lax.rem(z, 2) + upper
    return 3 - 3 * upper


def outermost(z, ctx_count):
    return (z == 0) | (z == ctx_count - 1)


def along_order(z, ctx_count, step, take):
    ends = outermost(z, ctx_count)
    if step <= 1:
        take(step)
    if step == 1:

        @pl.when(jnp.logical_not(ends))
        def _():
            take(2)

    if step >= 2:

        @pl.when(ends)
        def _():
            take(step)

        if step + 1 < ctx_count:

            @pl.when(jnp.logical_not(ends))
            def _():
                take(step + 1)


def remote(source, target, send, receive, z, f):
    return pltpu.make_async_remote_copy(
        src_ref=source,
        dst_ref=target,
        send_sem=send,
        recv_sem=receive,
        device_id={"ctx": z, "fsdp": f},
        device_id_type=MESH_ID,
    )


def greet(z, f, masks, ctx_count, whole_line=False):
    barrier = pltpu.get_barrier_semaphore()

    def hello(to_z, to_f):
        pl.semaphore_signal(
            barrier, inc=1, device_id={"ctx": to_z, "fsdp": to_f}, device_id_type=MESH_ID
        )

    for mask in masks:
        hello(z, toggled(f, mask))
    if whole_line:
        for step in range(1, ctx_count):
            hello(lax.rem(z + step, ctx_count), f)
        pl.semaphore_wait(barrier, len(masks) + ctx_count - 1)
        return

    @pl.when(z > 0)
    def _():
        hello(z - 1, f)

    @pl.when(z < ctx_count - 1)
    def _():
        hello(z + 1, f)

    along = lax.div(z + ctx_count - 1, ctx_count) + lax.div(2 * ctx_count - 2 - z, ctx_count)
    pl.semaphore_wait(barrier, len(masks) + along)


def both_ways(z, block, ctx_count, act):
    @pl.when((block <= z) & (z < ctx_count - 1))
    def _():
        act(0, z + 1)

    @pl.when((block >= z) & (z > 0))
    def _():
        act(1, z - 1)


def halves(rows, width):
    if rows % 32 == 0:
        return tuple((pl.ds(start, rows // 2), slice(None)) for start in (0, rows // 2))
    return tuple((slice(None), pl.ds(start, width // 2)) for start in (0, width // 2))


def add_rows(target, rows, *terms):
    @pl.loop(0, rows, step=16)
    def _(start):
        part = pl.ds(pl.multiple_of(start, 16), 16)
        total = terms[0][part, :].astype(FULL)
        for term in terms[1:]:
            total = total + term[part, :].astype(FULL)
        target[part, :] = total.astype(target.dtype)


def scatter_kernel(ctx_count, kinds, *refs):
    count = len(kinds)
    grads, outs = refs[:count], refs[count : 2 * count]
    banks = [refs[(2 + kind) * count : (3 + kind) * count] for kind in range(7)]
    load_sem, c_send, c_recv, p_send, p_recv, z_send, z_recv = refs[9 * count :]
    z, f = lax.axis_index("ctx"), lax.axis_index("fsdp")
    side = lax.rem(f, 2)
    chip = lax.div(f, 2)
    core, x_near, y_near = flip(f, 1), flip(f, 2), flip(f, 4)
    x_chip, y_chip = flip(chip, 1), flip(chip, 2)
    far_chip = flip(x_chip, 2)
    greet(z, f, (1, 2, 4), ctx_count, True)
    order = [nearest(z, ctx_count - 1 - step) for step in range(ctx_count)]

    def work(item):
        grad_ref, out_ref = grads[item], outs[item]
        mine, from_core, from_x, from_y, half_x, half_y, from_z = [bank[item] for bank in banks]
        rows, width = out_ref.shape[-2:]
        left, right = halves(rows, width)
        half_rows = half_x.shape[1]

        def load(block):
            return pltpu.make_async_copy(
                grad_ref.at[block, :, side], mine.at[block], load_sem.at[item, block]
            )

        def c_copy(block):
            return remote(
                grad_ref.at[block, :, 1 - side],
                from_core.at[block],
                c_send.at[item, block],
                c_recv.at[item, block],
                z,
                core,
            )

        def p_copy(block, which):
            source, target, to = (
                (mine.at[(block, far_chip) + left], half_y.at[block], y_near),
                (mine.at[(block, far_chip) + right], half_x.at[block], x_near),
                (mine.at[block, x_chip], from_x.at[block], x_near),
                (mine.at[block, y_chip], from_y.at[block], y_near),
            )[which]
            sems = (p_send.at[item, block, which], p_recv.at[item, block, which])
            return remote(source, target, *sems, z, to)

        def z_copy(block, way, target):
            return remote(
                mine.at[block, chip],
                from_z.at[way, block],
                z_send.at[item, block],
                z_recv.at[item, way, block],
                target,
                f,
            )

        def z_arrived(block, way):
            at = from_z.at[way, block]
            sems = (z_send.at[item, block], z_recv.at[item, way, block])
            remote(at, at, *sems, z, core).wait_recv()

        def piece(block):
            sems = (z_send.at[item, block], z_recv.at[item, 0, z])
            return remote(mine.at[block, chip], out_ref.at[z], *sems, block, f)

        def start(step):
            c_copy(order[step]).start()
            load(order[step]).start()

        def first(step):
            block = order[step]
            load(block).wait()
            c_copy(block).wait_recv()
            far_part = mine.at[block, far_chip]
            add_rows(far_part, rows, far_part, from_core.at[block, far_chip])
            p_copy(block, 0).start()
            p_copy(block, 1).start()

        def second(step):
            block = order[step]
            x_part, y_part = mine.at[block, x_chip], mine.at[block, y_chip]
            add_rows(x_part, rows, x_part, from_core.at[block, x_chip])
            add_rows(y_part, rows, y_part, from_core.at[block, y_chip])
            p_copy(block, 0).wait_recv()
            x_left = mine.at[(block, x_chip) + left]
            add_rows(x_left, half_rows, x_left, half_y.at[block])
            p_copy(block, 2).start()
            p_copy(block, 1).wait_recv()
            y_right = mine.at[(block, y_chip) + right]
            add_rows(y_right, half_rows, y_right, half_x.at[block])
            p_copy(block, 3).start()

        def third(step):
            block = order[step]
            p_copy(block, 2).wait_recv()
            p_copy(block, 3).wait_recv()
            own = mine.at[block, chip]
            terms = (own, from_core.at[block, chip], from_x.at[block], from_y.at[block])
            if kinds[item] == "line":
                add_rows(out_ref.at[z] if step == ctx_count - 1 else own, rows, *terms)
                if step < ctx_count - 1:
                    piece(block).start()
                return

            if step == ctx_count - 1:

                @pl.when(z > 0)
                def _():
                    z_arrived(block, 0)

                @pl.when(z < ctx_count - 1)
                def _():
                    z_arrived(block, 1)

                @pl.when(z == 0)
                def _():
                    add_rows(out_ref, rows, *terms, from_z.at[1, block])

                @pl.when(z == ctx_count - 1)
                def _():
                    add_rows(out_ref, rows, *terms, from_z.at[0, block])

                @pl.when((z > 0) & (z < ctx_count - 1))
                def _():
                    add_rows(out_ref, rows, *terms, from_z.at[0, block], from_z.at[1, block])

                return

            for way, above in ((1, True), (0, False)):
                heading = (block < z) if above else (block > z)
                has_more = (z < ctx_count - 1) if above else (z > 0)

                @pl.when(heading & has_more)
                def _():
                    z_arrived(block, way)
                    add_rows(own, rows, *terms, from_z.at[way, block])

                @pl.when(heading & jnp.logical_not(has_more))
                def _():
                    add_rows(own, rows, *terms)

                @pl.when(heading)
                def _():
                    z_copy(block, way, z - 1 if above else z + 1).start()

        def finish(step):
            block = order[step]
            c_copy(block).wait_send()
            for which in range(4):
                p_copy(block, which).wait_send()
            if step == ctx_count - 1:
                return
            if kinds[item] == "line":
                piece(block).wait_send()
                at = out_ref.at[block]
                sems = (z_send.at[item, block], z_recv.at[item, 0, block])
                remote(at, at, *sems, z, core).wait_recv()
            else:
                z_copy(block, 0, z).wait_send()

        return start, first, second, third, finish

    stages = list(zip(*[work(item) for item in range(count)]))
    for step in range(ctx_count):
        for act in stages[0]:
            act(step)
    for step in range(ctx_count + 2):
        for lag in (0, 1, 2):
            if 0 <= step - lag < ctx_count:
                for act in stages[1 + lag]:
                    act(step - lag)
    for step in range(ctx_count):
        for act in stages[4]:
            act(step)


def scatter_arrays(items, ctx_count, fsdp_count):
    kinds = tuple(kind for kind, grad in items)
    grads = [grad for kind, grad in items]
    count = len(grads)
    chips = fsdp_count // 2
    shapes = [
        (grad.shape[0] // (ctx_count * fsdp_count), grad.shape[1]) for grad in grads
    ]
    half_shapes = [
        (rows // 2, width) if rows % 32 == 0 else (rows, width // 2) for rows, width in shapes
    ]
    dma = pltpu.SemaphoreType.DMA
    leads = [(ctx_count, chips), (ctx_count, chips), (ctx_count,), (ctx_count,)]
    banks = [pltpu.VMEM(lead + shape, LOW) for lead in leads for shape in shapes]
    banks += [pltpu.VMEM((ctx_count,) + shape, LOW) for _ in range(2) for shape in half_shapes]
    banks += [
        pltpu.VMEM((2, ctx_count) + shape if kind == "all" else (1, 1, 16, 128), LOW)
        for kind, shape in zip(kinds, shapes)
    ]
    return pl.pallas_call(
        functools.partial(scatter_kernel, ctx_count, kinds),
        out_shape=[
            jax.ShapeDtypeStruct(shape, FULL)
            if kind == "all"
            else jax.ShapeDtypeStruct((ctx_count,) + shape, LOW)
            for kind, shape in zip(kinds, shapes)
        ],
        in_specs=[pl.BlockSpec(memory_space=pl.ANY)] * count,
        out_specs=[pl.BlockSpec(memory_space=pltpu.VMEM)] * count,
        scratch_shapes=banks
        + [
            dma((count, ctx_count)),
            dma((count, ctx_count)),
            dma((count, ctx_count)),
            dma((count, ctx_count, 4)),
            dma((count, ctx_count, 4)),
            dma((count, ctx_count)),
            dma((count, 2, ctx_count)),
        ],
        compiler_params=pltpu.CompilerParams(
            collective_id=1, has_side_effects=True, vmem_limit_bytes=BIG_VMEM
        ),
        cost_estimate=pl.CostEstimate(flops=0, bytes_accessed=500_000_000, transcendentals=0),
    )(
        *[
            grad.reshape((ctx_count, chips, 2) + shape)
            for grad, shape in zip(grads, shapes)
        ]
    )


HEAD_GROUP = 4
KEYS = 256


def dot_last(left, right):
    return lax.dot_general(left, right, (((1,), (1,)), ((), ())), preferred_element_type=FULL)


def dot_first(left, right):
    return lax.dot_general(left, right, (((0,), (0,)), ((), ())), preferred_element_type=FULL)


def reach(half, rows, ctx_count):
    ctx = lax.axis_index("ctx")
    first = jnp.where(half == 0, ctx, 2 * ctx_count - 1 - ctx) * rows
    return first, lax.div(first + rows + KEYS - 1, KEYS)


def block_scores(query, turned, keys_ref, rope_ref, index, first, rows, scale):
    part = pl.ds(pl.multiple_of(index * KEYS, KEYS), KEYS)
    keys, rope = keys_ref[part, :], rope_ref[part, :]
    scores = (dot_last(query, keys) + dot_last(turned, rope)) * scale
    shape = scores.shape
    at = first + lax.rem(lax.broadcasted_iota(jnp.int32, shape, 0), rows)
    key_at = index * KEYS + lax.broadcasted_iota(jnp.int32, shape, 1)
    return part, keys, rope, scores, at >= key_at


def attend_kernel(
    ctx_count, scale, query_ref, turned_ref, keys_ref, rope_ref, out_ref, log_ref, total, top, norm
):
    heads, rows, width = query_ref.shape
    first, blocks = reach(pl.program_id(0), rows, ctx_count)
    query = query_ref[...].reshape(heads * rows, width)
    turned = turned_ref[...].reshape(heads * rows, -1)
    total[...] = jnp.zeros_like(total)
    norm[...] = jnp.zeros_like(norm)
    top[...] = jnp.full_like(top, masked_score)

    @pl.loop(0, blocks)
    def _(index):
        part, keys, rope, scores, seen = block_scores(
            query, turned, keys_ref, rope_ref, index, first, rows, scale
        )
        scores = jnp.where(seen, scores, masked_score)
        old = top[...]
        new = jnp.maximum(old, jnp.max(scores, axis=1, keepdims=True))
        weights = jnp.exp(scores - new)
        shrink = jnp.exp(old - new)
        top[...] = new
        norm[...] = norm[...] * shrink + jnp.sum(weights, axis=1, keepdims=True)
        total[...] = total[...] * shrink + jnp.dot(
            weights.astype(LOW), keys, preferred_element_type=FULL
        )

    out_ref[...] = (total[...] / norm[...]).astype(LOW).reshape(out_ref.shape)
    log_ref[...] = (top[...] + jnp.log(norm[...])).reshape(log_ref.shape)


def attend_back_kernel(
    ctx_count,
    scale,
    query_ref,
    turned_ref,
    keys_ref,
    rope_ref,
    out_ref,
    log_ref,
    grad_ref,
    query_grad_ref,
    turned_grad_ref,
    keys_grad_ref,
    rope_grad_ref,
    query_total,
    turned_total,
):
    heads, rows, width = query_ref.shape
    first, blocks = reach(pl.program_id(0), rows, ctx_count)
    query = query_ref[...].reshape(heads * rows, width)
    turned = turned_ref[...].reshape(heads * rows, -1)
    grad = grad_ref[...].reshape(heads * rows, width)
    out = out_ref[...].reshape(heads * rows, width)
    logs = log_ref[...].reshape(heads * rows, 1)
    inner = jnp.sum(grad.astype(FULL) * out.astype(FULL), axis=1, keepdims=True)
    query_total[...] = jnp.zeros_like(query_total)
    turned_total[...] = jnp.zeros_like(turned_total)

    @pl.when((pl.program_id(0) == 0) & (pl.program_id(1) == 0))
    def _():
        keys_grad_ref[...] = jnp.zeros_like(keys_grad_ref)
        rope_grad_ref[...] = jnp.zeros_like(rope_grad_ref)

    @pl.loop(0, blocks)
    def _(index):
        part, keys, rope, scores, seen = block_scores(
            query, turned, keys_ref, rope_ref, index, first, rows, scale
        )
        weights = jnp.where(seen, jnp.exp(scores - logs), 0.0)
        change = (weights * (dot_last(grad, keys) - inner) * scale).astype(LOW)
        query_total[...] += jnp.dot(change, keys, preferred_element_type=FULL)
        turned_total[...] += jnp.dot(change, rope, preferred_element_type=FULL)
        keys_grad_ref[part, :] += dot_first(change, query) + dot_first(weights.astype(LOW), grad)
        rope_grad_ref[part, :] += dot_first(change, turned)

    query_grad_ref[...] = query_total[...].astype(LOW).reshape(query_grad_ref.shape)
    turned_grad_ref[...] = turned_total[...].reshape(turned_grad_ref.shape)


def attend_specs(heads, group, rows, widths):
    return [pl.BlockSpec((group, rows, width), lambda half, g: (g, half, 0)) for width in widths]


def whole_spec(array):
    return pl.BlockSpec(array.shape, lambda half, g: (0, 0))


def attend(query, turned, keys, rope, ctx_count, scale):
    heads, count, width = query.shape
    group, rows = HEAD_GROUP, count // 2
    lanes = turned.shape[2]
    return pl.pallas_call(
        functools.partial(attend_kernel, ctx_count, scale),
        grid=(2, heads // group),
        out_shape=(
            jax.ShapeDtypeStruct((heads, count, width), LOW),
            jax.ShapeDtypeStruct((heads, count, 1), FULL),
        ),
        in_specs=attend_specs(heads, group, rows, (width, lanes))
        + [whole_spec(keys), whole_spec(rope)],
        out_specs=tuple(attend_specs(heads, group, rows, (width, 1))),
        scratch_shapes=[
            pltpu.VMEM((group * rows, width), FULL),
            pltpu.VMEM((group * rows, 1), FULL),
            pltpu.VMEM((group * rows, 1), FULL),
        ],
        compiler_params=pltpu.CompilerParams(vmem_limit_bytes=BIG_VMEM),
        cost_estimate=pl.CostEstimate(
            flops=12_000_000_000, bytes_accessed=12_000_000, transcendentals=3_000_000
        ),
    )(query, turned, keys, rope)


def attend_back(query, turned, keys, rope, out, logs, grad, ctx_count, scale):
    heads, count, width = query.shape
    group, rows = HEAD_GROUP, count // 2
    lanes = turned.shape[2]
    return pl.pallas_call(
        functools.partial(attend_back_kernel, ctx_count, scale),
        grid=(2, heads // group),
        out_shape=(
            jax.ShapeDtypeStruct((heads, count, width), LOW),
            jax.ShapeDtypeStruct((heads, count, lanes), FULL),
            jax.ShapeDtypeStruct(keys.shape, FULL),
            jax.ShapeDtypeStruct(rope.shape, FULL),
        ),
        in_specs=attend_specs(heads, group, rows, (width, lanes))
        + [whole_spec(keys), whole_spec(rope)]
        + attend_specs(heads, group, rows, (width, 1, width)),
        out_specs=tuple(
            attend_specs(heads, group, rows, (width, lanes)) + [whole_spec(keys), whole_spec(rope)]
        ),
        scratch_shapes=[
            pltpu.VMEM((group * rows, width), FULL),
            pltpu.VMEM((group * rows, lanes), FULL),
        ],
        compiler_params=pltpu.CompilerParams(vmem_limit_bytes=BIG_VMEM),
        cost_estimate=pl.CostEstimate(
            flops=30_000_000_000, bytes_accessed=30_000_000, transcendentals=3_000_000
        ),
    )(query, turned, keys, rope, out, logs, grad)


PEERS = (6, 7, 2, 4, 3, 5, 1)
COLUMN_AT, GATE_AT, INFO_ROWS = 8, 16, 24


def one_hot(info, z, slots, gated):
    count = info.shape[1]
    at = lax.broadcasted_iota(jnp.int32, (slots, count), 0).astype(FULL)
    plane = z.astype(FULL)
    total = jnp.zeros((slots, count), FULL)
    for route in range(TOP):
        hit = (info[COLUMN_AT + route][None, :] == at) & (info[route][None, :] == plane)
        value = info[GATE_AT + route][None, :] if gated else 1.0
        total = total + jnp.where(hit, value, 0.0)
    return total.astype(LOW)


class Dispatch:
    def __init__(self, ctx_count, gated, rows_ref, info_ref, all_ref, blocks, chosen, arrived, sems):
        self.own_sem, self.all_sem, self.keep_sem = sems[:3]
        self.z_send, self.z_recv, self.p_send, self.p_recv = sems[3:]
        self.ctx_count, self.gated = ctx_count, gated
        self.rows_ref, self.info_ref, self.all_ref = rows_ref, info_ref, all_ref
        self.blocks, self.chosen, self.arrived = blocks, chosen, arrived
        self.z, self.f = lax.axis_index("ctx"), lax.axis_index("fsdp")
        self.core = flip(self.f, 1)

    def z_copy(self, block, way, target):
        at = self.blocks.at[block]
        sems = (self.z_send.at[block, way], self.z_recv.at[block])
        return remote(at, at, *sems, target, self.f)

    def p_copy(self, block, place):
        to = toggled(self.f, PEERS[place])
        sems = (self.p_send.at[block, place], self.p_recv.at[block, place])
        return remote(
            self.chosen.at[block, to], self.arrived.at[block, self.f], *sems, self.z, to
        )

    def keep(self, block):
        source, target = self.chosen.at[block, self.f], self.arrived.at[block, self.f]
        return pltpu.make_async_copy(source, target, self.keep_sem.at[block])

    def store(self, block):
        source, target = self.blocks.at[block], self.all_ref.at[block]
        return pltpu.make_async_copy(source, target, self.all_sem.at[block])

    def begin(self):
        own = pltpu.make_async_copy(self.rows_ref, self.blocks.at[self.z], self.own_sem)
        own.start()
        own.wait()

    def take(self, step):
        block = nearest(self.z, step)
        if step > 0:
            at = self.blocks.at[block]
            sems = (self.z_send.at[block, 0], self.z_recv.at[block])
            remote(at, at, *sems, self.z, self.core).wait_recv()
        both_ways(
            self.z, block, self.ctx_count, lambda way, to: self.z_copy(block, way, to).start()
        )
        self.store(block).start()

    def choose(self, block):
        groups, share, width = self.chosen.shape[1:]
        choose = one_hot(self.info_ref[block], self.z, groups * share, self.gated)

        @pl.loop(0, width, step=256)
        def _(start):
            part = pl.ds(pl.multiple_of(start, 256), 256)
            tile = jnp.dot(choose, self.blocks[block, :, part], preferred_element_type=FULL)
            self.chosen[block, :, :, part] = tile.astype(LOW).reshape(groups, share, 256)

        for place in range(len(PEERS)):
            self.p_copy(block, place).start()
        self.keep(block).start()

    def await_slots(self, block):
        self.keep(block).wait()
        for place in range(len(PEERS)):
            at = self.arrived.at[block, toggled(self.f, PEERS[place])]
            sems = (self.p_send.at[block, place], self.p_recv.at[block, place])
            remote(at, at, *sems, self.z, self.core).wait_recv()

    def finish(self):
        for step in range(self.ctx_count):
            block = nearest(self.z, step)
            self.store(block).wait()
            both_ways(
                self.z,
                block,
                self.ctx_count,
                lambda way, to: self.z_copy(block, way, to).wait_send(),
            )
            for place in range(len(PEERS)):
                self.p_copy(block, place).wait_send()


def dispatch_scratch(ctx_count, fsdp_count, count, share, width):
    dma = pltpu.SemaphoreType.DMA
    return [
        pltpu.VMEM((ctx_count, count, width), LOW),
        pltpu.VMEM((ctx_count, fsdp_count, share, width), LOW),
    ], [
        dma,
        dma((ctx_count,)),
        dma((ctx_count,)),
        dma((ctx_count, 2)),
        dma((ctx_count,)),
        dma((ctx_count, len(PEERS))),
        dma((ctx_count, len(PEERS))),
    ]


def gather_kernel(ctx_count, kinds, *refs):
    count = len(kinds)
    shards, rows_ref = refs[:count], refs[count]
    outs, all_ref, slots_ref = refs[count + 1 : 2 * count + 1], refs[2 * count + 1], refs[2 * count + 2]
    blocks, chosen = refs[2 * count + 3 : 2 * count + 5]
    own_sem, z_send, z_recv, p_send, p_recv, c_send, c_recv = refs[2 * count + 5 : 2 * count + 12]
    z, f = lax.axis_index("ctx"), lax.axis_index("fsdp")
    core, x_near, y_near = flip(f, 1), flip(f, 2), flip(f, 4)
    far = flip(x_near, 4)
    move = Dispatch(
        ctx_count, True, rows_ref, outs[0], all_ref, blocks, chosen, slots_ref, refs[2 * count + 12 :]
    )
    greet(z, f, PEERS, ctx_count, True)

    def slot(item, step):
        return 0 if kinds[item] == "plane" else nearest(z, step)

    def steps(item, step):
        return step == 0 if kinds[item] == "plane" else 0 <= step < ctx_count

    def z_view(item, block):
        return outs[item].at[block] if kinds[item] == "column" else outs[item].at[block, f]

    def own(item):
        source = shards[item].at[z] if kinds[item] == "line" else shards[item]
        return pltpu.make_async_copy(source, z_view(item, slot(item, 0)), own_sem.at[item])

    def z_copy(item, block, way, target):
        at = z_view(item, block)
        return remote(at, at, z_send.at[item, block, way], z_recv.at[item, block], target, f)

    def piece(item, step):
        target = lax.rem(z + step, ctx_count)
        return remote(
            shards[item].at[target],
            outs[item].at[z, f],
            z_send.at[item, target, 0],
            z_recv.at[item, z],
            target,
            f,
        )

    def part(item, block, at, which):
        rows, columns = halves(*outs[item].shape[2:])[which]
        return outs[item].at[block, at, rows, columns]

    def p_copy(item, block, which):
        at = (
            lambda: outs[item].at[block, f],
            lambda: outs[item].at[block, f],
            lambda: part(item, block, x_near, 0),
            lambda: part(item, block, y_near, 1),
        )[which]()
        to = (x_near, y_near, y_near, x_near)[which]
        sems = (p_send.at[item, block, which], p_recv.at[item, block, which])
        return remote(at, at, *sems, z, to)

    def p_arrived(item, block, which):
        at = (
            lambda: outs[item].at[block, x_near],
            lambda: outs[item].at[block, y_near],
            lambda: part(item, block, far, 0),
            lambda: part(item, block, far, 1),
        )[which]()
        sems = (p_send.at[item, block, which], p_recv.at[item, block, which])
        remote(at, at, *sems, z, x_near).wait_recv()

    def c_copy(item, block, which):
        at = outs[item].at[block, (f, x_near, y_near, far)[which]]
        sems = (c_send.at[item, block, which], c_recv.at[item, block, which])
        return remote(at, at, *sems, z, core)

    def c_arrived(item, block, which):
        at = outs[item].at[block, flip((f, x_near, y_near, far)[which], 1)]
        sems = (c_send.at[item, block, which], c_recv.at[item, block, which])
        remote(at, at, *sems, z, core).wait_recv()

    def take(step):
        for item in range(count):
            if not steps(item, step):
                continue
            block = slot(item, step)
            if step == 0:
                own(item).wait()
            else:
                at = z_view(item, block)
                sems = (z_send.at[item, block, 0], z_recv.at[item, block])
                remote(at, at, *sems, z, core).wait_recv()
            if kinds[item] in ("all", "column"):
                both_ways(
                    z, block, ctx_count, lambda way, to: z_copy(item, block, way, to).start()
                )
        move.take(step)

    def first(item, step):
        block = slot(item, step)
        p_copy(item, block, 0).start()
        p_copy(item, block, 1).start()
        c_copy(item, block, 0).start()

    def second(item, step):
        block = slot(item, step)
        for which in (0, 1):
            p_arrived(item, block, which)
            p_copy(item, block, which + 2).start()
            c_copy(item, block, which + 1).start()

    def third(item, step):
        block = slot(item, step)
        p_arrived(item, block, 2)
        p_arrived(item, block, 3)
        c_copy(item, block, 3).start()

    for item in range(count):
        own(item).start()
        if kinds[item] == "line":
            for step in range(1, ctx_count):
                piece(item, step).start()
    move.begin()
    for step in range(ctx_count + 2):
        if step < ctx_count:
            along_order(z, ctx_count, step, take)
        for lag, stage in ((0, first), (1, second), (2, third)):
            for item in range(count):
                if steps(item, step - lag) and kinds[item] != "column":
                    stage(item, step - lag)
            if lag == 0 and step < ctx_count:
                move.choose(nearest(z, step))
    for step in range(ctx_count):
        move.await_slots(nearest(z, step))
    move.finish()
    for item in range(count):
        for step in range(ctx_count):
            if not steps(item, step):
                continue
            block = slot(item, step)
            if kinds[item] != "column":
                for which in range(4):
                    c_arrived(item, block, which)
                    p_copy(item, block, which).wait_send()
                    c_copy(item, block, which).wait_send()
            if kinds[item] == "line" and step > 0:
                piece(item, step).wait_send()
            if kinds[item] in ("all", "column"):
                both_ways(
                    z, block, ctx_count, lambda way, to: z_copy(item, block, way, to).wait_send()
                )


def gather_arrays(items, rows, slots, ctx_count, fsdp_count):
    kinds = tuple(kind for kind, shard in items)
    shards = [shard for kind, shard in items]
    lead = {
        "all": (ctx_count, fsdp_count),
        "line": (ctx_count, fsdp_count),
        "plane": (1, fsdp_count),
        "column": (ctx_count,),
    }
    shapes = [
        lead[kind] + (shard.shape[1:] if kind == "line" else shard.shape) for kind, shard in items
    ]
    row_count, width = rows.shape
    share = slots // fsdp_count
    shapes += [(ctx_count, row_count, width), (ctx_count, fsdp_count, share, width)]
    buffers, sems = dispatch_scratch(ctx_count, fsdp_count, row_count, share, width)
    count = len(items)
    dma = pltpu.SemaphoreType.DMA
    four = dma((count, ctx_count, 4))
    anywhere = pl.BlockSpec(memory_space=pl.ANY)
    results = pl.pallas_call(
        functools.partial(gather_kernel, ctx_count, kinds),
        out_shape=[
            jax.ShapeDtypeStruct(shape, item.dtype)
            for shape, item in zip(shapes, shards + [rows, rows])
        ],
        in_specs=[anywhere] * (count + 1),
        out_specs=[pl.BlockSpec(memory_space=pltpu.VMEM)] + [anywhere] * (count + 1),
        scratch_shapes=buffers
        + [
            dma((count,)),
            dma((count, ctx_count, 2)),
            dma((count, ctx_count)),
            four,
            four,
            four,
            four,
        ]
        + sems,
        compiler_params=pltpu.CompilerParams(
            collective_id=0, has_side_effects=True, vmem_limit_bytes=BIG_VMEM
        ),
        cost_estimate=pl.CostEstimate(
            flops=2_000_000_000, bytes_accessed=800_000_000, transcendentals=0
        ),
    )(*shards, rows)
    return results[:count], results[count], results[count + 1]


def tiles(width, size=256):
    return width // size, width % size


def each_tile(width, act, size=256):
    whole, rest = tiles(width, size)

    @pl.loop(0, whole)
    def _(index):
        act(pl.ds(pl.multiple_of(index * size, size), size))

    if rest:
        act(pl.ds(whole * size, rest))


def expert_kernel(ctx_count, rows_ref, info_ref, gate_ref, up_ref, down_ref, grads_ref, *refs):
    all_ref, slots_ref, hidden_ref, gate_back_ref, up_back_ref, back_ref = refs[:6]
    blocks, chosen, arrived, gate, up, down, grads, hidden, gate_back, up_back, back = refs[6:17]
    weight_sem, grad_sem, slot_sem, side_sem, back_sem = refs[17:22]
    move = Dispatch(
        ctx_count, False, rows_ref, info_ref, all_ref, blocks, chosen, arrived, refs[22:]
    )
    slots, width = back.shape
    units = hidden.shape[1]
    order = [nearest(move.z, step) for step in range(ctx_count)]

    def block_at(step):
        block = order[0]
        for place in range(1, ctx_count):
            block = jnp.where(step == place, order[place], block)
        return block

    loads = [
        pltpu.make_async_copy(source, target, weight_sem.at[place])
        for place, (source, target) in enumerate(((gate_ref, gate), (up_ref, up), (down_ref, down)))
    ]

    def load_grads(step):
        slot = lax.rem(step, 2)
        return pltpu.make_async_copy(
            grads_ref.at[block_at(step)], grads.at[slot], grad_sem.at[slot]
        )

    def store_slots(block):
        return pltpu.make_async_copy(arrived.at[block], slots_ref.at[block], slot_sem.at[block])

    def store_sides(block):
        return [
            pltpu.make_async_copy(source, target.at[block], side_sem.at[place])
            for place, (source, target) in enumerate(
                ((hidden, hidden_ref), (gate_back, gate_back_ref), (up_back, up_back_ref))
            )
        ]

    def store_back(block):
        return pltpu.make_async_copy(back, back_ref.at[block], back_sem)

    greet(move.z, move.f, PEERS, ctx_count)
    move.begin()
    for load in loads:
        load.start()
    load_grads(0).start()
    along_order(move.z, ctx_count, 0, move.take)
    move.choose(order[0])
    along_order(move.z, ctx_count, 1, move.take)
    move.choose(order[1])
    for load in loads:
        load.wait()

    @pl.loop(0, ctx_count)
    def _(step):
        block = block_at(step)
        slot = lax.rem(step, 2)

        @pl.when(step + 1 < ctx_count)
        def _():
            load_grads(step + 1).start()

        load_grads(step).wait()
        move.await_slots(block)
        store_slots(block).start()

        @pl.when(step > 0)
        def _():
            for copy in store_sides(block):
                copy.wait()

        rows = arrived[block].reshape(slots, width)

        def hidden_tile(part):
            pre = jnp.dot(rows, gate[:, part], preferred_element_type=FULL)
            linear = jnp.dot(rows, up[:, part], preferred_element_type=FULL)
            grad = dot_last(grads[slot], down[part, :])
            sigma = jax.nn.sigmoid(pre)
            act = pre * sigma
            hidden[:, part] = (act * linear).astype(LOW)
            up_back[:, part] = (grad * act).astype(LOW)
            gate_back[:, part] = (
                grad * linear * (sigma * (1.0 + pre * (1.0 - sigma)))
            ).astype(LOW)

        each_tile(units, hidden_tile)
        for copy in store_sides(block):
            copy.start()

        @pl.when(step > 0)
        def _():
            store_back(block).wait()

        def back_tile(part):
            total = dot_last(gate_back[...], gate[part, :]) + dot_last(up_back[...], up[part, :])
            back[:, part] = total.astype(LOW)

        each_tile(width, back_tile)
        store_back(block).start()

        for later in range(2, ctx_count):

            @pl.when(step + 2 == later)
            def _():
                along_order(move.z, ctx_count, later, move.take)

        @pl.when(step + 2 < ctx_count)
        def _():
            move.choose(block_at(step + 2))

    for step in range(ctx_count):
        store_slots(order[step]).wait()
    for copy in store_sides(order[-1]):
        copy.wait()
    store_back(order[-1]).wait()
    move.finish()


def expert_rows(rows, info, gate, up, down, grads, ctx_count, fsdp_count):
    count, width = rows.shape
    slots = grads.shape[1]
    share = slots // fsdp_count
    units = gate.shape[1]
    buffers, sems = dispatch_scratch(ctx_count, fsdp_count, count, share, width)
    dma = pltpu.SemaphoreType.DMA
    anywhere = pl.BlockSpec(memory_space=pl.ANY)
    low = lambda *shape: jax.ShapeDtypeStruct((ctx_count,) + shape, LOW)
    vmem = lambda *shape: pltpu.VMEM(shape, LOW)
    return pl.pallas_call(
        functools.partial(expert_kernel, ctx_count),
        out_shape=(
            low(count, width),
            low(fsdp_count, share, width),
            low(slots, units),
            low(slots, units),
            low(slots, units),
            low(slots, width),
        ),
        in_specs=[anywhere, pl.BlockSpec(memory_space=pltpu.VMEM)] + [anywhere] * 4,
        out_specs=(anywhere,) * 6,
        scratch_shapes=buffers
        + [
            vmem(ctx_count, fsdp_count, share, width),
            vmem(width, units),
            vmem(width, units),
            vmem(units, width),
            vmem(2, slots, width),
            vmem(slots, units),
            vmem(slots, units),
            vmem(slots, units),
            vmem(slots, width),
            dma((3,)),
            dma((2,)),
            dma((ctx_count,)),
            dma((3,)),
            dma,
        ]
        + sems,
        compiler_params=pltpu.CompilerParams(
            collective_id=4, has_side_effects=True, vmem_limit_bytes=BIG_VMEM
        ),
        cost_estimate=pl.CostEstimate(
            flops=60_000_000_000, bytes_accessed=400_000_000, transcendentals=3_000_000
        ),
    )(rows, info, gate, up, down, grads)


class Combine:
    def __init__(
        self, ctx_count, gated, slots_ref, info_ref, extra_ref, out_ref, buffers, sems
    ):
        self.ctx_count, self.gated = ctx_count, gated
        self.slots_ref, self.info_ref = slots_ref, info_ref
        self.extra_ref, self.out_ref = extra_ref, out_ref
        self.arrived, self.extra, self.parts, self.from_z = buffers
        self.keep_sem, self.extra_sem, self.p_send, self.p_recv, self.z_send, self.z_recv = sems
        self.z, self.f = lax.axis_index("ctx"), lax.axis_index("fsdp")
        self.core = flip(self.f, 1)
        self.order = [nearest(self.z, ctx_count - 1 - step) for step in range(ctx_count)]

    def p_copy(self, block, place):
        to = toggled(self.f, PEERS[place])
        sems = (self.p_send.at[block, place], self.p_recv.at[block, place])
        return remote(
            self.slots_ref.at[block, to], self.arrived.at[block, self.f], *sems, self.z, to
        )

    def keep(self, block):
        source, target = self.slots_ref.at[block, self.f], self.arrived.at[block, self.f]
        return pltpu.make_async_copy(source, target, self.keep_sem.at[block])

    def load(self, step):
        return pltpu.make_async_copy(
            self.extra_ref.at[self.order[step]], self.extra, self.extra_sem
        )

    def place(self, way, block, z):
        return jnp.where(block == z, self.ctx_count, block) if way == 0 else block

    def send_along(self, step, way, to):
        block = self.order[step]
        sems = (self.z_send.at[step], self.z_recv.at[way, block])
        target = self.from_z.at[self.place(way, block, to)]
        return remote(self.parts.at[step], target, *sems, to, self.f)

    def z_arrived(self, block, way):
        at = self.from_z.at[self.place(way, block, self.z)]
        sems = (self.z_send.at[0], self.z_recv.at[way, block])
        remote(at, at, *sems, self.z, self.core).wait_recv()

    def start(self):
        for block in self.order:
            for place in range(len(PEERS)):
                self.p_copy(block, place).start()
            self.keep(block).start()
        self.load(0).start()

    def mix(self, block, target, *ways):
        slots = self.arrived.shape[1] * self.arrived.shape[2]
        choose = one_hot(self.info_ref[block], self.z, slots, self.gated)

        @pl.loop(0, target.shape[1], step=256)
        def _(start):
            part = pl.ds(pl.multiple_of(start, 256), 256)
            total = dot_first(choose, self.arrived[block, :, :, part].reshape(slots, 256))
            total = total + self.extra[:, part].astype(FULL)
            for way in ways:
                total = total + self.from_z[self.place(way, block, self.z), :, part].astype(FULL)
            target[:, part] = total.astype(target.dtype)

    def step(self, step):
        block, z, last = self.order[step], self.z, self.ctx_count - 1
        self.keep(block).wait()
        self.load(step).wait()
        for place in range(len(PEERS)):
            at = self.arrived.at[block, toggled(self.f, PEERS[place])]
            sems = (self.p_send.at[block, place], self.p_recv.at[block, place])
            remote(at, at, *sems, z, self.core).wait_recv()
        if step < last:
            target = self.parts.at[step]
            for way, above in ((1, True), (0, False)):
                heading = (block < z) if above else (block > z)
                has_more = (z < last) if above else (z > 0)

                @pl.when(heading & has_more)
                def _():
                    self.z_arrived(block, way)
                    self.mix(block, target, way)

                @pl.when(heading & jnp.logical_not(has_more))
                def _():
                    self.mix(block, target)

                @pl.when(heading)
                def _():
                    self.send_along(step, way, z - 1 if above else z + 1).start()

            self.load(step + 1).start()
            return

        @pl.when(z > 0)
        def _():
            self.z_arrived(block, 0)

        @pl.when(z < last)
        def _():
            self.z_arrived(block, 1)

        @pl.when(z == 0)
        def _():
            self.mix(block, self.out_ref, 1)

        @pl.when(z == last)
        def _():
            self.mix(block, self.out_ref, 0)

        @pl.when((z > 0) & (z < last))
        def _():
            self.mix(block, self.out_ref, 0, 1)

    def finish(self):
        for step in range(self.ctx_count):
            for place in range(len(PEERS)):
                self.p_copy(self.order[step], place).wait_send()
            if step < self.ctx_count - 1:
                self.send_along(step, 0, self.z).wait_send()


def combine_kernel(ctx_count, info_ref, *refs):
    streams = refs[0:4]
    rows_ref, grads_ref, hidden_ref, gate_back_ref, up_back_ref = refs[4:9]
    outs = refs[9:11]
    gate_grad_ref, up_grad_ref, down_grad_ref = refs[11:14]
    narrow, left, right, gate_tile, up_tile = refs[14:19]
    side_sem, tile_sem, store_sem = refs[19:22]
    buffers, sems = refs[22:30], refs[30:42]
    moves = [
        Combine(
            ctx_count,
            place == 1,
            streams[2 * place],
            info_ref,
            streams[2 * place + 1],
            outs[place],
            buffers[4 * place : 4 * place + 4],
            sems[6 * place : 6 * place + 6],
        )
        for place in range(2)
    ]
    greet(moves[0].z, moves[0].f, PEERS, ctx_count)
    tile_count = rows_ref.shape[1] // 256

    def sides(source, target, place):
        return pltpu.make_async_copy(source, target, side_sem.at[place])

    first_sides = [sides(gate_back_ref, left, 0), sides(up_back_ref, right, 1)]
    last_side = sides(hidden_ref, left, 2)

    def fetch(source, index):
        part = pl.ds(pl.multiple_of(index * 256, 256), 256)
        slot = lax.rem(index, 2)
        return pltpu.make_async_copy(source.at[:, part], narrow.at[slot], tile_sem.at[slot])

    def store(tile, target, place, index):
        part = pl.ds(pl.multiple_of(index * 256, 256), 256)
        return pltpu.make_async_copy(tile, target.at[part, :], store_sem.at[place])

    def products(source, begin, end, pairs):
        @pl.loop(begin, end)
        def _(index):
            @pl.when(index + 1 < tile_count)
            def _():
                fetch(source, index + 1).start()

            fetch(source, index).wait()
            turned = narrow[lax.rem(index, 2)]
            for place, (factor, tile, target) in enumerate(pairs):
                part = dot_first(turned, factor[...]).astype(LOW)

                @pl.when(index > 0)
                def _():
                    store(tile, target, place, index).wait()

                tile[...] = part
                store(tile, target, place, index).start()

    both = ((left, gate_tile, gate_grad_ref), (right, up_tile, up_grad_ref))
    alone = ((left, gate_tile, down_grad_ref),)
    half = tile_count // 2
    for copy in first_sides:
        copy.start()
    fetch(rows_ref, 0).start()
    for move in moves:
        move.start()
    for copy in first_sides:
        copy.wait()
    products(rows_ref, 0, half, both)
    moves[0].step(0)
    products(rows_ref, half, tile_count, both)
    for place, (factor, tile, target) in enumerate(both):
        store(tile, target, place, 0).wait()
    last_side.start()
    fetch(grads_ref, 0).start()
    moves[0].step(1)
    last_side.wait()
    products(grads_ref, 0, half, alone)
    moves[0].step(2)
    products(grads_ref, half, tile_count, alone)
    store(gate_tile, down_grad_ref, 0, 0).wait()
    for step in range(3, ctx_count):
        moves[0].step(step)
    for step in range(ctx_count):
        moves[1].step(step)
    for move in moves:
        move.finish()


def combine_rows(
    slots, extra, out_slots, out_extra, info, sides, ctx_count, fsdp_count
):
    share, width = slots.shape[2:]
    count = extra.shape[1]
    total, units = sides[2].shape
    dma = pltpu.SemaphoreType.DMA
    anywhere = pl.BlockSpec(memory_space=pl.ANY)
    resident = pl.BlockSpec(memory_space=pltpu.VMEM)
    vmem = lambda *shape: pltpu.VMEM(shape, LOW)
    buffers = [
        vmem(ctx_count, fsdp_count, share, width),
        vmem(count, width),
        vmem(ctx_count - 1, count, width),
        vmem(ctx_count + 1, count, width),
    ]
    sems = [
        dma((ctx_count,)),
        dma,
        dma((ctx_count, len(PEERS))),
        dma((ctx_count, len(PEERS))),
        dma((ctx_count - 1,)),
        dma((2, ctx_count)),
    ]
    return pl.pallas_call(
        functools.partial(combine_kernel, ctx_count),
        out_shape=(jax.ShapeDtypeStruct((count, width), FULL),) * 2
        + (jax.ShapeDtypeStruct((width, units), LOW),) * 3,
        in_specs=[resident] + [anywhere] * 9,
        out_specs=(resident,) * 2 + (anywhere,) * 3,
        scratch_shapes=[
            vmem(2, total, 256),
            vmem(total, units),
            vmem(total, units),
            vmem(256, units),
            vmem(256, units),
            dma((3,)),
            dma((2,)),
            dma((2,)),
        ]
        + buffers * 2
        + sems * 2,
        compiler_params=pltpu.CompilerParams(
            collective_id=3, has_side_effects=True, vmem_limit_bytes=BIG_VMEM
        ),
        cost_estimate=pl.CostEstimate(
            flops=40_000_000_000, bytes_accessed=600_000_000, transcendentals=0
        ),
    )(info, slots, extra, out_slots, out_extra, *sides)


def mm(subscripts, left, right):
    return jnp.einsum(subscripts, left, right, preferred_element_type=FULL)


def member_pairs(fsdp_count, members, step):
    return [
        (f, f // members * members + (f % members + step) % members) for f in range(fsdp_count)
    ]


def by_member(own, others, member, members):
    if members == 2:
        first = member == 0
        return jnp.stack([jnp.where(first, own, others[0]), jnp.where(first, others[0], own)])
    stack = jnp.stack([own] + others)
    return jnp.take(stack, (member - jnp.arange(members)) % members, axis=0)


def part_of(array, member, step, members):
    return lax.dynamic_index_in_dim(array, (member + step) % members, 0, keepdims=False)


def swap_parts(array, members, fsdp_count):
    member = lax.axis_index("fsdp") % members
    others = [
        lax.ppermute(
            part_of(array, member, step, members), "fsdp", member_pairs(fsdp_count, members, step)
        )
        for step in range(1, members)
    ]
    return by_member(part_of(array, member, 0, members), others, member, members)


def share_parts(array, members, fsdp_count):
    member = lax.axis_index("fsdp") % members
    others = [
        lax.ppermute(array, "fsdp", member_pairs(fsdp_count, members, step))
        for step in range(1, members)
    ]
    return by_member(array, others, member, members)


def sum_parts(array, members, fsdp_count):
    member = lax.axis_index("fsdp") % members
    total = part_of(array, member, 0, members).astype(FULL)
    for step in range(1, members):
        total = total + lax.ppermute(
            part_of(array, member, step, members), "fsdp", member_pairs(fsdp_count, members, step)
        ).astype(FULL)
    return total.astype(LOW)


def routing(info, z, slots, gated):
    at = jnp.arange(slots, dtype=jnp.int32).astype(FULL)[:, None, None]
    hit = (info[:, None, COLUMN_AT : COLUMN_AT + TOP].swapaxes(2, 3) == at.reshape(-1, 1, 1)) & (
        info[:, None, :TOP].swapaxes(2, 3) == z.astype(FULL)
    )
    values = info[:, None, GATE_AT : GATE_AT + TOP].swapaxes(2, 3) if gated else 1.0
    return jnp.sum(jnp.where(hit, values, 0.0), axis=3).astype(LOW)


def swap_slots(slots):
    return lax.all_to_all(slots, "fsdp", split_axis=1, concat_axis=1, tiled=True)


def send_rows(rows, info, slots, gated, ctx_count, fsdp_count):
    every = lax.all_gather(rows, "ctx", axis=0)
    choose = routing(info, lax.axis_index("ctx"), slots, gated)
    chosen = mm("bst,btd->bsd", choose, every).astype(LOW)
    return every, swap_slots(chosen.reshape(ctx_count, fsdp_count, -1, rows.shape[1]))


def run_expert(rows, info, gate, up, down, grads, ctx_count, fsdp_count):
    if (ctx_count, fsdp_count) == (4, 8):
        return expert_rows(rows, info, gate, up, down, grads, ctx_count, fsdp_count)
    every, arrived = send_rows(rows, info, grads.shape[1], False, ctx_count, fsdp_count)
    slots = arrived.reshape(grads.shape)
    pre = mm("bsd,df->bsf", slots, gate)
    linear = mm("bsd,df->bsf", slots, up)
    act, slope = silu_slope(pre)
    grad = mm("bsd,fd->bsf", grads, down)
    hidden = (act * linear).astype(LOW)
    up_back = (grad * act).astype(LOW)
    gate_back = (grad * linear * slope).astype(LOW)
    back = (mm("bsf,df->bsd", gate_back, gate) + mm("bsf,df->bsd", up_back, up)).astype(LOW)
    return every, arrived, hidden, gate_back, up_back, back


def return_slots(slots, info, extra, gated):
    back = swap_slots(slots).reshape(slots.shape[0], -1, slots.shape[3])
    choose = routing(info, lax.axis_index("ctx"), back.shape[1], gated)
    total = (mm("bst,bsd->btd", choose, back) + extra).astype(LOW)
    return lax.psum_scatter(total, "ctx", scatter_dimension=0, tiled=False).astype(FULL)


def return_both(slots, extra, out_slots, out_extra, info, sides, ctx_count, fsdp_count):
    extra, out_extra = extra.astype(LOW), out_extra.astype(LOW)
    if (ctx_count, fsdp_count) == (4, 8):
        return combine_rows(
            slots, extra, out_slots, out_extra, info, sides, ctx_count, fsdp_count
        )
    rows, grads, hidden, gate_back, up_back = sides
    return (
        return_slots(slots, info, extra, False),
        return_slots(out_slots, info, out_extra, True),
        mm("sd,sf->df", rows, gate_back).astype(LOW),
        mm("sd,sf->df", rows, up_back).astype(LOW),
        mm("sd,sf->df", grads, hidden).astype(LOW),
    )


def gather_all(items, rows, slots, ctx_count, fsdp_count):
    if (ctx_count, fsdp_count) == (4, 8):
        return gather_arrays(items, rows, slots, ctx_count, fsdp_count)
    results = []
    for kind, shard in items:
        if kind == "line":
            shard = lax.all_to_all(shard, "ctx", split_axis=0, concat_axis=0, tiled=True)
            result = lax.all_gather(shard, "fsdp", axis=1)
        elif kind == "plane":
            result = lax.all_gather(shard, "fsdp", axis=0)[None]
        elif kind == "column":
            result = lax.all_gather(shard, "ctx", axis=0)
        else:
            result = lax.all_gather(shard, ("ctx", "fsdp"), axis=0)
            result = result.reshape((ctx_count, fsdp_count) + shard.shape)
        results.append(result)
    return (results,) + send_rows(rows, results[0], slots, True, ctx_count, fsdp_count)


def scatter_all(items, ctx_count, fsdp_count):
    items = [(kind, grad.astype(LOW)) for kind, grad in items]
    if (ctx_count, fsdp_count) == (4, 8):
        return scatter_arrays(items, ctx_count, fsdp_count)
    results = []
    for kind, grad in items:
        if kind == "line":
            grad = grad.reshape(ctx_count, fsdp_count, -1, grad.shape[1]).swapaxes(0, 1)
            grad = lax.psum_scatter(grad, "fsdp", scatter_dimension=0, tiled=False)
            results.append(along_line(grad))
        else:
            total = lax.psum_scatter(grad, ("ctx", "fsdp"), scatter_dimension=0, tiled=True)
            results.append(total.astype(FULL))
    return results


def along_line(array):
    return lax.all_to_all(array, "ctx", split_axis=0, concat_axis=0, tiled=True)


def after(values, *others):
    tied = lax.optimization_barrier((tuple(values), others))
    return tied[0]


def local(
    tokens,
    routes,
    gate_values,
    cotangent,
    attention_gain,
    query_weight,
    latent_weight,
    latent_gain,
    expand_weight,
    output_weight,
    feedforward_gain,
    shared_gate,
    shared_up,
    shared_down,
    expert_gate,
    expert_up,
    expert_down,
):
    row_count = tokens.shape[1]
    model_width = tokens.shape[2]
    ctx_count = lax.axis_size("ctx")
    fsdp_count = lax.axis_size("fsdp")
    device_count = ctx_count * fsdp_count
    experts_total = EXP_DEV * fsdp_count
    capacity = row_count * TOP * 4 // (3 * experts_total)
    members = ctx_count // EXP_DEV
    plane_experts = experts_total // ctx_count
    plane_slots = plane_experts * capacity
    share = capacity // members
    sequence = ctx_count * row_count
    z = lax.axis_index("ctx")
    score_scale = (NOPE + ROPE) ** (-0.5)
    source = tokens[0].astype(FULL)
    cot_low = cotangent[0]
    cot_full = cot_low.astype(FULL)
    positions = stored_positions(
        z * row_count + jnp.arange(row_count, dtype=jnp.int32), row_count, 2 * ctx_count
    )
    dense_rows = latent_weight.shape[0]
    gain_rows = latent_gain.shape[0]
    rotary_end = LATENT + ROPE
    hidden_units = expert_gate.shape[2]
    shared_units = shared_gate.shape[1] // ctx_count

    def by_part(weight):
        return weight.reshape(
            (EXP_DEV, members, weight.shape[1] // members) + weight.shape[2:]
        ).swapaxes(0, 1)

    def swapped(pieces):
        pieces = swap_parts(pieces, members, fsdp_count)
        return pieces.reshape((ctx_count,) + pieces.shape[2:])

    pair_swapped = swapped(jnp.stack([by_part(expert_gate), by_part(expert_up)], axis=2))
    down_swapped = swapped(by_part(expert_down))
    pair_moved = along_line(pair_swapped)

    local_routes = routes[0]
    expert_index = jnp.arange(experts_total, dtype=jnp.int32)
    member_of = (local_routes[..., None] == expert_index).astype(FULL)
    counts = jnp.sum(member_of, axis=1)
    before = jnp.cumsum(counts, axis=0) - counts
    within = jnp.sum(member_of * before[:, None, :], axis=-1).astype(jnp.int32)
    info = jnp.zeros((INFO_ROWS, row_count), FULL)
    info = info.at[:TOP].set((local_routes % ctx_count).astype(FULL).T)
    info = info.at[COLUMN_AT : COLUMN_AT + TOP].set(
        (local_routes // ctx_count * capacity + within).astype(FULL).T
    )
    info = info.at[GATE_AT : GATE_AT + TOP].set(gate_values[0].T)

    tail = jnp.concatenate(
        [
            latent_weight,
            attention_gain[:, None],
            feedforward_gain[:, None],
            jnp.pad(latent_gain, (0, dense_rows - gain_rows))[:, None],
            jnp.zeros((dense_rows, 256 - ROPE - 3), LOW),
        ],
        axis=1,
    )

    def by_line(weight):
        return weight.reshape(dense_rows, ctx_count, shared_units).swapaxes(0, 1)

    dense = (
        info,
        query_weight,
        tail,
        expand_weight,
        output_weight,
        by_line(shared_gate),
        by_line(shared_up),
        shared_down,
    )
    dense = after(dense, pair_swapped)
    kinds = ("column", "all", "all", "all", "all", "line", "line", "plane")
    gathered, all_cot, arrived_grad = gather_all(
        list(zip(kinds, dense)), cot_low, plane_slots, ctx_count, fsdp_count
    )
    all_info = gathered[0]
    full_query, full_tail, full_expand, full_output, full_sgate, full_sup, full_sdown = [
        item.reshape(-1, item.shape[-1]) for item in gathered[1:]
    ]
    full_latent = full_tail[:, :rotary_end]
    gain_one = full_tail[:, rotary_end].astype(FULL)
    gain_two = full_tail[:, rotary_end + 1].astype(FULL)
    gain_latent = (
        full_tail[:, rotary_end + 2].reshape(device_count, dense_rows)[:, :gain_rows]
    ).reshape(LATENT).astype(FULL)

    all_cot = all_cot.reshape(sequence, model_width)
    arrived_grad = arrived_grad.reshape(ctx_count, plane_slots, model_width)

    plain_one, inverse_one = norm_forward(source)
    normed = (plain_one * gain_one).astype(LOW)
    (normed,) = after((normed,), pair_moved)
    (query_raw,) = after((jnp.dot(normed, full_query, preferred_element_type=FULL),))
    query_raw = query_raw.reshape(row_count, HEADS, NOPE + ROPE)
    query_nope = query_raw[:, :, :NOPE].astype(LOW)
    query_rope = rotary(query_raw[:, :, NOPE:], positions, 1.0).astype(LOW)
    latent_raw = jnp.dot(normed, full_latent, preferred_element_type=FULL)
    plain_latent, inverse_latent = norm_forward(latent_raw[:, :LATENT])
    latent_norm = (plain_latent * gain_latent).astype(LOW)
    key_rope = rotary(latent_raw[:, LATENT:], positions, 1.0).astype(LOW)
    half_rows = row_count // 2
    pad_rope = ((0, 0), (0, 128 - ROPE))
    keys = lax.all_gather(
        jnp.concatenate([latent_norm, jnp.pad(key_rope, pad_rope)], axis=1), "ctx", axis=0
    )
    keys = keys.reshape(ctx_count, 2, half_rows, LATENT + 128)
    keys = jnp.concatenate([keys[:, 0], keys[::-1, 1]]).reshape(sequence, LATENT + 128)
    all_latent, all_keys = (keys[:, :LATENT], keys[:, LATENT:])
    expand = full_expand.reshape(LATENT, HEADS, NOPE + VDIM)
    expand_key = expand[:, :, :NOPE]
    expand_value = expand[:, :, NOPE:]
    query_latent = mm("thd,chd->htc", query_nope, expand_key).astype(LOW)
    (down_swapped,) = after((down_swapped,), pair_moved, normed)
    down_moved = along_line(down_swapped)
    query_turned = jnp.pad(query_rope.swapaxes(0, 1), ((0, 0),) + pad_rope)
    latent_out, log_total = attend(
        query_latent, query_turned, all_latent, all_keys, ctx_count, score_scale
    )
    values_out = (
        mm("htc,chv->thv", latent_out, expand_value).astype(LOW).reshape(row_count, HEADS * VDIM)
    )
    middle = source + jnp.dot(values_out, full_output, preferred_element_type=FULL)
    plain_two, inverse_two = norm_forward(middle)
    second = (plain_two * gain_two).astype(LOW)

    def whole(moved):
        return share_parts(moved, members, fsdp_count).swapaxes(0, 1)

    pair_whole = whole(pair_moved)
    gate_all = pair_whole[:, :, 0].reshape(model_width, hidden_units)
    up_all = pair_whole[:, :, 1].reshape(model_width, hidden_units)
    down_all = whole(down_moved).transpose(1, 2, 0, 3).reshape(hidden_units, model_width)
    (second_sent,) = after((second,), down_moved)
    all_second, arrived_rows, hidden_act, gate_back, up_back, arrived_back = run_expert(
        second_sent, all_info, gate_all, up_all, down_all, arrived_grad, ctx_count, fsdp_count
    )
    all_second = all_second.reshape(sequence, model_width)
    hidden_act, gate_back, up_back = [
        item.reshape(-1, hidden_units) for item in (hidden_act, gate_back, up_back)
    ]
    shared_g = jnp.dot(all_second, full_sgate, preferred_element_type=FULL)
    shared_u = jnp.dot(all_second, full_sup, preferred_element_type=FULL)
    shared_silu, shared_slope = silu_slope(shared_g)
    shared_hidden = (shared_silu * shared_u).astype(LOW)
    shared_hidden_grad = mm("td,fd->tf", all_cot, full_sdown)
    sup_back = (shared_hidden_grad * shared_silu).astype(LOW)
    sgate_back = (shared_hidden_grad * shared_u * shared_slope).astype(LOW)
    shared_second_grad = mm("tf,df->td", sgate_back, full_sgate) + mm(
        "tf,df->td", sup_back, full_sup
    )
    slots_shape = (ctx_count, fsdp_count, share, model_width)
    rows_shape = (ctx_count, row_count, model_width)
    shared_out = jnp.dot(shared_hidden, full_sdown, preferred_element_type=FULL)
    result = jnp.dot(hidden_act, down_all, preferred_element_type=FULL).astype(LOW)
    second_grad, out_sum, gate_grad, up_grad, down_grad = return_both(
        arrived_back.reshape(slots_shape),
        shared_second_grad.reshape(rows_shape),
        result.reshape(slots_shape),
        shared_out.reshape(rows_shape),
        all_info,
        (
            arrived_rows.reshape(-1, model_width),
            arrived_grad.reshape(-1, model_width),
            hidden_act,
            gate_back,
            up_back,
        ),
        ctx_count,
        fsdp_count,
    )
    layer_out = (middle + out_sum).astype(LOW)[None]

    def line_sum(grad):
        grad = grad.reshape(ctx_count, members, -1, hidden_units).swapaxes(0, 1)
        return sum_parts(grad, members, fsdp_count)

    gate_sum, up_sum, down_sum = (line_sum(gate_grad), line_sum(up_grad), line_sum(down_grad))
    gate_returned = along_line(gate_sum)
    sgate_back, sup_back = after((sgate_back, sup_back), gate_sum)
    shared_hidden, sgate_back, sup_back = after(
        (shared_hidden, sgate_back, sup_back), second_grad
    )
    sgate_grad = mm("td,tf->df", all_second, sgate_back).astype(LOW)
    sup_grad = mm("td,tf->df", all_second, sup_back).astype(LOW)
    sdown_grad = mm("tf,td->fd", shared_hidden, all_cot).astype(LOW)
    (second_grad,) = after(
        (second_grad,), gate_sum, up_sum, down_sum, sgate_grad, sup_grad, sdown_grad
    )
    sdown_grad = lax.psum_scatter(sdown_grad, "fsdp", scatter_dimension=0, tiled=True)

    middle_part, gain_two_grad = norm_backward(second_grad, plain_two, inverse_two, gain_two)
    middle_grad = cot_full + middle_part
    attended_grad = middle_grad.astype(LOW)
    output_weight_grad = mm("tv,td->vd", values_out, attended_grad)
    values_grad = (
        mm("td,vd->tv", attended_grad, full_output).astype(LOW).reshape(row_count, HEADS, VDIM)
    )
    latent_out_grad = mm("thv,chv->htc", values_grad, expand_value).astype(LOW)
    (latent_out_grad,) = after((latent_out_grad,), gate_returned)
    (up_sum,) = after((up_sum,), gate_returned, latent_out_grad)
    up_returned = along_line(up_sum)
    query_latent_grad, turned_grad, all_latent_grad, all_keys_grad = attend_back(
        query_latent,
        query_turned,
        all_latent,
        all_keys,
        latent_out,
        log_total,
        latent_out_grad,
        ctx_count,
        score_scale,
    )
    query_rope_grad = turned_grad[:, :, :ROPE].swapaxes(0, 1)
    keys_part = jnp.concatenate([all_latent_grad, all_keys_grad[:, :ROPE]], axis=1)
    keys_part = keys_part.reshape(2, ctx_count, half_rows, LATENT + ROPE)
    keys_part = jnp.stack([keys_part[0], keys_part[1, ::-1]], axis=1)
    keys_part = lax.psum_scatter(
        keys_part.reshape(sequence, LATENT + ROPE).astype(LOW),
        "ctx",
        scatter_dimension=0,
        tiled=True,
    ).astype(FULL)
    latent_grad, keys_grad = (keys_part[:, :LATENT], keys_part[:, LATENT:])
    expand_value_grad = mm("htc,thv->chv", latent_out, values_grad)

    sdown_grad = sdown_grad.astype(FULL)

    query_nope_grad = mm("htc,chd->thd", query_latent_grad, expand_key)
    expand_key_grad = mm("thd,htc->chd", query_nope, query_latent_grad)
    expand_grad = jnp.concatenate([expand_key_grad, expand_value_grad], axis=-1).reshape(
        LATENT, HEADS * (NOPE + VDIM)
    )
    query_grad = (
        jnp.concatenate([query_nope_grad, rotary(query_rope_grad, positions, -1.0)], axis=-1)
        .astype(LOW)
        .reshape(row_count, HEADS * (NOPE + ROPE))
    )
    latent_part_grad, gain_latent_grad = norm_backward(
        latent_grad, plain_latent, inverse_latent, gain_latent
    )
    latent_raw_grad = jnp.concatenate(
        [latent_part_grad, rotary(keys_grad, positions, -1.0)], axis=-1
    ).astype(LOW)
    query_weight_grad = mm("td,tq->dq", normed, query_grad)
    latent_weight_grad = mm("td,tq->dq", normed, latent_raw_grad)
    normed_grad = mm("tq,dq->td", query_grad, full_query) + mm(
        "tq,dq->td", latent_raw_grad, full_latent
    )
    source_part, gain_one_grad = norm_backward(normed_grad, plain_one, inverse_one, gain_one)
    tokens_grad = (middle_grad + source_part)[None]

    gain_latent_column = jnp.pad(
        gain_latent_grad.reshape(device_count, gain_rows), ((0, 0), (0, dense_rows - gain_rows))
    ).reshape(model_width)
    gains_grad = jnp.stack([gain_one_grad, gain_two_grad, gain_latent_column], axis=1)
    gains_grad = jnp.pad(gains_grad, ((0, 0), (0, 125)))
    (down_sum,) = after((down_sum,), up_returned, query_nope_grad)
    down_returned = along_line(down_sum)
    (gains_grad,) = after((gains_grad,), up_returned)
    dense_grads = (
        query_weight_grad,
        latent_weight_grad,
        gains_grad,
        expand_grad,
        output_weight_grad,
        sgate_grad,
        sup_grad,
    )
    kinds = ("all",) * 5 + ("line",) * 2
    query_sum, latent_sum, gains_sum, expand_sum, output_sum, sgate_sum, sup_sum = scatter_all(
        list(zip(kinds, dense_grads)), ctx_count, fsdp_count
    )

    def joined(pieces):
        return pieces.swapaxes(0, 1).reshape(dense_rows, -1).astype(FULL)

    def owned(moved):
        moved = moved.reshape((members, EXP_DEV) + moved.shape[1:])
        moved = swap_parts(moved, members, fsdp_count).swapaxes(0, 1)
        return moved.reshape(EXP_DEV, -1, hidden_units).astype(FULL)

    expert_grads = (
        owned(gate_returned),
        owned(up_returned),
        owned(down_returned).swapaxes(1, 2),
    )
    return (
        layer_out,
        tokens_grad,
        gains_sum[:, 0],
        query_sum,
        latent_sum,
        gains_sum[:gain_rows, 2],
        expand_sum,
        output_sum,
        gains_sum[:, 1],
        joined(sgate_sum),
        joined(sup_sum),
        sdown_grad,
        expert_grads[0],
        expert_grads[1],
        expert_grads[2],
    )


def solution(mesh):
    in_specs = (
        P("fsdp", "ctx", None),
        P("fsdp", "ctx", None),
        P("fsdp", "ctx", None),
        P("fsdp", "ctx", None),
        P(("ctx", "fsdp")),
        P(("ctx", "fsdp"), None),
        P(("ctx", "fsdp"), None),
        P(("ctx", "fsdp")),
        P(("ctx", "fsdp"), None),
        P(("ctx", "fsdp"), None),
        P(("ctx", "fsdp")),
        P(("ctx", "fsdp"), None),
        P(("ctx", "fsdp"), None),
        P(("ctx", "fsdp"), None),
        P("fsdp", "ctx", None),
        P("fsdp", "ctx", None),
        P("fsdp", None, "ctx"),
    )
    out_specs = (
        P("fsdp", "ctx", None),
        P("fsdp", "ctx", None),
        P(("ctx", "fsdp")),
        P(("ctx", "fsdp"), None),
        P(("ctx", "fsdp"), None),
        P(("ctx", "fsdp")),
        P(("ctx", "fsdp"), None),
        P(("ctx", "fsdp"), None),
        P(("ctx", "fsdp")),
        P(("ctx", "fsdp"), None),
        P(("ctx", "fsdp"), None),
        P(("ctx", "fsdp"), None),
        P("fsdp", "ctx", None),
        P("fsdp", "ctx", None),
        P("fsdp", None, "ctx"),
    )
    return jax.shard_map(local, mesh=mesh, in_specs=in_specs, out_specs=out_specs, check_vma=False)
```

```python
import functools

import jax
import jax.numpy as jnp
from jax import lax
from jax.experimental import pallas as pl
from jax.experimental.pallas import tpu as pltpu
from jax.sharding import PartitionSpec as P

HEADS = 16
NOPE = 128
ROPE = 64
LATENT = 512
VDIM = 128
TOP = 6
EXP_DEV = 2


epsilon = 1e-06
rope_base = 10000.0
masked_score = -1e30


def stored_positions(row_index, per_device, block_count):
    device = row_index // per_device
    within = row_index % per_device
    half_block = per_device // 2
    return jnp.where(
        within >= half_block,
        (block_count - 1 - device) * half_block + within - half_block,
        device * half_block + within,
    )


def rotary(values, positions, direction):
    half_rope = values.shape[-1] // 2
    frequency = rope_base ** (-jnp.arange(half_rope, dtype=jnp.float32) / half_rope)
    angles = positions.astype(jnp.float32)[:, None] * frequency[None, :]
    cosine_table = jnp.cos(angles)
    sine_table = direction * jnp.sin(angles)
    if values.ndim == 3:
        cosine_table = cosine_table[:, None, :]
        sine_table = sine_table[:, None, :]
    front_half = values[..., :half_rope]
    back_half = values[..., half_rope:]
    return jnp.concatenate(
        [
            front_half * cosine_table - back_half * sine_table,
            back_half * cosine_table + front_half * sine_table,
        ],
        axis=-1,
    )


def norm_forward(values):
    inverse = lax.rsqrt(jnp.mean(values * values, axis=-1, keepdims=True) + epsilon)
    return (values * inverse, inverse)


def norm_backward(normed_grad, plain, inverse, gain):
    gain_grad = jnp.sum(normed_grad * plain, axis=0)
    scaled = normed_grad * gain
    return (
        inverse * (scaled - plain * jnp.mean(scaled * plain, axis=-1, keepdims=True)),
        gain_grad,
    )


def silu_slope(values):
    sigma = jax.nn.sigmoid(values)
    return (values * sigma, sigma * (1.0 + values * (1.0 - sigma)))


LOW = jnp.bfloat16
FULL = jnp.float32


MESH_ID = pl.DeviceIdType.MESH
BIG_VMEM = 60 * 1024 * 1024


def flip(index, bit):
    return index + bit - 2 * bit * lax.rem(lax.div(index, bit), 2)


def toggled(index, mask):
    for bit in (1, 2, 4):
        if mask & bit:
            index = flip(index, bit)
    return index


def nearest(z, step):
    upper = lax.div(z, 2)
    if step == 0:
        return z
    if step == 1:
        return z + 1 - 2 * upper
    if step == 2:
        return 2 - 2 * lax.rem(z, 2) + upper
    return 3 - 3 * upper


def outermost(z, ctx_count):
    return (z == 0) | (z == ctx_count - 1)


def along_order(z, ctx_count, step, take):
    ends = outermost(z, ctx_count)
    if step <= 1:
        take(step)
    if step == 1:

        @pl.when(jnp.logical_not(ends))
        def _():
            take(2)

    if step >= 2:

        @pl.when(ends)
        def _():
            take(step)

        if step + 1 < ctx_count:

            @pl.when(jnp.logical_not(ends))
            def _():
                take(step + 1)


def remote(source, target, send, receive, z, f):
    return pltpu.make_async_remote_copy(
        src_ref=source,
        dst_ref=target,
        send_sem=send,
        recv_sem=receive,
        device_id={"ctx": z, "fsdp": f},
        device_id_type=MESH_ID,
    )


def greet(z, f, masks, ctx_count, whole_line=False):
    barrier = pltpu.get_barrier_semaphore()

    def hello(to_z, to_f):
        pl.semaphore_signal(
            barrier, inc=1, device_id={"ctx": to_z, "fsdp": to_f}, device_id_type=MESH_ID
        )

    for mask in masks:
        hello(z, toggled(f, mask))
    if whole_line:
        for step in range(1, ctx_count):
            hello(lax.rem(z + step, ctx_count), f)
            hello(lax.rem(z + step, ctx_count), flip(f, 1))
        pl.semaphore_wait(barrier, len(masks) + 2 * (ctx_count - 1))
        return

    @pl.when(z > 0)
    def _():
        hello(z - 1, f)

    @pl.when(z < ctx_count - 1)
    def _():
        hello(z + 1, f)

    along = lax.div(z + ctx_count - 1, ctx_count) + lax.div(2 * ctx_count - 2 - z, ctx_count)
    pl.semaphore_wait(barrier, len(masks) + along)


def both_ways(z, block, ctx_count, act):
    @pl.when((block <= z) & (z < ctx_count - 1))
    def _():
        act(0, z + 1)

    @pl.when((block >= z) & (z > 0))
    def _():
        act(1, z - 1)


def halves(rows, width):
    if rows % 32 == 0:
        return tuple((pl.ds(start, rows // 2), slice(None)) for start in (0, rows // 2))
    return tuple((slice(None), pl.ds(start, width // 2)) for start in (0, width // 2))


def add_rows(target, rows, *terms):
    @pl.loop(0, rows, step=16)
    def _(start):
        part = pl.ds(pl.multiple_of(start, 16), 16)
        total = terms[0][part, :].astype(FULL)
        for term in terms[1:]:
            total = total + term[part, :].astype(FULL)
        target[part, :] = total.astype(target.dtype)


def scatter_kernel(ctx_count, kinds, *refs):
    count = len(kinds)
    grads, outs = refs[:count], refs[count : 2 * count]
    banks = [refs[(2 + kind) * count : (3 + kind) * count] for kind in range(7)]
    load_sem, c_send, c_recv, p_send, p_recv, z_send, z_recv = refs[9 * count :]
    z, f = lax.axis_index("ctx"), lax.axis_index("fsdp")
    side = lax.rem(f, 2)
    chip = lax.div(f, 2)
    core, x_near, y_near = flip(f, 1), flip(f, 2), flip(f, 4)
    x_chip, y_chip = flip(chip, 1), flip(chip, 2)
    far_chip = flip(x_chip, 2)
    greet(z, f, (1, 2, 4), ctx_count, True)
    order = [nearest(z, ctx_count - 1 - step) for step in range(ctx_count)]

    def work(item):
        grad_ref, out_ref = grads[item], outs[item]
        mine, from_core, from_x, from_y, half_x, half_y, from_z = [bank[item] for bank in banks]
        rows, width = out_ref.shape[-2:]
        left, right = halves(rows, width)
        half_rows = half_x.shape[1]

        def load(block):
            return pltpu.make_async_copy(
                grad_ref.at[block, :, side], mine.at[block], load_sem.at[item, block]
            )

        def c_copy(block):
            return remote(
                grad_ref.at[block, :, 1 - side],
                from_core.at[block],
                c_send.at[item, block],
                c_recv.at[item, block],
                z,
                core,
            )

        def p_copy(block, which):
            source, target, to = (
                (mine.at[(block, far_chip) + left], half_y.at[block], y_near),
                (mine.at[(block, far_chip) + right], half_x.at[block], x_near),
                (mine.at[block, x_chip], from_x.at[block], x_near),
                (mine.at[block, y_chip], from_y.at[block], y_near),
            )[which]
            sems = (p_send.at[item, block, which], p_recv.at[item, block, which])
            return remote(source, target, *sems, z, to)

        def z_copy(block, way, target):
            return remote(
                mine.at[block, chip],
                from_z.at[way, block],
                z_send.at[item, block],
                z_recv.at[item, way, block],
                target,
                f,
            )

        def z_arrived(block, way):
            at = from_z.at[way, block]
            sems = (z_send.at[item, block], z_recv.at[item, way, block])
            remote(at, at, *sems, z, core).wait_recv()

        def piece(block):
            sems = (z_send.at[item, block], z_recv.at[item, 0, z])
            return remote(mine.at[block, chip], out_ref.at[z], *sems, block, f)

        def start(step):
            c_copy(order[step]).start()
            load(order[step]).start()

        def first(step):
            block = order[step]
            load(block).wait()
            c_copy(block).wait_recv()
            far_part = mine.at[block, far_chip]
            add_rows(far_part, rows, far_part, from_core.at[block, far_chip])
            p_copy(block, 0).start()
            p_copy(block, 1).start()

        def second(step):
            block = order[step]
            x_part, y_part = mine.at[block, x_chip], mine.at[block, y_chip]
            add_rows(x_part, rows, x_part, from_core.at[block, x_chip])
            add_rows(y_part, rows, y_part, from_core.at[block, y_chip])
            p_copy(block, 0).wait_recv()
            x_left = mine.at[(block, x_chip) + left]
            add_rows(x_left, half_rows, x_left, half_y.at[block])
            p_copy(block, 2).start()
            p_copy(block, 1).wait_recv()
            y_right = mine.at[(block, y_chip) + right]
            add_rows(y_right, half_rows, y_right, half_x.at[block])
            p_copy(block, 3).start()

        def third(step):
            block = order[step]
            p_copy(block, 2).wait_recv()
            p_copy(block, 3).wait_recv()
            own = mine.at[block, chip]
            terms = (own, from_core.at[block, chip], from_x.at[block], from_y.at[block])
            if kinds[item] == "line":
                add_rows(out_ref.at[z] if step == ctx_count - 1 else own, rows, *terms)
                if step < ctx_count - 1:
                    piece(block).start()
                return

            if step == ctx_count - 1:

                @pl.when(z > 0)
                def _():
                    z_arrived(block, 0)

                @pl.when(z < ctx_count - 1)
                def _():
                    z_arrived(block, 1)

                @pl.when(z == 0)
                def _():
                    add_rows(out_ref, rows, *terms, from_z.at[1, block])

                @pl.when(z == ctx_count - 1)
                def _():
                    add_rows(out_ref, rows, *terms, from_z.at[0, block])

                @pl.when((z > 0) & (z < ctx_count - 1))
                def _():
                    add_rows(out_ref, rows, *terms, from_z.at[0, block], from_z.at[1, block])

                return

            for way, above in ((1, True), (0, False)):
                heading = (block < z) if above else (block > z)
                has_more = (z < ctx_count - 1) if above else (z > 0)

                @pl.when(heading & has_more)
                def _():
                    z_arrived(block, way)
                    add_rows(own, rows, *terms, from_z.at[way, block])

                @pl.when(heading & jnp.logical_not(has_more))
                def _():
                    add_rows(own, rows, *terms)

                @pl.when(heading)
                def _():
                    z_copy(block, way, z - 1 if above else z + 1).start()

        def finish(step):
            block = order[step]
            c_copy(block).wait_send()
            for which in range(4):
                p_copy(block, which).wait_send()
            if step == ctx_count - 1:
                return
            if kinds[item] == "line":
                piece(block).wait_send()
                at = out_ref.at[block]
                sems = (z_send.at[item, block], z_recv.at[item, 0, block])
                remote(at, at, *sems, z, core).wait_recv()
            else:
                z_copy(block, 0, z).wait_send()

        return start, first, second, third, finish

    stages = list(zip(*[work(item) for item in range(count)]))
    for step in range(ctx_count):
        for act in stages[0]:
            act(step)
    for step in range(ctx_count + 2):
        for lag in (0, 1, 2):
            if 0 <= step - lag < ctx_count:
                for act in stages[1 + lag]:
                    act(step - lag)
    for step in range(ctx_count):
        for act in stages[4]:
            act(step)


def scatter_arrays(items, ctx_count, fsdp_count):
    kinds = tuple(kind for kind, grad in items)
    grads = [grad for kind, grad in items]
    count = len(grads)
    chips = fsdp_count // 2
    shapes = [
        (grad.shape[0] // (ctx_count * fsdp_count), grad.shape[1]) for grad in grads
    ]
    half_shapes = [
        (rows // 2, width) if rows % 32 == 0 else (rows, width // 2) for rows, width in shapes
    ]
    dma = pltpu.SemaphoreType.DMA
    leads = [(ctx_count, chips), (ctx_count, chips), (ctx_count,), (ctx_count,)]
    banks = [pltpu.VMEM(lead + shape, LOW) for lead in leads for shape in shapes]
    banks += [pltpu.VMEM((ctx_count,) + shape, LOW) for _ in range(2) for shape in half_shapes]
    banks += [
        pltpu.VMEM((2, ctx_count) + shape if kind == "all" else (1, 1, 16, 128), LOW)
        for kind, shape in zip(kinds, shapes)
    ]
    return pl.pallas_call(
        functools.partial(scatter_kernel, ctx_count, kinds),
        out_shape=[
            jax.ShapeDtypeStruct(shape, FULL)
            if kind == "all"
            else jax.ShapeDtypeStruct((ctx_count,) + shape, LOW)
            for kind, shape in zip(kinds, shapes)
        ],
        in_specs=[pl.BlockSpec(memory_space=pl.ANY)] * count,
        out_specs=[pl.BlockSpec(memory_space=pltpu.VMEM)] * count,
        scratch_shapes=banks
        + [
            dma((count, ctx_count)),
            dma((count, ctx_count)),
            dma((count, ctx_count)),
            dma((count, ctx_count, 4)),
            dma((count, ctx_count, 4)),
            dma((count, ctx_count)),
            dma((count, 2, ctx_count)),
        ],
        compiler_params=pltpu.CompilerParams(
            collective_id=1, has_side_effects=True, vmem_limit_bytes=BIG_VMEM
        ),
        cost_estimate=pl.CostEstimate(flops=0, bytes_accessed=500_000_000, transcendentals=0),
    )(
        *[
            grad.reshape((ctx_count, chips, 2) + shape)
            for grad, shape in zip(grads, shapes)
        ]
    )


HEAD_GROUP = 4
KEYS = 256


def dot_last(left, right):
    return lax.dot_general(left, right, (((1,), (1,)), ((), ())), preferred_element_type=FULL)


def dot_first(left, right):
    return lax.dot_general(left, right, (((0,), (0,)), ((), ())), preferred_element_type=FULL)


def reach(half, rows, ctx_count):
    ctx = lax.axis_index("ctx")
    first = jnp.where(half == 0, ctx, 2 * ctx_count - 1 - ctx) * rows
    return first, lax.div(first + rows + KEYS - 1, KEYS)


def block_scores(query, turned, keys_ref, rope_ref, index, first, rows, scale):
    part = pl.ds(pl.multiple_of(index * KEYS, KEYS), KEYS)
    keys, rope = keys_ref[part, :], rope_ref[part, :]
    scores = (dot_last(query, keys) + dot_last(turned, rope)) * scale
    shape = scores.shape
    at = first + lax.rem(lax.broadcasted_iota(jnp.int32, shape, 0), rows)
    key_at = index * KEYS + lax.broadcasted_iota(jnp.int32, shape, 1)
    return part, keys, rope, scores, at >= key_at


def attend_kernel(
    ctx_count, scale, query_ref, turned_ref, keys_ref, rope_ref, out_ref, log_ref, total, top, norm
):
    heads, rows, width = query_ref.shape
    first, blocks = reach(pl.program_id(0), rows, ctx_count)
    query = query_ref[...].reshape(heads * rows, width)
    turned = turned_ref[...].reshape(heads * rows, -1)
    total[...] = jnp.zeros_like(total)
    norm[...] = jnp.zeros_like(norm)
    top[...] = jnp.full_like(top, masked_score)

    @pl.loop(0, blocks)
    def _(index):
        part, keys, rope, scores, seen = block_scores(
            query, turned, keys_ref, rope_ref, index, first, rows, scale
        )
        scores = jnp.where(seen, scores, masked_score)
        old = top[...]
        new = jnp.maximum(old, jnp.max(scores, axis=1, keepdims=True))
        weights = jnp.exp(scores - new)
        shrink = jnp.exp(old - new)
        top[...] = new
        norm[...] = norm[...] * shrink + jnp.sum(weights, axis=1, keepdims=True)
        total[...] = total[...] * shrink + jnp.dot(
            weights.astype(LOW), keys, preferred_element_type=FULL
        )

    out_ref[...] = (total[...] / norm[...]).astype(LOW).reshape(out_ref.shape)
    log_ref[...] = (top[...] + jnp.log(norm[...])).reshape(log_ref.shape)


def attend_back_kernel(
    ctx_count,
    scale,
    query_ref,
    turned_ref,
    keys_ref,
    rope_ref,
    out_ref,
    log_ref,
    grad_ref,
    query_grad_ref,
    turned_grad_ref,
    keys_grad_ref,
    rope_grad_ref,
    query_total,
    turned_total,
):
    heads, rows, width = query_ref.shape
    first, blocks = reach(pl.program_id(0), rows, ctx_count)
    query = query_ref[...].reshape(heads * rows, width)
    turned = turned_ref[...].reshape(heads * rows, -1)
    grad = grad_ref[...].reshape(heads * rows, width)
    out = out_ref[...].reshape(heads * rows, width)
    logs = log_ref[...].reshape(heads * rows, 1)
    inner = jnp.sum(grad.astype(FULL) * out.astype(FULL), axis=1, keepdims=True)
    query_total[...] = jnp.zeros_like(query_total)
    turned_total[...] = jnp.zeros_like(turned_total)

    @pl.when((pl.program_id(0) == 0) & (pl.program_id(1) == 0))
    def _():
        keys_grad_ref[...] = jnp.zeros_like(keys_grad_ref)
        rope_grad_ref[...] = jnp.zeros_like(rope_grad_ref)

    @pl.loop(0, blocks)
    def _(index):
        part, keys, rope, scores, seen = block_scores(
            query, turned, keys_ref, rope_ref, index, first, rows, scale
        )
        weights = jnp.where(seen, jnp.exp(scores - logs), 0.0)
        change = (weights * (dot_last(grad, keys) - inner) * scale).astype(LOW)
        query_total[...] += jnp.dot(change, keys, preferred_element_type=FULL)
        turned_total[...] += jnp.dot(change, rope, preferred_element_type=FULL)
        keys_grad_ref[part, :] += dot_first(change, query) + dot_first(weights.astype(LOW), grad)
        rope_grad_ref[part, :] += dot_first(change, turned)

    query_grad_ref[...] = query_total[...].astype(LOW).reshape(query_grad_ref.shape)
    turned_grad_ref[...] = turned_total[...].reshape(turned_grad_ref.shape)


def attend_specs(heads, group, rows, widths):
    return [pl.BlockSpec((group, rows, width), lambda half, g: (g, half, 0)) for width in widths]


def whole_spec(array):
    return pl.BlockSpec(array.shape, lambda half, g: (0, 0))


def attend(query, turned, keys, rope, ctx_count, scale):
    heads, count, width = query.shape
    group, rows = HEAD_GROUP, count // 2
    lanes = turned.shape[2]
    return pl.pallas_call(
        functools.partial(attend_kernel, ctx_count, scale),
        grid=(2, heads // group),
        out_shape=(
            jax.ShapeDtypeStruct((heads, count, width), LOW),
            jax.ShapeDtypeStruct((heads, count, 1), FULL),
        ),
        in_specs=attend_specs(heads, group, rows, (width, lanes))
        + [whole_spec(keys), whole_spec(rope)],
        out_specs=tuple(attend_specs(heads, group, rows, (width, 1))),
        scratch_shapes=[
            pltpu.VMEM((group * rows, width), FULL),
            pltpu.VMEM((group * rows, 1), FULL),
            pltpu.VMEM((group * rows, 1), FULL),
        ],
        compiler_params=pltpu.CompilerParams(vmem_limit_bytes=BIG_VMEM),
        cost_estimate=pl.CostEstimate(
            flops=12_000_000_000, bytes_accessed=12_000_000, transcendentals=3_000_000
        ),
    )(query, turned, keys, rope)


def attend_back(query, turned, keys, rope, out, logs, grad, ctx_count, scale):
    heads, count, width = query.shape
    group, rows = HEAD_GROUP, count // 2
    lanes = turned.shape[2]
    return pl.pallas_call(
        functools.partial(attend_back_kernel, ctx_count, scale),
        grid=(2, heads // group),
        out_shape=(
            jax.ShapeDtypeStruct((heads, count, width), LOW),
            jax.ShapeDtypeStruct((heads, count, lanes), FULL),
            jax.ShapeDtypeStruct(keys.shape, FULL),
            jax.ShapeDtypeStruct(rope.shape, FULL),
        ),
        in_specs=attend_specs(heads, group, rows, (width, lanes))
        + [whole_spec(keys), whole_spec(rope)]
        + attend_specs(heads, group, rows, (width, 1, width)),
        out_specs=tuple(
            attend_specs(heads, group, rows, (width, lanes)) + [whole_spec(keys), whole_spec(rope)]
        ),
        scratch_shapes=[
            pltpu.VMEM((group * rows, width), FULL),
            pltpu.VMEM((group * rows, lanes), FULL),
        ],
        compiler_params=pltpu.CompilerParams(vmem_limit_bytes=BIG_VMEM),
        cost_estimate=pl.CostEstimate(
            flops=30_000_000_000, bytes_accessed=30_000_000, transcendentals=3_000_000
        ),
    )(query, turned, keys, rope, out, logs, grad)


PEERS = (6, 7, 2, 4, 3, 5, 1)
COLUMN_AT, GATE_AT, INFO_ROWS = 8, 16, 24


def one_hot(info, z, slots, gated):
    count = info.shape[1]
    at = lax.broadcasted_iota(jnp.int32, (slots, count), 0).astype(FULL)
    plane = z.astype(FULL)
    total = jnp.zeros((slots, count), FULL)
    for route in range(TOP):
        hit = (info[COLUMN_AT + route][None, :] == at) & (info[route][None, :] == plane)
        value = info[GATE_AT + route][None, :] if gated else 1.0
        total = total + jnp.where(hit, value, 0.0)
    return total.astype(LOW)


class Dispatch:
    def __init__(self, ctx_count, gated, rows_ref, info_ref, all_ref, blocks, chosen, arrived, sems):
        self.own_sem, self.all_sem, self.keep_sem = sems[:3]
        self.z_send, self.z_recv, self.p_send, self.p_recv = sems[3:]
        self.ctx_count, self.gated = ctx_count, gated
        self.rows_ref, self.info_ref, self.all_ref = rows_ref, info_ref, all_ref
        self.blocks, self.chosen, self.arrived = blocks, chosen, arrived
        self.z, self.f = lax.axis_index("ctx"), lax.axis_index("fsdp")
        self.core = flip(self.f, 1)

    def z_copy(self, block, way, target):
        at = self.blocks.at[block]
        sems = (self.z_send.at[block, way], self.z_recv.at[block])
        return remote(at, at, *sems, target, self.f)

    def p_copy(self, block, place):
        to = toggled(self.f, PEERS[place])
        sems = (self.p_send.at[block, place], self.p_recv.at[block, place])
        return remote(
            self.chosen.at[block, to], self.arrived.at[block, self.f], *sems, self.z, to
        )

    def keep(self, block):
        source, target = self.chosen.at[block, self.f], self.arrived.at[block, self.f]
        return pltpu.make_async_copy(source, target, self.keep_sem.at[block])

    def store(self, block):
        source, target = self.blocks.at[block], self.all_ref.at[block]
        return pltpu.make_async_copy(source, target, self.all_sem.at[block])

    def begin(self):
        own = pltpu.make_async_copy(self.rows_ref, self.blocks.at[self.z], self.own_sem)
        own.start()
        own.wait()

    def take(self, step):
        block = nearest(self.z, step)
        if step > 0:
            at = self.blocks.at[block]
            sems = (self.z_send.at[block, 0], self.z_recv.at[block])
            remote(at, at, *sems, self.z, self.core).wait_recv()
        both_ways(
            self.z, block, self.ctx_count, lambda way, to: self.z_copy(block, way, to).start()
        )
        self.store(block).start()

    def choose(self, block):
        groups, share, width = self.chosen.shape[1:]
        choose = one_hot(self.info_ref[block], self.z, groups * share, self.gated)

        @pl.loop(0, width, step=256)
        def _(start):
            part = pl.ds(pl.multiple_of(start, 256), 256)
            tile = jnp.dot(choose, self.blocks[block, :, part], preferred_element_type=FULL)
            self.chosen[block, :, :, part] = tile.astype(LOW).reshape(groups, share, 256)

        for place in range(len(PEERS)):
            self.p_copy(block, place).start()
        self.keep(block).start()

    def await_slots(self, block):
        self.keep(block).wait()
        for place in range(len(PEERS)):
            at = self.arrived.at[block, toggled(self.f, PEERS[place])]
            sems = (self.p_send.at[block, place], self.p_recv.at[block, place])
            remote(at, at, *sems, self.z, self.core).wait_recv()

    def finish(self):
        for step in range(self.ctx_count):
            block = nearest(self.z, step)
            self.store(block).wait()
            both_ways(
                self.z,
                block,
                self.ctx_count,
                lambda way, to: self.z_copy(block, way, to).wait_send(),
            )
            for place in range(len(PEERS)):
                self.p_copy(block, place).wait_send()


def dispatch_scratch(ctx_count, fsdp_count, count, share, width):
    dma = pltpu.SemaphoreType.DMA
    return [
        pltpu.VMEM((ctx_count, count, width), LOW),
        pltpu.VMEM((ctx_count, fsdp_count, share, width), LOW),
    ], [
        dma,
        dma((ctx_count,)),
        dma((ctx_count,)),
        dma((ctx_count, 2)),
        dma((ctx_count,)),
        dma((ctx_count, len(PEERS))),
        dma((ctx_count, len(PEERS))),
    ]


def gather_kernel(ctx_count, kinds, *refs):
    count = len(kinds)
    shards, rows_ref = refs[:count], refs[count]
    outs, all_ref, slots_ref = refs[count + 1 : 2 * count + 1], refs[2 * count + 1], refs[2 * count + 2]
    blocks, chosen = refs[2 * count + 3 : 2 * count + 5]
    own_sem, z_send, z_recv, p_send, p_recv, c_send, c_recv = refs[2 * count + 5 : 2 * count + 12]
    z, f = lax.axis_index("ctx"), lax.axis_index("fsdp")
    core, x_near, y_near = flip(f, 1), flip(f, 2), flip(f, 4)
    far = flip(x_near, 4)
    move = Dispatch(
        ctx_count, True, rows_ref, outs[0], all_ref, blocks, chosen, slots_ref, refs[2 * count + 12 :]
    )
    greet(z, f, PEERS, ctx_count, True)

    def slot(item, step):
        return 0 if kinds[item] == "plane" else nearest(z, step)

    def steps(item, step):
        if kinds[item] == "expert":
            return False
        return step == 0 if kinds[item] == "plane" else 0 <= step < ctx_count

    side = lax.rem(f, 2)

    def expert_pieces(item, act):
        half = shards[item].shape[1] // 2
        for which in range(2):
            for part in range(2):
                source = shards[item].at[which, pl.ds(part * half, half)]
                target = outs[item].at[z]
                to_z = 2 * side + which
                here = (to_z == z) & (side == part)

                @pl.when(here)
                def _():
                    act(pltpu.make_async_copy(source, target, own_sem.at[item]), True)

                @pl.when(jnp.logical_not(here))
                def _():
                    sems = (z_send.at[item, 2 * which + part, 0], z_recv.at[item, z])
                    act(remote(source, target, *sems, to_z, f - side + part), False)

    def expert_arrived(item):
        for origin in range(ctx_count):
            at = outs[item].at[origin]
            mine = (origin == z) & (lax.div(z, 2) == side)

            @pl.when(jnp.logical_not(mine))
            def _():
                sems = (z_send.at[item, 0, 0], z_recv.at[item, origin])
                remote(at, at, *sems, z, core).wait_recv()

    def z_view(item, block):
        return outs[item].at[block] if kinds[item] == "column" else outs[item].at[block, f]

    def own(item):
        source = shards[item].at[z] if kinds[item] == "line" else shards[item]
        return pltpu.make_async_copy(source, z_view(item, slot(item, 0)), own_sem.at[item])

    def z_copy(item, block, way, target):
        at = z_view(item, block)
        return remote(at, at, z_send.at[item, block, way], z_recv.at[item, block], target, f)

    def piece(item, step):
        target = lax.rem(z + step, ctx_count)
        return remote(
            shards[item].at[target],
            outs[item].at[z, f],
            z_send.at[item, target, 0],
            z_recv.at[item, z],
            target,
            f,
        )

    def part(item, block, at, which):
        rows, columns = halves(*outs[item].shape[2:])[which]
        return outs[item].at[block, at, rows, columns]

    def p_copy(item, block, which):
        at = (
            lambda: outs[item].at[block, f],
            lambda: outs[item].at[block, f],
            lambda: part(item, block, x_near, 0),
            lambda: part(item, block, y_near, 1),
        )[which]()
        to = (x_near, y_near, y_near, x_near)[which]
        sems = (p_send.at[item, block, which], p_recv.at[item, block, which])
        return remote(at, at, *sems, z, to)

    def p_arrived(item, block, which):
        at = (
            lambda: outs[item].at[block, x_near],
            lambda: outs[item].at[block, y_near],
            lambda: part(item, block, far, 0),
            lambda: part(item, block, far, 1),
        )[which]()
        sems = (p_send.at[item, block, which], p_recv.at[item, block, which])
        remote(at, at, *sems, z, x_near).wait_recv()

    def c_copy(item, block, which):
        at = outs[item].at[block, (f, x_near, y_near, far)[which]]
        sems = (c_send.at[item, block, which], c_recv.at[item, block, which])
        return remote(at, at, *sems, z, core)

    def c_arrived(item, block, which):
        at = outs[item].at[block, flip((f, x_near, y_near, far)[which], 1)]
        sems = (c_send.at[item, block, which], c_recv.at[item, block, which])
        remote(at, at, *sems, z, core).wait_recv()

    def take(step):
        for item in range(count):
            if not steps(item, step):
                continue
            block = slot(item, step)
            if step == 0:
                own(item).wait()
            else:
                at = z_view(item, block)
                sems = (z_send.at[item, block, 0], z_recv.at[item, block])
                remote(at, at, *sems, z, core).wait_recv()
            if kinds[item] in ("all", "column"):
                both_ways(
                    z, block, ctx_count, lambda way, to: z_copy(item, block, way, to).start()
                )
        move.take(step)

    def first(item, step):
        block = slot(item, step)
        p_copy(item, block, 0).start()
        p_copy(item, block, 1).start()
        c_copy(item, block, 0).start()

    def second(item, step):
        block = slot(item, step)
        for which in (0, 1):
            p_arrived(item, block, which)
            p_copy(item, block, which + 2).start()
            c_copy(item, block, which + 1).start()

    def third(item, step):
        block = slot(item, step)
        p_arrived(item, block, 2)
        p_arrived(item, block, 3)
        c_copy(item, block, 3).start()

    experts = [item for item in range(count) if kinds[item] == "expert"]
    for item in range(count):
        if kinds[item] == "expert":
            continue
        own(item).start()
        if kinds[item] == "line":
            for step in range(1, ctx_count):
                piece(item, step).start()
    move.begin()
    for step in range(ctx_count + 2):
        if step < ctx_count:
            along_order(z, ctx_count, step, take)
        if step in (1, 3):
            for item in experts[step // 2 :: 2]:
                expert_pieces(item, lambda copy, local: copy.start())
        for lag, stage in ((0, first), (1, second), (2, third)):
            for item in range(count):
                if steps(item, step - lag) and kinds[item] != "column":
                    stage(item, step - lag)
            if lag == 0 and step < ctx_count:
                move.choose(nearest(z, step))
    for step in range(ctx_count):
        move.await_slots(nearest(z, step))
    move.finish()
    for item in experts:
        expert_arrived(item)
        expert_pieces(item, lambda copy, local: copy.wait() if local else copy.wait_send())
    for item in range(count):
        for step in range(ctx_count):
            if not steps(item, step):
                continue
            block = slot(item, step)
            if kinds[item] != "column":
                for which in range(4):
                    c_arrived(item, block, which)
                    p_copy(item, block, which).wait_send()
                    c_copy(item, block, which).wait_send()
            if kinds[item] == "line" and step > 0:
                piece(item, step).wait_send()
            if kinds[item] in ("all", "column"):
                both_ways(
                    z, block, ctx_count, lambda way, to: z_copy(item, block, way, to).wait_send()
                )


def gather_arrays(items, rows, slots, ctx_count, fsdp_count):
    kinds = tuple(kind for kind, shard in items)
    shards = [shard for kind, shard in items]
    lead = {
        "all": (ctx_count, fsdp_count),
        "line": (ctx_count, fsdp_count),
        "plane": (1, fsdp_count),
        "column": (ctx_count,),
    }
    shapes = [
        (ctx_count, shard.shape[1] // 2, shard.shape[2])
        if kind == "expert"
        else lead[kind] + (shard.shape[1:] if kind == "line" else shard.shape)
        for kind, shard in items
    ]
    row_count, width = rows.shape
    share = slots // fsdp_count
    shapes += [(ctx_count, row_count, width), (ctx_count, fsdp_count, share, width)]
    buffers, sems = dispatch_scratch(ctx_count, fsdp_count, row_count, share, width)
    count = len(items)
    dma = pltpu.SemaphoreType.DMA
    four = dma((count, ctx_count, 4))
    anywhere = pl.BlockSpec(memory_space=pl.ANY)
    results = pl.pallas_call(
        functools.partial(gather_kernel, ctx_count, kinds),
        out_shape=[
            jax.ShapeDtypeStruct(shape, item.dtype)
            for shape, item in zip(shapes, shards + [rows, rows])
        ],
        in_specs=[anywhere] * (count + 1),
        out_specs=[pl.BlockSpec(memory_space=pltpu.VMEM)] + [anywhere] * (count + 1),
        scratch_shapes=buffers
        + [
            dma((count,)),
            dma((count, ctx_count, 2)),
            dma((count, ctx_count)),
            four,
            four,
            four,
            four,
        ]
        + sems,
        compiler_params=pltpu.CompilerParams(
            collective_id=0, has_side_effects=True, vmem_limit_bytes=BIG_VMEM
        ),
        cost_estimate=pl.CostEstimate(
            flops=2_000_000_000, bytes_accessed=800_000_000, transcendentals=0
        ),
    )(*shards, rows)
    return results[:count], results[count], results[count + 1]


def tiles(width, size=256):
    return width // size, width % size


def each_tile(width, act, size=256):
    whole, rest = tiles(width, size)

    @pl.loop(0, whole)
    def _(index):
        act(pl.ds(pl.multiple_of(index * size, size), size))

    if rest:
        act(pl.ds(whole * size, rest))


def expert_kernel(ctx_count, rows_ref, info_ref, *refs):
    weight_refs, grads_ref = (refs[0:2], refs[2:4], refs[4:6]), refs[6]
    all_ref, slots_ref, hidden_ref, gate_back_ref, up_back_ref, back_ref, result_ref = refs[7:14]
    blocks, chosen, arrived, gate, up, down, grads = refs[14:21]
    hidden, gate_back, up_back, back, result = refs[21:26]
    weight_sem, grad_sem, slot_sem, side_sem, back_sem = refs[26:31]
    move = Dispatch(
        ctx_count, False, rows_ref, info_ref, all_ref, blocks, chosen, arrived, refs[31:]
    )
    slots, width = back.shape
    units = hidden.shape[1]
    order = [nearest(move.z, step) for step in range(ctx_count)]

    def block_at(step):
        block = order[0]
        for place in range(1, ctx_count):
            block = jnp.where(step == place, order[place], block)
        return block

    loads = []
    for which, target in enumerate((gate, up, down)):
        for place, source in enumerate(weight_refs[which]):
            side = lax.rem(move.f, 2)
            member = 1 - side if place else side
            half, piece_width = source.shape[1:]
            for origin in range(ctx_count):
                if which < 2:
                    start = pl.multiple_of((2 * origin + member) * half, half)
                    at = target.at[pl.ds(start, half)]
                else:
                    start = pl.multiple_of(member * half, half)
                    at = target.at[pl.ds(start, half), pl.ds(origin * piece_width, piece_width)]
                sem = weight_sem.at[which, place, origin]
                loads.append(pltpu.make_async_copy(source.at[origin], at, sem))

    def load_grads(step):
        slot = lax.rem(step, 2)
        return pltpu.make_async_copy(
            grads_ref.at[block_at(step)], grads.at[slot], grad_sem.at[slot]
        )

    def store_slots(block):
        return pltpu.make_async_copy(arrived.at[block], slots_ref.at[block], slot_sem.at[block])

    def store_sides(block):
        return [
            pltpu.make_async_copy(source, target.at[block], side_sem.at[place])
            for place, (source, target) in enumerate(
                ((hidden, hidden_ref), (gate_back, gate_back_ref), (up_back, up_back_ref))
            )
        ]

    def store_back(block):
        return pltpu.make_async_copy(back, back_ref.at[block], back_sem.at[0])

    def store_result(block):
        return pltpu.make_async_copy(result, result_ref.at[block], back_sem.at[1])

    greet(move.z, move.f, PEERS, ctx_count)
    move.begin()
    for load in loads:
        load.start()
    load_grads(0).start()
    along_order(move.z, ctx_count, 0, move.take)
    move.choose(order[0])
    along_order(move.z, ctx_count, 1, move.take)
    move.choose(order[1])
    for load in loads:
        load.wait()

    @pl.loop(0, ctx_count)
    def _(step):
        block = block_at(step)
        slot = lax.rem(step, 2)

        @pl.when(step + 1 < ctx_count)
        def _():
            load_grads(step + 1).start()

        load_grads(step).wait()
        move.await_slots(block)
        store_slots(block).start()

        @pl.when(step > 0)
        def _():
            for copy in store_sides(block):
                copy.wait()

        rows = arrived[block].reshape(slots, width)

        def hidden_tile(part):
            pre = jnp.dot(rows, gate[:, part], preferred_element_type=FULL)
            linear = jnp.dot(rows, up[:, part], preferred_element_type=FULL)
            grad = dot_last(grads[slot], down[part, :])
            sigma = jax.nn.sigmoid(pre)
            act = pre * sigma
            hidden[:, part] = (act * linear).astype(LOW)
            up_back[:, part] = (grad * act).astype(LOW)
            gate_back[:, part] = (
                grad * linear * (sigma * (1.0 + pre * (1.0 - sigma)))
            ).astype(LOW)

        each_tile(units, hidden_tile)
        for copy in store_sides(block):
            copy.start()

        @pl.when(step > 0)
        def _():
            store_back(block).wait()
            store_result(block).wait()

        def result_tile(part):
            total = jnp.dot(hidden[...], down[:, part], preferred_element_type=FULL)
            result[:, part] = total.astype(LOW)

        each_tile(width, result_tile)
        store_result(block).start()

        def back_tile(part):
            total = dot_last(gate_back[...], gate[part, :]) + dot_last(up_back[...], up[part, :])
            back[:, part] = total.astype(LOW)

        each_tile(width, back_tile)
        store_back(block).start()

        for later in range(2, ctx_count):

            @pl.when(step + 2 == later)
            def _():
                along_order(move.z, ctx_count, later, move.take)

        @pl.when(step + 2 < ctx_count)
        def _():
            move.choose(block_at(step + 2))

    for step in range(ctx_count):
        store_slots(order[step]).wait()
    for copy in store_sides(order[-1]):
        copy.wait()
    store_back(order[-1]).wait()
    store_result(order[-1]).wait()
    move.finish()


def expert_rows(rows, info, weights, grads, ctx_count, fsdp_count):
    count, width = rows.shape
    slots = grads.shape[1]
    share = slots // fsdp_count
    units = weights[0].shape[2]
    buffers, sems = dispatch_scratch(ctx_count, fsdp_count, count, share, width)
    dma = pltpu.SemaphoreType.DMA
    anywhere = pl.BlockSpec(memory_space=pl.ANY)
    low = lambda *shape: jax.ShapeDtypeStruct((ctx_count,) + shape, LOW)
    vmem = lambda *shape: pltpu.VMEM(shape, LOW)
    return pl.pallas_call(
        functools.partial(expert_kernel, ctx_count),
        out_shape=(
            low(count, width),
            low(fsdp_count, share, width),
            low(slots, units),
            low(slots, units),
            low(slots, units),
            low(slots, width),
            low(slots, width),
        ),
        in_specs=[anywhere, pl.BlockSpec(memory_space=pltpu.VMEM)] + [anywhere] * 7,
        out_specs=(anywhere,) * 7,
        scratch_shapes=buffers
        + [
            vmem(ctx_count, fsdp_count, share, width),
            vmem(width, units),
            vmem(width, units),
            vmem(units, width),
            vmem(2, slots, width),
            vmem(slots, units),
            vmem(slots, units),
            vmem(slots, units),
            vmem(slots, width),
            vmem(slots, width),
            dma((3, 2, ctx_count)),
            dma((2,)),
            dma((ctx_count,)),
            dma((3,)),
            dma((2,)),
        ]
        + sems,
        compiler_params=pltpu.CompilerParams(
            collective_id=4, has_side_effects=True, vmem_limit_bytes=BIG_VMEM
        ),
        cost_estimate=pl.CostEstimate(
            flops=60_000_000_000, bytes_accessed=400_000_000, transcendentals=3_000_000
        ),
    )(rows, info, *weights, grads)


class Combine:
    def __init__(
        self, ctx_count, gated, slots_ref, info_ref, extra_ref, out_ref, buffers, sems
    ):
        self.ctx_count, self.gated = ctx_count, gated
        self.slots_ref, self.info_ref = slots_ref, info_ref
        self.extra_ref, self.out_ref = extra_ref, out_ref
        self.arrived, self.extra, self.parts, self.from_z = buffers
        self.keep_sem, self.extra_sem, self.p_send, self.p_recv, self.z_send, self.z_recv = sems
        self.z, self.f = lax.axis_index("ctx"), lax.axis_index("fsdp")
        self.core = flip(self.f, 1)
        self.order = [nearest(self.z, ctx_count - 1 - step) for step in range(ctx_count)]

    def p_copy(self, block, place):
        to = toggled(self.f, PEERS[place])
        sems = (self.p_send.at[block, place], self.p_recv.at[block, place])
        return remote(
            self.slots_ref.at[block, to], self.arrived.at[block, self.f], *sems, self.z, to
        )

    def keep(self, block):
        source, target = self.slots_ref.at[block, self.f], self.arrived.at[block, self.f]
        return pltpu.make_async_copy(source, target, self.keep_sem.at[block])

    def load(self, step):
        return pltpu.make_async_copy(
            self.extra_ref.at[self.order[step]], self.extra, self.extra_sem
        )

    def place(self, way, block, z):
        return jnp.where(block == z, self.ctx_count, block) if way == 0 else block

    def send_along(self, step, way, to):
        block = self.order[step]
        sems = (self.z_send.at[step], self.z_recv.at[way, block])
        target = self.from_z.at[self.place(way, block, to)]
        return remote(self.parts.at[step], target, *sems, to, self.f)

    def z_arrived(self, block, way):
        at = self.from_z.at[self.place(way, block, self.z)]
        sems = (self.z_send.at[0], self.z_recv.at[way, block])
        remote(at, at, *sems, self.z, self.core).wait_recv()

    def start(self):
        for block in self.order:
            for place in range(len(PEERS)):
                self.p_copy(block, place).start()
            self.keep(block).start()
        self.load(0).start()

    def mix(self, block, target, *ways):
        slots = self.arrived.shape[1] * self.arrived.shape[2]
        choose = one_hot(self.info_ref[block], self.z, slots, self.gated)

        @pl.loop(0, target.shape[1], step=256)
        def _(start):
            part = pl.ds(pl.multiple_of(start, 256), 256)
            total = dot_first(choose, self.arrived[block, :, :, part].reshape(slots, 256))
            total = total + self.extra[:, part].astype(FULL)
            for way in ways:
                total = total + self.from_z[self.place(way, block, self.z), :, part].astype(FULL)
            target[:, part] = total.astype(target.dtype)

    def step(self, step):
        block, z, last = self.order[step], self.z, self.ctx_count - 1
        self.keep(block).wait()
        self.load(step).wait()
        for place in range(len(PEERS)):
            at = self.arrived.at[block, toggled(self.f, PEERS[place])]
            sems = (self.p_send.at[block, place], self.p_recv.at[block, place])
            remote(at, at, *sems, z, self.core).wait_recv()
        if step < last:
            target = self.parts.at[step]
            for way, above in ((1, True), (0, False)):
                heading = (block < z) if above else (block > z)
                has_more = (z < last) if above else (z > 0)

                @pl.when(heading & has_more)
                def _():
                    self.z_arrived(block, way)
                    self.mix(block, target, way)

                @pl.when(heading & jnp.logical_not(has_more))
                def _():
                    self.mix(block, target)

                @pl.when(heading)
                def _():
                    self.send_along(step, way, z - 1 if above else z + 1).start()

            self.load(step + 1).start()
            return

        @pl.when(z > 0)
        def _():
            self.z_arrived(block, 0)

        @pl.when(z < last)
        def _():
            self.z_arrived(block, 1)

        @pl.when(z == 0)
        def _():
            self.mix(block, self.out_ref, 1)

        @pl.when(z == last)
        def _():
            self.mix(block, self.out_ref, 0)

        @pl.when((z > 0) & (z < last))
        def _():
            self.mix(block, self.out_ref, 0, 1)

    def finish(self):
        for step in range(self.ctx_count):
            for place in range(len(PEERS)):
                self.p_copy(self.order[step], place).wait_send()
            if step < self.ctx_count - 1:
                self.send_along(step, 0, self.z).wait_send()


def combine_kernel(ctx_count, info_ref, *refs):
    streams = refs[0:4]
    rows_ref, grads_ref, hidden_ref, gate_back_ref, up_back_ref = refs[4:9]
    outs = refs[9:11]
    gate_grad_ref, up_grad_ref, down_grad_ref = refs[11:14]
    narrow, left, right, gate_tile, up_tile = refs[14:19]
    side_sem, tile_sem, store_sem = refs[19:22]
    buffers, sems = refs[22:30], refs[30:42]
    moves = [
        Combine(
            ctx_count,
            place == 1,
            streams[2 * place],
            info_ref,
            streams[2 * place + 1],
            outs[place],
            buffers[4 * place : 4 * place + 4],
            sems[6 * place : 6 * place + 6],
        )
        for place in range(2)
    ]
    greet(moves[0].z, moves[0].f, PEERS, ctx_count)
    tile_count = rows_ref.shape[1] // 256

    def sides(source, target, place):
        return pltpu.make_async_copy(source, target, side_sem.at[place])

    first_sides = [sides(gate_back_ref, left, 0), sides(up_back_ref, right, 1)]
    last_side = sides(hidden_ref, left, 2)

    def fetch(source, index):
        part = pl.ds(pl.multiple_of(index * 256, 256), 256)
        slot = lax.rem(index, 2)
        return pltpu.make_async_copy(source.at[:, part], narrow.at[slot], tile_sem.at[slot])

    def store(tile, target, place, index):
        part = pl.ds(pl.multiple_of(index * 256, 256), 256)
        return pltpu.make_async_copy(tile, target.at[part, :], store_sem.at[place])

    def products(source, begin, end, pairs):
        @pl.loop(begin, end)
        def _(index):
            @pl.when(index + 1 < tile_count)
            def _():
                fetch(source, index + 1).start()

            fetch(source, index).wait()
            turned = narrow[lax.rem(index, 2)]
            for place, (factor, tile, target) in enumerate(pairs):
                part = dot_first(turned, factor[...]).astype(LOW)

                @pl.when(index > 0)
                def _():
                    store(tile, target, place, index).wait()

                tile[...] = part
                store(tile, target, place, index).start()

    both = ((left, gate_tile, gate_grad_ref), (right, up_tile, up_grad_ref))
    alone = ((left, gate_tile, down_grad_ref),)
    half = tile_count // 2
    for copy in first_sides:
        copy.start()
    fetch(rows_ref, 0).start()
    for move in moves:
        move.start()
    for copy in first_sides:
        copy.wait()
    products(rows_ref, 0, half, both)
    moves[0].step(0)
    products(rows_ref, half, tile_count, both)
    for place, (factor, tile, target) in enumerate(both):
        store(tile, target, place, 0).wait()
    last_side.start()
    fetch(grads_ref, 0).start()
    moves[0].step(1)
    last_side.wait()
    products(grads_ref, 0, half, alone)
    moves[0].step(2)
    products(grads_ref, half, tile_count, alone)
    store(gate_tile, down_grad_ref, 0, 0).wait()
    for step in range(3, ctx_count):
        moves[0].step(step)
    for step in range(ctx_count):
        moves[1].step(step)
    for move in moves:
        move.finish()


def combine_rows(
    slots, extra, out_slots, out_extra, info, sides, ctx_count, fsdp_count
):
    share, width = slots.shape[2:]
    count = extra.shape[1]
    total, units = sides[2].shape
    dma = pltpu.SemaphoreType.DMA
    anywhere = pl.BlockSpec(memory_space=pl.ANY)
    resident = pl.BlockSpec(memory_space=pltpu.VMEM)
    vmem = lambda *shape: pltpu.VMEM(shape, LOW)
    buffers = [
        vmem(ctx_count, fsdp_count, share, width),
        vmem(count, width),
        vmem(ctx_count - 1, count, width),
        vmem(ctx_count + 1, count, width),
    ]
    sems = [
        dma((ctx_count,)),
        dma,
        dma((ctx_count, len(PEERS))),
        dma((ctx_count, len(PEERS))),
        dma((ctx_count - 1,)),
        dma((2, ctx_count)),
    ]
    return pl.pallas_call(
        functools.partial(combine_kernel, ctx_count),
        out_shape=(jax.ShapeDtypeStruct((count, width), FULL),) * 2
        + (jax.ShapeDtypeStruct((width, units), LOW),) * 3,
        in_specs=[resident] + [anywhere] * 9,
        out_specs=(resident,) * 2 + (anywhere,) * 3,
        scratch_shapes=[
            vmem(2, total, 256),
            vmem(total, units),
            vmem(total, units),
            vmem(256, units),
            vmem(256, units),
            dma((3,)),
            dma((2,)),
            dma((2,)),
        ]
        + buffers * 2
        + sems * 2,
        compiler_params=pltpu.CompilerParams(
            collective_id=3, has_side_effects=True, vmem_limit_bytes=BIG_VMEM
        ),
        cost_estimate=pl.CostEstimate(
            flops=40_000_000_000, bytes_accessed=600_000_000, transcendentals=0
        ),
    )(info, slots, extra, out_slots, out_extra, *sides)


def mm(subscripts, left, right):
    return jnp.einsum(subscripts, left, right, preferred_element_type=FULL)


def member_pairs(fsdp_count, members, step):
    return [
        (f, f // members * members + (f % members + step) % members) for f in range(fsdp_count)
    ]


def by_member(own, others, member, members):
    if members == 2:
        first = member == 0
        return jnp.stack([jnp.where(first, own, others[0]), jnp.where(first, others[0], own)])
    stack = jnp.stack([own] + others)
    return jnp.take(stack, (member - jnp.arange(members)) % members, axis=0)


def part_of(array, member, step, members):
    return lax.dynamic_index_in_dim(array, (member + step) % members, 0, keepdims=False)


def swap_parts(array, members, fsdp_count):
    member = lax.axis_index("fsdp") % members
    others = [
        lax.ppermute(
            part_of(array, member, step, members), "fsdp", member_pairs(fsdp_count, members, step)
        )
        for step in range(1, members)
    ]
    return by_member(part_of(array, member, 0, members), others, member, members)


def share_parts(array, members, fsdp_count):
    member = lax.axis_index("fsdp") % members
    others = [
        lax.ppermute(array, "fsdp", member_pairs(fsdp_count, members, step))
        for step in range(1, members)
    ]
    return by_member(array, others, member, members)


def sum_parts(array, members, fsdp_count):
    member = lax.axis_index("fsdp") % members
    total = part_of(array, member, 0, members).astype(FULL)
    for step in range(1, members):
        total = total + lax.ppermute(
            part_of(array, member, step, members), "fsdp", member_pairs(fsdp_count, members, step)
        ).astype(FULL)
    return total.astype(LOW)


def routing(info, z, slots, gated):
    at = jnp.arange(slots, dtype=jnp.int32).astype(FULL)[:, None, None]
    hit = (info[:, None, COLUMN_AT : COLUMN_AT + TOP].swapaxes(2, 3) == at.reshape(-1, 1, 1)) & (
        info[:, None, :TOP].swapaxes(2, 3) == z.astype(FULL)
    )
    values = info[:, None, GATE_AT : GATE_AT + TOP].swapaxes(2, 3) if gated else 1.0
    return jnp.sum(jnp.where(hit, values, 0.0), axis=3).astype(LOW)


def swap_slots(slots):
    return lax.all_to_all(slots, "fsdp", split_axis=1, concat_axis=1, tiled=True)


def send_rows(rows, info, slots, gated, ctx_count, fsdp_count):
    every = lax.all_gather(rows, "ctx", axis=0)
    choose = routing(info, lax.axis_index("ctx"), slots, gated)
    chosen = mm("bst,btd->bsd", choose, every).astype(LOW)
    return every, swap_slots(chosen.reshape(ctx_count, fsdp_count, -1, rows.shape[1]))


def run_expert(rows, info, pieces, grads, ctx_count, fsdp_count):
    members = ctx_count // EXP_DEV
    if (ctx_count, fsdp_count) == (4, 8):
        pairs = member_pairs(fsdp_count, members, 1)
        weights = []
        for piece in pieces:
            weights += [piece, lax.ppermute(piece, "fsdp", pairs)]
        return expert_rows(rows, info, weights, grads, ctx_count, fsdp_count)
    whole = [share_parts(piece, members, fsdp_count).swapaxes(0, 1) for piece in pieces]
    units = whole[0].shape[3]
    gate, up = [item.reshape(-1, units) for item in whole[:2]]
    down = whole[2].transpose(1, 2, 0, 3).reshape(units, -1)
    every, arrived = send_rows(rows, info, grads.shape[1], False, ctx_count, fsdp_count)
    slots = arrived.reshape(grads.shape)
    pre = mm("bsd,df->bsf", slots, gate)
    linear = mm("bsd,df->bsf", slots, up)
    act, slope = silu_slope(pre)
    grad = mm("bsd,fd->bsf", grads, down)
    hidden = (act * linear).astype(LOW)
    up_back = (grad * act).astype(LOW)
    gate_back = (grad * linear * slope).astype(LOW)
    back = (mm("bsf,df->bsd", gate_back, gate) + mm("bsf,df->bsd", up_back, up)).astype(LOW)
    result = mm("bsf,fd->bsd", hidden, down).astype(LOW)
    return every, arrived, hidden, gate_back, up_back, back, result


def return_slots(slots, info, extra, gated):
    back = swap_slots(slots).reshape(slots.shape[0], -1, slots.shape[3])
    choose = routing(info, lax.axis_index("ctx"), back.shape[1], gated)
    total = (mm("bst,bsd->btd", choose, back) + extra).astype(LOW)
    return lax.psum_scatter(total, "ctx", scatter_dimension=0, tiled=False).astype(FULL)


def return_both(slots, extra, out_slots, out_extra, info, sides, ctx_count, fsdp_count):
    extra, out_extra = extra.astype(LOW), out_extra.astype(LOW)
    if (ctx_count, fsdp_count) == (4, 8):
        return combine_rows(
            slots, extra, out_slots, out_extra, info, sides, ctx_count, fsdp_count
        )
    rows, grads, hidden, gate_back, up_back = sides
    return (
        return_slots(slots, info, extra, False),
        return_slots(out_slots, info, out_extra, True),
        mm("sd,sf->df", rows, gate_back).astype(LOW),
        mm("sd,sf->df", rows, up_back).astype(LOW),
        mm("sd,sf->df", grads, hidden).astype(LOW),
    )


def swap_experts(weight, members, fsdp_count):
    pieces = weight.reshape((EXP_DEV, members, weight.shape[1] // members) + weight.shape[2:])
    pieces = swap_parts(pieces.swapaxes(0, 1), members, fsdp_count)
    return pieces.reshape((-1,) + pieces.shape[2:])


def gather_all(items, rows, slots, ctx_count, fsdp_count):
    if (ctx_count, fsdp_count) == (4, 8):
        return gather_arrays(items, rows, slots, ctx_count, fsdp_count)
    results = []
    for kind, shard in items:
        if kind == "line":
            shard = lax.all_to_all(shard, "ctx", split_axis=0, concat_axis=0, tiled=True)
            result = lax.all_gather(shard, "fsdp", axis=1)
        elif kind == "plane":
            result = lax.all_gather(shard, "fsdp", axis=0)[None]
        elif kind == "column":
            result = lax.all_gather(shard, "ctx", axis=0)
        elif kind == "expert":
            result = along_line(swap_experts(shard, ctx_count // EXP_DEV, fsdp_count))
        else:
            result = lax.all_gather(shard, ("ctx", "fsdp"), axis=0)
            result = result.reshape((ctx_count, fsdp_count) + shard.shape)
        results.append(result)
    return (results,) + send_rows(rows, results[0], slots, True, ctx_count, fsdp_count)


def scatter_all(items, ctx_count, fsdp_count):
    items = [(kind, grad.astype(LOW)) for kind, grad in items]
    if (ctx_count, fsdp_count) == (4, 8):
        return scatter_arrays(items, ctx_count, fsdp_count)
    results = []
    for kind, grad in items:
        if kind == "line":
            grad = grad.reshape(ctx_count, fsdp_count, -1, grad.shape[1]).swapaxes(0, 1)
            grad = lax.psum_scatter(grad, "fsdp", scatter_dimension=0, tiled=False)
            results.append(along_line(grad))
        else:
            total = lax.psum_scatter(grad, ("ctx", "fsdp"), scatter_dimension=0, tiled=True)
            results.append(total.astype(FULL))
    return results


def along_line(array):
    return lax.all_to_all(array, "ctx", split_axis=0, concat_axis=0, tiled=True)


def after(values, *others):
    tied = lax.optimization_barrier((tuple(values), others))
    return tied[0]


def local(
    tokens,
    routes,
    gate_values,
    cotangent,
    attention_gain,
    query_weight,
    latent_weight,
    latent_gain,
    expand_weight,
    output_weight,
    feedforward_gain,
    shared_gate,
    shared_up,
    shared_down,
    expert_gate,
    expert_up,
    expert_down,
):
    row_count = tokens.shape[1]
    model_width = tokens.shape[2]
    ctx_count = lax.axis_size("ctx")
    fsdp_count = lax.axis_size("fsdp")
    device_count = ctx_count * fsdp_count
    experts_total = EXP_DEV * fsdp_count
    capacity = row_count * TOP * 4 // (3 * experts_total)
    members = ctx_count // EXP_DEV
    plane_experts = experts_total // ctx_count
    plane_slots = plane_experts * capacity
    share = capacity // members
    sequence = ctx_count * row_count
    z = lax.axis_index("ctx")
    score_scale = (NOPE + ROPE) ** (-0.5)
    source = tokens[0].astype(FULL)
    cot_low = cotangent[0]
    cot_full = cot_low.astype(FULL)
    positions = stored_positions(
        z * row_count + jnp.arange(row_count, dtype=jnp.int32), row_count, 2 * ctx_count
    )
    dense_rows = latent_weight.shape[0]
    gain_rows = latent_gain.shape[0]
    rotary_end = LATENT + ROPE
    hidden_units = expert_gate.shape[2]
    shared_units = shared_gate.shape[1] // ctx_count

    down_swapped = swap_experts(expert_down, members, fsdp_count)

    local_routes = routes[0]
    expert_index = jnp.arange(experts_total, dtype=jnp.int32)
    member_of = (local_routes[..., None] == expert_index).astype(FULL)
    counts = jnp.sum(member_of, axis=1)
    before = jnp.cumsum(counts, axis=0) - counts
    within = jnp.sum(member_of * before[:, None, :], axis=-1).astype(jnp.int32)
    info = jnp.zeros((INFO_ROWS, row_count), FULL)
    info = info.at[:TOP].set((local_routes % ctx_count).astype(FULL).T)
    info = info.at[COLUMN_AT : COLUMN_AT + TOP].set(
        (local_routes // ctx_count * capacity + within).astype(FULL).T
    )
    info = info.at[GATE_AT : GATE_AT + TOP].set(gate_values[0].T)

    tail = jnp.concatenate(
        [
            latent_weight,
            attention_gain[:, None],
            feedforward_gain[:, None],
            jnp.pad(latent_gain, (0, dense_rows - gain_rows))[:, None],
            jnp.zeros((dense_rows, 256 - ROPE - 3), LOW),
        ],
        axis=1,
    )

    def by_line(weight):
        return weight.reshape(dense_rows, ctx_count, shared_units).swapaxes(0, 1)

    dense = (
        info,
        query_weight,
        tail,
        expand_weight,
        output_weight,
        by_line(shared_gate),
        by_line(shared_up),
        shared_down,
        expert_gate,
        expert_up,
    )
    kinds = ("column", "all", "all", "all", "all", "line", "line", "plane", "expert", "expert")
    gathered, all_cot, arrived_grad = gather_all(
        list(zip(kinds, dense)), cot_low, plane_slots, ctx_count, fsdp_count
    )
    all_info = gathered[0]
    full_query, full_tail, full_expand, full_output, full_sgate, full_sup, full_sdown = [
        item.reshape(-1, item.shape[-1]) for item in gathered[1:-2]
    ]
    gate_moved, up_moved = gathered[-2:]
    full_latent = full_tail[:, :rotary_end]
    gain_one = full_tail[:, rotary_end].astype(FULL)
    gain_two = full_tail[:, rotary_end + 1].astype(FULL)
    gain_latent = (
        full_tail[:, rotary_end + 2].reshape(device_count, dense_rows)[:, :gain_rows]
    ).reshape(LATENT).astype(FULL)

    all_cot = all_cot.reshape(sequence, model_width)
    arrived_grad = arrived_grad.reshape(ctx_count, plane_slots, model_width)

    plain_one, inverse_one = norm_forward(source)
    normed = (plain_one * gain_one).astype(LOW)
    (query_raw,) = after((jnp.dot(normed, full_query, preferred_element_type=FULL),))
    query_raw = query_raw.reshape(row_count, HEADS, NOPE + ROPE)
    query_nope = query_raw[:, :, :NOPE].astype(LOW)
    query_rope = rotary(query_raw[:, :, NOPE:], positions, 1.0).astype(LOW)
    latent_raw = jnp.dot(normed, full_latent, preferred_element_type=FULL)
    plain_latent, inverse_latent = norm_forward(latent_raw[:, :LATENT])
    latent_norm = (plain_latent * gain_latent).astype(LOW)
    key_rope = rotary(latent_raw[:, LATENT:], positions, 1.0).astype(LOW)
    half_rows = row_count // 2
    pad_rope = ((0, 0), (0, 128 - ROPE))
    keys = lax.all_gather(
        jnp.concatenate([latent_norm, jnp.pad(key_rope, pad_rope)], axis=1), "ctx", axis=0
    )
    keys = keys.reshape(ctx_count, 2, half_rows, LATENT + 128)
    keys = jnp.concatenate([keys[:, 0], keys[::-1, 1]]).reshape(sequence, LATENT + 128)
    all_latent, all_keys = (keys[:, :LATENT], keys[:, LATENT:])
    expand = full_expand.reshape(LATENT, HEADS, NOPE + VDIM)
    expand_key = expand[:, :, :NOPE]
    expand_value = expand[:, :, NOPE:]
    query_latent = mm("thd,chd->htc", query_nope, expand_key).astype(LOW)
    (down_swapped,) = after((down_swapped,), normed)
    down_moved = along_line(down_swapped)
    query_turned = jnp.pad(query_rope.swapaxes(0, 1), ((0, 0),) + pad_rope)
    latent_out, log_total = attend(
        query_latent, query_turned, all_latent, all_keys, ctx_count, score_scale
    )
    values_out = (
        mm("htc,chv->thv", latent_out, expand_value).astype(LOW).reshape(row_count, HEADS * VDIM)
    )
    middle = source + jnp.dot(values_out, full_output, preferred_element_type=FULL)
    plain_two, inverse_two = norm_forward(middle)
    second = (plain_two * gain_two).astype(LOW)

    (down_moved,) = after((down_moved,), latent_out)
    (second_sent,) = after((second,), down_moved)
    all_second, arrived_rows, hidden_act, gate_back, up_back, arrived_back, result = run_expert(
        second_sent,
        all_info,
        (gate_moved, up_moved, down_moved),
        arrived_grad,
        ctx_count,
        fsdp_count,
    )
    all_second = all_second.reshape(sequence, model_width)
    hidden_act, gate_back, up_back = [
        item.reshape(-1, hidden_units) for item in (hidden_act, gate_back, up_back)
    ]
    shared_g = jnp.dot(all_second, full_sgate, preferred_element_type=FULL)
    shared_u = jnp.dot(all_second, full_sup, preferred_element_type=FULL)
    shared_silu, shared_slope = silu_slope(shared_g)
    shared_hidden = (shared_silu * shared_u).astype(LOW)
    shared_hidden_grad = mm("td,fd->tf", all_cot, full_sdown)
    sup_back = (shared_hidden_grad * shared_silu).astype(LOW)
    sgate_back = (shared_hidden_grad * shared_u * shared_slope).astype(LOW)
    shared_second_grad = mm("tf,df->td", sgate_back, full_sgate) + mm(
        "tf,df->td", sup_back, full_sup
    )
    slots_shape = (ctx_count, fsdp_count, share, model_width)
    rows_shape = (ctx_count, row_count, model_width)
    shared_out = jnp.dot(shared_hidden, full_sdown, preferred_element_type=FULL)
    second_grad, out_sum, gate_grad, up_grad, down_grad = return_both(
        arrived_back.reshape(slots_shape),
        shared_second_grad.reshape(rows_shape),
        result.reshape(slots_shape),
        shared_out.reshape(rows_shape),
        all_info,
        (
            arrived_rows.reshape(-1, model_width),
            arrived_grad.reshape(-1, model_width),
            hidden_act,
            gate_back,
            up_back,
        ),
        ctx_count,
        fsdp_count,
    )
    layer_out = (middle + out_sum).astype(LOW)[None]

    def line_sum(grad):
        grad = grad.reshape(ctx_count, members, -1, hidden_units).swapaxes(0, 1)
        return sum_parts(grad, members, fsdp_count)

    gate_sum, up_sum, down_sum = (line_sum(gate_grad), line_sum(up_grad), line_sum(down_grad))
    gate_returned = along_line(gate_sum)
    sgate_back, sup_back = after((sgate_back, sup_back), gate_sum)
    shared_hidden, sgate_back, sup_back = after(
        (shared_hidden, sgate_back, sup_back), second_grad
    )
    sgate_grad = mm("td,tf->df", all_second, sgate_back).astype(LOW)
    sup_grad = mm("td,tf->df", all_second, sup_back).astype(LOW)
    sdown_grad = mm("tf,td->fd", shared_hidden, all_cot).astype(LOW)
    (second_grad,) = after(
        (second_grad,), gate_sum, up_sum, down_sum, sgate_grad, sup_grad, sdown_grad
    )
    sdown_grad = lax.psum_scatter(sdown_grad, "fsdp", scatter_dimension=0, tiled=True)

    middle_part, gain_two_grad = norm_backward(second_grad, plain_two, inverse_two, gain_two)
    middle_grad = cot_full + middle_part
    attended_grad = middle_grad.astype(LOW)
    output_weight_grad = mm("tv,td->vd", values_out, attended_grad)
    values_grad = (
        mm("td,vd->tv", attended_grad, full_output).astype(LOW).reshape(row_count, HEADS, VDIM)
    )
    latent_out_grad = mm("thv,chv->htc", values_grad, expand_value).astype(LOW)
    (latent_out_grad,) = after((latent_out_grad,), gate_returned)
    (up_sum,) = after((up_sum,), gate_returned, latent_out_grad)
    up_returned = along_line(up_sum)
    query_latent_grad, turned_grad, all_latent_grad, all_keys_grad = attend_back(
        query_latent,
        query_turned,
        all_latent,
        all_keys,
        latent_out,
        log_total,
        latent_out_grad,
        ctx_count,
        score_scale,
    )
    query_rope_grad = turned_grad[:, :, :ROPE].swapaxes(0, 1)
    keys_part = jnp.concatenate([all_latent_grad, all_keys_grad[:, :ROPE]], axis=1)
    keys_part = keys_part.reshape(2, ctx_count, half_rows, LATENT + ROPE)
    keys_part = jnp.stack([keys_part[0], keys_part[1, ::-1]], axis=1)
    keys_part = lax.psum_scatter(
        keys_part.reshape(sequence, LATENT + ROPE).astype(LOW),
        "ctx",
        scatter_dimension=0,
        tiled=True,
    ).astype(FULL)
    latent_grad, keys_grad = (keys_part[:, :LATENT], keys_part[:, LATENT:])
    expand_value_grad = mm("htc,thv->chv", latent_out, values_grad)

    sdown_grad = sdown_grad.astype(FULL)

    query_nope_grad = mm("htc,chd->thd", query_latent_grad, expand_key)
    expand_key_grad = mm("thd,htc->chd", query_nope, query_latent_grad)
    expand_grad = jnp.concatenate([expand_key_grad, expand_value_grad], axis=-1).reshape(
        LATENT, HEADS * (NOPE + VDIM)
    )
    query_grad = (
        jnp.concatenate([query_nope_grad, rotary(query_rope_grad, positions, -1.0)], axis=-1)
        .astype(LOW)
        .reshape(row_count, HEADS * (NOPE + ROPE))
    )
    latent_part_grad, gain_latent_grad = norm_backward(
        latent_grad, plain_latent, inverse_latent, gain_latent
    )
    latent_raw_grad = jnp.concatenate(
        [latent_part_grad, rotary(keys_grad, positions, -1.0)], axis=-1
    ).astype(LOW)
    query_weight_grad = mm("td,tq->dq", normed, query_grad)
    latent_weight_grad = mm("td,tq->dq", normed, latent_raw_grad)
    normed_grad = mm("tq,dq->td", query_grad, full_query) + mm(
        "tq,dq->td", latent_raw_grad, full_latent
    )
    source_part, gain_one_grad = norm_backward(normed_grad, plain_one, inverse_one, gain_one)
    tokens_grad = (middle_grad + source_part)[None]

    gain_latent_column = jnp.pad(
        gain_latent_grad.reshape(device_count, gain_rows), ((0, 0), (0, dense_rows - gain_rows))
    ).reshape(model_width)
    gains_grad = jnp.stack([gain_one_grad, gain_two_grad, gain_latent_column], axis=1)
    gains_grad = jnp.pad(gains_grad, ((0, 0), (0, 125)))
    (down_sum,) = after((down_sum,), up_returned, query_nope_grad)
    down_returned = along_line(down_sum)
    (gains_grad,) = after((gains_grad,), up_returned)
    dense_grads = (
        query_weight_grad,
        latent_weight_grad,
        gains_grad,
        expand_grad,
        output_weight_grad,
        sgate_grad,
        sup_grad,
    )
    kinds = ("all",) * 5 + ("line",) * 2
    query_sum, latent_sum, gains_sum, expand_sum, output_sum, sgate_sum, sup_sum = scatter_all(
        list(zip(kinds, dense_grads)), ctx_count, fsdp_count
    )

    def joined(pieces):
        return pieces.swapaxes(0, 1).reshape(dense_rows, -1).astype(FULL)

    def owned(moved):
        moved = moved.reshape((members, EXP_DEV) + moved.shape[1:])
        moved = swap_parts(moved, members, fsdp_count).swapaxes(0, 1)
        return moved.reshape(EXP_DEV, -1, hidden_units).astype(FULL)

    expert_grads = (
        owned(gate_returned),
        owned(up_returned),
        owned(down_returned).swapaxes(1, 2),
    )
    return (
        layer_out,
        tokens_grad,
        gains_sum[:, 0],
        query_sum,
        latent_sum,
        gains_sum[:gain_rows, 2],
        expand_sum,
        output_sum,
        gains_sum[:, 1],
        joined(sgate_sum),
        joined(sup_sum),
        sdown_grad,
        expert_grads[0],
        expert_grads[1],
        expert_grads[2],
    )


def solution(mesh):
    in_specs = (
        P("fsdp", "ctx", None),
        P("fsdp", "ctx", None),
        P("fsdp", "ctx", None),
        P("fsdp", "ctx", None),
        P(("ctx", "fsdp")),
        P(("ctx", "fsdp"), None),
        P(("ctx", "fsdp"), None),
        P(("ctx", "fsdp")),
        P(("ctx", "fsdp"), None),
        P(("ctx", "fsdp"), None),
        P(("ctx", "fsdp")),
        P(("ctx", "fsdp"), None),
        P(("ctx", "fsdp"), None),
        P(("ctx", "fsdp"), None),
        P("fsdp", "ctx", None),
        P("fsdp", "ctx", None),
        P("fsdp", None, "ctx"),
    )
    out_specs = (
        P("fsdp", "ctx", None),
        P("fsdp", "ctx", None),
        P(("ctx", "fsdp")),
        P(("ctx", "fsdp"), None),
        P(("ctx", "fsdp"), None),
        P(("ctx", "fsdp")),
        P(("ctx", "fsdp"), None),
        P(("ctx", "fsdp"), None),
        P(("ctx", "fsdp")),
        P(("ctx", "fsdp"), None),
        P(("ctx", "fsdp"), None),
        P(("ctx", "fsdp"), None),
        P("fsdp", "ctx", None),
        P("fsdp", "ctx", None),
        P("fsdp", None, "ctx"),
    )
    return jax.shard_map(local, mesh=mesh, in_specs=in_specs, out_specs=out_specs, check_vma=False)
```

```python
import functools

import jax
import jax.numpy as jnp
from jax import lax
from jax.experimental import pallas as pl
from jax.experimental.pallas import tpu as pltpu
from jax.sharding import PartitionSpec as P

HEADS = 16
NOPE = 128
ROPE = 64
LATENT = 512
VDIM = 128
TOP = 6
EXP_DEV = 2


epsilon = 1e-06
rope_base = 10000.0
masked_score = -1e30


def stored_positions(row_index, per_device, block_count):
    device = row_index // per_device
    within = row_index % per_device
    half_block = per_device // 2
    return jnp.where(
        within >= half_block,
        (block_count - 1 - device) * half_block + within - half_block,
        device * half_block + within,
    )


def rotary(values, positions, direction):
    half_rope = values.shape[-1] // 2
    frequency = rope_base ** (-jnp.arange(half_rope, dtype=jnp.float32) / half_rope)
    angles = positions.astype(jnp.float32)[:, None] * frequency[None, :]
    cosine_table = jnp.cos(angles)
    sine_table = direction * jnp.sin(angles)
    if values.ndim == 3:
        cosine_table = cosine_table[:, None, :]
        sine_table = sine_table[:, None, :]
    front_half = values[..., :half_rope]
    back_half = values[..., half_rope:]
    return jnp.concatenate(
        [
            front_half * cosine_table - back_half * sine_table,
            back_half * cosine_table + front_half * sine_table,
        ],
        axis=-1,
    )


def norm_forward(values):
    inverse = lax.rsqrt(jnp.mean(values * values, axis=-1, keepdims=True) + epsilon)
    return (values * inverse, inverse)


def norm_backward(normed_grad, plain, inverse, gain):
    gain_grad = jnp.sum(normed_grad * plain, axis=0)
    scaled = normed_grad * gain
    return (
        inverse * (scaled - plain * jnp.mean(scaled * plain, axis=-1, keepdims=True)),
        gain_grad,
    )


def silu_slope(values):
    sigma = jax.nn.sigmoid(values)
    return (values * sigma, sigma * (1.0 + values * (1.0 - sigma)))


LOW = jnp.bfloat16
FULL = jnp.float32


MESH_ID = pl.DeviceIdType.MESH
BIG_VMEM = 60 * 1024 * 1024


def flip(index, bit):
    return index + bit - 2 * bit * lax.rem(lax.div(index, bit), 2)


def toggled(index, mask):
    for bit in (1, 2, 4):
        if mask & bit:
            index = flip(index, bit)
    return index


def nearest(z, step):
    upper = lax.div(z, 2)
    if step == 0:
        return z
    if step == 1:
        return z + 1 - 2 * upper
    if step == 2:
        return 2 - 2 * lax.rem(z, 2) + upper
    return 3 - 3 * upper


def outermost(z, ctx_count):
    return (z == 0) | (z == ctx_count - 1)


def along_order(z, ctx_count, step, take):
    ends = outermost(z, ctx_count)
    if step <= 1:
        take(step)
    if step == 1:

        @pl.when(jnp.logical_not(ends))
        def _():
            take(2)

    if step >= 2:

        @pl.when(ends)
        def _():
            take(step)

        if step + 1 < ctx_count:

            @pl.when(jnp.logical_not(ends))
            def _():
                take(step + 1)


def remote(source, target, send, receive, z, f):
    return pltpu.make_async_remote_copy(
        src_ref=source,
        dst_ref=target,
        send_sem=send,
        recv_sem=receive,
        device_id={"ctx": z, "fsdp": f},
        device_id_type=MESH_ID,
    )


def greet(z, f, masks, ctx_count, whole_line=False):
    barrier = pltpu.get_barrier_semaphore()

    def hello(to_z, to_f):
        pl.semaphore_signal(
            barrier, inc=1, device_id={"ctx": to_z, "fsdp": to_f}, device_id_type=MESH_ID
        )

    for mask in masks:
        hello(z, toggled(f, mask))
    if whole_line:
        for step in range(1, ctx_count):
            hello(lax.rem(z + step, ctx_count), f)
            hello(lax.rem(z + step, ctx_count), flip(f, 1))
        pl.semaphore_wait(barrier, len(masks) + 2 * (ctx_count - 1))
        return

    @pl.when(z > 0)
    def _():
        hello(z - 1, f)

    @pl.when(z < ctx_count - 1)
    def _():
        hello(z + 1, f)

    along = lax.div(z + ctx_count - 1, ctx_count) + lax.div(2 * ctx_count - 2 - z, ctx_count)
    pl.semaphore_wait(barrier, len(masks) + along)


def both_ways(z, block, ctx_count, act):
    @pl.when((block <= z) & (z < ctx_count - 1))
    def _():
        act(0, z + 1)

    @pl.when((block >= z) & (z > 0))
    def _():
        act(1, z - 1)


def halves(rows, width):
    if rows % 32 == 0:
        return tuple((pl.ds(start, rows // 2), slice(None)) for start in (0, rows // 2))
    return tuple((slice(None), pl.ds(start, width // 2)) for start in (0, width // 2))


def add_rows(target, rows, *terms):
    @pl.loop(0, rows, step=16)
    def _(start):
        part = pl.ds(pl.multiple_of(start, 16), 16)
        total = terms[0][part, :].astype(FULL)
        for term in terms[1:]:
            total = total + term[part, :].astype(FULL)
        target[part, :] = total.astype(target.dtype)


def scatter_kernel(ctx_count, kinds, *refs):
    count = len(kinds)
    grads, outs = refs[:count], refs[count : 2 * count]
    banks = [refs[(2 + kind) * count : (3 + kind) * count] for kind in range(7)]
    load_sem, c_send, c_recv, p_send, p_recv, z_send, z_recv = refs[9 * count :]
    z, f = lax.axis_index("ctx"), lax.axis_index("fsdp")
    side = lax.rem(f, 2)
    chip = lax.div(f, 2)
    core, x_near, y_near = flip(f, 1), flip(f, 2), flip(f, 4)
    x_chip, y_chip = flip(chip, 1), flip(chip, 2)
    far_chip = flip(x_chip, 2)
    greet(z, f, (1, 2, 4), ctx_count, True)
    order = [nearest(z, ctx_count - 1 - step) for step in range(ctx_count)]

    def work(item):
        grad_ref, out_ref = grads[item], outs[item]
        mine, from_core, from_x, from_y, half_x, half_y, from_z = [bank[item] for bank in banks]
        rows, width = out_ref.shape[-2:]
        left, right = halves(rows, width)
        half_rows = half_x.shape[1]

        def load(block):
            return pltpu.make_async_copy(
                grad_ref.at[block, :, side], mine.at[block], load_sem.at[item, block]
            )

        def c_copy(block):
            return remote(
                grad_ref.at[block, :, 1 - side],
                from_core.at[block],
                c_send.at[item, block],
                c_recv.at[item, block],
                z,
                core,
            )

        def p_copy(block, which):
            source, target, to = (
                (mine.at[(block, far_chip) + left], half_y.at[block], y_near),
                (mine.at[(block, far_chip) + right], half_x.at[block], x_near),
                (mine.at[block, x_chip], from_x.at[block], x_near),
                (mine.at[block, y_chip], from_y.at[block], y_near),
            )[which]
            sems = (p_send.at[item, block, which], p_recv.at[item, block, which])
            return remote(source, target, *sems, z, to)

        def z_copy(block, way, target):
            return remote(
                mine.at[block, chip],
                from_z.at[way, block],
                z_send.at[item, block],
                z_recv.at[item, way, block],
                target,
                f,
            )

        def z_arrived(block, way):
            at = from_z.at[way, block]
            sems = (z_send.at[item, block], z_recv.at[item, way, block])
            remote(at, at, *sems, z, core).wait_recv()

        def piece(block):
            sems = (z_send.at[item, block], z_recv.at[item, 0, z])
            return remote(mine.at[block, chip], out_ref.at[z], *sems, block, f)

        def start(step):
            c_copy(order[step]).start()
            load(order[step]).start()

        def first(step):
            block = order[step]
            load(block).wait()
            c_copy(block).wait_recv()
            far_part = mine.at[block, far_chip]
            add_rows(far_part, rows, far_part, from_core.at[block, far_chip])
            p_copy(block, 0).start()
            p_copy(block, 1).start()

        def second(step):
            block = order[step]
            x_part, y_part = mine.at[block, x_chip], mine.at[block, y_chip]
            add_rows(x_part, rows, x_part, from_core.at[block, x_chip])
            add_rows(y_part, rows, y_part, from_core.at[block, y_chip])
            p_copy(block, 0).wait_recv()
            x_left = mine.at[(block, x_chip) + left]
            add_rows(x_left, half_rows, x_left, half_y.at[block])
            p_copy(block, 2).start()
            p_copy(block, 1).wait_recv()
            y_right = mine.at[(block, y_chip) + right]
            add_rows(y_right, half_rows, y_right, half_x.at[block])
            p_copy(block, 3).start()

        def third(step):
            block = order[step]
            p_copy(block, 2).wait_recv()
            p_copy(block, 3).wait_recv()
            own = mine.at[block, chip]
            terms = (own, from_core.at[block, chip], from_x.at[block], from_y.at[block])
            if kinds[item] == "line":
                add_rows(out_ref.at[z] if step == ctx_count - 1 else own, rows, *terms)
                if step < ctx_count - 1:
                    piece(block).start()
                return

            if step == ctx_count - 1:

                @pl.when(z > 0)
                def _():
                    z_arrived(block, 0)

                @pl.when(z < ctx_count - 1)
                def _():
                    z_arrived(block, 1)

                @pl.when(z == 0)
                def _():
                    add_rows(out_ref, rows, *terms, from_z.at[1, block])

                @pl.when(z == ctx_count - 1)
                def _():
                    add_rows(out_ref, rows, *terms, from_z.at[0, block])

                @pl.when((z > 0) & (z < ctx_count - 1))
                def _():
                    add_rows(out_ref, rows, *terms, from_z.at[0, block], from_z.at[1, block])

                return

            for way, above in ((1, True), (0, False)):
                heading = (block < z) if above else (block > z)
                has_more = (z < ctx_count - 1) if above else (z > 0)

                @pl.when(heading & has_more)
                def _():
                    z_arrived(block, way)
                    add_rows(own, rows, *terms, from_z.at[way, block])

                @pl.when(heading & jnp.logical_not(has_more))
                def _():
                    add_rows(own, rows, *terms)

                @pl.when(heading)
                def _():
                    z_copy(block, way, z - 1 if above else z + 1).start()

        def finish(step):
            block = order[step]
            c_copy(block).wait_send()
            for which in range(4):
                p_copy(block, which).wait_send()
            if step == ctx_count - 1:
                return
            if kinds[item] == "line":
                piece(block).wait_send()
                at = out_ref.at[block]
                sems = (z_send.at[item, block], z_recv.at[item, 0, block])
                remote(at, at, *sems, z, core).wait_recv()
            else:
                z_copy(block, 0, z).wait_send()

        return start, first, second, third, finish

    stages = list(zip(*[work(item) for item in range(count)]))
    for step in range(ctx_count):
        for act in stages[0]:
            act(step)
    for step in range(ctx_count + 2):
        for lag in (0, 1, 2):
            if 0 <= step - lag < ctx_count:
                for act in stages[1 + lag]:
                    act(step - lag)
    for step in range(ctx_count):
        for act in stages[4]:
            act(step)


def scatter_arrays(items, ctx_count, fsdp_count):
    kinds = tuple(kind for kind, grad in items)
    grads = [grad for kind, grad in items]
    count = len(grads)
    chips = fsdp_count // 2
    shapes = [
        (grad.shape[0] // (ctx_count * fsdp_count), grad.shape[1]) for grad in grads
    ]
    half_shapes = [
        (rows // 2, width) if rows % 32 == 0 else (rows, width // 2) for rows, width in shapes
    ]
    dma = pltpu.SemaphoreType.DMA
    leads = [(ctx_count, chips), (ctx_count, chips), (ctx_count,), (ctx_count,)]
    banks = [pltpu.VMEM(lead + shape, LOW) for lead in leads for shape in shapes]
    banks += [pltpu.VMEM((ctx_count,) + shape, LOW) for _ in range(2) for shape in half_shapes]
    banks += [
        pltpu.VMEM((2, ctx_count) + shape if kind == "all" else (1, 1, 16, 128), LOW)
        for kind, shape in zip(kinds, shapes)
    ]
    return pl.pallas_call(
        functools.partial(scatter_kernel, ctx_count, kinds),
        out_shape=[
            jax.ShapeDtypeStruct(shape, FULL)
            if kind == "all"
            else jax.ShapeDtypeStruct((ctx_count,) + shape, LOW)
            for kind, shape in zip(kinds, shapes)
        ],
        in_specs=[pl.BlockSpec(memory_space=pl.ANY)] * count,
        out_specs=[pl.BlockSpec(memory_space=pltpu.VMEM)] * count,
        scratch_shapes=banks
        + [
            dma((count, ctx_count)),
            dma((count, ctx_count)),
            dma((count, ctx_count)),
            dma((count, ctx_count, 4)),
            dma((count, ctx_count, 4)),
            dma((count, ctx_count)),
            dma((count, 2, ctx_count)),
        ],
        compiler_params=pltpu.CompilerParams(
            collective_id=1, has_side_effects=True, vmem_limit_bytes=BIG_VMEM
        ),
        cost_estimate=pl.CostEstimate(flops=0, bytes_accessed=500_000_000, transcendentals=0),
    )(
        *[
            grad.reshape((ctx_count, chips, 2) + shape)
            for grad, shape in zip(grads, shapes)
        ]
    )


HEAD_GROUP = 4
KEYS = 256


def dot_last(left, right):
    return lax.dot_general(left, right, (((1,), (1,)), ((), ())), preferred_element_type=FULL)


def dot_first(left, right):
    return lax.dot_general(left, right, (((0,), (0,)), ((), ())), preferred_element_type=FULL)


def reach(half, rows, ctx_count):
    ctx = lax.axis_index("ctx")
    first = jnp.where(half == 0, ctx, 2 * ctx_count - 1 - ctx) * rows
    return first, lax.div(first + rows + KEYS - 1, KEYS)


def block_scores(query, turned, keys_ref, rope_ref, index, first, rows, scale):
    part = pl.ds(pl.multiple_of(index * KEYS, KEYS), KEYS)
    keys, rope = keys_ref[part, :], rope_ref[part, :]
    scores = (dot_last(query, keys) + dot_last(turned, rope)) * scale
    shape = scores.shape
    at = first + lax.rem(lax.broadcasted_iota(jnp.int32, shape, 0), rows)
    key_at = index * KEYS + lax.broadcasted_iota(jnp.int32, shape, 1)
    return part, keys, rope, scores, at >= key_at


def attend_kernel(
    ctx_count, scale, query_ref, turned_ref, keys_ref, rope_ref, out_ref, log_ref, total, top, norm
):
    heads, rows, width = query_ref.shape
    first, blocks = reach(pl.program_id(0), rows, ctx_count)
    query = query_ref[...].reshape(heads * rows, width)
    turned = turned_ref[...].reshape(heads * rows, -1)
    total[...] = jnp.zeros_like(total)
    norm[...] = jnp.zeros_like(norm)
    top[...] = jnp.full_like(top, masked_score)

    @pl.loop(0, blocks)
    def _(index):
        part, keys, rope, scores, seen = block_scores(
            query, turned, keys_ref, rope_ref, index, first, rows, scale
        )
        scores = jnp.where(seen, scores, masked_score)
        old = top[...]
        new = jnp.maximum(old, jnp.max(scores, axis=1, keepdims=True))
        weights = jnp.exp(scores - new)
        shrink = jnp.exp(old - new)
        top[...] = new
        norm[...] = norm[...] * shrink + jnp.sum(weights, axis=1, keepdims=True)
        total[...] = total[...] * shrink + jnp.dot(
            weights.astype(LOW), keys, preferred_element_type=FULL
        )

    out_ref[...] = (total[...] / norm[...]).astype(LOW).reshape(out_ref.shape)
    log_ref[...] = (top[...] + jnp.log(norm[...])).reshape(log_ref.shape)


def attend_back_kernel(
    ctx_count,
    scale,
    query_ref,
    turned_ref,
    keys_ref,
    rope_ref,
    out_ref,
    log_ref,
    grad_ref,
    query_grad_ref,
    turned_grad_ref,
    keys_grad_ref,
    rope_grad_ref,
    query_total,
    turned_total,
):
    heads, rows, width = query_ref.shape
    first, blocks = reach(pl.program_id(0), rows, ctx_count)
    query = query_ref[...].reshape(heads * rows, width)
    turned = turned_ref[...].reshape(heads * rows, -1)
    grad = grad_ref[...].reshape(heads * rows, width)
    out = out_ref[...].reshape(heads * rows, width)
    logs = log_ref[...].reshape(heads * rows, 1)
    inner = jnp.sum(grad.astype(FULL) * out.astype(FULL), axis=1, keepdims=True)
    query_total[...] = jnp.zeros_like(query_total)
    turned_total[...] = jnp.zeros_like(turned_total)

    @pl.when((pl.program_id(0) == 0) & (pl.program_id(1) == 0))
    def _():
        keys_grad_ref[...] = jnp.zeros_like(keys_grad_ref)
        rope_grad_ref[...] = jnp.zeros_like(rope_grad_ref)

    @pl.loop(0, blocks)
    def _(index):
        part, keys, rope, scores, seen = block_scores(
            query, turned, keys_ref, rope_ref, index, first, rows, scale
        )
        weights = jnp.where(seen, jnp.exp(scores - logs), 0.0)
        change = (weights * (dot_last(grad, keys) - inner) * scale).astype(LOW)
        query_total[...] += jnp.dot(change, keys, preferred_element_type=FULL)
        turned_total[...] += jnp.dot(change, rope, preferred_element_type=FULL)
        keys_grad_ref[part, :] += dot_first(change, query) + dot_first(weights.astype(LOW), grad)
        rope_grad_ref[part, :] += dot_first(change, turned)

    query_grad_ref[...] = query_total[...].astype(LOW).reshape(query_grad_ref.shape)
    turned_grad_ref[...] = turned_total[...].reshape(turned_grad_ref.shape)


def attend_specs(heads, group, rows, widths):
    return [pl.BlockSpec((group, rows, width), lambda half, g: (g, half, 0)) for width in widths]


def whole_spec(array):
    return pl.BlockSpec(array.shape, lambda half, g: (0, 0))


def attend(query, turned, keys, rope, ctx_count, scale):
    heads, count, width = query.shape
    group, rows = HEAD_GROUP, count // 2
    lanes = turned.shape[2]
    return pl.pallas_call(
        functools.partial(attend_kernel, ctx_count, scale),
        grid=(2, heads // group),
        out_shape=(
            jax.ShapeDtypeStruct((heads, count, width), LOW),
            jax.ShapeDtypeStruct((heads, count, 1), FULL),
        ),
        in_specs=attend_specs(heads, group, rows, (width, lanes))
        + [whole_spec(keys), whole_spec(rope)],
        out_specs=tuple(attend_specs(heads, group, rows, (width, 1))),
        scratch_shapes=[
            pltpu.VMEM((group * rows, width), FULL),
            pltpu.VMEM((group * rows, 1), FULL),
            pltpu.VMEM((group * rows, 1), FULL),
        ],
        compiler_params=pltpu.CompilerParams(vmem_limit_bytes=BIG_VMEM),
        cost_estimate=pl.CostEstimate(
            flops=12_000_000_000, bytes_accessed=12_000_000, transcendentals=3_000_000
        ),
    )(query, turned, keys, rope)


def attend_back(query, turned, keys, rope, out, logs, grad, ctx_count, scale):
    heads, count, width = query.shape
    group, rows = HEAD_GROUP, count // 2
    lanes = turned.shape[2]
    return pl.pallas_call(
        functools.partial(attend_back_kernel, ctx_count, scale),
        grid=(2, heads // group),
        out_shape=(
            jax.ShapeDtypeStruct((heads, count, width), LOW),
            jax.ShapeDtypeStruct((heads, count, lanes), FULL),
            jax.ShapeDtypeStruct(keys.shape, FULL),
            jax.ShapeDtypeStruct(rope.shape, FULL),
        ),
        in_specs=attend_specs(heads, group, rows, (width, lanes))
        + [whole_spec(keys), whole_spec(rope)]
        + attend_specs(heads, group, rows, (width, 1, width)),
        out_specs=tuple(
            attend_specs(heads, group, rows, (width, lanes)) + [whole_spec(keys), whole_spec(rope)]
        ),
        scratch_shapes=[
            pltpu.VMEM((group * rows, width), FULL),
            pltpu.VMEM((group * rows, lanes), FULL),
        ],
        compiler_params=pltpu.CompilerParams(vmem_limit_bytes=BIG_VMEM),
        cost_estimate=pl.CostEstimate(
            flops=30_000_000_000, bytes_accessed=30_000_000, transcendentals=3_000_000
        ),
    )(query, turned, keys, rope, out, logs, grad)


PEERS = (6, 7, 2, 4, 3, 5, 1)
COLUMN_AT, GATE_AT, INFO_ROWS = 8, 16, 24


def one_hot(info, z, slots, gated):
    count = info.shape[1]
    at = lax.broadcasted_iota(jnp.int32, (slots, count), 0).astype(FULL)
    plane = z.astype(FULL)
    total = jnp.zeros((slots, count), FULL)
    for route in range(TOP):
        hit = (info[COLUMN_AT + route][None, :] == at) & (info[route][None, :] == plane)
        value = info[GATE_AT + route][None, :] if gated else 1.0
        total = total + jnp.where(hit, value, 0.0)
    return total.astype(LOW)


class Dispatch:
    def __init__(self, ctx_count, gated, rows_ref, info_ref, all_ref, blocks, chosen, arrived, sems):
        self.own_sem, self.all_sem, self.keep_sem = sems[:3]
        self.z_send, self.z_recv, self.p_send, self.p_recv = sems[3:]
        self.ctx_count, self.gated = ctx_count, gated
        self.rows_ref, self.info_ref, self.all_ref = rows_ref, info_ref, all_ref
        self.blocks, self.chosen, self.arrived = blocks, chosen, arrived
        self.z, self.f = lax.axis_index("ctx"), lax.axis_index("fsdp")
        self.core = flip(self.f, 1)

    def z_copy(self, block, way, target):
        at = self.blocks.at[block]
        sems = (self.z_send.at[block, way], self.z_recv.at[block])
        return remote(at, at, *sems, target, self.f)

    def p_copy(self, block, place):
        to = toggled(self.f, PEERS[place])
        sems = (self.p_send.at[block, place], self.p_recv.at[block, place])
        return remote(
            self.chosen.at[block, to], self.arrived.at[block, self.f], *sems, self.z, to
        )

    def keep(self, block):
        source, target = self.chosen.at[block, self.f], self.arrived.at[block, self.f]
        return pltpu.make_async_copy(source, target, self.keep_sem.at[block])

    def store(self, block):
        source, target = self.blocks.at[block], self.all_ref.at[block]
        return pltpu.make_async_copy(source, target, self.all_sem.at[block])

    def begin(self):
        own = pltpu.make_async_copy(self.rows_ref, self.blocks.at[self.z], self.own_sem)
        own.start()
        own.wait()

    def take(self, step):
        block = nearest(self.z, step)
        if step > 0:
            at = self.blocks.at[block]
            sems = (self.z_send.at[block, 0], self.z_recv.at[block])
            remote(at, at, *sems, self.z, self.core).wait_recv()
        both_ways(
            self.z, block, self.ctx_count, lambda way, to: self.z_copy(block, way, to).start()
        )
        self.store(block).start()

    def choose(self, block):
        groups, share, width = self.chosen.shape[1:]
        choose = one_hot(self.info_ref[block], self.z, groups * share, self.gated)

        @pl.loop(0, width, step=256)
        def _(start):
            part = pl.ds(pl.multiple_of(start, 256), 256)
            tile = jnp.dot(choose, self.blocks[block, :, part], preferred_element_type=FULL)
            self.chosen[block, :, :, part] = tile.astype(LOW).reshape(groups, share, 256)

        for place in range(len(PEERS)):
            self.p_copy(block, place).start()
        self.keep(block).start()

    def await_slots(self, block):
        self.keep(block).wait()
        for place in range(len(PEERS)):
            at = self.arrived.at[block, toggled(self.f, PEERS[place])]
            sems = (self.p_send.at[block, place], self.p_recv.at[block, place])
            remote(at, at, *sems, self.z, self.core).wait_recv()

    def finish(self):
        for step in range(self.ctx_count):
            block = nearest(self.z, step)
            self.store(block).wait()
            both_ways(
                self.z,
                block,
                self.ctx_count,
                lambda way, to: self.z_copy(block, way, to).wait_send(),
            )
            for place in range(len(PEERS)):
                self.p_copy(block, place).wait_send()


def dispatch_scratch(ctx_count, fsdp_count, count, share, width):
    dma = pltpu.SemaphoreType.DMA
    return [
        pltpu.VMEM((ctx_count, count, width), LOW),
        pltpu.VMEM((ctx_count, fsdp_count, share, width), LOW),
    ], [
        dma,
        dma((ctx_count,)),
        dma((ctx_count,)),
        dma((ctx_count, 2)),
        dma((ctx_count,)),
        dma((ctx_count, len(PEERS))),
        dma((ctx_count, len(PEERS))),
    ]


def gather_kernel(ctx_count, kinds, *refs):
    count = len(kinds)
    shards, rows_ref = refs[:count], refs[count]
    outs, all_ref, slots_ref = refs[count + 1 : 2 * count + 1], refs[2 * count + 1], refs[2 * count + 2]
    blocks, chosen = refs[2 * count + 3 : 2 * count + 5]
    own_sem, z_send, z_recv, p_send, p_recv, c_send, c_recv = refs[2 * count + 5 : 2 * count + 12]
    z, f = lax.axis_index("ctx"), lax.axis_index("fsdp")
    core, x_near, y_near = flip(f, 1), flip(f, 2), flip(f, 4)
    far = flip(x_near, 4)
    move = Dispatch(
        ctx_count, True, rows_ref, outs[0], all_ref, blocks, chosen, slots_ref, refs[2 * count + 12 :]
    )
    greet(z, f, PEERS, ctx_count, True)

    def slot(item, step):
        return 0 if kinds[item] == "plane" else nearest(z, step)

    def steps(item, step):
        if kinds[item] == "expert":
            return False
        return step == 0 if kinds[item] == "plane" else 0 <= step < ctx_count

    side = lax.rem(f, 2)

    def expert_pieces(item, act):
        half = shards[item].shape[1] // 2
        for which in range(2):
            for part in range(2):
                source = shards[item].at[which, pl.ds(part * half, half)]
                target = outs[item].at[z]
                to_z = 2 * side + which
                here = (to_z == z) & (side == part)

                @pl.when(here)
                def _():
                    act(pltpu.make_async_copy(source, target, own_sem.at[item]), True)

                @pl.when(jnp.logical_not(here))
                def _():
                    sems = (z_send.at[item, 2 * which + part, 0], z_recv.at[item, z])
                    act(remote(source, target, *sems, to_z, f - side + part), False)

    def expert_arrived(item):
        for origin in range(ctx_count):
            at = outs[item].at[origin]
            mine = (origin == z) & (lax.div(z, 2) == side)

            @pl.when(jnp.logical_not(mine))
            def _():
                sems = (z_send.at[item, 0, 0], z_recv.at[item, origin])
                remote(at, at, *sems, z, core).wait_recv()

    def z_view(item, block):
        return outs[item].at[block] if kinds[item] == "column" else outs[item].at[block, f]

    def own(item):
        source = shards[item].at[z] if kinds[item] == "line" else shards[item]
        return pltpu.make_async_copy(source, z_view(item, slot(item, 0)), own_sem.at[item])

    def z_copy(item, block, way, target):
        at = z_view(item, block)
        return remote(at, at, z_send.at[item, block, way], z_recv.at[item, block], target, f)

    def piece(item, step):
        target = lax.rem(z + step, ctx_count)
        return remote(
            shards[item].at[target],
            outs[item].at[z, f],
            z_send.at[item, target, 0],
            z_recv.at[item, z],
            target,
            f,
        )

    def part(item, block, at, which):
        rows, columns = halves(*outs[item].shape[2:])[which]
        return outs[item].at[block, at, rows, columns]

    def p_copy(item, block, which):
        at = (
            lambda: outs[item].at[block, f],
            lambda: outs[item].at[block, f],
            lambda: part(item, block, x_near, 0),
            lambda: part(item, block, y_near, 1),
        )[which]()
        to = (x_near, y_near, y_near, x_near)[which]
        sems = (p_send.at[item, block, which], p_recv.at[item, block, which])
        return remote(at, at, *sems, z, to)

    def p_arrived(item, block, which):
        at = (
            lambda: outs[item].at[block, x_near],
            lambda: outs[item].at[block, y_near],
            lambda: part(item, block, far, 0),
            lambda: part(item, block, far, 1),
        )[which]()
        sems = (p_send.at[item, block, which], p_recv.at[item, block, which])
        remote(at, at, *sems, z, x_near).wait_recv()

    def c_copy(item, block, which):
        at = outs[item].at[block, (f, x_near, y_near, far)[which]]
        sems = (c_send.at[item, block, which], c_recv.at[item, block, which])
        return remote(at, at, *sems, z, core)

    def c_arrived(item, block, which):
        at = outs[item].at[block, flip((f, x_near, y_near, far)[which], 1)]
        sems = (c_send.at[item, block, which], c_recv.at[item, block, which])
        remote(at, at, *sems, z, core).wait_recv()

    def take(step):
        for item in range(count):
            if not steps(item, step):
                continue
            block = slot(item, step)
            if step == 0:
                own(item).wait()
            else:
                at = z_view(item, block)
                sems = (z_send.at[item, block, 0], z_recv.at[item, block])
                remote(at, at, *sems, z, core).wait_recv()
            if kinds[item] in ("all", "column"):
                both_ways(
                    z, block, ctx_count, lambda way, to: z_copy(item, block, way, to).start()
                )
        move.take(step)

    def first(item, step):
        block = slot(item, step)
        p_copy(item, block, 0).start()
        p_copy(item, block, 1).start()
        c_copy(item, block, 0).start()

    def second(item, step):
        block = slot(item, step)
        for which in (0, 1):
            p_arrived(item, block, which)
            p_copy(item, block, which + 2).start()
            c_copy(item, block, which + 1).start()

    def third(item, step):
        block = slot(item, step)
        p_arrived(item, block, 2)
        p_arrived(item, block, 3)
        c_copy(item, block, 3).start()

    experts = [item for item in range(count) if kinds[item] == "expert"]
    for item in range(count):
        if kinds[item] == "expert":
            continue
        own(item).start()
        if kinds[item] == "line":
            for step in range(1, ctx_count):
                piece(item, step).start()
    move.begin()
    for step in range(ctx_count + 2):
        if step < ctx_count:
            along_order(z, ctx_count, step, take)
        if step in (1, 3):
            for item in experts[step // 2 :: 2]:
                expert_pieces(item, lambda copy, local: copy.start())
        for lag, stage in ((0, first), (1, second), (2, third)):
            for item in range(count):
                if steps(item, step - lag) and kinds[item] != "column":
                    stage(item, step - lag)
            if lag == 0 and step < ctx_count:
                move.choose(nearest(z, step))
    for step in range(ctx_count):
        move.await_slots(nearest(z, step))
    move.finish()
    for item in experts:
        expert_arrived(item)
        expert_pieces(item, lambda copy, local: copy.wait() if local else copy.wait_send())
    for item in range(count):
        for step in range(ctx_count):
            if not steps(item, step):
                continue
            block = slot(item, step)
            if kinds[item] != "column":
                for which in range(4):
                    c_arrived(item, block, which)
                    p_copy(item, block, which).wait_send()
                    c_copy(item, block, which).wait_send()
            if kinds[item] == "line" and step > 0:
                piece(item, step).wait_send()
            if kinds[item] in ("all", "column"):
                both_ways(
                    z, block, ctx_count, lambda way, to: z_copy(item, block, way, to).wait_send()
                )


def gather_arrays(items, rows, slots, ctx_count, fsdp_count):
    kinds = tuple(kind for kind, shard in items)
    shards = [shard for kind, shard in items]
    lead = {
        "all": (ctx_count, fsdp_count),
        "line": (ctx_count, fsdp_count),
        "plane": (1, fsdp_count),
        "column": (ctx_count,),
    }
    shapes = [
        (ctx_count, shard.shape[1] // 2, shard.shape[2])
        if kind == "expert"
        else lead[kind] + (shard.shape[1:] if kind == "line" else shard.shape)
        for kind, shard in items
    ]
    row_count, width = rows.shape
    share = slots // fsdp_count
    shapes += [(ctx_count, row_count, width), (ctx_count, fsdp_count, share, width)]
    buffers, sems = dispatch_scratch(ctx_count, fsdp_count, row_count, share, width)
    count = len(items)
    dma = pltpu.SemaphoreType.DMA
    four = dma((count, ctx_count, 4))
    anywhere = pl.BlockSpec(memory_space=pl.ANY)
    results = pl.pallas_call(
        functools.partial(gather_kernel, ctx_count, kinds),
        out_shape=[
            jax.ShapeDtypeStruct(shape, item.dtype)
            for shape, item in zip(shapes, shards + [rows, rows])
        ],
        in_specs=[anywhere] * (count + 1),
        out_specs=[pl.BlockSpec(memory_space=pltpu.VMEM)] + [anywhere] * (count + 1),
        scratch_shapes=buffers
        + [
            dma((count,)),
            dma((count, ctx_count, 2)),
            dma((count, ctx_count)),
            four,
            four,
            four,
            four,
        ]
        + sems,
        compiler_params=pltpu.CompilerParams(
            collective_id=0, has_side_effects=True, vmem_limit_bytes=BIG_VMEM
        ),
        cost_estimate=pl.CostEstimate(
            flops=2_000_000_000, bytes_accessed=800_000_000, transcendentals=0
        ),
    )(*shards, rows)
    return results[:count], results[count], results[count + 1]


def tiles(width, size=256):
    return width // size, width % size


def each_tile(width, act, size=256):
    whole, rest = tiles(width, size)

    @pl.loop(0, whole)
    def _(index):
        act(pl.ds(pl.multiple_of(index * size, size), size))

    if rest:
        act(pl.ds(whole * size, rest))


def expert_kernel(ctx_count, rows_ref, info_ref, *refs):
    weight_refs, grads_ref = (refs[0:2], refs[2:4], refs[4:6]), refs[6]
    all_ref, slots_ref, hidden_ref, gate_back_ref, up_back_ref, back_ref, result_ref = refs[7:14]
    blocks, chosen, arrived, gate, up, down, grads = refs[14:21]
    hidden, gate_back, up_back, back, result = refs[21:26]
    weight_sem, grad_sem, slot_sem, side_sem, back_sem = refs[26:31]
    move = Dispatch(
        ctx_count, False, rows_ref, info_ref, all_ref, blocks, chosen, arrived, refs[31:]
    )
    slots, width = back.shape
    units = hidden.shape[1]
    order = [nearest(move.z, step) for step in range(ctx_count)]

    def block_at(step):
        block = order[0]
        for place in range(1, ctx_count):
            block = jnp.where(step == place, order[place], block)
        return block

    loads = []
    for which, target in enumerate((gate, up, down)):
        for place, source in enumerate(weight_refs[which]):
            side = lax.rem(move.f, 2)
            member = 1 - side if place else side
            half, piece_width = source.shape[1:]
            for origin in range(ctx_count):
                if which < 2:
                    start = pl.multiple_of((2 * origin + member) * half, half)
                    at = target.at[pl.ds(start, half)]
                else:
                    start = pl.multiple_of(member * half, half)
                    at = target.at[pl.ds(start, half), pl.ds(origin * piece_width, piece_width)]
                sem = weight_sem.at[which, place, origin]
                loads.append(pltpu.make_async_copy(source.at[origin], at, sem))

    def load_grads(step):
        slot = lax.rem(step, 2)
        return pltpu.make_async_copy(
            grads_ref.at[block_at(step)], grads.at[slot], grad_sem.at[slot]
        )

    def store_slots(block):
        return pltpu.make_async_copy(arrived.at[block], slots_ref.at[block], slot_sem.at[block])

    def store_sides(block):
        return [
            pltpu.make_async_copy(source, target.at[block], side_sem.at[place])
            for place, (source, target) in enumerate(
                ((hidden, hidden_ref), (gate_back, gate_back_ref), (up_back, up_back_ref))
            )
        ]

    def store_back(block):
        return pltpu.make_async_copy(back, back_ref.at[block], back_sem.at[0])

    def store_result(block):
        return pltpu.make_async_copy(result, result_ref.at[block], back_sem.at[1])

    greet(move.z, move.f, PEERS, ctx_count)
    move.begin()
    for load in loads:
        load.start()
    load_grads(0).start()
    along_order(move.z, ctx_count, 0, move.take)
    move.choose(order[0])
    along_order(move.z, ctx_count, 1, move.take)
    move.choose(order[1])
    for load in loads:
        load.wait()

    @pl.loop(0, ctx_count)
    def _(step):
        block = block_at(step)
        slot = lax.rem(step, 2)

        @pl.when(step + 1 < ctx_count)
        def _():
            load_grads(step + 1).start()

        load_grads(step).wait()
        move.await_slots(block)
        store_slots(block).start()

        @pl.when(step > 0)
        def _():
            for copy in store_sides(block):
                copy.wait()

        rows = arrived[block].reshape(slots, width)

        def hidden_tile(part):
            pre = jnp.dot(rows, gate[:, part], preferred_element_type=FULL)
            linear = jnp.dot(rows, up[:, part], preferred_element_type=FULL)
            grad = dot_last(grads[slot], down[part, :])
            sigma = jax.nn.sigmoid(pre)
            act = pre * sigma
            hidden[:, part] = (act * linear).astype(LOW)
            up_back[:, part] = (grad * act).astype(LOW)
            gate_back[:, part] = (
                grad * linear * (sigma * (1.0 + pre * (1.0 - sigma)))
            ).astype(LOW)

        each_tile(units, hidden_tile)
        for copy in store_sides(block):
            copy.start()

        for later in range(2, ctx_count):

            @pl.when(step + 2 == later)
            def _():
                along_order(move.z, ctx_count, later, move.take)

        @pl.when(step + 2 < ctx_count)
        def _():
            move.choose(block_at(step + 2))

        @pl.when(step > 0)
        def _():
            store_back(block).wait()
            store_result(block).wait()

        def result_tile(part):
            total = jnp.dot(hidden[...], down[:, part], preferred_element_type=FULL)
            result[:, part] = total.astype(LOW)

        each_tile(width, result_tile)
        store_result(block).start()

        def back_tile(part):
            total = dot_last(gate_back[...], gate[part, :]) + dot_last(up_back[...], up[part, :])
            back[:, part] = total.astype(LOW)

        each_tile(width, back_tile)
        store_back(block).start()

    for step in range(ctx_count):
        store_slots(order[step]).wait()
    for copy in store_sides(order[-1]):
        copy.wait()
    store_back(order[-1]).wait()
    store_result(order[-1]).wait()
    move.finish()


def expert_rows(rows, info, weights, grads, ctx_count, fsdp_count):
    count, width = rows.shape
    slots = grads.shape[1]
    share = slots // fsdp_count
    units = weights[0].shape[2]
    buffers, sems = dispatch_scratch(ctx_count, fsdp_count, count, share, width)
    dma = pltpu.SemaphoreType.DMA
    anywhere = pl.BlockSpec(memory_space=pl.ANY)
    low = lambda *shape: jax.ShapeDtypeStruct((ctx_count,) + shape, LOW)
    vmem = lambda *shape: pltpu.VMEM(shape, LOW)
    return pl.pallas_call(
        functools.partial(expert_kernel, ctx_count),
        out_shape=(
            low(count, width),
            low(fsdp_count, share, width),
            low(slots, units),
            low(slots, units),
            low(slots, units),
            low(slots, width),
            low(slots, width),
        ),
        in_specs=[anywhere, pl.BlockSpec(memory_space=pltpu.VMEM)] + [anywhere] * 7,
        out_specs=(anywhere,) * 7,
        scratch_shapes=buffers
        + [
            vmem(ctx_count, fsdp_count, share, width),
            vmem(width, units),
            vmem(width, units),
            vmem(units, width),
            vmem(2, slots, width),
            vmem(slots, units),
            vmem(slots, units),
            vmem(slots, units),
            vmem(slots, width),
            vmem(slots, width),
            dma((3, 2, ctx_count)),
            dma((2,)),
            dma((ctx_count,)),
            dma((3,)),
            dma((2,)),
        ]
        + sems,
        compiler_params=pltpu.CompilerParams(
            collective_id=4, has_side_effects=True, vmem_limit_bytes=BIG_VMEM
        ),
        cost_estimate=pl.CostEstimate(
            flops=60_000_000_000, bytes_accessed=400_000_000, transcendentals=3_000_000
        ),
    )(rows, info, *weights, grads)


class Combine:
    def __init__(
        self, ctx_count, gated, slots_ref, info_ref, extra_ref, out_ref, buffers, sems
    ):
        self.ctx_count, self.gated = ctx_count, gated
        self.slots_ref, self.info_ref = slots_ref, info_ref
        self.extra_ref, self.out_ref = extra_ref, out_ref
        self.arrived, self.extra, self.parts, self.from_z = buffers
        self.keep_sem, self.extra_sem, self.p_send, self.p_recv, self.z_send, self.z_recv = sems
        self.z, self.f = lax.axis_index("ctx"), lax.axis_index("fsdp")
        self.core = flip(self.f, 1)
        self.order = [nearest(self.z, ctx_count - 1 - step) for step in range(ctx_count)]

    def p_copy(self, block, place):
        to = toggled(self.f, PEERS[place])
        sems = (self.p_send.at[block, place], self.p_recv.at[block, place])
        return remote(
            self.slots_ref.at[block, to], self.arrived.at[block, self.f], *sems, self.z, to
        )

    def keep(self, block):
        source, target = self.slots_ref.at[block, self.f], self.arrived.at[block, self.f]
        return pltpu.make_async_copy(source, target, self.keep_sem.at[block])

    def load(self, step):
        return pltpu.make_async_copy(
            self.extra_ref.at[self.order[step]], self.extra, self.extra_sem
        )

    def place(self, way, block, z):
        return jnp.where(block == z, self.ctx_count, block) if way == 0 else block

    def send_along(self, step, way, to):
        block = self.order[step]
        sems = (self.z_send.at[step], self.z_recv.at[way, block])
        target = self.from_z.at[self.place(way, block, to)]
        return remote(self.parts.at[step], target, *sems, to, self.f)

    def z_arrived(self, block, way):
        at = self.from_z.at[self.place(way, block, self.z)]
        sems = (self.z_send.at[0], self.z_recv.at[way, block])
        remote(at, at, *sems, self.z, self.core).wait_recv()

    def start(self):
        for block in self.order:
            for place in range(len(PEERS)):
                self.p_copy(block, place).start()
            self.keep(block).start()
        self.load(0).start()

    def mix(self, block, target, *ways):
        slots = self.arrived.shape[1] * self.arrived.shape[2]
        choose = one_hot(self.info_ref[block], self.z, slots, self.gated)

        @pl.loop(0, target.shape[1], step=256)
        def _(start):
            part = pl.ds(pl.multiple_of(start, 256), 256)
            total = dot_first(choose, self.arrived[block, :, :, part].reshape(slots, 256))
            total = total + self.extra[:, part].astype(FULL)
            for way in ways:
                total = total + self.from_z[self.place(way, block, self.z), :, part].astype(FULL)
            target[:, part] = total.astype(target.dtype)

    def step(self, step):
        block, z, last = self.order[step], self.z, self.ctx_count - 1
        self.keep(block).wait()
        self.load(step).wait()
        for place in range(len(PEERS)):
            at = self.arrived.at[block, toggled(self.f, PEERS[place])]
            sems = (self.p_send.at[block, place], self.p_recv.at[block, place])
            remote(at, at, *sems, z, self.core).wait_recv()
        if step < last:
            target = self.parts.at[step]
            for way, above in ((1, True), (0, False)):
                heading = (block < z) if above else (block > z)
                has_more = (z < last) if above else (z > 0)

                @pl.when(heading & has_more)
                def _():
                    self.z_arrived(block, way)
                    self.mix(block, target, way)

                @pl.when(heading & jnp.logical_not(has_more))
                def _():
                    self.mix(block, target)

                @pl.when(heading)
                def _():
                    self.send_along(step, way, z - 1 if above else z + 1).start()

            self.load(step + 1).start()
            return

        @pl.when(z > 0)
        def _():
            self.z_arrived(block, 0)

        @pl.when(z < last)
        def _():
            self.z_arrived(block, 1)

        @pl.when(z == 0)
        def _():
            self.mix(block, self.out_ref, 1)

        @pl.when(z == last)
        def _():
            self.mix(block, self.out_ref, 0)

        @pl.when((z > 0) & (z < last))
        def _():
            self.mix(block, self.out_ref, 0, 1)

    def finish(self):
        for step in range(self.ctx_count):
            for place in range(len(PEERS)):
                self.p_copy(self.order[step], place).wait_send()
            if step < self.ctx_count - 1:
                self.send_along(step, 0, self.z).wait_send()


def combine_kernel(ctx_count, info_ref, *refs):
    streams = refs[0:4]
    rows_ref, grads_ref, hidden_ref, gate_back_ref, up_back_ref = refs[4:9]
    outs = refs[9:11]
    gate_grad_ref, up_grad_ref, down_grad_ref = refs[11:14]
    narrow, left, right, gate_tile, up_tile = refs[14:19]
    side_sem, tile_sem, store_sem = refs[19:22]
    buffers, sems = refs[22:30], refs[30:42]
    moves = [
        Combine(
            ctx_count,
            place == 1,
            streams[2 * place],
            info_ref,
            streams[2 * place + 1],
            outs[place],
            buffers[4 * place : 4 * place + 4],
            sems[6 * place : 6 * place + 6],
        )
        for place in range(2)
    ]
    greet(moves[0].z, moves[0].f, PEERS, ctx_count)
    tile_count = rows_ref.shape[1] // 256

    def sides(source, target, place):
        return pltpu.make_async_copy(source, target, side_sem.at[place])

    first_sides = [sides(gate_back_ref, left, 0), sides(up_back_ref, right, 1)]
    last_side = sides(hidden_ref, left, 2)

    def fetch(source, index):
        part = pl.ds(pl.multiple_of(index * 256, 256), 256)
        slot = lax.rem(index, 2)
        return pltpu.make_async_copy(source.at[:, part], narrow.at[slot], tile_sem.at[slot])

    def store(tile, target, place, index):
        part = pl.ds(pl.multiple_of(index * 256, 256), 256)
        return pltpu.make_async_copy(tile, target.at[part, :], store_sem.at[place])

    def products(source, begin, end, pairs):
        @pl.loop(begin, end)
        def _(index):
            @pl.when(index + 1 < tile_count)
            def _():
                fetch(source, index + 1).start()

            fetch(source, index).wait()
            turned = narrow[lax.rem(index, 2)]
            for place, (factor, tile, target) in enumerate(pairs):
                part = dot_first(turned, factor[...]).astype(LOW)

                @pl.when(index > 0)
                def _():
                    store(tile, target, place, index).wait()

                tile[...] = part
                store(tile, target, place, index).start()

    both = ((left, gate_tile, gate_grad_ref), (right, up_tile, up_grad_ref))
    alone = ((left, gate_tile, down_grad_ref),)
    half = tile_count // 2
    for copy in first_sides:
        copy.start()
    fetch(rows_ref, 0).start()
    for move in moves:
        move.start()
    for copy in first_sides:
        copy.wait()
    products(rows_ref, 0, half, both)
    moves[0].step(0)
    products(rows_ref, half, tile_count, both)
    for place, (factor, tile, target) in enumerate(both):
        store(tile, target, place, 0).wait()
    last_side.start()
    fetch(grads_ref, 0).start()
    moves[0].step(1)
    last_side.wait()
    products(grads_ref, 0, half, alone)
    moves[0].step(2)
    products(grads_ref, half, tile_count, alone)
    store(gate_tile, down_grad_ref, 0, 0).wait()
    for step in range(3, ctx_count):
        moves[0].step(step)
    for step in range(ctx_count):
        moves[1].step(step)
    for move in moves:
        move.finish()


def combine_rows(
    slots, extra, out_slots, out_extra, info, sides, ctx_count, fsdp_count
):
    share, width = slots.shape[2:]
    count = extra.shape[1]
    total, units = sides[2].shape
    dma = pltpu.SemaphoreType.DMA
    anywhere = pl.BlockSpec(memory_space=pl.ANY)
    resident = pl.BlockSpec(memory_space=pltpu.VMEM)
    vmem = lambda *shape: pltpu.VMEM(shape, LOW)
    buffers = [
        vmem(ctx_count, fsdp_count, share, width),
        vmem(count, width),
        vmem(ctx_count - 1, count, width),
        vmem(ctx_count + 1, count, width),
    ]
    sems = [
        dma((ctx_count,)),
        dma,
        dma((ctx_count, len(PEERS))),
        dma((ctx_count, len(PEERS))),
        dma((ctx_count - 1,)),
        dma((2, ctx_count)),
    ]
    return pl.pallas_call(
        functools.partial(combine_kernel, ctx_count),
        out_shape=(jax.ShapeDtypeStruct((count, width), FULL),) * 2
        + (jax.ShapeDtypeStruct((width, units), LOW),) * 3,
        in_specs=[resident] + [anywhere] * 9,
        out_specs=(resident,) * 2 + (anywhere,) * 3,
        scratch_shapes=[
            vmem(2, total, 256),
            vmem(total, units),
            vmem(total, units),
            vmem(256, units),
            vmem(256, units),
            dma((3,)),
            dma((2,)),
            dma((2,)),
        ]
        + buffers * 2
        + sems * 2,
        compiler_params=pltpu.CompilerParams(
            collective_id=3, has_side_effects=True, vmem_limit_bytes=BIG_VMEM
        ),
        cost_estimate=pl.CostEstimate(
            flops=40_000_000_000, bytes_accessed=600_000_000, transcendentals=0
        ),
    )(info, slots, extra, out_slots, out_extra, *sides)


def mm(subscripts, left, right):
    return jnp.einsum(subscripts, left, right, preferred_element_type=FULL)


def member_pairs(fsdp_count, members, step):
    return [
        (f, f // members * members + (f % members + step) % members) for f in range(fsdp_count)
    ]


def by_member(own, others, member, members):
    if members == 2:
        first = member == 0
        return jnp.stack([jnp.where(first, own, others[0]), jnp.where(first, others[0], own)])
    stack = jnp.stack([own] + others)
    return jnp.take(stack, (member - jnp.arange(members)) % members, axis=0)


def part_of(array, member, step, members):
    return lax.dynamic_index_in_dim(array, (member + step) % members, 0, keepdims=False)


def swap_parts(array, members, fsdp_count):
    member = lax.axis_index("fsdp") % members
    others = [
        lax.ppermute(
            part_of(array, member, step, members), "fsdp", member_pairs(fsdp_count, members, step)
        )
        for step in range(1, members)
    ]
    return by_member(part_of(array, member, 0, members), others, member, members)


def share_parts(array, members, fsdp_count):
    member = lax.axis_index("fsdp") % members
    others = [
        lax.ppermute(array, "fsdp", member_pairs(fsdp_count, members, step))
        for step in range(1, members)
    ]
    return by_member(array, others, member, members)


def sum_parts(array, members, fsdp_count):
    member = lax.axis_index("fsdp") % members
    total = part_of(array, member, 0, members).astype(FULL)
    for step in range(1, members):
        total = total + lax.ppermute(
            part_of(array, member, step, members), "fsdp", member_pairs(fsdp_count, members, step)
        ).astype(FULL)
    return total.astype(LOW)


def routing(info, z, slots, gated):
    at = jnp.arange(slots, dtype=jnp.int32).astype(FULL)[:, None, None]
    hit = (info[:, None, COLUMN_AT : COLUMN_AT + TOP].swapaxes(2, 3) == at.reshape(-1, 1, 1)) & (
        info[:, None, :TOP].swapaxes(2, 3) == z.astype(FULL)
    )
    values = info[:, None, GATE_AT : GATE_AT + TOP].swapaxes(2, 3) if gated else 1.0
    return jnp.sum(jnp.where(hit, values, 0.0), axis=3).astype(LOW)


def swap_slots(slots):
    return lax.all_to_all(slots, "fsdp", split_axis=1, concat_axis=1, tiled=True)


def send_rows(rows, info, slots, gated, ctx_count, fsdp_count):
    every = lax.all_gather(rows, "ctx", axis=0)
    choose = routing(info, lax.axis_index("ctx"), slots, gated)
    chosen = mm("bst,btd->bsd", choose, every).astype(LOW)
    return every, swap_slots(chosen.reshape(ctx_count, fsdp_count, -1, rows.shape[1]))


def run_expert(rows, info, pieces, grads, ctx_count, fsdp_count):
    members = ctx_count // EXP_DEV
    if (ctx_count, fsdp_count) == (4, 8):
        pairs = member_pairs(fsdp_count, members, 1)
        weights = []
        for piece in pieces:
            weights += [piece, lax.ppermute(piece, "fsdp", pairs)]
        return expert_rows(rows, info, weights, grads, ctx_count, fsdp_count)
    whole = [share_parts(piece, members, fsdp_count).swapaxes(0, 1) for piece in pieces]
    units = whole[0].shape[3]
    gate, up = [item.reshape(-1, units) for item in whole[:2]]
    down = whole[2].transpose(1, 2, 0, 3).reshape(units, -1)
    every, arrived = send_rows(rows, info, grads.shape[1], False, ctx_count, fsdp_count)
    slots = arrived.reshape(grads.shape)
    pre = mm("bsd,df->bsf", slots, gate)
    linear = mm("bsd,df->bsf", slots, up)
    act, slope = silu_slope(pre)
    grad = mm("bsd,fd->bsf", grads, down)
    hidden = (act * linear).astype(LOW)
    up_back = (grad * act).astype(LOW)
    gate_back = (grad * linear * slope).astype(LOW)
    back = (mm("bsf,df->bsd", gate_back, gate) + mm("bsf,df->bsd", up_back, up)).astype(LOW)
    result = mm("bsf,fd->bsd", hidden, down).astype(LOW)
    return every, arrived, hidden, gate_back, up_back, back, result


def return_slots(slots, info, extra, gated):
    back = swap_slots(slots).reshape(slots.shape[0], -1, slots.shape[3])
    choose = routing(info, lax.axis_index("ctx"), back.shape[1], gated)
    total = (mm("bst,bsd->btd", choose, back) + extra).astype(LOW)
    return lax.psum_scatter(total, "ctx", scatter_dimension=0, tiled=False).astype(FULL)


def return_both(slots, extra, out_slots, out_extra, info, sides, ctx_count, fsdp_count):
    extra, out_extra = extra.astype(LOW), out_extra.astype(LOW)
    if (ctx_count, fsdp_count) == (4, 8):
        return combine_rows(
            slots, extra, out_slots, out_extra, info, sides, ctx_count, fsdp_count
        )
    rows, grads, hidden, gate_back, up_back = sides
    return (
        return_slots(slots, info, extra, False),
        return_slots(out_slots, info, out_extra, True),
        mm("sd,sf->df", rows, gate_back).astype(LOW),
        mm("sd,sf->df", rows, up_back).astype(LOW),
        mm("sd,sf->df", grads, hidden).astype(LOW),
    )


def swap_experts(weight, members, fsdp_count):
    pieces = weight.reshape((EXP_DEV, members, weight.shape[1] // members) + weight.shape[2:])
    pieces = swap_parts(pieces.swapaxes(0, 1), members, fsdp_count)
    return pieces.reshape((-1,) + pieces.shape[2:])


def gather_all(items, rows, slots, ctx_count, fsdp_count):
    if (ctx_count, fsdp_count) == (4, 8):
        return gather_arrays(items, rows, slots, ctx_count, fsdp_count)
    results = []
    for kind, shard in items:
        if kind == "line":
            shard = lax.all_to_all(shard, "ctx", split_axis=0, concat_axis=0, tiled=True)
            result = lax.all_gather(shard, "fsdp", axis=1)
        elif kind == "plane":
            result = lax.all_gather(shard, "fsdp", axis=0)[None]
        elif kind == "column":
            result = lax.all_gather(shard, "ctx", axis=0)
        elif kind == "expert":
            result = along_line(swap_experts(shard, ctx_count // EXP_DEV, fsdp_count))
        else:
            result = lax.all_gather(shard, ("ctx", "fsdp"), axis=0)
            result = result.reshape((ctx_count, fsdp_count) + shard.shape)
        results.append(result)
    return (results,) + send_rows(rows, results[0], slots, True, ctx_count, fsdp_count)


def scatter_all(items, ctx_count, fsdp_count):
    items = [(kind, grad.astype(LOW)) for kind, grad in items]
    if (ctx_count, fsdp_count) == (4, 8):
        return scatter_arrays(items, ctx_count, fsdp_count)
    results = []
    for kind, grad in items:
        if kind == "line":
            grad = grad.reshape(ctx_count, fsdp_count, -1, grad.shape[1]).swapaxes(0, 1)
            grad = lax.psum_scatter(grad, "fsdp", scatter_dimension=0, tiled=False)
            results.append(along_line(grad))
        else:
            total = lax.psum_scatter(grad, ("ctx", "fsdp"), scatter_dimension=0, tiled=True)
            results.append(total.astype(FULL))
    return results


def along_line(array):
    return lax.all_to_all(array, "ctx", split_axis=0, concat_axis=0, tiled=True)


def after(values, *others):
    tied = lax.optimization_barrier((tuple(values), others))
    return tied[0]


def local(
    tokens,
    routes,
    gate_values,
    cotangent,
    attention_gain,
    query_weight,
    latent_weight,
    latent_gain,
    expand_weight,
    output_weight,
    feedforward_gain,
    shared_gate,
    shared_up,
    shared_down,
    expert_gate,
    expert_up,
    expert_down,
):
    row_count = tokens.shape[1]
    model_width = tokens.shape[2]
    ctx_count = lax.axis_size("ctx")
    fsdp_count = lax.axis_size("fsdp")
    device_count = ctx_count * fsdp_count
    experts_total = EXP_DEV * fsdp_count
    capacity = row_count * TOP * 4 // (3 * experts_total)
    members = ctx_count // EXP_DEV
    plane_experts = experts_total // ctx_count
    plane_slots = plane_experts * capacity
    share = capacity // members
    sequence = ctx_count * row_count
    z = lax.axis_index("ctx")
    score_scale = (NOPE + ROPE) ** (-0.5)
    source = tokens[0].astype(FULL)
    cot_low = cotangent[0]
    cot_full = cot_low.astype(FULL)
    positions = stored_positions(
        z * row_count + jnp.arange(row_count, dtype=jnp.int32), row_count, 2 * ctx_count
    )
    dense_rows = latent_weight.shape[0]
    gain_rows = latent_gain.shape[0]
    rotary_end = LATENT + ROPE
    hidden_units = expert_gate.shape[2]
    shared_units = shared_gate.shape[1] // ctx_count

    down_swapped = swap_experts(expert_down, members, fsdp_count)

    local_routes = routes[0]
    expert_index = jnp.arange(experts_total, dtype=jnp.int32)
    member_of = (local_routes[..., None] == expert_index).astype(FULL)
    counts = jnp.sum(member_of, axis=1)
    before = jnp.cumsum(counts, axis=0) - counts
    within = jnp.sum(member_of * before[:, None, :], axis=-1).astype(jnp.int32)
    info = jnp.zeros((INFO_ROWS, row_count), FULL)
    info = info.at[:TOP].set((local_routes % ctx_count).astype(FULL).T)
    info = info.at[COLUMN_AT : COLUMN_AT + TOP].set(
        (local_routes // ctx_count * capacity + within).astype(FULL).T
    )
    info = info.at[GATE_AT : GATE_AT + TOP].set(gate_values[0].T)

    tail = jnp.concatenate(
        [
            latent_weight,
            attention_gain[:, None],
            feedforward_gain[:, None],
            jnp.pad(latent_gain, (0, dense_rows - gain_rows))[:, None],
            jnp.zeros((dense_rows, 256 - ROPE - 3), LOW),
        ],
        axis=1,
    )

    def by_line(weight):
        return weight.reshape(dense_rows, ctx_count, shared_units).swapaxes(0, 1)

    dense = (
        info,
        query_weight,
        tail,
        expand_weight,
        output_weight,
        by_line(shared_gate),
        by_line(shared_up),
        shared_down,
        expert_gate,
        expert_up,
    )
    kinds = ("column", "all", "all", "all", "all", "line", "line", "plane", "expert", "expert")
    gathered, all_cot, arrived_grad = gather_all(
        list(zip(kinds, dense)), cot_low, plane_slots, ctx_count, fsdp_count
    )
    all_info = gathered[0]
    full_query, full_tail, full_expand, full_output, full_sgate, full_sup, full_sdown = [
        item.reshape(-1, item.shape[-1]) for item in gathered[1:-2]
    ]
    gate_moved, up_moved = gathered[-2:]
    full_latent = full_tail[:, :rotary_end]
    gain_one = full_tail[:, rotary_end].astype(FULL)
    gain_two = full_tail[:, rotary_end + 1].astype(FULL)
    gain_latent = (
        full_tail[:, rotary_end + 2].reshape(device_count, dense_rows)[:, :gain_rows]
    ).reshape(LATENT).astype(FULL)

    all_cot = all_cot.reshape(sequence, model_width)
    arrived_grad = arrived_grad.reshape(ctx_count, plane_slots, model_width)

    plain_one, inverse_one = norm_forward(source)
    normed = (plain_one * gain_one).astype(LOW)
    (query_raw,) = after((jnp.dot(normed, full_query, preferred_element_type=FULL),))
    query_raw = query_raw.reshape(row_count, HEADS, NOPE + ROPE)
    query_nope = query_raw[:, :, :NOPE].astype(LOW)
    query_rope = rotary(query_raw[:, :, NOPE:], positions, 1.0).astype(LOW)
    latent_raw = jnp.dot(normed, full_latent, preferred_element_type=FULL)
    plain_latent, inverse_latent = norm_forward(latent_raw[:, :LATENT])
    latent_norm = (plain_latent * gain_latent).astype(LOW)
    key_rope = rotary(latent_raw[:, LATENT:], positions, 1.0).astype(LOW)
    half_rows = row_count // 2
    pad_rope = ((0, 0), (0, 128 - ROPE))
    keys = lax.all_gather(
        jnp.concatenate([latent_norm, jnp.pad(key_rope, pad_rope)], axis=1), "ctx", axis=0
    )
    keys = keys.reshape(ctx_count, 2, half_rows, LATENT + 128)
    keys = jnp.concatenate([keys[:, 0], keys[::-1, 1]]).reshape(sequence, LATENT + 128)
    all_latent, all_keys = (keys[:, :LATENT], keys[:, LATENT:])
    expand = full_expand.reshape(LATENT, HEADS, NOPE + VDIM)
    expand_key = expand[:, :, :NOPE]
    expand_value = expand[:, :, NOPE:]
    query_latent = mm("thd,chd->htc", query_nope, expand_key).astype(LOW)
    (down_swapped,) = after((down_swapped,), normed)
    down_moved = along_line(down_swapped)
    query_turned = jnp.pad(query_rope.swapaxes(0, 1), ((0, 0),) + pad_rope)
    latent_out, log_total = attend(
        query_latent, query_turned, all_latent, all_keys, ctx_count, score_scale
    )
    values_out = (
        mm("htc,chv->thv", latent_out, expand_value).astype(LOW).reshape(row_count, HEADS * VDIM)
    )
    middle = source + jnp.dot(values_out, full_output, preferred_element_type=FULL)
    plain_two, inverse_two = norm_forward(middle)
    second = (plain_two * gain_two).astype(LOW)

    (down_moved,) = after((down_moved,), latent_out)
    (second_sent,) = after((second,), down_moved)
    all_second, arrived_rows, hidden_act, gate_back, up_back, arrived_back, result = run_expert(
        second_sent,
        all_info,
        (gate_moved, up_moved, down_moved),
        arrived_grad,
        ctx_count,
        fsdp_count,
    )
    all_second = all_second.reshape(sequence, model_width)
    hidden_act, gate_back, up_back = [
        item.reshape(-1, hidden_units) for item in (hidden_act, gate_back, up_back)
    ]
    shared_g = jnp.dot(all_second, full_sgate, preferred_element_type=FULL)
    shared_u = jnp.dot(all_second, full_sup, preferred_element_type=FULL)
    shared_silu, shared_slope = silu_slope(shared_g)
    shared_hidden = (shared_silu * shared_u).astype(LOW)
    shared_hidden_grad = mm("td,fd->tf", all_cot, full_sdown)
    sup_back = (shared_hidden_grad * shared_silu).astype(LOW)
    sgate_back = (shared_hidden_grad * shared_u * shared_slope).astype(LOW)
    shared_second_grad = mm("tf,df->td", sgate_back, full_sgate) + mm(
        "tf,df->td", sup_back, full_sup
    )
    slots_shape = (ctx_count, fsdp_count, share, model_width)
    rows_shape = (ctx_count, row_count, model_width)
    shared_out = jnp.dot(shared_hidden, full_sdown, preferred_element_type=FULL)
    second_grad, out_sum, gate_grad, up_grad, down_grad = return_both(
        arrived_back.reshape(slots_shape),
        shared_second_grad.reshape(rows_shape),
        result.reshape(slots_shape),
        shared_out.reshape(rows_shape),
        all_info,
        (
            arrived_rows.reshape(-1, model_width),
            arrived_grad.reshape(-1, model_width),
            hidden_act,
            gate_back,
            up_back,
        ),
        ctx_count,
        fsdp_count,
    )
    layer_out = (middle + out_sum).astype(LOW)[None]

    def line_sum(grad):
        grad = grad.reshape(ctx_count, members, -1, hidden_units).swapaxes(0, 1)
        return sum_parts(grad, members, fsdp_count)

    gate_sum, up_sum, down_sum = (line_sum(gate_grad), line_sum(up_grad), line_sum(down_grad))
    gate_returned = along_line(gate_sum)
    sgate_back, sup_back = after((sgate_back, sup_back), gate_sum)
    shared_hidden, sgate_back, sup_back = after(
        (shared_hidden, sgate_back, sup_back), second_grad
    )
    sgate_grad = mm("td,tf->df", all_second, sgate_back).astype(LOW)
    sup_grad = mm("td,tf->df", all_second, sup_back).astype(LOW)
    sdown_grad = mm("tf,td->fd", shared_hidden, all_cot).astype(LOW)
    (second_grad,) = after(
        (second_grad,), gate_sum, up_sum, down_sum, sgate_grad, sup_grad, sdown_grad
    )
    sdown_grad = lax.psum_scatter(sdown_grad, "fsdp", scatter_dimension=0, tiled=True)

    middle_part, gain_two_grad = norm_backward(second_grad, plain_two, inverse_two, gain_two)
    middle_grad = cot_full + middle_part
    attended_grad = middle_grad.astype(LOW)
    output_weight_grad = mm("tv,td->vd", values_out, attended_grad)
    values_grad = (
        mm("td,vd->tv", attended_grad, full_output).astype(LOW).reshape(row_count, HEADS, VDIM)
    )
    latent_out_grad = mm("thv,chv->htc", values_grad, expand_value).astype(LOW)
    (latent_out_grad,) = after((latent_out_grad,), gate_returned)
    (up_sum,) = after((up_sum,), gate_returned, latent_out_grad)
    up_returned = along_line(up_sum)
    query_latent_grad, turned_grad, all_latent_grad, all_keys_grad = attend_back(
        query_latent,
        query_turned,
        all_latent,
        all_keys,
        latent_out,
        log_total,
        latent_out_grad,
        ctx_count,
        score_scale,
    )
    query_rope_grad = turned_grad[:, :, :ROPE].swapaxes(0, 1)
    keys_part = jnp.concatenate([all_latent_grad, all_keys_grad[:, :ROPE]], axis=1)
    keys_part = keys_part.reshape(2, ctx_count, half_rows, LATENT + ROPE)
    keys_part = jnp.stack([keys_part[0], keys_part[1, ::-1]], axis=1)
    keys_part = lax.psum_scatter(
        keys_part.reshape(sequence, LATENT + ROPE).astype(LOW),
        "ctx",
        scatter_dimension=0,
        tiled=True,
    ).astype(FULL)
    latent_grad, keys_grad = (keys_part[:, :LATENT], keys_part[:, LATENT:])
    expand_value_grad = mm("htc,thv->chv", latent_out, values_grad)

    sdown_grad = sdown_grad.astype(FULL)

    query_nope_grad = mm("htc,chd->thd", query_latent_grad, expand_key)
    expand_key_grad = mm("htc,thd->chd", query_latent_grad, query_nope)
    expand_grad = jnp.concatenate([expand_key_grad, expand_value_grad], axis=-1).reshape(
        LATENT, HEADS * (NOPE + VDIM)
    )
    query_grad = (
        jnp.concatenate([query_nope_grad, rotary(query_rope_grad, positions, -1.0)], axis=-1)
        .astype(LOW)
        .reshape(row_count, HEADS * (NOPE + ROPE))
    )
    latent_part_grad, gain_latent_grad = norm_backward(
        latent_grad, plain_latent, inverse_latent, gain_latent
    )
    latent_raw_grad = jnp.concatenate(
        [latent_part_grad, rotary(keys_grad, positions, -1.0)], axis=-1
    ).astype(LOW)
    query_weight_grad = mm("td,tq->dq", normed, query_grad)
    latent_weight_grad = mm("td,tq->dq", normed, latent_raw_grad)
    normed_grad = mm("tq,dq->td", query_grad, full_query) + mm(
        "tq,dq->td", latent_raw_grad, full_latent
    )
    source_part, gain_one_grad = norm_backward(normed_grad, plain_one, inverse_one, gain_one)
    tokens_grad = (middle_grad + source_part)[None]

    gain_latent_column = jnp.pad(
        gain_latent_grad.reshape(device_count, gain_rows), ((0, 0), (0, dense_rows - gain_rows))
    ).reshape(model_width)
    gains_grad = jnp.stack([gain_one_grad, gain_two_grad, gain_latent_column], axis=1)
    gains_grad = jnp.pad(gains_grad, ((0, 0), (0, 125)))
    (down_sum,) = after((down_sum,), up_returned, query_nope_grad)
    down_returned = along_line(down_sum)
    (gains_grad,) = after((gains_grad,), up_returned)
    dense_grads = (
        query_weight_grad,
        latent_weight_grad,
        gains_grad,
        expand_grad,
        output_weight_grad,
        sgate_grad,
        sup_grad,
    )
    kinds = ("all",) * 5 + ("line",) * 2
    query_sum, latent_sum, gains_sum, expand_sum, output_sum, sgate_sum, sup_sum = scatter_all(
        list(zip(kinds, dense_grads)), ctx_count, fsdp_count
    )

    def joined(pieces):
        return pieces.swapaxes(0, 1).reshape(dense_rows, -1).astype(FULL)

    def owned(moved):
        moved = moved.reshape((members, EXP_DEV) + moved.shape[1:])
        moved = swap_parts(moved, members, fsdp_count).swapaxes(0, 1)
        return moved.reshape(EXP_DEV, -1, hidden_units).astype(FULL)

    expert_grads = (
        owned(gate_returned),
        owned(up_returned),
        owned(down_returned).swapaxes(1, 2),
    )
    return (
        layer_out,
        tokens_grad,
        gains_sum[:, 0],
        query_sum,
        latent_sum,
        gains_sum[:gain_rows, 2],
        expand_sum,
        output_sum,
        gains_sum[:, 1],
        joined(sgate_sum),
        joined(sup_sum),
        sdown_grad,
        expert_grads[0],
        expert_grads[1],
        expert_grads[2],
    )


def solution(mesh):
    in_specs = (
        P("fsdp", "ctx", None),
        P("fsdp", "ctx", None),
        P("fsdp", "ctx", None),
        P("fsdp", "ctx", None),
        P(("ctx", "fsdp")),
        P(("ctx", "fsdp"), None),
        P(("ctx", "fsdp"), None),
        P(("ctx", "fsdp")),
        P(("ctx", "fsdp"), None),
        P(("ctx", "fsdp"), None),
        P(("ctx", "fsdp")),
        P(("ctx", "fsdp"), None),
        P(("ctx", "fsdp"), None),
        P(("ctx", "fsdp"), None),
        P("fsdp", "ctx", None),
        P("fsdp", "ctx", None),
        P("fsdp", None, "ctx"),
    )
    out_specs = (
        P("fsdp", "ctx", None),
        P("fsdp", "ctx", None),
        P(("ctx", "fsdp")),
        P(("ctx", "fsdp"), None),
        P(("ctx", "fsdp"), None),
        P(("ctx", "fsdp")),
        P(("ctx", "fsdp"), None),
        P(("ctx", "fsdp"), None),
        P(("ctx", "fsdp")),
        P(("ctx", "fsdp"), None),
        P(("ctx", "fsdp"), None),
        P(("ctx", "fsdp"), None),
        P("fsdp", "ctx", None),
        P("fsdp", "ctx", None),
        P("fsdp", None, "ctx"),
    )
    return jax.shard_map(local, mesh=mesh, in_specs=in_specs, out_specs=out_specs, check_vma=False)
```
